32 devices in a mesh: gx: 4 (over x, core), gy: 2 (over y), gz: 4 (over z).
Axes of the slice: x: 2, y: 2, z: 4, core: 2. Of those that a mesh axis runs over, the one named last changes fastest.
Arguments:
- right_side: float32 [3, 512, 1024], P(None, None, ('gx', 'gy', 'gz')), may hold values from -6 to 6
- geometry: float32 [6, 32, 32, 512], P(None, 'gx', 'gy', 'gz'), may hold values from -1.4 to 4, as said below
- viscosity: float32 [32, 32, 512], P('gx', 'gy', 'gz'), may hold values from 0.3 to 3
- eig_low: float32 [1], replicated, may hold values from 0.2 to 2
- eig_high: float32 [1], replicated, may hold values from 8 to 12
- element_slot: int32 [32, 32], P(('gx', 'gy', 'gz')), may hold values from 0 to 31, each once within a row
- dirichlet: int32 [2, 3, 32, 512], P(None, None, 'gy', 'gz'), may hold values 0 or 1
Outputs:
- solution_field: float32 [3, 512, 1024], P(None, None, ('gx', 'gy', 'gz'))
The draws below stay inside these ranges and needn't reach their ends.
Inputs may be any that keep to these rules, and one draw needn't show every extreme that they name: `element_slot`: each row holds each number from 0 to 31 once. `geometry`: the six entries of each node, in the order xx, yy, zz, xy, xz, yz, form a symmetric positive definite matrix.
All inputs are finite; a program needn't handle non-finite values. No bound on the sum of `dirichlet` on one device may be relied on, other than what follows from the above.
Results may differ from the reference program's by a relative error of at most 0.0003.
Values sent between devices are 32-bit elements; how exact they have to be, the bound alone decides.
No kernel may reach another device: no remote copies, remote signals or barrier semaphores. Data moves between devices by JAX's collectives and lax.ppermute only.
A program may use at most 64 MiB of HBM per device.

```python
import math
import jax
import jax.numpy as jnp
import numpy as np
from jax import lax

DEGREE = 7
COMPS = 3
EX = 1
EY = 2
EZ = 16
ITERS = 3
NODES_EL = 512
ELEM_DEV = 32
ELEMS = 1024
NX = 32
NY = 32
NZ = 512
N_GX = 4
N_GY = 2
N_GZ = 4
DEVICES = 32


def draw_right_side(key, part):
    full_shape = (COMPS, NODES_EL, ELEMS)
    return jnp.clip(jax.random.normal(key, full_shape, jnp.float32), -6.0, 6.0)


def draw_geometry(key, part):
    key_scale = jax.random.fold_in(key, 11)
    key_link = jax.random.fold_in(key, 12)
    lattice_shape = (3, NX, NY, NZ)
    scales = jnp.exp(jax.random.uniform(key_scale, lattice_shape, jnp.float32, math.log(0.6), math.log(1.6)))
    links = jax.random.uniform(key_link, lattice_shape, jnp.float32, -0.35, 0.35)
    return jnp.stack([scales[0] * scales[0], scales[1] * scales[1], scales[2] * scales[2], links[0] * scales[0] * scales[1], links[1] * scales[0] * scales[2], links[2] * scales[1] * scales[2]])


def plant(drawn, own_key, smallest, largest):
    longest = drawn.shape.index(max(drawn.shape))
    spots = []
    for shift in (0, 1):
        where = [jax.random.randint(jax.random.fold_in(own_key, axis), (), 0, length) for axis, length in enumerate(drawn.shape)]
        where[longest] = (where[longest] + shift) % drawn.shape[longest]
        spots.append(tuple(where))
    return drawn.at[spots[0]].set(smallest).at[spots[1]].set(largest)


def steps_of(key, shape, cuts, low, largest):
    loudness = 1.0
    for axis_at, shards_of in cuts:
        steps = jax.random.uniform(jax.random.fold_in(jax.random.fold_in(key, 6), axis_at), (shards_of,), jnp.float32, low / len(cuts), largest / len(cuts))
        loudness = loudness * jnp.repeat(jnp.exp(steps), shape[axis_at] // shards_of).reshape((-1,) + (1,) * (len(shape) - 1 - axis_at))
    return loudness


def setup_inputs(seed: int = 0) -> dict:
    arg_keys = jax.random.split(jax.random.key(seed), 8)
    return {
        "right_side": draw_right_side(jax.random.fold_in(arg_keys[7], 71), 0),
        "geometry": draw_geometry(jax.random.fold_in(arg_keys[7], 71), 0),
        "viscosity": jnp.clip(jnp.exp(math.log(3.0) - 2.3025851 * jax.random.uniform(arg_keys[2], (NX, NY, NZ), jnp.float32) ** steps_of(arg_keys[2], (NX, NY, NZ), ((0, 4), (1, 2), (2, 4)), -0.2, 0.2)), 0.3, 3.0),
        "eig_low": jnp.clip(jax.random.uniform(arg_keys[3], (1,), jnp.float32, 0.2, 2.0), 0.2, 2.0),
        "eig_high": jnp.clip(jax.random.uniform(arg_keys[4], (1,), jnp.float32, 8.0, 12.0), 8.0, 12.0),
        "element_slot": jax.vmap(lambda own: jax.random.permutation(own, ELEM_DEV))(jax.random.split(arg_keys[5], DEVICES)).reshape((DEVICES, ELEM_DEV)).astype(jnp.int32),
        "dirichlet": plant((jax.random.randint(arg_keys[6], (2, COMPS, NY, NZ), 0, 3) < 1).astype(jnp.int32), jax.random.fold_in(arg_keys[6], 1), 0, 1),
    }


helm_coefficient = 10.0


def legendre_pair(values, degree):
    previous = 0.0 * values + 1.0
    current = values.copy()
    for order in range(2, degree + 1):
        previous, current = current, ((2 * order - 1) * values * current - (order - 1) * previous) / order
    return current, previous


def gll_tables(degree):
    start = np.cos(np.pi * np.arange(degree + 1) / degree)
    nodes_now = start.copy()
    for sweep in range(80):
        top_value, lower_value = legendre_pair(nodes_now, degree)
        nodes_now = nodes_now - (nodes_now * top_value - lower_value) / ((degree + 1) * top_value)
    gll_nodes = nodes_now[::-1].copy()
    gll_nodes[0] = -1.0
    gll_nodes[degree] = 1.0
    legendre_values = legendre_pair(gll_nodes, degree)[0]
    weights = 2.0 / (degree * (degree + 1) * legendre_values ** 2)
    differences = gll_nodes[:, None] - gll_nodes[None, :] + np.eye(degree + 1)
    derivative = legendre_values[:, None] / legendre_values[None, :] / differences
    derivative = derivative * (1.0 - np.eye(degree + 1))
    derivative[0, 0] = -degree * (degree + 1) / 4.0
    derivative[degree, degree] = degree * (degree + 1) / 4.0
    return weights, derivative


def pad_dimension(lattice, dimension):
    widths = [(0, 0)] * lattice.ndim
    widths[dimension] = (1, 1)
    return jnp.pad(lattice, widths)


def fold_rims(extended, dimension, points):
    length = extended.shape[dimension] - 2
    center = lax.slice_in_dim(extended, 1, length + 1, axis=dimension)
    upper_side = lax.slice_in_dim(extended, 2, length + 2, axis=dimension)
    lower_side = lax.slice_in_dim(extended, 0, length, axis=dimension)
    shape_ones = [1] * extended.ndim
    shape_ones[dimension] = length
    position = (jnp.arange(length, dtype=jnp.int32) % points).reshape(tuple(shape_ones))
    upper_flag = (position == points - 1).astype(extended.dtype)
    lower_flag = (position == 0).astype(extended.dtype)
    return center + upper_flag * upper_side + lower_flag * lower_side


def assemble_global(lattice, points):
    for dimension in range(3):
        lattice = fold_rims(pad_dimension(lattice, dimension), dimension, points)
    return lattice


def along(lattice, matrix, dimension, points):
    full_shape = lattice.shape
    split_shape = full_shape[:dimension] + (full_shape[dimension] // points, points) + full_shape[dimension + 1:]
    moved = jnp.moveaxis(lattice.reshape(split_shape), dimension + 1, -1)
    result = jnp.einsum("...i,ai->...a", moved, matrix, precision=lax.Precision.HIGHEST)
    return jnp.moveaxis(result, -1, dimension + 1).reshape(full_shape)


def helmholtz(lattice, geometry, weighted, mass, forward, points):
    slope_first = along(lattice, forward, 0, points)
    slope_second = along(lattice, forward, 1, points)
    slope_third = along(lattice, forward, 2, points)
    flux_first = weighted * (geometry[0] * slope_first + geometry[3] * slope_second + geometry[4] * slope_third)
    flux_second = weighted * (geometry[3] * slope_first + geometry[1] * slope_second + geometry[5] * slope_third)
    flux_third = weighted * (geometry[4] * slope_first + geometry[5] * slope_second + geometry[2] * slope_third)
    backward = forward.T
    return along(flux_first, backward, 0, points) + along(flux_second, backward, 1, points) + along(flux_third, backward, 2, points) + mass * lattice


def reference(right_side, geometry, viscosity, eig_low, eig_high, element_slot, dirichlet):
    points = DEGREE + 1
    weights, derivative = gll_tables(DEGREE)
    forward = jnp.asarray(derivative, jnp.float32)
    squared = forward * forward
    weight_table = jnp.asarray(weights, jnp.float32)
    diagonal_table = jnp.diagonal(forward)
    quadrature = (jnp.tile(weight_table, NX // points)[:, None, None] * jnp.tile(weight_table, NY // points)[None, :, None]) * jnp.tile(weight_table, NZ // points)[None, None, :]
    weighted = quadrature * viscosity
    determinant = (geometry[0] * (geometry[1] * geometry[2] - geometry[5] * geometry[5]) - geometry[3] * (geometry[3] * geometry[2] - geometry[5] * geometry[4]) + geometry[4] * (geometry[3] * geometry[5] - geometry[1] * geometry[4]))
    mass = helm_coefficient * quadrature * determinant
    end_first = jnp.tile(diagonal_table, NX // points)[:, None, None]
    end_second = jnp.tile(diagonal_table, NY // points)[None, :, None]
    end_third = jnp.tile(diagonal_table, NZ // points)[None, None, :]
    cross = 2.0 * weighted * (end_first * end_second * geometry[3] + end_first * end_third * geometry[4] + end_second * end_third * geometry[5])
    diagonal_local = (along(weighted * geometry[0], squared.T, 0, points) + along(weighted * geometry[1], squared.T, 1, points) + along(weighted * geometry[2], squared.T, 2, points)) + cross + mass
    diagonal_sum = assemble_global(diagonal_local, points)

    blocks = right_side.reshape(COMPS, NODES_EL, DEVICES, ELEM_DEV)
    inverse = jnp.argsort(element_slot, axis=1).astype(jnp.int32)
    bricks = jnp.take_along_axis(blocks, jnp.broadcast_to(inverse[None, None], blocks.shape), axis=3)
    bricks = bricks.reshape(COMPS, points, points, points, N_GX, N_GY, N_GZ, EX, EY, EZ)
    rhs_lattice = bricks.transpose(0, 4, 7, 1, 5, 8, 2, 6, 9, 3).reshape(COMPS, NX, NY, NZ)

    midpoint = (eig_high[0] + eig_low[0]) * 0.5
    halfwidth = (eig_high[0] - eig_low[0]) * 0.5
    ratio_start = midpoint / halfwidth
    middle = jnp.zeros((NX - 2, NY, NZ), jnp.float32)
    solutions = []
    for component in range(COMPS):
        indicator = jnp.concatenate([dirichlet[0, component][None].astype(jnp.float32), middle, dirichlet[1, component][None].astype(jnp.float32)], axis=0)
        keep = jnp.where(assemble_global(indicator, points) > 0.5, 0.0, 1.0).astype(jnp.float32)
        residual = keep * assemble_global(rhs_lattice[component], points)
        scaling = keep / diagonal_sum
        damping = 1.0 / ratio_start
        direction = (scaling * residual) / midpoint
        solution = jnp.zeros_like(residual)
        for iteration in range(ITERS):
            solution = solution + direction
            if iteration < ITERS - 1:
                image = assemble_global(helmholtz(direction, geometry, weighted, mass, forward, points), points)
                residual = residual - keep * image
                damping_next = 1.0 / (2.0 * ratio_start - damping)
                direction = (damping_next * damping) * direction + (2.0 * damping_next / halfwidth) * (scaling * residual)
                damping = damping_next
        solutions.append(solution)
    stacked = jnp.stack(solutions)
    back_bricks = stacked.reshape(COMPS, N_GX, EX, points, N_GY, EY, points, N_GZ, EZ, points)
    back_bricks = back_bricks.transpose(0, 3, 6, 9, 1, 4, 7, 2, 5, 8).reshape(COMPS, NODES_EL, DEVICES, ELEM_DEV)
    slotted = jnp.take_along_axis(back_bricks, jnp.broadcast_to(element_slot[None, None], back_bricks.shape), axis=3)
    return slotted.reshape(COMPS, NODES_EL, ELEMS)
```

```python
import functools
import math

import jax
import jax.numpy as jnp
import numpy as np
from jax import lax
from jax.experimental import pallas as pl
from jax.experimental.pallas import tpu as pltpu
from jax.sharding import PartitionSpec as P

DEGREE = 7
ITERS = 3


helm_coefficient = 10.0


def legendre_pair(values, degree):
    previous = 0.0 * values + 1.0
    current = values.copy()
    for order in range(2, degree + 1):
        previous, current = (
            current,
            ((2 * order - 1) * values * current - (order - 1) * previous) / order,
        )
    return (current, previous)


def gll_tables(degree):
    start = np.cos(np.pi * np.arange(degree + 1) / degree)
    nodes_now = start.copy()
    for sweep in range(80):
        top_value, lower_value = legendre_pair(nodes_now, degree)
        nodes_now = nodes_now - (nodes_now * top_value - lower_value) / ((degree + 1) * top_value)
    gll_nodes = nodes_now[::-1].copy()
    gll_nodes[0] = -1.0
    gll_nodes[degree] = 1.0
    legendre_values = legendre_pair(gll_nodes, degree)[0]
    weights = 2.0 / (degree * (degree + 1) * legendre_values**2)
    differences = gll_nodes[:, None] - gll_nodes[None, :] + np.eye(degree + 1)
    derivative = legendre_values[:, None] / legendre_values[None, :] / differences
    derivative = derivative * (1.0 - np.eye(degree + 1))
    derivative[0, 0] = -degree * (degree + 1) / 4.0
    derivative[degree, degree] = degree * (degree + 1) / 4.0
    return (weights, derivative)


HALO = 2
F32 = jnp.float32
BF16 = jnp.bfloat16


def pairings(names, sizes, dim):
    size = sizes[dim]
    if size == 1:
        return []
    if size % 2:
        shifts = (1, size - 1)
        partners = [[(i + shift) % size for i in range(size)] for shift in shifts]
    else:
        partners = [[i ^ 1 for i in range(size)]]
        if size > 2:
            partners.append([((i + 1) ^ 1) - 1 for i in range(size)])
    result = []
    for partner in partners:
        pairs = []
        for flat in range(math.prod(sizes)):
            place = list(np.unravel_index(flat, sizes))
            to = partner[place[dim]]
            if 0 <= to < size:
                place[dim] = to
            elif len(sizes) > 1 and sizes[1 - dim] % 2 == 0:
                place[1 - dim] ^= 1
            else:
                place[dim] = size - 1 - place[dim]
            pairs.append((flat, int(np.ravel_multi_index(place, sizes))))
        result.append(pairs)
    return result


def roles(name, size):
    if size == 1:
        return []
    index = lax.axis_index(name)
    low, high = index > 0, index < size - 1
    if size % 2:
        yes = index >= 0
        no = index < 0
        return [(yes, no, low), (no, yes, high)]
    even = lax.rem(index, 2) == 0
    odd = jnp.logical_not(even)
    result = [(even, even, index >= 0)]
    if size > 2:
        result.append((odd, odd, jnp.logical_or(jnp.logical_and(odd, high), jnp.logical_and(even, low))))
    return result


def both_sides(received, role):
    low, high = 0.0, 0.0
    for data, (_, from_high, used) in zip(received, role):
        high = high + jnp.where(jnp.logical_and(used, from_high), data, 0.0)
        low = low + jnp.where(jnp.logical_and(used, jnp.logical_not(from_high)), data, 0.0)
    return low, high


def split(x):
    upper = x.astype(BF16)
    return upper, (x - upper.astype(F32)).astype(BF16)


def dot2(x, table):
    upper, lower = split(x)
    return jnp.dot(upper, table, preferred_element_type=F32) + jnp.dot(
        lower, table, preferred_element_type=F32
    )


class Plan:
    def __init__(self, components, viscosity_shape, mesh_sizes):
        points = DEGREE + 1
        self.p, self.c = points, components
        self.sizes = mesh_sizes
        ex, ey, ez = (n // points for n in viscosity_shape)
        assert ex == 1 and ez >= HALO
        self.ey, self.ez = ey, ez
        self.rows = points**3
        self.block = points * points
        self.step3, self.step4 = components * ey, (components + 1) * ey
        self.n3, self.n4 = (ez + 2 * HALO) * self.step3, ez * self.step4
        self.w3, self.w4 = -(-self.n3 // 128) * 128, -(-self.n4 // 128) * 128
        self.halo4 = HALO * self.step4
        assert points * self.halo4 <= self.w4 and 2 * self.halo4 <= self.w4
        weights, derivative = gll_tables(DEGREE)
        self.forward = derivative.astype(np.float32)
        self.squared = self.forward * self.forward
        self.weights = weights.astype(np.float32)
        self.end = np.diagonal(self.forward)
        self.tables()

    def lane3(self, g, c, f):
        return (g + HALO) * self.step3 + c * self.ey + f

    def lane4(self, g, c, f):
        return g * self.step4 + c * self.ey + f

    def tables(self):
        p, c, ey, ez = self.p, self.c, self.ey, self.ez
        lanes = ez * p
        every = [(g, cc, f) for g in range(ez) for cc in range(c) for f in range(ey)]
        spread = np.zeros((ey * lanes, self.w3), np.float32)
        flags = np.zeros((c * ey * lanes, self.w4), np.float32)
        diagonal = np.zeros((self.w3, self.w4), np.float32)
        widen = np.zeros((2 * self.w4, 2 * self.w3), np.float32)
        self.id3 = np.full((self.w3, 128), -1, np.int32)
        self.id4 = np.full((self.w4, 128), -1, np.int32)
        for g, cc, f in every:
            for k in range(p):
                spread[f * lanes + g * p + k, self.lane3(g, cc, f)] = 1
                flags[(cc * ey + f) * lanes + g * p + k, self.lane4(g, cc, f)] = 1
            diagonal[self.lane3(g, 0, f), self.lane4(g, c, f)] = 1
            widen[self.lane4(g, cc, f), self.lane3(g, cc, f)] = 1
            widen[self.lane4(g, c, f), self.w3 + self.lane3(g, cc, f)] = 1
            self.id3[self.lane3(g, cc, f), cc] = f * ez + g
            self.id4[self.lane4(g, cc, f), cc] = f * ez + g
        fields = 7
        part = HALO * p
        self.part = part
        assert fields * part <= lanes
        halo = np.zeros((2 * ey * lanes, fields * self.w3), np.float32)
        for side, first in ((0, -HALO), (1, ez)):
            for g in range(HALO):
                for cc in range(c):
                    for f in range(ey):
                        at = self.lane3(first + g, cc, f)
                        row = self.w4 + side * self.halo4 + g * self.step4
                        widen[row + cc * ey + f, at] = 1
                        widen[row + c * ey + f, self.w3 + at] = 1
                        for q in range(fields):
                            for k in range(p):
                                halo[(side * ey + f) * lanes + q * part + g * p + k, q * self.w3 + at] = 1
        self.spread, self.flags, self.diagonal, self.widen, self.halo = (
            x.astype(jnp.bfloat16) for x in (spread, flags, diagonal, widen, halo)
        )
        rolled = []
        for matrix in (self.forward, self.forward.T, self.squared.T):
            for d in range(p):
                rolled += [matrix[a, (a + d) % p] for a in range(p)]
        node = [(j, k) for j in range(p) for k in range(p)]
        wjk = [self.weights[j] * self.weights[k] for j, k in node]
        second = [self.end[j] for j, k in node]
        third = [self.end[k] for j, k in node]
        column = np.asarray(rolled + wjk + second + third, np.float32)
        self.table = np.ascontiguousarray(np.broadcast_to(column[:, None], (column.size, 128)))


    def rolled(self, table, which):
        p = self.p
        return [table[(which * p + d) * p : (which * p + d + 1) * p, :] for d in range(p)]

    def node_table(self, table, which):
        start = 3 * self.p * self.p + which * self.block
        return table[start : start + self.block, :]

    def along_j(self, x, matrix):
        p = self.p
        x = x.reshape(p, p, x.shape[-1])
        out = []
        for a in range(p):
            total = None
            for i in range(p):
                value = float(matrix[a, i])
                if value != 0.0:
                    term = value * x[i]
                    total = term if total is None else total + term
            out.append(total)
        return jnp.concatenate(out, axis=0)

    def along_k(self, x, coefficients):
        p = self.p
        x3 = x.reshape(p, p, x.shape[-1])
        total = coefficients[0][None] * x3
        for d in range(1, p):
            total = total + coefficients[d][None] * pltpu.roll(x3, p - d, 1)
        return total.reshape(x.shape)

    def along_i(self, source, matrix, write):
        p = self.p

        def body(j, carry):
            at = pl.multiple_of(j * p, p)
            x = [source[pl.ds(i * self.block + at, p), :] for i in range(p)]
            for a in range(p):
                total = None
                for i in range(p):
                    value = float(matrix[a, i])
                    if value != 0.0:
                        term = value * x[i]
                        total = term if total is None else total + term
                write(a * self.block + at, total)
            return carry

        lax.fori_loop(0, p, body, 0)

    def operator(self, v, g, out, slope, flux, table):
        p, block = self.p, self.block
        ahead, back = self.rolled(table, 0), self.rolled(table, 1)

        def store(row, value):
            slope[pl.ds(row, p), :] = value

        self.along_i(v, self.forward, store)

        def body(i, carry):
            at = pl.ds(pl.multiple_of(i * block, block), block)
            x = v[at, :]
            s1 = slope[at, :]
            s2 = self.along_j(x, self.forward)
            s3 = self.along_k(x, ahead)
            xy, xz, yz = g[3, at, :], g[4, at, :], g[5, at, :]
            flux[at, :] = g[0, at, :] * s1 + xy * s2 + xz * s3
            f2 = xy * s1 + g[1, at, :] * s2 + yz * s3
            f3 = xz * s1 + yz * s2 + g[2, at, :] * s3
            out[at, :] = (
                self.along_j(f2, self.forward.T) + self.along_k(f3, back) + g[6, at, :] * x
            )
            return carry

        lax.fori_loop(0, p, body, 0)

        def add(row, value):
            out[pl.ds(row, p), :] += value

        self.along_i(flux, self.forward.T, add)

    def fold_second(self, u):
        if self.ey == 1:
            return
        p, width = self.p, u.shape[-1]
        lane = lax.broadcasted_iota(jnp.int32, (p, width), 1)
        f = lax.rem(lane, self.ey)
        for start in range(0, u.shape[0], self.block):
            first, last = u[start : start + p, :], u[start + self.block - p : start + self.block, :]
            u[start + self.block - p : start + self.block, :] = last + jnp.where(
                f < self.ey - 1, pltpu.roll(first, width - 1, 1), 0.0
            )
            u[start : start + p, :] = first + jnp.where(f > 0, pltpu.roll(last, 1, 1), 0.0)

    def fold_third(self, u, step, take_upper, take_lower):
        p, (rows, width) = self.p, u.shape
        count = rows // p
        lane = lax.broadcasted_iota(jnp.int32, (count, width), 1)
        first, last = u[pl.ds(0, count, stride=p), :], u[pl.ds(p - 1, count, stride=p), :]
        u[pl.ds(p - 1, count, stride=p), :] = last + jnp.where(
            take_upper(lane), pltpu.roll(first, width - step, 1), 0.0
        )
        u[pl.ds(0, count, stride=p), :] = first + jnp.where(
            take_lower(lane), pltpu.roll(last, step, 1), 0.0
        )

    def emit(self, u, x_out, y_out):
        p, block = self.p, self.block
        for out, (high, _, _) in zip(x_out, roles("gx", self.sizes["gx"])):
            out[...] = jnp.where(high, u[self.rows - block :, :], u[:block, :])
        for out, (high, _, _) in zip(y_out, roles("gy", self.sizes["gy"])):
            for i in range(p):
                start = i * block
                out[i * p : (i + 1) * p, :] = jnp.where(
                    high, u[start + block - p : start + block, :], u[start : start + p, :]
                )

    def subtract_shared(self, t, scale, x_in, y_in):
        p, block, rows = self.p, self.block, self.rows
        low, high = both_sides([x[...] for x in x_in], roles("gx", self.sizes["gx"]))
        if x_in:
            t[:block, :] -= scale[:block, :] * low
            t[rows - block :, :] -= scale[rows - block :, :] * high
        low, high = both_sides([y[...] for y in y_in], roles("gy", self.sizes["gy"]))
        if y_in:
            for i in range(p):
                at, end = i * block, (i + 1) * block
                t[at : at + p, :] -= scale[at : at + p, :] * low[i * p : (i + 1) * p]
                t[end - p : end, :] -= scale[end - p : end, :] * high[i * p : (i + 1) * p]

    def iteration_fold(self, u):
        self.fold_second(u)
        last = self.n3 - self.step3
        self.fold_third(u, self.step3, lambda l: l < last, lambda l: (l >= self.step3) & (l < self.n3))

    def expand(self, source, upper, lower):
        p, ey = self.p, self.ey

        def body(i, carry):
            block = source(i)
            width = block.shape[-1]
            lane = lax.broadcasted_iota(jnp.int32, (p, width), 1)
            keep = lax.rem(lane, p) == lax.broadcasted_iota(jnp.int32, (p, width), 0)
            for f in range(ey):
                for j in range(0, p, 2):
                    row = f * p + j
                    x = jnp.concatenate(
                        [
                            jnp.where(keep, jnp.broadcast_to(block[r : r + 1, :], (p, width)), 0.0)
                            for r in (row, row + 1)
                        ],
                        axis=0,
                    )
                    at = pl.ds(pl.multiple_of(i * self.block + j * p, 2 * p), 2 * p)
                    first, second = split(x)
                    upper[at, f * width : (f + 1) * width] = first
                    lower[at, f * width : (f + 1) * width] = second
            return carry

        lax.fori_loop(0, p, body, 0)


    def pack_geometry(self, geometry, viscosity, *out):
        width = geometry.shape[-1]
        rows = self.p * self.ey * self.p
        role = roles("gz", self.sizes["gz"])
        lane = lax.broadcasted_iota(jnp.int32, (rows, width), 1)
        for target, (high, _, _) in zip(out, role):
            total = jnp.zeros((rows, width), F32)
            for q in range(7):
                field = (geometry[q] if q < 6 else viscosity[...]).reshape(rows, width)
                start = q * self.part
                upper = pltpu.roll(field, start + self.part, 1)
                lower = pltpu.roll(field, start, 1) if start else field
                here = (lane >= start) & (lane < start + self.part)
                total = jnp.where(here, jnp.where(high, upper, lower), total)
            target[...] = total

    def prepare(self, n_x, n_y, *refs):
        (right, slots, geometry, viscosity, dirichlet, low, high, spread, flags, diagonal, ids, table) = refs[:12]
        s4, ind, raw, coef = refs[12:16]
        x_out, y_out = refs[16 : 16 + n_x], refs[16 + n_x : 16 + n_x + n_y]
        upper, lower, stiff, work = refs[16 + n_x + n_y :]
        p, c, block, rows = self.p, self.c, self.block, self.rows
        top, bottom = jnp.full((8, 128), high[0], F32), jnp.full((8, 128), low[0], F32)
        midpoint, halfwidth = (top + bottom) * 0.5, (top - bottom) * 0.5
        ratio = midpoint / halfwidth
        damping = 1.0 / ratio
        coef[0:8, :] = 1.0 / midpoint
        for n in range(ITERS - 1):
            following = 1.0 / (2.0 * ratio - damping)
            coef[8 * (2 * n + 1) : 8 * (2 * n + 2), :] = following * damping
            coef[8 * (2 * n + 2) : 8 * (2 * n + 3), :] = 2.0 * following / halfwidth
            damping = following
        def convert(q, source):
            self.expand(source, upper, lower)
            raw[q] = jnp.dot(upper[...], spread[...], preferred_element_type=F32) + jnp.dot(
                lower[...], spread[...], preferred_element_type=F32
            )

        def each(q, carry):
            convert(q, lambda i: geometry[q, i])
            return carry

        lax.fori_loop(0, 6, each, 0)
        convert(6, lambda i: viscosity[i])
        wjk, second, third = (self.node_table(table, n) for n in range(3))
        square = self.rolled(table, 2)
        for i in range(p):
            at = slice(i * block, (i + 1) * block)
            xx, yy, zz, xy, xz, yz = (raw[q, at, :] for q in range(6))
            quadrature = float(self.weights[i]) * wjk
            weighted = quadrature * raw[6, at, :]
            mass = (helm_coefficient * quadrature) * (
                xx * (yy * zz - yz * yz) - xy * (xy * zz - yz * xz) + xz * (xy * yz - yy * xz)
            )
            cross = second * third * yz
            end = float(self.end[i])
            if end != 0.0:
                cross = cross + end * (second * xy + third * xz)
            stiff[at, :] = weighted * xx
            work[at, :] = (
                self.along_j(weighted * yy, self.squared.T)
                + self.along_k(weighted * zz, square)
                + (2.0 * weighted) * cross
                + mass
            )

        def add(row, value):
            work[pl.ds(row, p), :] += value

        self.along_i(stiff, self.squared.T, add)
        total = dot2(work[...], diagonal[...])
        for cc in range(c):
            hot = jnp.where(slots[...] == ids[:, cc : cc + 1], 1.0, 0.0).astype(BF16)
            for part in split(right[cc]):
                total = total + lax.dot_general(
                    part, hot, (((1,), (1,)), ((), ())), preferred_element_type=F32
                )
        s4[...] = total
        ends = (lax.axis_index("gx") == 0, lax.axis_index("gx") == self.sizes["gx"] - 1)
        width = dirichlet.shape[-1]
        lane = lax.broadcasted_iota(jnp.int32, (p, width), 1)
        keep = lax.rem(lane, p) == lax.broadcasted_iota(jnp.int32, (p, width), 0)
        for n, here in enumerate(ends):
            plane = jnp.zeros((block, self.w4), F32)
            for cc in range(c):
                face = dirichlet[n, cc].astype(F32)
                for f in range(self.ey):
                    x = jnp.concatenate(
                        [
                            jnp.where(keep, jnp.broadcast_to(face[f * p + j : f * p + j + 1, :], (p, width)), 0.0)
                            for j in range(p)
                        ],
                        axis=0,
                    ).astype(BF16)
                    start = (cc * self.ey + f) * width
                    plane = plane + jnp.dot(x, flags[start : start + width, :], preferred_element_type=F32)
            ind[n * block : (n + 1) * block, :] = jnp.where(here, plane, 0.0)
        last = self.n4 - self.step4
        for u in (s4, ind):
            self.fold_second(u)
            self.fold_third(u, self.step4, lambda l: l < last, lambda l: (l >= self.step4) & (l < self.n4))
        self.emit(s4, x_out, y_out)
        for out, (up, _, _) in zip(y_out, roles("gy", self.sizes["gy"])):
            for n in range(2):
                start = n * block
                out[block + n * p : block + (n + 1) * p, :] = jnp.where(
                    up, ind[start + block - p : start + block, :], ind[start : start + p, :]
                )

    def halo_geometry(self, n_z, *refs):
        raw, halo, table = refs[:3]
        z_in, g = refs[3 : 3 + n_z], refs[3 + n_z]
        upper, lower, sides = refs[4 + n_z :]
        p, block, rows, ey = self.p, self.block, self.rows, self.ey
        if n_z:
            low, high = both_sides([z[...] for z in z_in], roles("gz", self.sizes["gz"]))
            sides[0], sides[1] = low, high
            width = low.shape[-1]
            for side in range(2):
                at = slice(side * ey * width, (side + 1) * ey * width)
                self.expand(
                    lambda i: sides[side, pl.ds(pl.multiple_of(i * ey * p, ey * p), ey * p), :],
                    upper.at[:, at],
                    lower.at[:, at],
                )
        wjk = self.node_table(table, 0)
        fields = []
        for q in range(7):
            field = raw[q]
            if n_z:
                columns = halo[:, q * self.w3 : (q + 1) * self.w3]
                field = field + (
                    jnp.dot(upper[...], columns, preferred_element_type=F32)
                    + jnp.dot(lower[...], columns, preferred_element_type=F32)
                )
            g[q] = field
        for i in range(p):
            at = slice(i * block, (i + 1) * block)
            xx, yy, zz, xy, xz, yz = (g[q, at, :] for q in range(6))
            quadrature = float(self.weights[i]) * wjk
            weighted = quadrature * g[6, at, :]
            g[6, at, :] = (helm_coefficient * quadrature) * (
                xx * (yy * zz - yz * yz) - xy * (xy * zz - yz * xz) + xz * (xy * yz - yy * xz)
            )
            for q, entry in enumerate((xx, yy, zz, xy, xz, yz)):
                g[q, at, :] = weighted * entry

    def join(self, n_x, n_y, *refs):
        x_in, y_raw, y_out = refs[:n_x], refs[n_x : n_x + n_y], refs[n_x + n_y :]
        p, block, ey = self.p, self.block, self.ey
        low, high = both_sides([x[...] for x in x_in], roles("gx", self.sizes["gx"]))
        for raw, out, (up, _, _) in zip(y_raw, y_out, roles("gy", self.sizes["gy"])):
            width = raw.shape[-1]
            face = raw[...]
            if n_x:
                first, last = (jnp.where(up, x[block - p :], x[:p]) for x in (low, high))
                parts = [face[:p] + first, face[p : block - p], face[block - p : block] + last]
                parts += [face[block:]] if face.shape[0] > block else []
                face = jnp.concatenate(parts, axis=0)
            f = lax.rem(lax.broadcasted_iota(jnp.int32, face.shape, 1), ey)
            if ey > 1:
                to_first = jnp.where(f == 0, pltpu.roll(face, width - (ey - 1), 1), 0.0)
                to_last = jnp.where(f == ey - 1, pltpu.roll(face, ey - 1, 1), 0.0)
                face = jnp.where(up, to_first, to_last)
            out[...] = face

    def pack(self, n_x, n_y, *refs):
        s4, ind = refs[:2]
        x_in, y_in = refs[2 : 2 + n_x], refs[2 + n_x : 2 + n_x + n_y]
        s_out, i_out = refs[2 + n_x + n_y : 4 + n_x + n_y]
        z_out = refs[4 + n_x + n_y :]
        p, block, rows = self.p, self.block, self.rows
        s_out[...] = s4[...]
        i_out[...] = ind[...]
        if n_x:
            low, high = both_sides([x[...] for x in x_in], roles("gx", self.sizes["gx"]))
            s_out[:block, :] += low
            s_out[rows - block :, :] += high
        if n_y:
            low, high = both_sides([y[...] for y in y_in], roles("gy", self.sizes["gy"]))
            for u, first, count in ((s_out, 0, p), (i_out, p, 2)):
                for i in range(count):
                    at, end, row = i * block, (i + 1) * block, (first + i) * p
                    u[at : at + p, :] += low[row : row + p]
                    u[end - p : end, :] += high[row : row + p]
        width, size = self.w4, self.halo4
        for out, (up, _, _) in zip(z_out, roles("gz", self.sizes["gz"])):
            for u, count, start in ((s_out, block, 0), (i_out, p, block)):
                groups = u.shape[0] // count
                lane = lax.broadcasted_iota(jnp.int32, (count, width), 1)
                for section in range(0, groups, p):
                    total = jnp.zeros((count, width), F32)
                    for n in range(p):
                        at = (section + n) * count
                        x = u[at : at + count, :]
                        shift = n * size
                        below = pltpu.roll(x, shift, 1) if shift else x
                        above = pltpu.roll(x, (shift + width - self.n4 + size) % width, 1)
                        here = (lane >= shift) & (lane < shift + size)
                        total = jnp.where(here, jnp.where(up, above, below), total)
                    row = start + section // p * count
                    out[row : row + count, :] = total

    def wide(self, own, low, high, groups, count, put):
        size, width = self.halo4, self.w4
        lane = lax.broadcasted_iota(jnp.int32, (count, width), 1)
        for n in range(groups):
            shift = (width - (n % self.p) * size) % width
            row = (n // self.p) * count
            first = pltpu.roll(low[row : row + count], shift, 1) if shift else low[row : row + count]
            second = pltpu.roll(high[row : row + count], (shift + size) % width, 1)
            beside = jnp.where(lane < size, first, jnp.where(lane < 2 * size, second, 0.0))
            put(n * count, jnp.concatenate([own[n * count : (n + 1) * count, :], beside], axis=1))

    def start(self, n_x, n_y, n_z, *refs):
        s4, ind, g, coef, widen, table = refs[:6]
        z_in = refs[6 : 6 + n_z]
        t, d, scale, v = refs[6 + n_z : 10 + n_z]
        refs = refs[10 + n_z :]
        x_out, y_out = refs[:n_x], refs[n_x : n_x + n_y]
        upper, lower, flag_lhs, r, flag, slope, flux = refs[n_x + n_y :]
        p, block, rows, w3 = self.p, self.block, self.rows, self.w3
        size = self.sizes["gz"]
        if n_z:
            low, high = both_sides([z[...] for z in z_in], roles("gz", size))
        else:
            low = high = jnp.zeros((block + 2 * p, self.w4), F32)

        def put(at, x):
            first, second = split(x)
            upper[at : at + block, :] = first
            lower[at : at + block, :] = second

        self.wide(s4, low, high, p, block, put)

        def put_flag(at, x):
            flag_lhs[at : at + p, :] = x

        self.wide(ind, low[block:], high[block:], 2 * p, p, put_flag)
        both = jnp.dot(upper[...], widen[...], preferred_element_type=F32) + jnp.dot(
            lower[...], widen[...], preferred_element_type=F32
        )
        r[...] = both[:, :w3]
        scale[...] = both[:, w3:]
        flag[...] = jnp.dot(flag_lhs[...].astype(BF16), widen[:, :w3], preferred_element_type=F32)
        step, first_own, end_own = self.step3, HALO * self.step3, self.n3 - HALO * self.step3
        for u in (r, scale, flag):
            self.fold_third(
                u,
                step,
                lambda l: ((l >= first_own - step) & (l < first_own)) | ((l >= end_own - step) & (l < end_own)),
                lambda l: ((l >= first_own) & (l < first_own + step)) | ((l >= end_own) & (l < end_own + step)),
            )
        index = lax.axis_index("gz")
        begin = jnp.where(index > 0, 0, first_own)
        end = jnp.where(index < size - 1, self.n3, end_own)
        lane = lax.broadcasted_iota(jnp.int32, (block, w3), 1)
        valid = (lane >= begin) & (lane < end)
        middle = coef[0:1, :]
        for i in range(p):
            at = slice(i * block, (i + 1) * block)
            factor = jnp.where(valid, 1.0 / jnp.where(valid, scale[at, :], 1.0), 0.0)
            if i in (0, p - 1):
                row = 0 if i == 0 else block
                factor = jnp.where(flag[row : row + block, :] > 0.5, 0.0, factor)
            scale[at, :] = factor
            scaled = factor * r[at, :]
            t[at, :] = scaled
            d[at, :] = scaled * middle
        self.operator(d, g, v, slope, flux, table)
        self.iteration_fold(v)
        self.emit(v, x_out, y_out)

    def advance(self, t, t_new, d, v, scale, coef, which, x_in, y_in, put):
        t_new[...] = t[...] - scale[...] * v[...]
        self.subtract_shared(t_new, scale, x_in, y_in)
        keep, gain = (coef[8 * (2 * which + n) : 8 * (2 * which + n) + 1, :] for n in (1, 2))
        for i in range(self.p):
            at = slice(i * self.block, (i + 1) * self.block)
            put(at, keep * d[at, :] + gain * t_new[at, :])

    def middle(self, n_x, n_y, which, *refs):
        t, d, scale, v, total, g, coef, table = refs[:8]
        refs = refs[8:]
        x_in, y_in, refs = refs[:n_x], refs[n_x : n_x + n_y], refs[n_x + n_y :]
        t_new, d_new, v_new, total_new = refs[:4]
        x_out, y_out = refs[4 : 4 + n_x], refs[4 + n_x : 4 + n_x + n_y]
        slope, flux = refs[4 + n_x + n_y :]

        def put(at, x):
            d_new[at, :] = x
            total_new[at, :] = total[at, :] + x

        self.advance(t, t_new, d, v, scale, coef, which, x_in, y_in, put)
        self.operator(d_new, g, v_new, slope, flux, table)
        self.iteration_fold(v_new)
        self.emit(v_new, x_out, y_out)

    def finish(self, n_x, n_y, which, *refs):
        t, d, scale, v, total, coef, slots, ids = refs[:8]
        refs = refs[8:]
        x_in, y_in, refs = refs[:n_x], refs[n_x : n_x + n_y], refs[n_x + n_y :]
        out, t_new, field = refs

        def put(at, x):
            field[at, :] = total[at, :] + x

        self.advance(t, t_new, d, v, scale, coef, which, x_in, y_in, put)
        upper, lower = split(field[...])
        for cc in range(self.c):
            hot = jnp.where(slots[...] == ids[:, cc : cc + 1], 1.0, 0.0).astype(BF16)
            out[cc] = jnp.dot(upper, hot, preferred_element_type=F32) + jnp.dot(
                lower, hot, preferred_element_type=F32
            )


def shards(sizes, right_side, geometry, viscosity, eig_low, eig_high, element_slot, dirichlet):
    plan = Plan(right_side.shape[0], viscosity.shape, sizes)
    p, block, rows, w3, w4 = plan.p, plan.block, plan.rows, plan.w3, plan.w4
    x_pairs = pairings(("gx",), (sizes["gx"],), 0)
    y_pairs = pairings(("gy",), (sizes["gy"],), 0)
    z_pairs = pairings(("gy", "gz"), (sizes["gy"], sizes["gz"]), 1)
    n_x, n_y, n_z = len(x_pairs), len(y_pairs), len(z_pairs)

    def send(arrays, axis, pairs):
        return [lax.ppermute(x, axis, pair) for x, pair in zip(arrays, pairs)]

    def shape(*size, dtype=F32):
        return jax.ShapeDtypeStruct(size, dtype)

    def call(kernel, outputs, operands, scratch=(), scalars=(), flops=0, name=None):
        specs = [
            pl.BlockSpec(memory_space=pltpu.SMEM if n in scalars else pltpu.VMEM)
            for n in range(len(operands))
        ]
        return list(pl.pallas_call(
            kernel,
            out_shape=list(outputs),
            in_specs=specs,
            out_specs=[pl.BlockSpec(memory_space=pltpu.VMEM)] * len(outputs),
            scratch_shapes=list(scratch),
            compiler_params=pltpu.CompilerParams(vmem_limit_bytes=40 * 1024 * 1024),
            cost_estimate=pl.CostEstimate(flops=flops, bytes_accessed=0, transcendentals=0),
            name=name,
        )(*operands))

    def vmem(*size, dtype=F32):
        return pltpu.VMEM(size, dtype)

    lanes = plan.ez * p
    table = jnp.asarray(plan.table)
    faces = [shape(plan.p * plan.ey * p, lanes)] * n_z
    z_geometry = call(plan.pack_geometry, faces, (geometry, viscosity), name="pack_geometry") if n_z else []
    z_geometry = send(z_geometry, ("gy", "gz"), z_pairs)

    field3, field4 = shape(rows, w3), shape(rows, w4)
    results = call(
        functools.partial(plan.prepare, n_x, n_y),
        [field4, shape(2 * block, w4), shape(7, rows, w3), shape(8 * (2 * ITERS - 1), 128)]
        + [shape(block, w4)] * n_x
        + [shape(block + 2 * p, w4)] * n_y,
        (
            right_side,
            element_slot,
            geometry,
            viscosity,
            dirichlet,
            eig_low,
            eig_high,
            jnp.asarray(plan.spread),
            jnp.asarray(plan.flags),
            jnp.asarray(plan.diagonal),
            jnp.asarray(plan.id4),
            table,
        ),
        scratch=[vmem(rows, plan.ey * lanes, dtype=BF16)] * 2 + [vmem(rows, w3)] * 2,
        scalars=(5, 6),
        name="prepare",
    )
    s4, ind, raw, coef = results[:4]
    x_out, y_raw = results[4 : 4 + n_x], results[4 + n_x :]
    x_in = send(x_out, "gx", x_pairs)

    g = call(
        functools.partial(plan.halo_geometry, n_z),
        [shape(7, rows, w3)],
        [raw, jnp.asarray(plan.halo), table] + z_geometry,
        scratch=[vmem(rows, 2 * plan.ey * lanes, dtype=BF16)] * 2 + [vmem(2, plan.p * plan.ey * p, lanes)],
        flops=2000000,
        name="halo_geometry",
    )[0]

    def second(x_in, y_raw):
        if not y_raw:
            return []
        faces = [shape(*y.shape) for y in y_raw]
        return send(call(functools.partial(plan.join, n_x, n_y), faces, x_in + y_raw, name="join"), "gy", y_pairs)

    y_in = second(x_in, y_raw)
    results = call(
        functools.partial(plan.pack, n_x, n_y),
        [field4, shape(2 * block, w4)] + [shape(block + 2 * p, w4)] * n_z,
        [s4, ind] + x_in + y_in,
        name="pack",
    )
    s4, ind = results[:2]
    z_in = send(results[2:], ("gy", "gz"), z_pairs)

    messages = [shape(block, w3)] * (n_x + n_y)
    results = call(
        functools.partial(plan.start, n_x, n_y, n_z),
        [field3] * 4 + messages,
        [s4, ind, g, coef, jnp.asarray(plan.widen), table] + z_in,
        scratch=[vmem(rows, 2 * w4, dtype=BF16)] * 2
        + [vmem(2 * block, 2 * w4), vmem(rows, w3), vmem(2 * block, w3), vmem(rows, w3), vmem(rows, w3)],
        name="first_direction",
    )
    t, d, scale, v = results[:4]
    total = d
    for n in range(ITERS - 1):
        x_out, y_raw = results[4 : 4 + n_x], results[4 + n_x :]
        x_in = send(x_out, "gx", x_pairs)
        y_in = second(x_in, y_raw)
        if n < ITERS - 2:
            results = call(
                functools.partial(plan.middle, n_x, n_y, n),
                [field3] * 4 + messages,
                [t, d, scale, v, total, g, coef, table] + x_in + y_in,
                scratch=[vmem(rows, w3)] * 2,
                name="direction",
            )
            t, d, v, total = results[:4]
        else:
            return call(
                functools.partial(plan.finish, n_x, n_y, n),
                [shape(*right_side.shape)],
                [t, d, scale, v, total, coef, element_slot, jnp.asarray(plan.id3)] + x_in + y_in,
                scratch=[vmem(rows, w3)] * 2,
                name="field",
            )[0]


def solution(mesh):
    sizes = {name: mesh.shape[name] for name in ("gx", "gy", "gz")}
    return jax.shard_map(
        functools.partial(shards, sizes),
        mesh=mesh,
        in_specs=(
            P(None, None, ("gx", "gy", "gz")),
            P(None, "gx", "gy", "gz"),
            P("gx", "gy", "gz"),
            P(),
            P(),
            P(("gx", "gy", "gz"), None),
            P(None, None, "gy", "gz"),
        ),
        out_specs=P(None, None, ("gx", "gy", "gz")),
        check_vma=False,
    )
```

```python
import functools
import math

import jax
import jax.numpy as jnp
import numpy as np
from jax import lax
from jax.experimental import pallas as pl
from jax.experimental.pallas import tpu as pltpu
from jax.sharding import PartitionSpec as P

DEGREE = 7
ITERS = 3


helm_coefficient = 10.0


def legendre_pair(values, degree):
    previous = 0.0 * values + 1.0
    current = values.copy()
    for order in range(2, degree + 1):
        previous, current = (
            current,
            ((2 * order - 1) * values * current - (order - 1) * previous) / order,
        )
    return (current, previous)


def gll_tables(degree):
    start = np.cos(np.pi * np.arange(degree + 1) / degree)
    nodes_now = start.copy()
    for sweep in range(80):
        top_value, lower_value = legendre_pair(nodes_now, degree)
        nodes_now = nodes_now - (nodes_now * top_value - lower_value) / ((degree + 1) * top_value)
    gll_nodes = nodes_now[::-1].copy()
    gll_nodes[0] = -1.0
    gll_nodes[degree] = 1.0
    legendre_values = legendre_pair(gll_nodes, degree)[0]
    weights = 2.0 / (degree * (degree + 1) * legendre_values**2)
    differences = gll_nodes[:, None] - gll_nodes[None, :] + np.eye(degree + 1)
    derivative = legendre_values[:, None] / legendre_values[None, :] / differences
    derivative = derivative * (1.0 - np.eye(degree + 1))
    derivative[0, 0] = -degree * (degree + 1) / 4.0
    derivative[degree, degree] = degree * (degree + 1) / 4.0
    return (weights, derivative)


HALO = 2
FIELDS = 7
VMEM_BYTES = 40 * 1024 * 1024
FLOPS = 3 * 10**9
F32 = jnp.float32
BF16 = jnp.bfloat16


def pairings(names, sizes, dim):
    size = sizes[dim]
    if size == 1:
        return []
    if size % 2:
        shifts = (1, size - 1)
        partners = [[(i + shift) % size for i in range(size)] for shift in shifts]
    else:
        partners = [[i ^ 1 for i in range(size)]]
        if size > 2:
            partners.append([((i + 1) ^ 1) - 1 for i in range(size)])
    result = []
    for partner in partners:
        pairs = []
        for flat in range(math.prod(sizes)):
            place = list(np.unravel_index(flat, sizes))
            to = partner[place[dim]]
            if 0 <= to < size:
                place[dim] = to
            elif len(sizes) > 1 and sizes[1 - dim] % 2 == 0:
                place[1 - dim] ^= 1
            else:
                place[dim] = size - 1 - place[dim]
            pairs.append((flat, int(np.ravel_multi_index(place, sizes))))
        result.append(pairs)
    return result


def roles(name, size):
    if size == 1:
        return []
    index = lax.axis_index(name)
    low, high = index > 0, index < size - 1
    if size % 2:
        yes = index >= 0
        no = index < 0
        return [(yes, no, low), (no, yes, high)]
    even = lax.rem(index, 2) == 0
    odd = jnp.logical_not(even)
    result = [(even, even, index >= 0)]
    if size > 2:
        result.append((odd, odd, jnp.logical_or(jnp.logical_and(odd, high), jnp.logical_and(even, low))))
    return result


def both_sides(received, role):
    low, high = 0.0, 0.0
    for data, (_, from_high, used) in zip(received, role):
        high = high + jnp.where(jnp.logical_and(used, from_high), data, 0.0)
        low = low + jnp.where(jnp.logical_and(used, jnp.logical_not(from_high)), data, 0.0)
    return low, high


def split(x):
    upper = x.astype(BF16)
    return upper, (x - upper.astype(F32)).astype(BF16)


def dot2(x, table):
    upper, lower = split(x)
    return jnp.dot(upper, table, preferred_element_type=F32) + jnp.dot(
        lower, table, preferred_element_type=F32
    )


class Plan:
    def __init__(self, components, viscosity_shape, mesh_sizes):
        points = DEGREE + 1
        self.p, self.c = points, components
        self.sizes = mesh_sizes
        ex, ey, ez = (n // points for n in viscosity_shape)
        assert ex == 1 and ez >= HALO
        self.ey, self.ez = ey, ez
        self.rows = points**3
        self.block = points * points
        self.step3, self.step4 = components * ey, (components + 1) * ey
        self.n3, self.n4 = (ez + 2 * HALO) * self.step3, ez * self.step4
        self.w3, self.w4 = -(-self.n3 // 128) * 128, -(-self.n4 // 128) * 128
        self.halo4 = HALO * self.step4
        assert points * self.halo4 <= self.w4 and 2 * self.halo4 <= self.w4
        weights, derivative = gll_tables(DEGREE)
        self.forward = derivative.astype(np.float32)
        self.squared = self.forward * self.forward
        self.weights = weights.astype(np.float32)
        self.end = np.diagonal(self.forward)
        self.tables()

    def lane3(self, g, c, f):
        return (g + HALO) * self.step3 + c * self.ey + f

    def lane4(self, g, c, f):
        return g * self.step4 + c * self.ey + f

    def tables(self):
        p, c, ey, ez = self.p, self.c, self.ey, self.ez
        lanes = ez * p
        every = [(g, cc, f) for g in range(ez) for cc in range(c) for f in range(ey)]
        diagonal = np.zeros((self.w3, self.w4), np.float32)
        widen = np.zeros((2 * self.w4, 2 * self.w3), np.float32)
        ids = np.full((2 * c, 128, 128), -1, np.int32)
        for g, cc, f in every:
            diagonal[self.lane3(g, 0, f), self.lane4(g, c, f)] = 1
            widen[self.lane4(g, cc, f), self.lane3(g, cc, f)] = 1
            widen[self.lane4(g, c, f), self.w3 + self.lane3(g, cc, f)] = 1
            ids[cc, :, self.lane4(g, cc, f)] = f * ez + g
            ids[c + cc, :, self.lane3(g, cc, f)] = f * ez + g
        self.ids = np.ascontiguousarray(ids[:, :1, :]).reshape(2 * c, 128)
        part = HALO * p
        self.part = part
        assert FIELDS * part <= lanes and 2 * ey * part <= 128
        halo = np.zeros((128, p, self.w3), np.float32)
        for side, first in ((0, -HALO), (1, ez)):
            for g in range(HALO):
                for cc in range(c):
                    for f in range(ey):
                        at = self.lane3(first + g, cc, f)
                        row = self.w4 + side * self.halo4 + g * self.step4
                        widen[row + cc * ey + f, at] = 1
                        widen[row + c * ey + f, self.w3 + at] = 1
                        for k in range(p):
                            halo[(side * ey + f) * part + g * p + k, k, at] = 1
        self.halo = halo.reshape(128, -1).astype(jnp.bfloat16)
        self.diagonal, self.widen = (x.astype(jnp.bfloat16) for x in (diagonal, widen))
        rolled = []
        for matrix in (self.forward, self.forward.T, self.squared.T):
            for d in range(p):
                rolled += [matrix[a, (a + d) % p] for a in range(p)]
        node = [(j, k) for j in range(p) for k in range(p)]
        wjk = [self.weights[j] * self.weights[k] for j, k in node]
        second = [self.end[j] for j, k in node]
        third = [self.end[k] for j, k in node]
        column = np.asarray(rolled + wjk + second + third, np.float32)
        self.table = np.ascontiguousarray(np.broadcast_to(column[:, None], (column.size, 128)))


    def rolled(self, table, which):
        p = self.p
        return [table[(which * p + d) * p : (which * p + d + 1) * p, :] for d in range(p)]

    def node_table(self, table, which):
        start = 3 * self.p * self.p + which * self.block
        return table[start : start + self.block, :]

    def along_j(self, x, matrix):
        p = self.p
        x = x.reshape(p, p, x.shape[-1])
        out = []
        for a in range(p):
            total = None
            for i in range(p):
                value = float(matrix[a, i])
                if value != 0.0:
                    term = value * x[i]
                    total = term if total is None else total + term
            out.append(total)
        return jnp.concatenate(out, axis=0)

    def along_k(self, x, coefficients):
        p = self.p
        x3 = x.reshape(p, p, x.shape[-1])
        total = coefficients[0][None] * x3
        for d in range(1, p):
            total = total + coefficients[d][None] * pltpu.roll(x3, p - d, 1)
        return total.reshape(x.shape)

    def along_i(self, source, matrix, write):
        p = self.p

        def body(j, carry):
            at = pl.multiple_of(j * p, p)
            x = [source[pl.ds(i * self.block + at, p), :] for i in range(p)]
            for a in range(p):
                total = None
                for i in range(p):
                    value = float(matrix[a, i])
                    if value != 0.0:
                        term = value * x[i]
                        total = term if total is None else total + term
                write(a * self.block + at, total)
            return carry

        lax.fori_loop(0, p, body, 0)

    def operator(self, v, g, out, slope, flux, table):
        p, block = self.p, self.block
        ahead, back = self.rolled(table, 0), self.rolled(table, 1)

        def store(row, value):
            slope[pl.ds(row, p), :] = value

        self.along_i(v, self.forward, store)

        def body(i, carry):
            at = pl.ds(pl.multiple_of(i * block, block), block)
            x = v[at, :]
            s1 = slope[at, :]
            s2 = self.along_j(x, self.forward)
            s3 = self.along_k(x, ahead)
            xy, xz, yz = g[3, at, :], g[4, at, :], g[5, at, :]
            flux[at, :] = g[0, at, :] * s1 + xy * s2 + xz * s3
            f2 = xy * s1 + g[1, at, :] * s2 + yz * s3
            f3 = xz * s1 + yz * s2 + g[2, at, :] * s3
            out[at, :] = (
                self.along_j(f2, self.forward.T) + self.along_k(f3, back) + g[6, at, :] * x
            )
            return carry

        lax.fori_loop(0, p, body, 0)

        def add(row, value):
            out[pl.ds(row, p), :] += value

        self.along_i(flux, self.forward.T, add)

    def fold_second(self, u):
        if self.ey == 1:
            return
        p, width = self.p, u.shape[-1]
        lane = lax.broadcasted_iota(jnp.int32, (p, width), 1)
        f = lax.rem(lane, self.ey)
        for start in range(0, u.shape[0], self.block):
            first, last = u[start : start + p, :], u[start + self.block - p : start + self.block, :]
            u[start + self.block - p : start + self.block, :] = last + jnp.where(
                f < self.ey - 1, pltpu.roll(first, width - 1, 1), 0.0
            )
            u[start : start + p, :] = first + jnp.where(f > 0, pltpu.roll(last, 1, 1), 0.0)

    def fold_third(self, u, step, take_upper, take_lower):
        p, (rows, width) = self.p, u.shape
        count = rows // p
        lane = lax.broadcasted_iota(jnp.int32, (count, width), 1)
        first, last = u[pl.ds(0, count, stride=p), :], u[pl.ds(p - 1, count, stride=p), :]
        u[pl.ds(p - 1, count, stride=p), :] = last + jnp.where(
            take_upper(lane), pltpu.roll(first, width - step, 1), 0.0
        )
        u[pl.ds(0, count, stride=p), :] = first + jnp.where(
            take_lower(lane), pltpu.roll(last, step, 1), 0.0
        )

    def emit(self, u, x_out, y_out):
        p, block = self.p, self.block
        for out, (high, _, _) in zip(x_out, roles("gx", self.sizes["gx"])):
            out[...] = jnp.where(high, u[self.rows - block :, :], u[:block, :])
        for out, (high, _, _) in zip(y_out, roles("gy", self.sizes["gy"])):
            for i in range(p):
                start = i * block
                out[i * p : (i + 1) * p, :] = jnp.where(
                    high, u[start + block - p : start + block, :], u[start : start + p, :]
                )

    def subtract_shared(self, t, scale, x_in, y_in):
        p, block, rows = self.p, self.block, self.rows
        low, high = both_sides([x[...] for x in x_in], roles("gx", self.sizes["gx"]))
        if x_in:
            t[:block, :] -= scale[:block, :] * low
            t[rows - block :, :] -= scale[rows - block :, :] * high
        low, high = both_sides([y[...] for y in y_in], roles("gy", self.sizes["gy"]))
        if y_in:
            for i in range(p):
                at, end = i * block, (i + 1) * block
                t[at : at + p, :] -= scale[at : at + p, :] * low[i * p : (i + 1) * p]
                t[end - p : end, :] -= scale[end - p : end, :] * high[i * p : (i + 1) * p]

    def iteration_fold(self, u):
        self.fold_second(u)
        last = self.n3 - self.step3
        self.fold_third(u, self.step3, lambda l: l < last, lambda l: (l >= self.step3) & (l < self.n3))


    def pack_geometry(self, field, out):
        for target, (high, _, _) in zip(out, roles("gz", self.sizes["gz"])):
            rows, width = target.shape
            lane = lax.broadcasted_iota(jnp.int32, (rows, width), 1)
            total = jnp.zeros((rows, width), F32)
            for q in range(FIELDS):
                start = q * self.part
                upper = pltpu.roll(field(q), start + self.part, 1)
                lower = pltpu.roll(field(q), start, 1) if start else field(q)
                here = (lane >= start) & (lane < start + self.part)
                total = jnp.where(here, jnp.where(high, upper, lower), total)
            target[...] = total

    def by_nodes(self, upper, lower, table, store):
        w3 = self.w3
        for k in range(0, self.p, 2):
            columns = table[:, k * w3 : (k + 2) * w3]
            both = jnp.dot(upper[...], columns, preferred_element_type=F32) + jnp.dot(
                lower[...], columns, preferred_element_type=F32
            )
            store(k, both[:, :w3])
            store(k + 1, both[:, w3:])

    def one_hot(self, slots, ids):
        count = slots.shape[-1]
        column = jnp.broadcast_to(slots[...], (count, count))
        column = jnp.concatenate([column, jnp.zeros((count, 128 - count), jnp.int32)], axis=1)
        column = jnp.concatenate([column, jnp.zeros((128 - count, 128), jnp.int32)], axis=0)
        column = column.astype(F32).T[:count, :1]
        return jnp.concatenate(
            [jnp.where(column == ids[n : n + 1, :].astype(F32), 1.0, 0.0) for n in range(self.c)], axis=0
        ).astype(BF16)

    def spread_table(self, out):
        p, ey, ez, w3 = self.p, self.ey, self.ez, self.w3
        shape = (ey * ez * p, w3)
        row = lax.broadcasted_iota(jnp.int32, shape, 0)
        lane = lax.broadcasted_iota(jnp.int32, (1, w3), 1)
        g = lane // self.step3 - HALO
        element = jnp.where((g >= 0) & (g < ez), lax.rem(lane, ey) * ez + g, -1)
        same = row // p == element
        node = lax.rem(row, p)
        for k in range(p):
            out[:, k * w3 : (k + 1) * w3] = jnp.where(same & (node == k), 1.0, 0.0).astype(BF16)

    def prepare(self, n_x, n_y, n_z, *refs):
        geometry, viscosity, spread, dirichlet, table, diagonal, right, slots, ids = refs[:9]
        s4, ind, raw, hot3 = refs[9:13]
        refs = refs[13:]
        x_out, y_out, z_out = refs[:n_x], refs[n_x : n_x + n_y], refs[n_x + n_y : n_x + n_y + n_z]
        upper, lower, stiff, work = refs[n_x + n_y + n_z :]
        p, c, block, rows, ey = self.p, self.c, self.block, self.rows, self.ey
        width = geometry.shape[-1]

        def field(q):
            return (geometry[q] if q < FIELDS - 1 else viscosity[...]).reshape(p * ey * p, width)

        for q in range(FIELDS):
            value = field(q).reshape(p, ey, p, width)
            for f in range(ey):
                at = (slice(q * block, (q + 1) * block), slice(f * width, (f + 1) * width))
                upper[at], lower[at] = split(value[:, f].reshape(block, width))
        first_flag, flags = FIELDS * block, 2 * p
        for cc in range(c):
            for f in range(ey):
                at = slice(f * p, (f + 1) * p)
                face = jnp.concatenate([dirichlet[0, cc, at, :], dirichlet[1, cc, at, :]], axis=0)
                to = slice(first_flag + cc * flags, first_flag + (cc + 1) * flags)
                upper[to, f * width : (f + 1) * width] = face.astype(F32).astype(BF16)
                lower[to, f * width : (f + 1) * width] = jnp.zeros((flags, width), BF16)
        row = lax.broadcasted_iota(jnp.int32, (flags, self.w3), 0)
        lane = lax.broadcasted_iota(jnp.int32, (flags, self.w3), 1)
        ends = (lax.axis_index("gx") == 0, lax.axis_index("gx") == self.sizes["gx"] - 1)
        here = ((row < p) & ends[0]) | ((row >= p) & ends[1])
        owner = lax.rem(lane, self.step3) // ey

        def store(k, value):
            raw[pl.ds(k, first_flag, stride=p), :] = value[:first_flag]
            total = jnp.zeros((flags, self.w3), F32)
            for cc in range(c):
                at = first_flag + cc * flags
                total = jnp.where(owner == cc, value[at : at + flags], total)
            ind[pl.ds(k, flags, stride=p), :] = jnp.where(here, total, 0.0)

        self.by_nodes(upper, lower, spread, store)
        self.pack_geometry(field, z_out)
        wjk, second, third = (self.node_table(table, n) for n in range(3))
        square = self.rolled(table, 2)
        for i in range(p):
            at = slice(i * block, (i + 1) * block)
            xx, yy, zz, xy, xz, yz = (raw[q * rows + i * block : q * rows + (i + 1) * block, :] for q in range(6))
            quadrature = float(self.weights[i]) * wjk
            weighted = quadrature * raw[6 * rows + i * block : 6 * rows + (i + 1) * block, :]
            mass = (helm_coefficient * quadrature) * (
                xx * (yy * zz - yz * yz) - xy * (xy * zz - yz * xz) + xz * (xy * yz - yy * xz)
            )
            cross = second * third * yz
            end = float(self.end[i])
            if end != 0.0:
                cross = cross + end * (second * xy + third * xz)
            stiff[at, :] = weighted * xx
            work[at, :] = (
                self.along_j(weighted * yy, self.squared.T)
                + self.along_k(weighted * zz, square)
                + (2.0 * weighted) * cross
                + mass
            )

        def add(row, value):
            work[pl.ds(row, p), :] += value

        self.along_i(stiff, self.squared.T, add)
        total = dot2(work[...], diagonal[...])
        hot = self.one_hot(slots, ids)
        hot3[...] = self.one_hot(slots, ids[c:, :])
        for part in split(right[...].reshape(hot.shape[0], rows)):
            total = total + lax.dot_general(
                part, hot, (((0,), (0,)), ((), ())), preferred_element_type=F32
            )
        s4[...] = total
        self.fold_second(s4)
        self.fold_second(ind)
        last = self.n4 - self.step4
        self.fold_third(s4, self.step4, lambda l: l < last, lambda l: (l >= self.step4) & (l < self.n4))
        first_own, end_own = HALO * self.step3, self.n3 - HALO * self.step3
        self.fold_third(
            ind,
            self.step3,
            lambda l: (l >= first_own) & (l < end_own - self.step3),
            lambda l: (l >= first_own + self.step3) & (l < end_own),
        )
        self.emit(s4, x_out, y_out)
        for out, (up, _, _) in zip(y_out, roles("gy", self.sizes["gy"])):
            for n in range(2):
                start = n * block
                out[block + n * p : block + (n + 1) * p, :] = jnp.where(
                    up, ind[start + block - p : start + block, :], ind[start : start + p, :]
                )

    def halo_geometry(self, n_z, *refs):
        raw, halo, table, low, high = refs[:5]
        z_in, (g, coef) = refs[5 : 5 + n_z], refs[5 + n_z : 7 + n_z]
        upper, lower, total = refs[7 + n_z :]
        p, block, rows, ey = self.p, self.block, self.rows, self.ey
        top, bottom = jnp.full((8, 128), high[0], F32), jnp.full((8, 128), low[0], F32)
        midpoint, halfwidth = (top + bottom) * 0.5, (top - bottom) * 0.5
        ratio = midpoint / halfwidth
        damping = 1.0 / ratio
        coef[0:8, :] = 1.0 / midpoint
        for n in range(ITERS - 1):
            following = 1.0 / (2.0 * ratio - damping)
            coef[8 * (2 * n + 1) : 8 * (2 * n + 2), :] = following * damping
            coef[8 * (2 * n + 2) : 8 * (2 * n + 3), :] = 2.0 * following / halfwidth
            damping = following
        source = raw
        if n_z:
            sides = both_sides([z[...] for z in z_in], roles("gz", self.sizes["gz"]))
            width, part = sides[0].shape[-1], self.part
            sides = [side.reshape(p, ey, p, width) for side in sides]
            lane = lax.broadcasted_iota(jnp.int32, (block, width), 1)
            for q in range(FIELDS):
                value = jnp.zeros((block, width), F32)
                for side in range(2):
                    for f in range(ey):
                        to = (side * ey + f) * part
                        shift = (to - q * part) % width
                        x = sides[side][:, f].reshape(block, width)
                        x = pltpu.roll(x, shift, 1) if shift else x
                        value = jnp.where((lane >= to) & (lane < to + part), x, value)
                at = slice(q * block, (q + 1) * block)
                upper[at, :], lower[at, :] = split(value)

            def store(k, value):
                at = pl.ds(k, FIELDS * block, stride=p)
                total[at, :] = raw[at, :] + value

            self.by_nodes(upper, lower, halo, store)
            source = total
        wjk = self.node_table(table, 0)
        for i in range(p):
            at = slice(i * block, (i + 1) * block)
            entries = [source[q * rows + i * block : q * rows + (i + 1) * block, :] for q in range(FIELDS)]
            xx, yy, zz, xy, xz, yz = entries[:6]
            quadrature = float(self.weights[i]) * wjk
            weighted = quadrature * entries[6]
            g[6, at, :] = (helm_coefficient * quadrature) * (
                xx * (yy * zz - yz * yz) - xy * (xy * zz - yz * xz) + xz * (xy * yz - yy * xz)
            )
            for q in range(6):
                g[q, at, :] = weighted * entries[q]

    def join(self, n_x, n_y, *refs):
        x_in, y_raw, y_out = refs[:n_x], refs[n_x : n_x + n_y], refs[n_x + n_y :]
        p, block, ey = self.p, self.block, self.ey
        low, high = both_sides([x[...] for x in x_in], roles("gx", self.sizes["gx"]))
        for raw, out, (up, _, _) in zip(y_raw, y_out, roles("gy", self.sizes["gy"])):
            width = raw.shape[-1]
            face = raw[...]
            if n_x:
                first, last = (jnp.where(up, x[block - p :], x[:p]) for x in (low, high))
                parts = [face[:p] + first, face[p : block - p], face[block - p : block] + last]
                parts += [face[block:]] if face.shape[0] > block else []
                face = jnp.concatenate(parts, axis=0)
            f = lax.rem(lax.broadcasted_iota(jnp.int32, face.shape, 1), ey)
            if ey > 1:
                to_first = jnp.where(f == 0, pltpu.roll(face, width - (ey - 1), 1), 0.0)
                to_last = jnp.where(f == ey - 1, pltpu.roll(face, ey - 1, 1), 0.0)
                face = jnp.where(up, to_first, to_last)
            out[...] = face

    def pack(self, n_x, n_y, *refs):
        s4, ind = refs[:2]
        x_in, y_in = refs[2 : 2 + n_x], refs[2 + n_x : 2 + n_x + n_y]
        s_out, i_out = refs[2 + n_x + n_y : 4 + n_x + n_y]
        z_out = refs[4 + n_x + n_y :]
        p, block, rows = self.p, self.block, self.rows
        s_out[...] = s4[...]
        i_out[...] = ind[...]
        if n_x:
            low, high = both_sides([x[...] for x in x_in], roles("gx", self.sizes["gx"]))
            s_out[:block, :] += low
            s_out[rows - block :, :] += high
        if n_y:
            low, high = both_sides([y[...] for y in y_in], roles("gy", self.sizes["gy"]))
            for u, first, count in ((s_out, 0, p), (i_out, p, 2)):
                for i in range(count):
                    at, end, row = i * block, (i + 1) * block, (first + i) * p
                    u[at : at + p, :] += low[row : row + p]
                    u[end - p : end, :] += high[row : row + p]
        width, size = self.w4, self.halo4
        own3, halo3 = HALO * self.step3, HALO * self.step3
        for out, (up, _, _) in zip(z_out, roles("gz", self.sizes["gz"])):
            for u, count, first, last, start in (
                (s_out, block, 0, self.n4 - size, 0),
                (i_out, p, own3, self.n3 - 2 * halo3, block),
            ):
                lane = lax.broadcasted_iota(jnp.int32, (count, width), 1)
                for section in range(0, u.shape[0] // count, p):
                    total = jnp.zeros((count, width), F32)
                    for n in range(p):
                        at = (section + n) * count
                        x = u[at : at + count, :]
                        shift = n * size
                        below = pltpu.roll(x, (shift - first) % width, 1) if (shift - first) % width else x
                        above = pltpu.roll(x, (shift - last) % width, 1)
                        here = (lane >= shift) & (lane < shift + size)
                        total = jnp.where(here, jnp.where(up, above, below), total)
                    row = start + section // p * count
                    out[row : row + count, :] = total

    def start(self, n_x, n_y, n_z, *refs):
        s4, ind, g, coef, widen, table = refs[:6]
        z_in = refs[6 : 6 + n_z]
        t, d, scale, v = refs[6 + n_z : 10 + n_z]
        refs = refs[10 + n_z :]
        x_out, y_out = refs[:n_x], refs[n_x : n_x + n_y]
        upper, lower, r, flag, slope, flux = refs[n_x + n_y :]
        p, block, rows, w3, w4 = self.p, self.block, self.rows, self.w3, self.w4
        step, first_own, end_own = self.step3, HALO * self.step3, self.n3 - HALO * self.step3
        size, part = self.sizes["gz"], self.halo4
        if n_z:
            low, high = both_sides([z[...] for z in z_in], roles("gz", size))
        else:
            low = high = jnp.zeros((block + 2 * p, w4), F32)
        lane = lax.broadcasted_iota(jnp.int32, (block, w4), 1)
        for n in range(p):
            first = pltpu.roll(low[:block], w4 - n * part, 1) if n else low[:block]
            second = pltpu.roll(high[:block], (part - n * part) % w4, 1) if n != 1 else high[:block]
            beside = jnp.where(lane < part, first, jnp.where(lane < 2 * part, second, 0.0))
            at = slice(n * block, (n + 1) * block)
            upper[at, :w4], lower[at, :w4] = split(s4[at, :])
            upper[at, w4:], lower[at, w4:] = split(beside)
        both = jnp.dot(upper[...], widen[...], preferred_element_type=F32) + jnp.dot(
            lower[...], widen[...], preferred_element_type=F32
        )
        r[...] = both[:, :w3]
        scale[...] = both[:, w3:]
        lane = lax.broadcasted_iota(jnp.int32, (p, w3), 1)
        for n in range(2 * p):
            row, shift = block + n // p * p, n % p * part
            first = pltpu.roll(low[row : row + p], w3 - shift, 1) if shift else low[row : row + p]
            second = pltpu.roll(high[row : row + p], (end_own - shift) % w3, 1)
            flag[n * p : (n + 1) * p, :] = jnp.where(
                lane < first_own,
                first,
                jnp.where(lane < end_own, ind[n * p : (n + 1) * p, :], jnp.where(lane < self.n3, second, 0.0)),
            )
        for u in (r, scale, flag):
            self.fold_third(
                u,
                step,
                lambda l: ((l >= first_own - step) & (l < first_own)) | ((l >= end_own - step) & (l < end_own)),
                lambda l: ((l >= first_own) & (l < first_own + step)) | ((l >= end_own) & (l < end_own + step)),
            )
        index = lax.axis_index("gz")
        begin = jnp.where(index > 0, 0, first_own)
        end = jnp.where(index < size - 1, self.n3, end_own)
        lane = lax.broadcasted_iota(jnp.int32, (block, w3), 1)
        valid = (lane >= begin) & (lane < end)
        middle = coef[0:1, :]
        for i in range(p):
            at = slice(i * block, (i + 1) * block)
            factor = jnp.where(valid, 1.0 / jnp.where(valid, scale[at, :], 1.0), 0.0)
            if i in (0, p - 1):
                row = 0 if i == 0 else block
                factor = jnp.where(flag[row : row + block, :] > 0.5, 0.0, factor)
            scale[at, :] = factor
            scaled = factor * r[at, :]
            t[at, :] = scaled
            d[at, :] = scaled * middle
        self.operator(d, g, v, slope, flux, table)
        self.iteration_fold(v)
        self.emit(v, x_out, y_out)

    def advance(self, t, t_new, d, v, scale, coef, which, x_in, y_in, put):
        t_new[...] = t[...] - scale[...] * v[...]
        self.subtract_shared(t_new, scale, x_in, y_in)
        keep, gain = (coef[8 * (2 * which + n) : 8 * (2 * which + n) + 1, :] for n in (1, 2))
        for i in range(self.p):
            at = slice(i * self.block, (i + 1) * self.block)
            put(at, keep * d[at, :] + gain * t_new[at, :])

    def middle(self, n_x, n_y, which, *refs):
        t, d, scale, v, total, g, coef, table = refs[:8]
        refs = refs[8:]
        x_in, y_in, refs = refs[:n_x], refs[n_x : n_x + n_y], refs[n_x + n_y :]
        t_new, d_new, v_new, total_new = refs[:4]
        x_out, y_out = refs[4 : 4 + n_x], refs[4 + n_x : 4 + n_x + n_y]
        slope, flux = refs[4 + n_x + n_y :]

        def put(at, x):
            d_new[at, :] = x
            total_new[at, :] = total[at, :] + x

        self.advance(t, t_new, d, v, scale, coef, which, x_in, y_in, put)
        self.operator(d_new, g, v_new, slope, flux, table)
        self.iteration_fold(v_new)
        self.emit(v_new, x_out, y_out)

    def finish(self, n_x, n_y, which, *refs):
        t, d, scale, v, total, coef, hot = refs[:7]
        refs = refs[7:]
        x_in, y_in, refs = refs[:n_x], refs[n_x : n_x + n_y], refs[n_x + n_y :]
        out, t_new, field = refs

        def put(at, x):
            field[at, :] = total[at, :] + x

        self.advance(t, t_new, d, v, scale, coef, which, x_in, y_in, put)
        value = None
        for part in split(field[...]):
            term = lax.dot_general(
                hot[...], part, (((1,), (1,)), ((), ())), preferred_element_type=F32
            )
            value = term if value is None else value + term
        out[...] = value.reshape(out.shape)


def shards(sizes, right_side, geometry, viscosity, eig_low, eig_high, element_slot, dirichlet):
    plan = Plan(right_side.shape[0], viscosity.shape, sizes)
    p, block, rows, w3, w4 = plan.p, plan.block, plan.rows, plan.w3, plan.w4
    x_pairs = pairings(("gx",), (sizes["gx"],), 0)
    y_pairs = pairings(("gy",), (sizes["gy"],), 0)
    z_pairs = pairings(("gy", "gz"), (sizes["gy"], sizes["gz"]), 1)
    n_x, n_y, n_z = len(x_pairs), len(y_pairs), len(z_pairs)

    def send(arrays, axis, pairs):
        return [lax.ppermute(x, axis, pair) for x, pair in zip(arrays, pairs)]

    def shape(*size, dtype=F32):
        return jax.ShapeDtypeStruct(size, dtype)

    def call(kernel, outputs, operands, scratch=(), spaces={}, flops=0, name=None):
        specs = [pl.BlockSpec(memory_space=spaces.get(n, pltpu.VMEM)) for n in range(len(operands))]
        return list(
            pl.pallas_call(
                kernel,
                out_shape=list(outputs),
                in_specs=specs,
                out_specs=[pl.BlockSpec(memory_space=pltpu.VMEM)] * len(outputs),
                scratch_shapes=list(scratch),
                compiler_params=pltpu.CompilerParams(vmem_limit_bytes=VMEM_BYTES),
                cost_estimate=pl.CostEstimate(flops=flops, bytes_accessed=0, transcendentals=0),
                name=name,
            )(*operands)
        )

    def vmem(*size, dtype=F32):
        return pltpu.VMEM(size, dtype)

    lanes = plan.ez * p
    table = jnp.asarray(plan.table)
    field3, field4 = shape(rows, w3), shape(rows, w4)
    elements = element_slot.shape[-1]
    spread = call(
        plan.spread_table, [shape(plan.ey * lanes, p * w3, dtype=BF16)], (), flops=FLOPS, name="spread_table"
    )[0]
    operands = (
        geometry,
        viscosity,
        spread,
        dirichlet,
        table,
        jnp.asarray(plan.diagonal),
        jnp.swapaxes(right_side, 1, 2),
        element_slot,
        jnp.asarray(plan.ids),
    )
    lhs = FIELDS * block + 2 * plan.c * p
    results = call(
        functools.partial(plan.prepare, n_x, n_y, n_z),
        [
            field4,
            shape(2 * block, w3),
            shape(FIELDS * rows, w3),
            shape(plan.c * elements, w3, dtype=BF16),
        ]
        + [shape(block, w4)] * n_x
        + [shape(block + 2 * p, w4)] * n_y
        + [shape(p * plan.ey * p, lanes)] * n_z,
        operands,
        scratch=[vmem(lhs, plan.ey * lanes, dtype=BF16)] * 2 + [vmem(rows, w3)] * 2,
        name="prepare",
    )
    s4, ind, raw, hot3 = results[:4]
    results = results[4:]
    x_out, y_raw, z_geometry = results[:n_x], results[n_x : n_x + n_y], results[n_x + n_y :]
    x_in = send(x_out, "gx", x_pairs)
    def joined(x_in, y_raw):
        if not y_raw:
            return []
        faces = [shape(*y.shape) for y in y_raw]
        return call(functools.partial(plan.join, n_x, n_y), faces, x_in + y_raw, name="join")

    y_in = send(joined(x_in, y_raw), "gy", y_pairs)
    z_geometry = send(z_geometry, ("gy", "gz"), z_pairs)
    g, coef = call(
        functools.partial(plan.halo_geometry, n_z),
        [shape(FIELDS, rows, w3), shape(8 * (2 * ITERS - 1), 128)],
        [raw, jnp.asarray(plan.halo), table, eig_low, eig_high] + z_geometry,
        scratch=[vmem(FIELDS * block, 128, dtype=BF16)] * 2 + [vmem(FIELDS * rows, w3)],
        spaces={3: pltpu.SMEM, 4: pltpu.SMEM},
        flops=2000000,
        name="halo_geometry",
    )

    results = call(
        functools.partial(plan.pack, n_x, n_y),
        [field4, shape(2 * block, w3)] + [shape(block + 2 * p, w4)] * n_z,
        [s4, ind] + x_in + y_in,
        name="pack",
    )
    s4, ind = results[:2]
    z_in = send(results[2:], ("gy", "gz"), z_pairs)

    messages = [shape(block, w3)] * (n_x + n_y)
    results = call(
        functools.partial(plan.start, n_x, n_y, n_z),
        [field3] * 4 + messages,
        [s4, ind, g, coef, jnp.asarray(plan.widen), table] + z_in,
        scratch=[vmem(rows, 2 * w4, dtype=BF16)] * 2
        + [vmem(rows, w3), vmem(2 * block, w3), vmem(rows, w3), vmem(rows, w3)],
        name="first_direction",
    )
    t, d, scale, v = results[:4]
    total = d
    for n in range(ITERS - 1):
        x_out, y_raw = results[4 : 4 + n_x], results[4 + n_x :]
        x_in = send(x_out, "gx", x_pairs)
        y_in = send(joined(x_in, y_raw), "gy", y_pairs)
        if n < ITERS - 2:
            results = call(
                functools.partial(plan.middle, n_x, n_y, n),
                [field3] * 4 + messages,
                [t, d, scale, v, total, g, coef, table] + x_in + y_in,
                scratch=[vmem(rows, w3)] * 2,
                name="direction",
            )
            t, d, v, total = results[:4]
        else:
            out = call(
                functools.partial(plan.finish, n_x, n_y, n),
                [shape(plan.c, elements, rows)],
                [t, d, scale, v, total, coef, hot3] + x_in + y_in,
                scratch=[vmem(rows, w3)] * 2,
                name="field",
            )[0]
            return jnp.swapaxes(out, 1, 2)


def solution(mesh):
    sizes = {name: mesh.shape[name] for name in ("gx", "gy", "gz")}
    return jax.shard_map(
        functools.partial(shards, sizes),
        mesh=mesh,
        in_specs=(
            P(None, None, ("gx", "gy", "gz")),
            P(None, "gx", "gy", "gz"),
            P("gx", "gy", "gz"),
            P(),
            P(),
            P(("gx", "gy", "gz"), None),
            P(None, None, "gy", "gz"),
        ),
        out_specs=P(None, None, ("gx", "gy", "gz")),
        check_vma=False,
    )
```

```python
import functools
import math

import jax
import jax.numpy as jnp
import numpy as np
from jax import lax
from jax.experimental import pallas as pl
from jax.experimental.pallas import tpu as pltpu
from jax.sharding import PartitionSpec as P

DEGREE = 7
ITERS = 3


helm_coefficient = 10.0


def legendre_pair(values, degree):
    previous = 0.0 * values + 1.0
    current = values.copy()
    for order in range(2, degree + 1):
        previous, current = (
            current,
            ((2 * order - 1) * values * current - (order - 1) * previous) / order,
        )
    return (current, previous)


def gll_tables(degree):
    start = np.cos(np.pi * np.arange(degree + 1) / degree)
    nodes_now = start.copy()
    for sweep in range(80):
        top_value, lower_value = legendre_pair(nodes_now, degree)
        nodes_now = nodes_now - (nodes_now * top_value - lower_value) / ((degree + 1) * top_value)
    gll_nodes = nodes_now[::-1].copy()
    gll_nodes[0] = -1.0
    gll_nodes[degree] = 1.0
    legendre_values = legendre_pair(gll_nodes, degree)[0]
    weights = 2.0 / (degree * (degree + 1) * legendre_values**2)
    differences = gll_nodes[:, None] - gll_nodes[None, :] + np.eye(degree + 1)
    derivative = legendre_values[:, None] / legendre_values[None, :] / differences
    derivative = derivative * (1.0 - np.eye(degree + 1))
    derivative[0, 0] = -degree * (degree + 1) / 4.0
    derivative[degree, degree] = degree * (degree + 1) / 4.0
    return (weights, derivative)


HALO = 2
FIELDS = 7
VMEM_BYTES = 40 * 1024 * 1024
FLOPS = 3 * 10**9
F32 = jnp.float32
BF16 = jnp.bfloat16


def pairings(names, sizes, dim):
    size = sizes[dim]
    if size == 1:
        return []
    if size % 2:
        shifts = (1, size - 1)
        partners = [[(i + shift) % size for i in range(size)] for shift in shifts]
    else:
        partners = [[i ^ 1 for i in range(size)]]
        if size > 2:
            partners.append([((i + 1) ^ 1) - 1 for i in range(size)])
    result = []
    for partner in partners:
        pairs = []
        for flat in range(math.prod(sizes)):
            place = list(np.unravel_index(flat, sizes))
            to = partner[place[dim]]
            if 0 <= to < size:
                place[dim] = to
            elif len(sizes) > 1 and sizes[1 - dim] % 2 == 0:
                place[1 - dim] ^= 1
            else:
                place[dim] = size - 1 - place[dim]
            pairs.append((flat, int(np.ravel_multi_index(place, sizes))))
        result.append(pairs)
    return result


def roles(name, size):
    if size == 1:
        return []
    index = lax.axis_index(name)
    low, high = index > 0, index < size - 1
    if size % 2:
        yes = index >= 0
        no = index < 0
        return [(yes, no, low), (no, yes, high)]
    even = lax.rem(index, 2) == 0
    odd = jnp.logical_not(even)
    result = [(even, even, index >= 0)]
    if size > 2:
        result.append((odd, odd, jnp.logical_or(jnp.logical_and(odd, high), jnp.logical_and(even, low))))
    return result


def both_sides(received, role):
    low, high = 0.0, 0.0
    for data, (_, from_high, used) in zip(received, role):
        high = high + jnp.where(jnp.logical_and(used, from_high), data, 0.0)
        low = low + jnp.where(jnp.logical_and(used, jnp.logical_not(from_high)), data, 0.0)
    return low, high


def split(x):
    upper = x.astype(BF16)
    return upper, (x - upper.astype(F32)).astype(BF16)


def dot2(x, table):
    upper, lower = split(x)
    return jnp.dot(upper, table, preferred_element_type=F32) + jnp.dot(
        lower, table, preferred_element_type=F32
    )


class Plan:
    def __init__(self, components, viscosity_shape, mesh_sizes):
        points = DEGREE + 1
        self.p, self.c = points, components
        self.sizes = mesh_sizes
        ex, ey, ez = (n // points for n in viscosity_shape)
        assert ex == 1 and ez >= HALO
        self.ey, self.ez = ey, ez
        self.rows = points**3
        self.block = points * points
        self.step3, self.step4 = components * ey, (components + 1) * ey
        self.n3, self.n4 = (ez + 2 * HALO) * self.step3, ez * self.step4
        self.w3, self.w4 = -(-self.n3 // 128) * 128, -(-self.n4 // 128) * 128
        self.halo4 = HALO * self.step4
        assert points * self.halo4 <= self.w4 and 2 * self.halo4 <= self.w4
        weights, derivative = gll_tables(DEGREE)
        self.forward = derivative.astype(np.float32)
        self.squared = self.forward * self.forward
        self.weights = weights.astype(np.float32)
        self.end = np.diagonal(self.forward)
        self.tables()

    def lane3(self, g, c, f):
        return (g + HALO) * self.step3 + c * self.ey + f

    def lane4(self, g, c, f):
        return g * self.step4 + c * self.ey + f

    def tables(self):
        p, c, ey, ez = self.p, self.c, self.ey, self.ez
        lanes = ez * p
        every = [(g, cc, f) for g in range(ez) for cc in range(c) for f in range(ey)]
        diagonal = np.zeros((self.w3, self.w4), np.float32)
        widen = np.zeros((2 * self.w4, 2 * self.w3), np.float32)
        ids = np.full((2 * c, 128, 128), -1, np.int32)
        for g, cc, f in every:
            diagonal[self.lane3(g, 0, f), self.lane4(g, c, f)] = 1
            widen[self.lane4(g, cc, f), self.lane3(g, cc, f)] = 1
            widen[self.lane4(g, c, f), self.w3 + self.lane3(g, cc, f)] = 1
            ids[cc, :, self.lane4(g, cc, f)] = f * ez + g
            ids[c + cc, :, self.lane3(g, cc, f)] = f * ez + g
        self.ids = np.ascontiguousarray(ids[:, :1, :]).reshape(2 * c, 128)
        part = HALO * p
        self.part = part
        assert FIELDS * part <= lanes and 2 * ey * part <= 128
        halo = np.zeros((128, p, self.w3), np.float32)
        for side, first in ((0, -HALO), (1, ez)):
            for g in range(HALO):
                for cc in range(c):
                    for f in range(ey):
                        at = self.lane3(first + g, cc, f)
                        row = self.w4 + side * self.halo4 + g * self.step4
                        widen[row + cc * ey + f, at] = 1
                        widen[row + c * ey + f, self.w3 + at] = 1
                        for k in range(p):
                            halo[(side * ey + f) * part + g * p + k, k, at] = 1
        self.halo = halo.reshape(128, -1).astype(jnp.bfloat16)
        self.diagonal, self.widen = (x.astype(jnp.bfloat16) for x in (diagonal, widen))
        self.third = [self.block_terms(matrix) for matrix in (self.forward, self.forward.T, self.squared.T)]
        node = [(j, k) for j in range(p) for k in range(p)]
        wjk = [self.weights[j] * self.weights[k] for j, k in node]
        second = [self.end[j] for j, k in node]
        third = [self.end[k] for j, k in node]
        column = np.asarray(wjk + second + third, np.float32)
        self.table = np.ascontiguousarray(np.broadcast_to(column[:, None], (column.size, 128)))

    def block_terms(self, matrix):
        size = self.rows // 4
        blocks = np.kron(np.eye(size // self.p), matrix).astype(np.float32)
        upper = blocks.astype(jnp.bfloat16)
        lower = (blocks - upper.astype(np.float32)).astype(jnp.bfloat16)
        return np.concatenate([upper, upper, lower], axis=1)


    def node_table(self, table, which):
        start = which * self.block
        return table[start : start + self.block, :]

    def contract(self, x, matrix):
        p = self.p
        sign = 1.0 if matrix[0, 0] * matrix[p - 1, p - 1] > 0 else -1.0
        half = p // 2
        sums = [x[i] + x[p - 1 - i] for i in range(half)]
        differences = [x[i] - x[p - 1 - i] for i in range(half)]
        out = [None] * p
        for a in range(half):
            even, odd = None, None
            for i in range(half):
                first, second = float(matrix[a, i]), float(matrix[a, p - 1 - i])
                even = self.gather(even, 0.5 * (first + second), sums[i])
                odd = self.gather(odd, 0.5 * (first - second), differences[i])
            out[a] = odd + even
            out[p - 1 - a] = even - odd if sign > 0 else odd - even
        return out

    @staticmethod
    def gather(total, factor, x):
        if factor == 0.0:
            return total
        return factor * x if total is None else total + factor * x

    def along_j(self, x, matrix):
        x = x.reshape(self.p, self.p, x.shape[-1])
        return jnp.concatenate(self.contract([x[j] for j in range(self.p)], matrix), axis=0)

    def along_i(self, source, matrix, write):
        p, block = self.p, self.block
        for j in range(p):
            rows = [i * block + j * p for i in range(p)]
            for row, value in zip(rows, self.contract([source[r : r + p, :] for r in rows], matrix)):
                write(row, value)

    def along_k(self, source, table, out):
        size = table.shape[0]
        for start in range(0, self.rows, 2 * size):
            pieces = [split(source[at : at + size, :]) for at in (start, start + size)]
            upper, lower = (jnp.concatenate([piece[n] for piece in pieces], axis=1) for n in range(2))
            both = jnp.dot(
                table[...], jnp.concatenate([upper, lower, upper], axis=0), preferred_element_type=F32
            )
            width = source.shape[-1]
            out[start : start + size, :] = both[:, :width]
            out[start + size : start + 2 * size, :] = both[:, width:]

    def operator(self, v, g, out, slope, flux, third, work, ahead, back):
        block = self.block

        def store(row, value):
            slope[row : row + self.p, :] = value

        self.along_i(v, self.forward, store)
        self.along_k(v, ahead, third)
        for i in range(self.p):
            at = slice(i * block, (i + 1) * block)
            x, s1, s3 = v[at, :], slope[at, :], third[at, :]
            s2 = self.along_j(x, self.forward)
            xy, xz, yz = g[3, at, :], g[4, at, :], g[5, at, :]
            flux[at, :] = g[0, at, :] * s1 + xy * s2 + xz * s3
            f2 = xy * s1 + g[1, at, :] * s2 + yz * s3
            work[at, :] = xz * s1 + yz * s2 + g[2, at, :] * s3
            out[at, :] = self.along_j(f2, self.forward.T) + g[6, at, :] * x
        self.along_k(work, back, third)

        def add(row, value):
            out[row : row + self.p, :] += value + third[row : row + self.p, :]

        self.along_i(flux, self.forward.T, add)

    def fold_second(self, u):
        if self.ey == 1:
            return
        p, width = self.p, u.shape[-1]
        lane = lax.broadcasted_iota(jnp.int32, (p, width), 1)
        f = lax.rem(lane, self.ey)
        for start in range(0, u.shape[0], self.block):
            first, last = u[start : start + p, :], u[start + self.block - p : start + self.block, :]
            u[start + self.block - p : start + self.block, :] = last + jnp.where(
                f < self.ey - 1, pltpu.roll(first, width - 1, 1), 0.0
            )
            u[start : start + p, :] = first + jnp.where(f > 0, pltpu.roll(last, 1, 1), 0.0)

    def fold_third(self, u, step, take_upper, take_lower):
        p, (rows, width) = self.p, u.shape
        count = rows // p
        lane = lax.broadcasted_iota(jnp.int32, (count, width), 1)
        first, last = u[pl.ds(0, count, stride=p), :], u[pl.ds(p - 1, count, stride=p), :]
        u[pl.ds(p - 1, count, stride=p), :] = last + jnp.where(
            take_upper(lane), pltpu.roll(first, width - step, 1), 0.0
        )
        u[pl.ds(0, count, stride=p), :] = first + jnp.where(
            take_lower(lane), pltpu.roll(last, step, 1), 0.0
        )

    def emit(self, u, x_out, y_out):
        p, block = self.p, self.block
        for out, (high, _, _) in zip(x_out, roles("gx", self.sizes["gx"])):
            out[...] = jnp.where(high, u[self.rows - block :, :], u[:block, :])
        for out, (high, _, _) in zip(y_out, roles("gy", self.sizes["gy"])):
            for i in range(p):
                start = i * block
                out[i * p : (i + 1) * p, :] = jnp.where(
                    high, u[start + block - p : start + block, :], u[start : start + p, :]
                )

    def subtract_shared(self, t, scale, x_in, y_in):
        p, block, rows = self.p, self.block, self.rows
        low, high = both_sides([x[...] for x in x_in], roles("gx", self.sizes["gx"]))
        if x_in:
            t[:block, :] -= scale[:block, :] * low
            t[rows - block :, :] -= scale[rows - block :, :] * high
        low, high = both_sides([y[...] for y in y_in], roles("gy", self.sizes["gy"]))
        if y_in:
            for i in range(p):
                at, end = i * block, (i + 1) * block
                t[at : at + p, :] -= scale[at : at + p, :] * low[i * p : (i + 1) * p]
                t[end - p : end, :] -= scale[end - p : end, :] * high[i * p : (i + 1) * p]

    def iteration_fold(self, u):
        self.fold_second(u)
        last = self.n3 - self.step3
        self.fold_third(u, self.step3, lambda l: l < last, lambda l: (l >= self.step3) & (l < self.n3))


    def pack_geometry(self, field, out):
        for target, (high, _, _) in zip(out, roles("gz", self.sizes["gz"])):
            rows, width = target.shape
            lane = lax.broadcasted_iota(jnp.int32, (rows, width), 1)
            total = jnp.zeros((rows, width), F32)
            for q in range(FIELDS):
                start = q * self.part
                upper = pltpu.roll(field(q), start + self.part, 1)
                lower = pltpu.roll(field(q), start, 1) if start else field(q)
                here = (lane >= start) & (lane < start + self.part)
                total = jnp.where(here, jnp.where(high, upper, lower), total)
            target[...] = total

    def by_nodes(self, upper, lower, table, store):
        w3 = self.w3
        for k in range(0, self.p, 2):
            columns = table[:, k * w3 : (k + 2) * w3]
            both = jnp.dot(upper[...], columns, preferred_element_type=F32) + jnp.dot(
                lower[...], columns, preferred_element_type=F32
            )
            store(k, both[:, :w3])
            store(k + 1, both[:, w3:])

    def one_hot(self, slots, ids):
        count = slots.shape[-1]
        column = jnp.broadcast_to(slots[...], (count, count))
        column = jnp.concatenate([column, jnp.zeros((count, 128 - count), jnp.int32)], axis=1)
        column = jnp.concatenate([column, jnp.zeros((128 - count, 128), jnp.int32)], axis=0)
        column = column.astype(F32).T[:count, :1]
        return jnp.concatenate(
            [jnp.where(column == ids[n : n + 1, :].astype(F32), 1.0, 0.0) for n in range(self.c)], axis=0
        ).astype(BF16)

    def spread_table(self, out):
        p, ey, ez, w3 = self.p, self.ey, self.ez, self.w3
        shape = (ey * ez * p, w3)
        row = lax.broadcasted_iota(jnp.int32, shape, 0)
        lane = lax.broadcasted_iota(jnp.int32, (1, w3), 1)
        g = lane // self.step3 - HALO
        element = jnp.where((g >= 0) & (g < ez), lax.rem(lane, ey) * ez + g, -1)
        same = row // p == element
        node = lax.rem(row, p)
        for k in range(p):
            out[:, k * w3 : (k + 1) * w3] = jnp.where(same & (node == k), 1.0, 0.0).astype(BF16)

    def prepare(self, n_x, n_y, n_z, *refs):
        geometry, viscosity, spread, dirichlet, table, diagonal, right, slots, ids, square = refs[:10]
        s4, ind, raw, hot3 = refs[10:14]
        refs = refs[14:]
        x_out, y_out, z_out = refs[:n_x], refs[n_x : n_x + n_y], refs[n_x + n_y : n_x + n_y + n_z]
        upper, lower, stiff, third, work = refs[n_x + n_y + n_z :]
        p, c, block, rows, ey = self.p, self.c, self.block, self.rows, self.ey
        width = geometry.shape[-1]

        def field(q):
            return (geometry[q] if q < FIELDS - 1 else viscosity[...]).reshape(p * ey * p, width)

        for q in range(FIELDS):
            value = field(q).reshape(p, ey, p, width)
            for f in range(ey):
                at = (slice(q * block, (q + 1) * block), slice(f * width, (f + 1) * width))
                upper[at], lower[at] = split(value[:, f].reshape(block, width))
        first_flag, flags = FIELDS * block, 2 * p
        for cc in range(c):
            for f in range(ey):
                at = slice(f * p, (f + 1) * p)
                face = jnp.concatenate([dirichlet[0, cc, at, :], dirichlet[1, cc, at, :]], axis=0)
                to = slice(first_flag + cc * flags, first_flag + (cc + 1) * flags)
                upper[to, f * width : (f + 1) * width] = face.astype(F32).astype(BF16)
                lower[to, f * width : (f + 1) * width] = jnp.zeros((flags, width), BF16)
        row = lax.broadcasted_iota(jnp.int32, (flags, self.w3), 0)
        lane = lax.broadcasted_iota(jnp.int32, (flags, self.w3), 1)
        ends = (lax.axis_index("gx") == 0, lax.axis_index("gx") == self.sizes["gx"] - 1)
        here = ((row < p) & ends[0]) | ((row >= p) & ends[1])
        owner = lax.rem(lane, self.step3) // ey

        def store(k, value):
            raw[pl.ds(k, first_flag, stride=p), :] = value[:first_flag]
            total = jnp.zeros((flags, self.w3), F32)
            for cc in range(c):
                at = first_flag + cc * flags
                total = jnp.where(owner == cc, value[at : at + flags], total)
            ind[pl.ds(k, flags, stride=p), :] = jnp.where(here, total, 0.0)

        self.by_nodes(upper, lower, spread, store)
        self.pack_geometry(field, z_out)
        wjk, end_j, end_k = (self.node_table(table, n) for n in range(3))
        for i in range(p):
            at = slice(i * block, (i + 1) * block)
            xx, yy, zz, xy, xz, yz = (raw[q * rows + i * block : q * rows + (i + 1) * block, :] for q in range(6))
            quadrature = float(self.weights[i]) * wjk
            weighted = quadrature * raw[6 * rows + i * block : 6 * rows + (i + 1) * block, :]
            mass = (helm_coefficient * quadrature) * (
                xx * (yy * zz - yz * yz) - xy * (xy * zz - yz * xz) + xz * (xy * yz - yy * xz)
            )
            cross = end_j * end_k * yz
            end = float(self.end[i])
            if end != 0.0:
                cross = cross + end * (end_j * xy + end_k * xz)
            stiff[at, :] = weighted * xx
            third[at, :] = weighted * zz
            work[at, :] = self.along_j(weighted * yy, self.squared.T) + (2.0 * weighted) * cross + mass
        self.along_k(third, square, third)

        def add(row, value):
            work[row : row + p, :] += value + third[row : row + p, :]

        self.along_i(stiff, self.squared.T, add)
        total = dot2(work[...], diagonal[...])
        hot = self.one_hot(slots, ids)
        hot3[...] = self.one_hot(slots, ids[c:, :])
        for part in split(right[...].reshape(hot.shape[0], rows)):
            total = total + lax.dot_general(
                part, hot, (((0,), (0,)), ((), ())), preferred_element_type=F32
            )
        s4[...] = total
        self.fold_second(s4)
        self.fold_second(ind)
        last = self.n4 - self.step4
        self.fold_third(s4, self.step4, lambda l: l < last, lambda l: (l >= self.step4) & (l < self.n4))
        first_own, end_own = HALO * self.step3, self.n3 - HALO * self.step3
        self.fold_third(
            ind,
            self.step3,
            lambda l: (l >= first_own) & (l < end_own - self.step3),
            lambda l: (l >= first_own + self.step3) & (l < end_own),
        )
        self.emit(s4, x_out, y_out)
        for out, (up, _, _) in zip(y_out, roles("gy", self.sizes["gy"])):
            for n in range(2):
                start = n * block
                out[block + n * p : block + (n + 1) * p, :] = jnp.where(
                    up, ind[start + block - p : start + block, :], ind[start : start + p, :]
                )

    def halo_geometry(self, n_z, *refs):
        raw, halo, table, low, high = refs[:5]
        z_in, (g, coef) = refs[5 : 5 + n_z], refs[5 + n_z : 7 + n_z]
        upper, lower, total = refs[7 + n_z :]
        p, block, rows, ey = self.p, self.block, self.rows, self.ey
        top, bottom = jnp.full((8, 128), high[0], F32), jnp.full((8, 128), low[0], F32)
        midpoint, halfwidth = (top + bottom) * 0.5, (top - bottom) * 0.5
        ratio = midpoint / halfwidth
        damping = 1.0 / ratio
        coef[0:8, :] = 1.0 / midpoint
        for n in range(ITERS - 1):
            following = 1.0 / (2.0 * ratio - damping)
            coef[8 * (2 * n + 1) : 8 * (2 * n + 2), :] = following * damping
            coef[8 * (2 * n + 2) : 8 * (2 * n + 3), :] = 2.0 * following / halfwidth
            damping = following
        source = raw
        if n_z:
            sides = both_sides([z[...] for z in z_in], roles("gz", self.sizes["gz"]))
            width, part = sides[0].shape[-1], self.part
            sides = [side.reshape(p, ey, p, width) for side in sides]
            lane = lax.broadcasted_iota(jnp.int32, (block, width), 1)
            for q in range(FIELDS):
                value = jnp.zeros((block, width), F32)
                for side in range(2):
                    for f in range(ey):
                        to = (side * ey + f) * part
                        shift = (to - q * part) % width
                        x = sides[side][:, f].reshape(block, width)
                        x = pltpu.roll(x, shift, 1) if shift else x
                        value = jnp.where((lane >= to) & (lane < to + part), x, value)
                at = slice(q * block, (q + 1) * block)
                upper[at, :], lower[at, :] = split(value)

            def store(k, value):
                at = pl.ds(k, FIELDS * block, stride=p)
                total[at, :] = raw[at, :] + value

            self.by_nodes(upper, lower, halo, store)
            source = total
        wjk = self.node_table(table, 0)
        for i in range(p):
            at = slice(i * block, (i + 1) * block)
            entries = [source[q * rows + i * block : q * rows + (i + 1) * block, :] for q in range(FIELDS)]
            xx, yy, zz, xy, xz, yz = entries[:6]
            quadrature = float(self.weights[i]) * wjk
            weighted = quadrature * entries[6]
            g[6, at, :] = (helm_coefficient * quadrature) * (
                xx * (yy * zz - yz * yz) - xy * (xy * zz - yz * xz) + xz * (xy * yz - yy * xz)
            )
            for q in range(6):
                g[q, at, :] = weighted * entries[q]

    def join(self, n_x, n_y, *refs):
        x_in, y_raw, y_out = refs[:n_x], refs[n_x : n_x + n_y], refs[n_x + n_y :]
        p, block, ey = self.p, self.block, self.ey
        low, high = both_sides([x[...] for x in x_in], roles("gx", self.sizes["gx"]))
        for raw, out, (up, _, _) in zip(y_raw, y_out, roles("gy", self.sizes["gy"])):
            width = raw.shape[-1]
            face = raw[...]
            if n_x:
                first, last = (jnp.where(up, x[block - p :], x[:p]) for x in (low, high))
                parts = [face[:p] + first, face[p : block - p], face[block - p : block] + last]
                parts += [face[block:]] if face.shape[0] > block else []
                face = jnp.concatenate(parts, axis=0)
            f = lax.rem(lax.broadcasted_iota(jnp.int32, face.shape, 1), ey)
            if ey > 1:
                to_first = jnp.where(f == 0, pltpu.roll(face, width - (ey - 1), 1), 0.0)
                to_last = jnp.where(f == ey - 1, pltpu.roll(face, ey - 1, 1), 0.0)
                face = jnp.where(up, to_first, to_last)
            out[...] = face

    def pack(self, n_x, n_y, *refs):
        s4, ind = refs[:2]
        x_in, y_in = refs[2 : 2 + n_x], refs[2 + n_x : 2 + n_x + n_y]
        s_out, i_out = refs[2 + n_x + n_y : 4 + n_x + n_y]
        z_out = refs[4 + n_x + n_y :]
        p, block, rows = self.p, self.block, self.rows
        s_out[...] = s4[...]
        i_out[...] = ind[...]
        if n_x:
            low, high = both_sides([x[...] for x in x_in], roles("gx", self.sizes["gx"]))
            s_out[:block, :] += low
            s_out[rows - block :, :] += high
        if n_y:
            low, high = both_sides([y[...] for y in y_in], roles("gy", self.sizes["gy"]))
            for u, first, count in ((s_out, 0, p), (i_out, p, 2)):
                for i in range(count):
                    at, end, row = i * block, (i + 1) * block, (first + i) * p
                    u[at : at + p, :] += low[row : row + p]
                    u[end - p : end, :] += high[row : row + p]
        width, size = self.w4, self.halo4
        own3, halo3 = HALO * self.step3, HALO * self.step3
        for out, (up, _, _) in zip(z_out, roles("gz", self.sizes["gz"])):
            for u, count, first, last, start in (
                (s_out, block, 0, self.n4 - size, 0),
                (i_out, p, own3, self.n3 - 2 * halo3, block),
            ):
                lane = lax.broadcasted_iota(jnp.int32, (count, width), 1)
                for section in range(0, u.shape[0] // count, p):
                    total = jnp.zeros((count, width), F32)
                    for n in range(p):
                        at = (section + n) * count
                        x = u[at : at + count, :]
                        shift = n * size
                        below = pltpu.roll(x, (shift - first) % width, 1) if (shift - first) % width else x
                        above = pltpu.roll(x, (shift - last) % width, 1)
                        here = (lane >= shift) & (lane < shift + size)
                        total = jnp.where(here, jnp.where(up, above, below), total)
                    row = start + section // p * count
                    out[row : row + count, :] = total

    def start(self, n_x, n_y, n_z, *refs):
        s4, ind, g, coef, widen, ahead, back = refs[:7]
        z_in = refs[7 : 7 + n_z]
        t, d, scale, v = refs[7 + n_z : 11 + n_z]
        refs = refs[11 + n_z :]
        x_out, y_out = refs[:n_x], refs[n_x : n_x + n_y]
        upper, lower, r, flag = refs[n_x + n_y : n_x + n_y + 4]
        work = refs[n_x + n_y + 4 :]
        p, block, rows, w3, w4 = self.p, self.block, self.rows, self.w3, self.w4
        step, first_own, end_own = self.step3, HALO * self.step3, self.n3 - HALO * self.step3
        size, part = self.sizes["gz"], self.halo4
        if n_z:
            low, high = both_sides([z[...] for z in z_in], roles("gz", size))
        else:
            low = high = jnp.zeros((block + 2 * p, w4), F32)
        lane = lax.broadcasted_iota(jnp.int32, (block, w4), 1)
        for n in range(p):
            first = pltpu.roll(low[:block], w4 - n * part, 1) if n else low[:block]
            second = pltpu.roll(high[:block], (part - n * part) % w4, 1) if n != 1 else high[:block]
            beside = jnp.where(lane < part, first, jnp.where(lane < 2 * part, second, 0.0))
            at = slice(n * block, (n + 1) * block)
            upper[at, :w4], lower[at, :w4] = split(s4[at, :])
            upper[at, w4:], lower[at, w4:] = split(beside)
        both = jnp.dot(upper[...], widen[...], preferred_element_type=F32) + jnp.dot(
            lower[...], widen[...], preferred_element_type=F32
        )
        r[...] = both[:, :w3]
        scale[...] = both[:, w3:]
        lane = lax.broadcasted_iota(jnp.int32, (p, w3), 1)
        for n in range(2 * p):
            row, shift = block + n // p * p, n % p * part
            first = pltpu.roll(low[row : row + p], w3 - shift, 1) if shift else low[row : row + p]
            second = pltpu.roll(high[row : row + p], (end_own - shift) % w3, 1)
            flag[n * p : (n + 1) * p, :] = jnp.where(
                lane < first_own,
                first,
                jnp.where(lane < end_own, ind[n * p : (n + 1) * p, :], jnp.where(lane < self.n3, second, 0.0)),
            )
        for u in (r, scale, flag):
            self.fold_third(
                u,
                step,
                lambda l: ((l >= first_own - step) & (l < first_own)) | ((l >= end_own - step) & (l < end_own)),
                lambda l: ((l >= first_own) & (l < first_own + step)) | ((l >= end_own) & (l < end_own + step)),
            )
        index = lax.axis_index("gz")
        begin = jnp.where(index > 0, 0, first_own)
        end = jnp.where(index < size - 1, self.n3, end_own)
        lane = lax.broadcasted_iota(jnp.int32, (block, w3), 1)
        valid = (lane >= begin) & (lane < end)
        middle = coef[0:1, :]
        for i in range(p):
            at = slice(i * block, (i + 1) * block)
            factor = jnp.where(valid, 1.0 / jnp.where(valid, scale[at, :], 1.0), 0.0)
            if i in (0, p - 1):
                row = 0 if i == 0 else block
                factor = jnp.where(flag[row : row + block, :] > 0.5, 0.0, factor)
            scale[at, :] = factor
            scaled = factor * r[at, :]
            t[at, :] = scaled
            d[at, :] = scaled * middle
        self.operator(d, g, v, *work, ahead, back)
        self.iteration_fold(v)
        self.emit(v, x_out, y_out)

    def advance(self, t, t_new, d, v, scale, coef, which, x_in, y_in, put):
        t_new[...] = t[...] - scale[...] * v[...]
        self.subtract_shared(t_new, scale, x_in, y_in)
        keep, gain = (coef[8 * (2 * which + n) : 8 * (2 * which + n) + 1, :] for n in (1, 2))
        for i in range(self.p):
            at = slice(i * self.block, (i + 1) * self.block)
            put(at, keep * d[at, :] + gain * t_new[at, :])

    def middle(self, n_x, n_y, which, *refs):
        t, d, scale, v, total, g, coef, ahead, back = refs[:9]
        refs = refs[9:]
        x_in, y_in, refs = refs[:n_x], refs[n_x : n_x + n_y], refs[n_x + n_y :]
        t_new, d_new, v_new, total_new = refs[:4]
        x_out, y_out = refs[4 : 4 + n_x], refs[4 + n_x : 4 + n_x + n_y]
        work = refs[4 + n_x + n_y :]

        def put(at, x):
            d_new[at, :] = x
            total_new[at, :] = total[at, :] + x

        self.advance(t, t_new, d, v, scale, coef, which, x_in, y_in, put)
        self.operator(d_new, g, v_new, *work, ahead, back)
        self.iteration_fold(v_new)
        self.emit(v_new, x_out, y_out)

    def finish(self, n_x, n_y, which, *refs):
        t, d, scale, v, total, coef, hot = refs[:7]
        refs = refs[7:]
        x_in, y_in, refs = refs[:n_x], refs[n_x : n_x + n_y], refs[n_x + n_y :]
        out, t_new, field = refs

        def put(at, x):
            field[at, :] = total[at, :] + x

        self.advance(t, t_new, d, v, scale, coef, which, x_in, y_in, put)
        value = None
        for part in split(field[...]):
            term = lax.dot_general(
                hot[...], part, (((1,), (1,)), ((), ())), preferred_element_type=F32
            )
            value = term if value is None else value + term
        out[...] = value.reshape(out.shape)


def shards(sizes, right_side, geometry, viscosity, eig_low, eig_high, element_slot, dirichlet):
    plan = Plan(right_side.shape[0], viscosity.shape, sizes)
    p, block, rows, w3, w4 = plan.p, plan.block, plan.rows, plan.w3, plan.w4
    x_pairs = pairings(("gx",), (sizes["gx"],), 0)
    y_pairs = pairings(("gy",), (sizes["gy"],), 0)
    z_pairs = pairings(("gy", "gz"), (sizes["gy"], sizes["gz"]), 1)
    n_x, n_y, n_z = len(x_pairs), len(y_pairs), len(z_pairs)

    def send(arrays, axis, pairs):
        return [lax.ppermute(x, axis, pair) for x, pair in zip(arrays, pairs)]

    def shape(*size, dtype=F32):
        return jax.ShapeDtypeStruct(size, dtype)

    def call(kernel, outputs, operands, scratch=(), spaces={}, flops=0, name=None):
        specs = [pl.BlockSpec(memory_space=spaces.get(n, pltpu.VMEM)) for n in range(len(operands))]
        return list(
            pl.pallas_call(
                kernel,
                out_shape=list(outputs),
                in_specs=specs,
                out_specs=[pl.BlockSpec(memory_space=pltpu.VMEM)] * len(outputs),
                scratch_shapes=list(scratch),
                compiler_params=pltpu.CompilerParams(vmem_limit_bytes=VMEM_BYTES),
                cost_estimate=pl.CostEstimate(flops=flops, bytes_accessed=0, transcendentals=0),
                name=name,
            )(*operands)
        )

    def vmem(*size, dtype=F32):
        return pltpu.VMEM(size, dtype)

    lanes = plan.ez * p
    table = jnp.asarray(plan.table)
    ahead, back = jnp.asarray(plan.third[0]), jnp.asarray(plan.third[1])
    field3, field4 = shape(rows, w3), shape(rows, w4)
    elements = element_slot.shape[-1]
    spread = call(
        plan.spread_table, [shape(plan.ey * lanes, p * w3, dtype=BF16)], (), flops=FLOPS, name="spread_table"
    )[0]
    operands = (
        geometry,
        viscosity,
        spread,
        dirichlet,
        table,
        jnp.asarray(plan.diagonal),
        jnp.swapaxes(right_side, 1, 2),
        element_slot,
        jnp.asarray(plan.ids),
        jnp.asarray(plan.third[2]),
    )
    lhs = FIELDS * block + 2 * plan.c * p
    results = call(
        functools.partial(plan.prepare, n_x, n_y, n_z),
        [
            field4,
            shape(2 * block, w3),
            shape(FIELDS * rows, w3),
            shape(plan.c * elements, w3, dtype=BF16),
        ]
        + [shape(block, w4)] * n_x
        + [shape(block + 2 * p, w4)] * n_y
        + [shape(p * plan.ey * p, lanes)] * n_z,
        operands,
        scratch=[vmem(lhs, plan.ey * lanes, dtype=BF16)] * 2 + [vmem(rows, w3)] * 3,
        name="prepare",
    )
    s4, ind, raw, hot3 = results[:4]
    results = results[4:]
    x_out, y_raw, z_geometry = results[:n_x], results[n_x : n_x + n_y], results[n_x + n_y :]
    x_in = send(x_out, "gx", x_pairs)
    def joined(x_in, y_raw):
        if not y_raw:
            return []
        faces = [shape(*y.shape) for y in y_raw]
        return call(functools.partial(plan.join, n_x, n_y), faces, x_in + y_raw, name="join")

    y_in = send(joined(x_in, y_raw), "gy", y_pairs)
    z_geometry = send(z_geometry, ("gy", "gz"), z_pairs)
    g, coef = call(
        functools.partial(plan.halo_geometry, n_z),
        [shape(FIELDS, rows, w3), shape(8 * (2 * ITERS - 1), 128)],
        [raw, jnp.asarray(plan.halo), table, eig_low, eig_high] + z_geometry,
        scratch=[vmem(FIELDS * block, 128, dtype=BF16)] * 2 + [vmem(FIELDS * rows, w3)],
        spaces={3: pltpu.SMEM, 4: pltpu.SMEM},
        flops=2000000,
        name="halo_geometry",
    )

    results = call(
        functools.partial(plan.pack, n_x, n_y),
        [field4, shape(2 * block, w3)] + [shape(block + 2 * p, w4)] * n_z,
        [s4, ind] + x_in + y_in,
        name="pack",
    )
    s4, ind = results[:2]
    z_in = send(results[2:], ("gy", "gz"), z_pairs)

    messages = [shape(block, w3)] * (n_x + n_y)
    results = call(
        functools.partial(plan.start, n_x, n_y, n_z),
        [field3] * 4 + messages,
        [s4, ind, g, coef, jnp.asarray(plan.widen), ahead, back] + z_in,
        scratch=[vmem(rows, 2 * w4, dtype=BF16)] * 2
        + [vmem(rows, w3), vmem(2 * block, w3)]
        + [vmem(rows, w3)] * 4,
        name="first_direction",
    )
    t, d, scale, v = results[:4]
    total = d
    for n in range(ITERS - 1):
        x_out, y_raw = results[4 : 4 + n_x], results[4 + n_x :]
        x_in = send(x_out, "gx", x_pairs)
        y_in = send(joined(x_in, y_raw), "gy", y_pairs)
        if n < ITERS - 2:
            results = call(
                functools.partial(plan.middle, n_x, n_y, n),
                [field3] * 4 + messages,
                [t, d, scale, v, total, g, coef, ahead, back] + x_in + y_in,
                scratch=[vmem(rows, w3)] * 4,
                name="direction",
            )
            t, d, v, total = results[:4]
        else:
            out = call(
                functools.partial(plan.finish, n_x, n_y, n),
                [shape(plan.c, elements, rows)],
                [t, d, scale, v, total, coef, hot3] + x_in + y_in,
                scratch=[vmem(rows, w3)] * 2,
                name="field",
            )[0]
            return jnp.swapaxes(out, 1, 2)


def solution(mesh):
    sizes = {name: mesh.shape[name] for name in ("gx", "gy", "gz")}
    return jax.shard_map(
        functools.partial(shards, sizes),
        mesh=mesh,
        in_specs=(
            P(None, None, ("gx", "gy", "gz")),
            P(None, "gx", "gy", "gz"),
            P("gx", "gy", "gz"),
            P(),
            P(),
            P(("gx", "gy", "gz"), None),
            P(None, None, "gy", "gz"),
        ),
        out_specs=P(None, None, ("gx", "gy", "gz")),
        check_vma=False,
    )
```

```python
import functools
import math

import jax
import jax.numpy as jnp
import numpy as np
from jax import lax
from jax.experimental import pallas as pl
from jax.experimental.pallas import tpu as pltpu
from jax.sharding import PartitionSpec as P

DEGREE = 7
ITERS = 3


helm_coefficient = 10.0


def legendre_pair(values, degree):
    previous = 0.0 * values + 1.0
    current = values.copy()
    for order in range(2, degree + 1):
        previous, current = (
            current,
            ((2 * order - 1) * values * current - (order - 1) * previous) / order,
        )
    return (current, previous)


def gll_tables(degree):
    start = np.cos(np.pi * np.arange(degree + 1) / degree)
    nodes_now = start.copy()
    for sweep in range(80):
        top_value, lower_value = legendre_pair(nodes_now, degree)
        nodes_now = nodes_now - (nodes_now * top_value - lower_value) / ((degree + 1) * top_value)
    gll_nodes = nodes_now[::-1].copy()
    gll_nodes[0] = -1.0
    gll_nodes[degree] = 1.0
    legendre_values = legendre_pair(gll_nodes, degree)[0]
    weights = 2.0 / (degree * (degree + 1) * legendre_values**2)
    differences = gll_nodes[:, None] - gll_nodes[None, :] + np.eye(degree + 1)
    derivative = legendre_values[:, None] / legendre_values[None, :] / differences
    derivative = derivative * (1.0 - np.eye(degree + 1))
    derivative[0, 0] = -degree * (degree + 1) / 4.0
    derivative[degree, degree] = degree * (degree + 1) / 4.0
    return (weights, derivative)


HALO = 2
FIELDS = 7
VMEM_BYTES = 40 * 1024 * 1024
FLOPS = 3 * 10**9
F32 = jnp.float32
BF16 = jnp.bfloat16


def pairings(names, sizes, dim):
    size = sizes[dim]
    if size == 1:
        return []
    if size % 2:
        shifts = (1, size - 1)
        partners = [[(i + shift) % size for i in range(size)] for shift in shifts]
    else:
        partners = [[i ^ 1 for i in range(size)]]
        if size > 2:
            partners.append([((i + 1) ^ 1) - 1 for i in range(size)])
    result = []
    for partner in partners:
        pairs = []
        for flat in range(math.prod(sizes)):
            place = list(np.unravel_index(flat, sizes))
            to = partner[place[dim]]
            if 0 <= to < size:
                place[dim] = to
            elif len(sizes) > 1 and sizes[1 - dim] % 2 == 0:
                place[1 - dim] ^= 1
            else:
                place[dim] = size - 1 - place[dim]
            pairs.append((flat, int(np.ravel_multi_index(place, sizes))))
        result.append(pairs)
    return result


def roles(name, size):
    if size == 1:
        return []
    index = lax.axis_index(name)
    low, high = index > 0, index < size - 1
    if size % 2:
        yes = index >= 0
        no = index < 0
        return [(yes, no, low), (no, yes, high)]
    even = lax.rem(index, 2) == 0
    odd = jnp.logical_not(even)
    result = [(even, even, index >= 0)]
    if size > 2:
        result.append((odd, odd, jnp.logical_or(jnp.logical_and(odd, high), jnp.logical_and(even, low))))
    return result


def both_sides(received, role):
    low, high = 0.0, 0.0
    for data, (_, from_high, used) in zip(received, role):
        high = high + jnp.where(jnp.logical_and(used, from_high), data, 0.0)
        low = low + jnp.where(jnp.logical_and(used, jnp.logical_not(from_high)), data, 0.0)
    return low, high


def split(x):
    upper = x.astype(BF16)
    return upper, (x - upper.astype(F32)).astype(BF16)


def dot2(x, table):
    upper, lower = split(x)
    return jnp.dot(upper, table, preferred_element_type=F32) + jnp.dot(
        lower, table, preferred_element_type=F32
    )


class Plan:
    def __init__(self, components, viscosity_shape, mesh_sizes):
        points = DEGREE + 1
        self.p, self.c = points, components
        self.sizes = mesh_sizes
        ex, ey, ez = (n // points for n in viscosity_shape)
        assert ex == 1 and ez >= HALO
        self.ey, self.ez = ey, ez
        self.rows = points**3
        self.block = points * points
        self.step3, self.step4 = components * ey, (components + 1) * ey
        self.n3, self.n4 = (ez + 2 * HALO) * self.step3, ez * self.step4
        self.w3, self.w4 = -(-self.n3 // 128) * 128, -(-self.n4 // 128) * 128
        self.halo4 = HALO * self.step4
        assert points * self.halo4 <= self.w4 and 2 * self.halo4 <= self.w4
        weights, derivative = gll_tables(DEGREE)
        self.forward = derivative.astype(np.float32)
        self.squared = self.forward * self.forward
        self.weights = weights.astype(np.float32)
        self.end = np.diagonal(self.forward)
        self.tables()

    def lane3(self, g, c, f):
        return (g + HALO) * self.step3 + c * self.ey + f

    def lane4(self, g, c, f):
        return g * self.step4 + c * self.ey + f

    def tables(self):
        p, c, ey, ez = self.p, self.c, self.ey, self.ez
        lanes = ez * p
        every = [(g, cc, f) for g in range(ez) for cc in range(c) for f in range(ey)]
        widen = np.zeros((2 * self.w4, 2 * self.w3), np.float32)
        ids = np.full((2 * c, 128, 128), -1, np.int32)
        for g, cc, f in every:
            widen[self.lane4(g, cc, f), self.lane3(g, cc, f)] = 1
            widen[self.lane4(g, c, f), self.w3 + self.lane3(g, cc, f)] = 1
            ids[cc, :, self.lane4(g, cc, f)] = f * ez + g
            ids[c + cc, :, self.lane3(g, cc, f)] = f * ez + g
        self.ids = np.ascontiguousarray(ids[:, :1, :]).reshape(2 * c, 128)
        part = HALO * p
        self.part = part
        assert FIELDS * part <= lanes and 2 * ey * part <= 128
        halo = np.zeros((128, p, self.w3), np.float32)
        for side, first in ((0, -HALO), (1, ez)):
            for g in range(HALO):
                for cc in range(c):
                    for f in range(ey):
                        at = self.lane3(first + g, cc, f)
                        row = self.w4 + side * self.halo4 + g * self.step4
                        widen[row + cc * ey + f, at] = 1
                        widen[row + c * ey + f, self.w3 + at] = 1
                        for k in range(p):
                            halo[(side * ey + f) * part + g * p + k, k, at] = 1
        self.halo = halo.reshape(128, -1).astype(jnp.bfloat16)
        self.widen = widen.astype(jnp.bfloat16)
        self.third = [self.block_terms(matrix) for matrix in (self.forward, self.forward.T, self.squared.T)]
        column = np.asarray([wj * wk for wj in self.weights for wk in self.weights], np.float32)
        self.table = np.ascontiguousarray(np.broadcast_to(column[:, None], (column.size, 128)))
        face = (ey * p, lanes)
        second = np.tile(np.arange(p), ey)[:, None]
        third = np.tile(np.arange(p), ez)[None, :]
        self.face_table = np.concatenate(
            [
                self.weights[second] * self.weights[third],
                np.broadcast_to(self.end[second], face),
                np.broadcast_to(self.end[third], face),
            ]
        ).astype(np.float32)

    def block_terms(self, matrix):
        size = self.rows // 4
        blocks = np.kron(np.eye(size // self.p), matrix).astype(np.float32)
        upper = blocks.astype(jnp.bfloat16)
        lower = (blocks - upper.astype(np.float32)).astype(jnp.bfloat16)
        return np.concatenate([upper, upper, lower], axis=1)


    def contract(self, x, matrix):
        p = self.p
        sign = 1.0 if matrix[0, 0] * matrix[p - 1, p - 1] > 0 else -1.0
        half = p // 2
        sums = [x[i] + x[p - 1 - i] for i in range(half)]
        differences = [x[i] - x[p - 1 - i] for i in range(half)]
        out = [None] * p
        for a in range(half):
            even, odd = None, None
            for i in range(half):
                first, second = float(matrix[a, i]), float(matrix[a, p - 1 - i])
                even = self.gather(even, 0.5 * (first + second), sums[i])
                odd = self.gather(odd, 0.5 * (first - second), differences[i])
            out[a] = odd + even
            out[p - 1 - a] = even - odd if sign > 0 else odd - even
        return out

    @staticmethod
    def gather(total, factor, x):
        if factor == 0.0:
            return total
        return factor * x if total is None else total + factor * x

    def along_j(self, x, matrix):
        x = x.reshape(self.p, self.p, x.shape[-1])
        return jnp.concatenate(self.contract([x[j] for j in range(self.p)], matrix), axis=0)

    def along_i(self, source, matrix, write):
        p, block = self.p, self.block
        for j in range(p):
            rows = [i * block + j * p for i in range(p)]
            for row, value in zip(rows, self.contract([source[r : r + p, :] for r in rows], matrix)):
                write(row, value)

    def along_k(self, source, table, out):
        size = table.shape[0]
        for start in range(0, self.rows, 2 * size):
            pieces = [split(source[at : at + size, :]) for at in (start, start + size)]
            upper, lower = (jnp.concatenate([piece[n] for piece in pieces], axis=1) for n in range(2))
            both = jnp.dot(
                table[...], jnp.concatenate([upper, lower, upper], axis=0), preferred_element_type=F32
            )
            width = source.shape[-1]
            out[start : start + size, :] = both[:, :width]
            out[start + size : start + 2 * size, :] = both[:, width:]

    def operator(self, v, g, out, slope, flux, third, work, ahead, back):
        block = self.block

        def store(row, value):
            slope[row : row + self.p, :] = value

        self.along_i(v, self.forward, store)
        self.along_k(v, ahead, third)
        for i in range(self.p):
            at = slice(i * block, (i + 1) * block)
            x, s1, s3 = v[at, :], slope[at, :], third[at, :]
            s2 = self.along_j(x, self.forward)
            xy, xz, yz = g[3, at, :], g[4, at, :], g[5, at, :]
            flux[at, :] = g[0, at, :] * s1 + xy * s2 + xz * s3
            f2 = xy * s1 + g[1, at, :] * s2 + yz * s3
            work[at, :] = xz * s1 + yz * s2 + g[2, at, :] * s3
            out[at, :] = self.along_j(f2, self.forward.T) + g[6, at, :] * x
        self.along_k(work, back, third)

        def add(row, value):
            out[row : row + self.p, :] += value + third[row : row + self.p, :]

        self.along_i(flux, self.forward.T, add)

    def fold_second(self, u):
        if self.ey == 1:
            return
        p, width = self.p, u.shape[-1]
        lane = lax.broadcasted_iota(jnp.int32, (p, width), 1)
        f = lax.rem(lane, self.ey)
        for start in range(0, u.shape[0], self.block):
            first, last = u[start : start + p, :], u[start + self.block - p : start + self.block, :]
            u[start + self.block - p : start + self.block, :] = last + jnp.where(
                f < self.ey - 1, pltpu.roll(first, width - 1, 1), 0.0
            )
            u[start : start + p, :] = first + jnp.where(f > 0, pltpu.roll(last, 1, 1), 0.0)

    def fold_third(self, u, step, take_upper, take_lower):
        p, (rows, width) = self.p, u.shape
        count = rows // p
        lane = lax.broadcasted_iota(jnp.int32, (count, width), 1)
        first, last = u[pl.ds(0, count, stride=p), :], u[pl.ds(p - 1, count, stride=p), :]
        u[pl.ds(p - 1, count, stride=p), :] = last + jnp.where(
            take_upper(lane), pltpu.roll(first, width - step, 1), 0.0
        )
        u[pl.ds(0, count, stride=p), :] = first + jnp.where(
            take_lower(lane), pltpu.roll(last, step, 1), 0.0
        )

    def emit(self, u, x_out, y_out):
        p, block = self.p, self.block
        for out, (high, _, _) in zip(x_out, roles("gx", self.sizes["gx"])):
            out[...] = jnp.where(high, u[self.rows - block :, :], u[:block, :])
        for out, (high, _, _) in zip(y_out, roles("gy", self.sizes["gy"])):
            for i in range(p):
                start = i * block
                out[i * p : (i + 1) * p, :] = jnp.where(
                    high, u[start + block - p : start + block, :], u[start : start + p, :]
                )

    def iteration_fold(self, u):
        self.fold_second(u)
        last = self.n3 - self.step3
        self.fold_third(u, self.step3, lambda l: l < last, lambda l: (l >= self.step3) & (l < self.n3))


    def pack_geometry(self, field, out):
        for target, (high, _, _) in zip(out, roles("gz", self.sizes["gz"])):
            rows, width = target.shape
            lane = lax.broadcasted_iota(jnp.int32, (rows, width), 1)
            total = jnp.zeros((rows, width), F32)
            for q in range(FIELDS):
                start = q * self.part
                upper = pltpu.roll(field(q), start + self.part, 1)
                lower = pltpu.roll(field(q), start, 1) if start else field(q)
                here = (lane >= start) & (lane < start + self.part)
                total = jnp.where(here, jnp.where(high, upper, lower), total)
            target[...] = total

    def by_nodes(self, upper, lower, table, width, store):
        for k in range(0, self.p, 2):
            columns = table[:, k * width : (k + 2) * width]
            both = jnp.dot(upper, columns, preferred_element_type=F32) + jnp.dot(
                lower, columns, preferred_element_type=F32
            )
            store(k, both[:, :width])
            store(k + 1, both[:, width:])

    def one_hot(self, slots, ids):
        count = slots.shape[-1]
        column = jnp.broadcast_to(slots[...], (count, count))
        column = jnp.concatenate([column, jnp.zeros((count, 128 - count), jnp.int32)], axis=1)
        column = jnp.concatenate([column, jnp.zeros((128 - count, 128), jnp.int32)], axis=0)
        column = column.astype(F32).T[:count, :1]
        return jnp.concatenate(
            [jnp.where(column == ids[n : n + 1, :].astype(F32), 1.0, 0.0) for n in range(self.c)], axis=0
        ).astype(BF16)

    def spread_tables(self, out3, out4):
        p, ey, ez = self.p, self.ey, self.ez
        for out, width, step, offset, first in (
            (out3, self.w3, self.step3, HALO, 0),
            (out4, self.w4, self.step4, 0, self.c * ey),
        ):
            row = lax.broadcasted_iota(jnp.int32, (ey * ez * p, width), 0)
            lane = lax.broadcasted_iota(jnp.int32, (1, width), 1)
            g = lane // step - offset
            inside = (g >= 0) & (g < ez) & (lax.rem(lane, step) >= first)
            same = row // p == jnp.where(inside, lax.rem(lane, ey) * ez + g, -1)
            node = lax.rem(row, p)
            for k in range(p):
                out[:, k * width : (k + 1) * width] = jnp.where(same & (node == k), 1.0, 0.0).astype(BF16)

    def prepare(self, n_x, n_y, *refs):
        geometry, viscosity, spread, table, right, slots, ids, square = refs[:8]
        s4, hot3 = refs[8:10]
        refs = refs[10:]
        x_out, y_out, work = refs[:n_x], refs[n_x : n_x + n_y], refs[n_x + n_y]
        p, c, block, rows, ey = self.p, self.c, self.block, self.rows, self.ey
        face = ey * p
        wjk, end_j, end_k = (table[n * face : (n + 1) * face, :] for n in range(3))
        stiff, second, third, rest = [], [], [], []
        for i in range(p):
            xx, yy, zz, xy, xz, yz = (geometry[q, i] for q in range(6))
            quadrature = float(self.weights[i]) * wjk
            weighted = quadrature * viscosity[i]
            mass = (helm_coefficient * quadrature) * (
                xx * (yy * zz - yz * yz) - xy * (xy * zz - yz * xz) + xz * (xy * yz - yy * xz)
            )
            cross = end_j * end_k * yz
            end = float(self.end[i])
            if end != 0.0:
                cross = cross + end * (end_j * xy + end_k * xz)
            stiff.append(weighted * xx)
            second.append(weighted * yy)
            third.append(weighted * zz)
            rest.append((2.0 * weighted) * cross + mass)
        upper, lower = split(jnp.concatenate(second, axis=0))
        diagonal = jnp.dot(
            square[...], jnp.concatenate([upper, lower, upper], axis=0), preferred_element_type=F32
        )
        upper, lower = split(jnp.concatenate(third, axis=0))
        diagonal = diagonal + lax.dot_general(
            jnp.concatenate([upper, lower, upper], axis=1),
            square[...],
            (((1,), (1,)), ((), ())),
            preferred_element_type=F32,
        )
        first = self.contract(stiff, self.squared.T)
        diagonal = diagonal + jnp.concatenate([x + y for x, y in zip(first, rest)], axis=0)
        width = diagonal.shape[-1]
        value = diagonal.reshape(p, ey, p, width)
        value = jnp.concatenate([value[:, f].reshape(block, width) for f in range(ey)], axis=1)

        def store(k, part):
            work[pl.ds(k, block, stride=p), :] = part

        self.by_nodes(*split(value), spread, self.w4, store)
        hot = self.one_hot(slots, ids)
        hot3[...] = self.one_hot(slots, ids[c:, :])
        total = work[...]
        for part in split(right[...].reshape(hot.shape[0], rows)):
            total = total + lax.dot_general(
                part, hot, (((0,), (0,)), ((), ())), preferred_element_type=F32
            )
        s4[...] = total
        self.fold_second(s4)
        last = self.n4 - self.step4
        self.fold_third(s4, self.step4, lambda l: l < last, lambda l: (l >= self.step4) & (l < self.n4))
        self.emit(s4, x_out, y_out)

    def convert(self, n_y, n_z, *refs):
        geometry, viscosity, spread, dirichlet = refs[:4]
        raw, ind = refs[4:6]
        refs = refs[6:]
        y_out, z_out, (upper, lower) = refs[:n_y], refs[n_y : n_y + n_z], refs[n_y + n_z :]
        p, c, block, ey = self.p, self.c, self.block, self.ey
        width = geometry.shape[-1]

        def field(q):
            return (geometry[q] if q < FIELDS - 1 else viscosity[...]).reshape(p * ey * p, width)

        for q in range(FIELDS):
            value = field(q).reshape(p, ey, p, width)
            for f in range(ey):
                at = (slice(q * block, (q + 1) * block), slice(f * width, (f + 1) * width))
                upper[at], lower[at] = split(value[:, f].reshape(block, width))
        first_flag, flags = FIELDS * block, 2 * p
        for cc in range(c):
            for f in range(ey):
                at = slice(f * p, (f + 1) * p)
                face = jnp.concatenate([dirichlet[0, cc, at, :], dirichlet[1, cc, at, :]], axis=0)
                to = slice(first_flag + cc * flags, first_flag + (cc + 1) * flags)
                upper[to, f * width : (f + 1) * width] = face.astype(F32).astype(BF16)
                lower[to, f * width : (f + 1) * width] = jnp.zeros((flags, width), BF16)
        row = lax.broadcasted_iota(jnp.int32, (flags, self.w3), 0)
        lane = lax.broadcasted_iota(jnp.int32, (flags, self.w3), 1)
        ends = (lax.axis_index("gx") == 0, lax.axis_index("gx") == self.sizes["gx"] - 1)
        here = ((row < p) & ends[0]) | ((row >= p) & ends[1])
        owner = lax.rem(lane, self.step3) // ey

        def store(k, value):
            raw[pl.ds(k, first_flag, stride=p), :] = value[:first_flag]
            total = jnp.zeros((flags, self.w3), F32)
            for cc in range(c):
                at = first_flag + cc * flags
                total = jnp.where(owner == cc, value[at : at + flags], total)
            ind[pl.ds(k, flags, stride=p), :] = jnp.where(here, total, 0.0)

        self.by_nodes(upper[...], lower[...], spread, self.w3, store)
        self.pack_geometry(field, z_out)
        self.fold_second(ind)
        first_own, end_own = HALO * self.step3, self.n3 - HALO * self.step3
        self.fold_third(
            ind,
            self.step3,
            lambda l: (l >= first_own) & (l < end_own - self.step3),
            lambda l: (l >= first_own + self.step3) & (l < end_own),
        )
        for out, (up, _, _) in zip(y_out, roles("gy", self.sizes["gy"])):
            for n in range(2):
                start = n * block
                out[n * p : (n + 1) * p, :] = jnp.where(
                    up, ind[start + block - p : start + block, :], ind[start : start + p, :]
                )

    def halo_geometry(self, n_z, *refs):
        raw, halo, table = refs[:3]
        z_in, g = refs[3 : 3 + n_z], refs[3 + n_z]
        upper, lower, total = refs[4 + n_z :]
        p, block, rows, ey = self.p, self.block, self.rows, self.ey
        source = raw
        if n_z:
            sides = both_sides([z[...] for z in z_in], roles("gz", self.sizes["gz"]))
            width, part = sides[0].shape[-1], self.part
            sides = [side.reshape(p, ey, p, width) for side in sides]
            lane = lax.broadcasted_iota(jnp.int32, (block, width), 1)
            for q in range(FIELDS):
                value = jnp.zeros((block, width), F32)
                for side in range(2):
                    for f in range(ey):
                        to = (side * ey + f) * part
                        shift = (to - q * part) % width
                        x = sides[side][:, f].reshape(block, width)
                        x = pltpu.roll(x, shift, 1) if shift else x
                        value = jnp.where((lane >= to) & (lane < to + part), x, value)
                at = slice(q * block, (q + 1) * block)
                upper[at, :], lower[at, :] = split(value)

            def store(k, value):
                at = pl.ds(k, FIELDS * block, stride=p)
                total[at, :] = raw[at, :] + value

            self.by_nodes(upper[...], lower[...], halo, self.w3, store)
            source = total
        wjk = table[...]
        for i in range(p):
            at = slice(i * block, (i + 1) * block)
            entries = [source[q * rows + i * block : q * rows + (i + 1) * block, :] for q in range(FIELDS)]
            xx, yy, zz, xy, xz, yz = entries[:6]
            quadrature = float(self.weights[i]) * wjk
            weighted = quadrature * entries[6]
            g[6, at, :] = (helm_coefficient * quadrature) * (
                xx * (yy * zz - yz * yz) - xy * (xy * zz - yz * xz) + xz * (xy * yz - yy * xz)
            )
            for q in range(6):
                g[q, at, :] = weighted * entries[q]

    def coefficients(self, low, high, coef):
        top, bottom = jnp.full((8, 128), high[0], F32), jnp.full((8, 128), low[0], F32)
        midpoint, halfwidth = (top + bottom) * 0.5, (top - bottom) * 0.5
        ratio = midpoint / halfwidth
        damping = 1.0 / ratio
        coef[0:8, :] = 1.0 / midpoint
        for n in range(ITERS - 1):
            following = 1.0 / (2.0 * ratio - damping)
            coef[8 * (2 * n + 1) : 8 * (2 * n + 2), :] = following * damping
            coef[8 * (2 * n + 2) : 8 * (2 * n + 3), :] = 2.0 * following / halfwidth
            damping = following

    def join(self, n_x, n_y, *refs):
        x_in, refs = refs[:n_x], refs[n_x:]
        y_raw, y_more, y_out = refs[:n_y], refs[n_y:-n_y], refs[-n_y:]
        p, block, ey = self.p, self.block, self.ey
        low, high = both_sides([x[...] for x in x_in], roles("gx", self.sizes["gx"]))
        for n, (up, _, _) in enumerate(roles("gy", self.sizes["gy"])):
            face = y_raw[n][...]
            width = face.shape[-1]
            if n_x:
                first, last = (jnp.where(up, x[block - p :], x[:p]) for x in (low, high))
                face = jnp.concatenate([face[:p] + first, face[p : block - p], face[block - p :] + last], axis=0)
            if y_more:
                face = jnp.concatenate([face, y_more[n][...]], axis=0)
            if ey == 1:
                y_out[n][...] = face
                continue
            half = face.shape[0] // 2
            first, second = face[:half], face[half:]
            f = lax.rem(lax.broadcasted_iota(jnp.int32, first.shape, 1), ey)
            below = jnp.where(f == 0, pltpu.roll(first, width - (ey - 1), 1), 0.0) + jnp.where(
                f == 1, pltpu.roll(second, (width - (ey - 2)) % width, 1) if ey != 2 else second, 0.0
            )
            above = jnp.where(f == ey - 1, pltpu.roll(first, ey - 1, 1), 0.0) + jnp.where(
                f == ey - 2, pltpu.roll(second, ey - 2, 1) if ey != 2 else second, 0.0
            )
            y_out[n][...] = jnp.where(up, below, above)

    def second_sides(self, received):
        role, ey = roles("gy", self.sizes["gy"]), self.ey
        faces = []
        for message, (_, from_high, _) in zip(received, role):
            data = message[...]
            if ey > 1:
                width = data.shape[-1]
                f = lax.rem(lax.broadcasted_iota(jnp.int32, data.shape, 1), ey)
                beside = jnp.where(from_high, pltpu.roll(data, 1, 1), pltpu.roll(data, width - 1, 1))
                here = f == jnp.where(from_high, ey - 1, 0)
                data = jnp.concatenate([jnp.where(here, x, 0.0) for x in (data, beside)], axis=0)
            faces.append(data)
        return both_sides(faces, role)

    def pack_first(self, n_x, *refs):
        s4, ind = refs[:2]
        x_in, s_out, z_out = refs[2 : 2 + n_x], refs[2 + n_x], refs[3 + n_x :]
        p, block, rows = self.p, self.block, self.rows
        s_out[...] = s4[...]
        if n_x:
            low, high = both_sides([x[...] for x in x_in], roles("gx", self.sizes["gx"]))
            s_out[:block, :] += low
            s_out[rows - block :, :] += high
        halo3 = HALO * self.step3
        for out, (up, _, _) in zip(z_out, roles("gz", self.sizes["gz"])):
            self.pack(out, s_out, block, 0, self.n4 - self.halo4, up, 0)
            self.pack(out, ind, p, halo3, self.n3 - 2 * halo3, up, block)

    def pack(self, out, u, count, first, last, up, start):
        p, width, size = self.p, self.w4, self.halo4
        lane = lax.broadcasted_iota(jnp.int32, (count, width), 1)
        for section in range(0, u.shape[0] // count, p):
            total = jnp.zeros((count, width), F32)
            for n in range(p):
                at, shift = (section + n) * count, n * size
                x = u[at : at + count, :]
                below = pltpu.roll(x, (shift - first) % width, 1) if (shift - first) % width else x
                above = pltpu.roll(x, (shift - last) % width, 1)
                here = (lane >= shift) & (lane < shift + size)
                total = jnp.where(here, jnp.where(up, above, below), total)
            row = start + section // p * count
            out[row : row + count, :] = total

    def pack_second(self, n_y, n_z, *refs):
        y_in, z_in, z_out = refs[:n_y], refs[n_y : n_y + n_z], refs[n_y + n_z :]
        p, block, width, size = self.p, self.block, self.w4, self.halo4
        low, high = self.second_sides(y_in)
        halo3 = HALO * self.step3
        lane = lax.broadcasted_iota(jnp.int32, (p, width), 1)
        for packed, out, (up, _, _) in zip(z_in, z_out, roles("gz", self.sizes["gz"])):
            out[...] = packed[...]
            for face, row in ((low, 0), (high, block - p)):
                total = jnp.zeros((p, width), F32)
                for n in range(p):
                    shift = n * size
                    x = face[n * p : (n + 1) * p]
                    below = pltpu.roll(x, shift, 1) if shift else x
                    above = pltpu.roll(x, (shift - self.n4 + size) % width, 1)
                    here = (lane >= shift) & (lane < shift + size)
                    total = jnp.where(here, jnp.where(up, above, below), total)
                out[row : row + p, :] += total
            for n in range(2):
                row = block + n * p
                for face, group in ((low, 0), (high, p - 1)):
                    shift = group * size
                    x = face[row : row + p]
                    below = pltpu.roll(x, (shift - halo3) % width, 1)
                    above = pltpu.roll(x, (shift - self.n3 + 2 * halo3) % width, 1)
                    here = (lane >= shift) & (lane < shift + size)
                    out[row : row + p, :] += jnp.where(here, jnp.where(up, above, below), 0.0)

    def own(self, n_y, *refs):
        s4, ind, widen = refs[:3]
        y_in, (r, scale, flag, work) = refs[3 : 3 + n_y], refs[3 + n_y :]
        p, block, w3 = self.p, self.block, self.w3
        work[...] = s4[...]
        flag[...] = ind[...]
        if n_y:
            low, high = self.second_sides(y_in)
            for u, first, count in ((work, 0, p), (flag, p, 2)):
                for i in range(count):
                    at, end, row = i * block, (i + 1) * block, (first + i) * p
                    u[at : at + p, :] += low[row : row + p]
                    u[end - p : end, :] += high[row : row + p]
        both = dot2(work[...], widen[: self.w4, :])
        r[...] = both[:, :w3]
        scale[...] = both[:, w3:]

    def start(self, n_x, n_y, n_z, *refs):
        r_own, diagonal_own, flag_own, g, widen, ahead, back = refs[:7]
        z_in = refs[7 : 7 + n_z]
        t, scale, v = refs[7 + n_z : 10 + n_z]
        refs = refs[10 + n_z :]
        x_out, y_out = refs[:n_x], refs[n_x : n_x + n_y]
        beside, r, flag = refs[n_x + n_y : n_x + n_y + 3]
        work = refs[n_x + n_y + 3 :]
        p, block, rows, w3, w4 = self.p, self.block, self.rows, self.w3, self.w4
        step, first_own, end_own = self.step3, HALO * self.step3, self.n3 - HALO * self.step3
        size, part = self.sizes["gz"], self.halo4
        if n_z:
            low, high = both_sides([z[...] for z in z_in], roles("gz", size))
        else:
            low = high = jnp.zeros((block + 2 * p, w4), F32)
        lane = lax.broadcasted_iota(jnp.int32, (block, w4), 1)
        for n in range(p):
            first = pltpu.roll(low[:block], w4 - n * part, 1) if n else low[:block]
            second = pltpu.roll(high[:block], (part - n * part) % w4, 1) if n != 1 else high[:block]
            beside[n * block : (n + 1) * block, :] = jnp.where(
                lane < part, first, jnp.where(lane < 2 * part, second, 0.0)
            )
        both = dot2(beside[...], widen[w4:, :])
        r[...] = r_own[...] + both[:, :w3]
        scale[...] = diagonal_own[...] + both[:, w3:]
        lane = lax.broadcasted_iota(jnp.int32, (p, w3), 1)
        for n in range(2 * p):
            row, shift = block + n // p * p, n % p * part
            first = pltpu.roll(low[row : row + p], w3 - shift, 1) if shift else low[row : row + p]
            second = pltpu.roll(high[row : row + p], (end_own - shift) % w3, 1)
            flag[n * p : (n + 1) * p, :] = jnp.where(
                lane < first_own,
                first,
                jnp.where(lane < end_own, flag_own[n * p : (n + 1) * p, :], jnp.where(lane < self.n3, second, 0.0)),
            )
        for u in (r, scale, flag):
            self.fold_third(
                u,
                step,
                lambda l: ((l >= first_own - step) & (l < first_own)) | ((l >= end_own - step) & (l < end_own)),
                lambda l: ((l >= first_own) & (l < first_own + step)) | ((l >= end_own) & (l < end_own + step)),
            )
        index = lax.axis_index("gz")
        begin = jnp.where(index > 0, 0, first_own)
        end = jnp.where(index < size - 1, self.n3, end_own)
        lane = lax.broadcasted_iota(jnp.int32, (block, w3), 1)
        valid = (lane >= begin) & (lane < end)
        for i in range(p):
            at = slice(i * block, (i + 1) * block)
            factor = jnp.where(valid, 1.0 / jnp.where(valid, scale[at, :], 1.0), 0.0)
            if i in (0, p - 1):
                row = 0 if i == 0 else block
                factor = jnp.where(flag[row : row + block, :] > 0.5, 0.0, factor)
            scale[at, :] = factor
            t[at, :] = factor * r[at, :]
        self.operator(t, g, v, *work, ahead, back)
        self.iteration_fold(v)
        self.emit(v, x_out, y_out)

    def factors(self, coef, n):
        rows = [coef[8 * m : 8 * m + 1, :] for m in (0, 2 * n + 1, 2 * n + 2)]
        return (rows[0] if n == 0 else None), rows[1], rows[2]

    def shares(self, faces, scale, image, at):
        low, high = faces
        p, block = self.p, self.block
        i = at // block
        out = []
        for start, face in ((at, low), (at + block - p, high)):
            value = scale[start : start + p, :] * face[i * p : (i + 1) * p]
            out.append((start, -value if image is None else -image * value))
        return out

    def preview(self, n_x, n_y, n, last, *refs):
        t, t_old, d, scale, v, coef, hot = refs[:7]
        refs = refs[7:]
        x_in, y_old, refs = refs[:n_x], refs[n_x : -2 if not last else -3], refs[-2 if not last else -3 :]
        p, block, rows = self.p, self.block, self.rows
        image, keep, gain = self.factors(coef, n)
        start = coef[0:1, :]
        if last:
            out, t_new, field = refs
        else:
            t_new, d_new = refs
        low, high = both_sides([x[...] for x in x_in], roles("gx", self.sizes["gx"]))
        if n:
            faces = self.second_sides(y_old) if n_y else None
            image_old = self.factors(coef, n - 1)[0]
        for i in range(p):
            at = slice(i * block, (i + 1) * block)
            value = v[at, :]
            if n_x and i in (0, p - 1):
                value = value + (low if i == 0 else high)
            value = scale[at, :] * value
            t_new[at, :] = t_old[at, :] - (value if image is None else image * value)
            if n and n_y:
                for row, share in self.shares(faces, scale, image_old, i * block):
                    t_new[row : row + p, :] += share
            direction = d[at, :] if n else start * t[at, :]
            following = keep * direction + gain * t_new[at, :]
            if last:
                field[at, :] = start * t[at, :] + following + (direction if n else 0.0)
            else:
                d_new[at, :] = following
        if last:
            out[...] = self.by_slots(hot, field[...])

    def by_slots(self, hot, field):
        value = None
        for part in split(field):
            term = lax.dot_general(
                hot[...], part, (((1,), (1,)), ((), ())), preferred_element_type=F32
            )
            value = term if value is None else value + term
        return value

    def middle(self, n_x, n_y, n, *refs):
        d, scale, g, coef, ahead, back = refs[:6]
        y_in, refs = refs[6 : 6 + n_y], refs[6 + n_y :]
        d_new, v = refs[:2]
        x_out, y_out, work = refs[2 : 2 + n_x], refs[2 + n_x : 2 + n_x + n_y], refs[2 + n_x + n_y :]
        d_new[...] = d[...]
        image, _, gain = self.factors(coef, n)
        if n_y:
            faces = self.second_sides(y_in)
            for i in range(self.p):
                for row, share in self.shares(faces, scale, image, i * self.block):
                    d_new[row : row + self.p, :] += gain * share
        self.operator(d_new, g, v, *work, ahead, back)
        self.iteration_fold(v)
        self.emit(v, x_out, y_out)

    def finish(self, n_y, n, *refs):
        part, scale, coef, hot = refs[:4]
        y_in, (out, field) = refs[4 : 4 + n_y], refs[4 + n_y :]
        value = part[...]
        image, _, gain = self.factors(coef, n)
        if n_y:
            faces = self.second_sides(y_in)
            field[...] = jnp.zeros(field.shape, F32)
            for i in range(self.p):
                for row, share in self.shares(faces, scale, image, i * self.block):
                    field[row : row + self.p, :] = gain * share
            value = value + self.by_slots(hot, field[...])
        out[...] = value.reshape(out.shape)


def shards(sizes, right_side, geometry, viscosity, eig_low, eig_high, element_slot, dirichlet):
    plan = Plan(right_side.shape[0], viscosity.shape, sizes)
    p, block, rows, w3, w4 = plan.p, plan.block, plan.rows, plan.w3, plan.w4
    x_pairs = pairings(("gx",), (sizes["gx"],), 0)
    y_pairs = pairings(("gy",), (sizes["gy"],), 0)
    z_pairs = pairings(("gy", "gz"), (sizes["gy"], sizes["gz"]), 1)
    n_x, n_y, n_z = len(x_pairs), len(y_pairs), len(z_pairs)

    def send(arrays, axis, pairs):
        return [lax.ppermute(x, axis, pair) for x, pair in zip(arrays, pairs)]

    def shape(*size, dtype=F32):
        return jax.ShapeDtypeStruct(size, dtype)

    def call(kernel, outputs, operands, scratch=(), spaces={}, flops=0, name=None):
        specs = [pl.BlockSpec(memory_space=spaces.get(n, pltpu.VMEM)) for n in range(len(operands))]
        return list(
            pl.pallas_call(
                kernel,
                out_shape=list(outputs),
                in_specs=specs,
                out_specs=[pl.BlockSpec(memory_space=pltpu.VMEM)] * len(outputs),
                scratch_shapes=list(scratch),
                compiler_params=pltpu.CompilerParams(vmem_limit_bytes=VMEM_BYTES),
                cost_estimate=pl.CostEstimate(flops=flops, bytes_accessed=0, transcendentals=0),
                name=name,
            )(*operands)
        )

    def vmem(*size, dtype=F32):
        return pltpu.VMEM(size, dtype)

    lanes = plan.ez * p
    table = jnp.asarray(plan.table)
    ahead, back = jnp.asarray(plan.third[0]), jnp.asarray(plan.third[1])
    field3, field4 = shape(rows, w3), shape(rows, w4)
    elements = element_slot.shape[-1]
    spread3, spread4 = call(
        plan.spread_tables,
        [shape(plan.ey * lanes, p * w, dtype=BF16) for w in (w3, w4)],
        (),
        flops=FLOPS,
        name="spread_tables",
    )
    results = call(
        functools.partial(plan.prepare, n_x, n_y),
        [field4, shape(plan.c * elements, w3, dtype=BF16)] + [shape(block, w4)] * (n_x + n_y),
        (
            geometry,
            viscosity,
            spread4,
            jnp.asarray(plan.face_table),
            jnp.swapaxes(right_side, 1, 2),
            element_slot,
            jnp.asarray(plan.ids),
            jnp.asarray(plan.third[2]),
        ),
        scratch=[vmem(rows, w4)],
        name="prepare",
    )
    s4, hot3 = results[:2]
    x_out, y_raw = results[2 : 2 + n_x], results[2 + n_x :]
    x_in = send(x_out, "gx", x_pairs)

    lhs = FIELDS * block + 2 * plan.c * p
    results = call(
        functools.partial(plan.convert, n_y, n_z),
        [shape(FIELDS * rows, w3), shape(2 * block, w3)]
        + [shape(2 * p, w3)] * n_y
        + [shape(p * plan.ey * p, lanes)] * n_z,
        (geometry, viscosity, spread3, dirichlet),
        scratch=[vmem(lhs, plan.ey * lanes, dtype=BF16)] * 2,
        name="convert",
    )
    raw, ind = results[:2]
    y_more, z_geometry = results[2 : 2 + n_y], results[2 + n_y :]

    def joined(x_in, y_raw, y_more=()):
        if not y_raw:
            return []
        count = y_raw[0].shape[0] + (y_more[0].shape[0] if y_more else 0)
        faces = [shape(count // 2 if plan.ey > 1 else count, y.shape[1]) for y in y_raw]
        return call(functools.partial(plan.join, n_x, n_y), faces, x_in + y_raw + list(y_more), name="join")

    y_in = send(joined(x_in, y_raw, y_more), "gy", y_pairs)
    z_geometry = send(z_geometry, ("gy", "gz"), z_pairs)
    g = call(
        functools.partial(plan.halo_geometry, n_z),
        [shape(FIELDS, rows, w3)],
        [raw, jnp.asarray(plan.halo), table] + z_geometry,
        scratch=[vmem(FIELDS * block, 128, dtype=BF16)] * 2 + [vmem(FIELDS * rows, w3)],
        name="halo_geometry",
    )[0]
    results = call(
        functools.partial(plan.pack_first, n_x),
        [field4] + [shape(block + 2 * p, w4)] * n_z,
        [s4, ind] + x_in,
        name="pack_first",
    )
    s4, z_out = results[0], results[1:]
    if n_y and n_z:
        z_out = call(
            functools.partial(plan.pack_second, n_y, n_z),
            [shape(*z.shape) for z in z_out],
            y_in + z_out,
            flops=FLOPS,
            name="pack_second",
        )
    z_in = send(z_out, ("gy", "gz"), z_pairs)
    widen = jnp.asarray(plan.widen)
    own = call(
        functools.partial(plan.own, n_y),
        [field3, field3, shape(2 * block, w3)],
        [s4, ind, widen] + y_in,
        scratch=[vmem(rows, w4)],
        name="own",
    )

    messages = [shape(block, w3)] * (n_x + n_y)
    results = call(
        functools.partial(plan.start, n_x, n_y, n_z),
        [field3] * 3 + messages,
        own + [g, widen, ahead, back] + z_in,
        scratch=[vmem(rows, w4), vmem(rows, w3), vmem(2 * block, w3)] + [vmem(rows, w3)] * 4,
        name="first_direction",
    )
    t, scale, v = results[:3]
    x_out, y_raw = results[3 : 3 + n_x], results[3 + n_x :]
    x_out, low, high = lax.optimization_barrier((x_out, eig_low, eig_high))
    coef = call(
        plan.coefficients,
        [shape(8 * (2 * ITERS - 1), 128)],
        (low, high),
        spaces={0: pltpu.SMEM, 1: pltpu.SMEM},
        name="coefficients",
    )[0]
    t_old, d, y_in = t, t, []
    for n in range(ITERS - 1):
        last = n == ITERS - 2
        x_in = send(x_out, "gx", x_pairs)
        y_old, y_in = y_in, send(joined(x_in, y_raw), "gy", y_pairs)
        results = call(
            functools.partial(plan.preview, n_x, n_y, n, last),
            [shape(plan.c * elements, rows)] if last else [field3, field3],
            [t, t_old, d, scale, v, coef, hot3] + x_in + y_old,
            scratch=[vmem(rows, w3)] * 2 if last else [],
            name="preview",
        )
        if last:
            break
        t_old, d = results
        results = call(
            functools.partial(plan.middle, n_x, n_y, n),
            [field3] * 2 + messages,
            [d, scale, g, coef, ahead, back] + y_in,
            scratch=[vmem(rows, w3)] * 4,
            name="direction",
        )
        d, v = results[:2]
        x_out, y_raw = results[2 : 2 + n_x], results[2 + n_x :]
    out = call(
        functools.partial(plan.finish, n_y, n),
        [shape(plan.c, elements, rows)],
        [results[0], scale, coef, hot3] + y_in,
        scratch=[vmem(rows, w3)],
        name="field",
    )[0]
    return jnp.swapaxes(out, 1, 2)


def solution(mesh):
    sizes = {name: mesh.shape[name] for name in ("gx", "gy", "gz")}
    return jax.shard_map(
        functools.partial(shards, sizes),
        mesh=mesh,
        in_specs=(
            P(None, None, ("gx", "gy", "gz")),
            P(None, "gx", "gy", "gz"),
            P("gx", "gy", "gz"),
            P(),
            P(),
            P(("gx", "gy", "gz"), None),
            P(None, None, "gy", "gz"),
        ),
        out_specs=P(None, None, ("gx", "gy", "gz")),
        check_vma=False,
    )
```

```python
import functools
import math

import jax
import jax.numpy as jnp
import numpy as np
from jax import lax
from jax.experimental import pallas as pl
from jax.experimental.pallas import tpu as pltpu
from jax.sharding import PartitionSpec as P

DEGREE = 7
ITERS = 3


helm_coefficient = 10.0


def legendre_pair(values, degree):
    previous = 0.0 * values + 1.0
    current = values.copy()
    for order in range(2, degree + 1):
        previous, current = (
            current,
            ((2 * order - 1) * values * current - (order - 1) * previous) / order,
        )
    return (current, previous)


def gll_tables(degree):
    start = np.cos(np.pi * np.arange(degree + 1) / degree)
    nodes_now = start.copy()
    for sweep in range(80):
        top_value, lower_value = legendre_pair(nodes_now, degree)
        nodes_now = nodes_now - (nodes_now * top_value - lower_value) / ((degree + 1) * top_value)
    gll_nodes = nodes_now[::-1].copy()
    gll_nodes[0] = -1.0
    gll_nodes[degree] = 1.0
    legendre_values = legendre_pair(gll_nodes, degree)[0]
    weights = 2.0 / (degree * (degree + 1) * legendre_values**2)
    differences = gll_nodes[:, None] - gll_nodes[None, :] + np.eye(degree + 1)
    derivative = legendre_values[:, None] / legendre_values[None, :] / differences
    derivative = derivative * (1.0 - np.eye(degree + 1))
    derivative[0, 0] = -degree * (degree + 1) / 4.0
    derivative[degree, degree] = degree * (degree + 1) / 4.0
    return (weights, derivative)


HALO = 2
FIELDS = 7
VMEM_BYTES = 40 * 1024 * 1024
FLOPS = 3 * 10**9
F32 = jnp.float32
BF16 = jnp.bfloat16


def pairings(names, sizes, dim):
    size = sizes[dim]
    if size == 1:
        return []
    if size % 2:
        shifts = (1, size - 1)
        partners = [[(i + shift) % size for i in range(size)] for shift in shifts]
    else:
        partners = [[i ^ 1 for i in range(size)]]
        if size > 2:
            partners.append([((i + 1) ^ 1) - 1 for i in range(size)])
    result = []
    for partner in partners:
        pairs = []
        for flat in range(math.prod(sizes)):
            place = list(np.unravel_index(flat, sizes))
            to = partner[place[dim]]
            if 0 <= to < size:
                place[dim] = to
            elif len(sizes) > 1 and sizes[1 - dim] % 2 == 0:
                place[1 - dim] ^= 1
            else:
                place[dim] = size - 1 - place[dim]
            pairs.append((flat, int(np.ravel_multi_index(place, sizes))))
        result.append(pairs)
    return result


def roles(name, size):
    if size == 1:
        return []
    index = lax.axis_index(name)
    low, high = index > 0, index < size - 1
    if size % 2:
        yes = index >= 0
        no = index < 0
        return [(yes, no, low), (no, yes, high)]
    even = lax.rem(index, 2) == 0
    odd = jnp.logical_not(even)
    result = [(even, even, index >= 0)]
    if size > 2:
        result.append((odd, odd, jnp.logical_or(jnp.logical_and(odd, high), jnp.logical_and(even, low))))
    return result


def both_sides(received, role):
    low, high = 0.0, 0.0
    for data, (_, from_high, used) in zip(received, role):
        high = high + jnp.where(jnp.logical_and(used, from_high), data, 0.0)
        low = low + jnp.where(jnp.logical_and(used, jnp.logical_not(from_high)), data, 0.0)
    return low, high


def split(x):
    upper = x.astype(BF16)
    return upper, (x - upper.astype(F32)).astype(BF16)


def dot2(x, table):
    upper, lower = split(x)
    return jnp.dot(upper, table, preferred_element_type=F32) + jnp.dot(
        lower, table, preferred_element_type=F32
    )


class Plan:
    def __init__(self, components, viscosity_shape, mesh_sizes):
        points = DEGREE + 1
        self.p, self.c = points, components
        self.sizes = mesh_sizes
        ex, ey, ez = (n // points for n in viscosity_shape)
        assert ex == 1 and ez >= HALO
        self.ey, self.ez = ey, ez
        self.rows = points**3
        self.block = points * points
        self.step3, self.step4 = components * ey, (components + 1) * ey
        self.n3, self.n4 = (ez + 2 * HALO) * self.step3, ez * self.step4
        self.w3, self.w4 = -(-self.n3 // 128) * 128, -(-self.n4 // 128) * 128
        self.halo4 = HALO * self.step4
        assert points * self.halo4 <= self.w4 and 2 * self.halo4 <= self.w4
        weights, derivative = gll_tables(DEGREE)
        self.forward = derivative.astype(np.float32)
        self.squared = self.forward * self.forward
        self.weights = weights.astype(np.float32)
        self.end = np.diagonal(self.forward)
        self.tables()

    def lane3(self, g, c, f):
        return (g + HALO) * self.step3 + c * self.ey + f

    def lane4(self, g, c, f):
        return g * self.step4 + c * self.ey + f

    def tables(self):
        p, c, ey, ez = self.p, self.c, self.ey, self.ez
        lanes = ez * p
        every = [(g, cc, f) for g in range(ez) for cc in range(c) for f in range(ey)]
        widen = np.zeros((2 * self.w4, 2 * self.w3), np.float32)
        ids = np.full((2 * c, 128, 128), -1, np.int32)
        for g, cc, f in every:
            widen[self.lane4(g, cc, f), self.lane3(g, cc, f)] = 1
            widen[self.lane4(g, c, f), self.w3 + self.lane3(g, cc, f)] = 1
            ids[cc, :, self.lane4(g, cc, f)] = f * ez + g
            ids[c + cc, :, self.lane3(g, cc, f)] = f * ez + g
        self.ids = np.ascontiguousarray(ids[:, :1, :]).reshape(2 * c, 128)
        part = HALO * p
        self.part = part
        assert FIELDS * part <= lanes and 2 * ey * part <= 128
        halo = np.zeros((128, p, self.w3), np.float32)
        for side, first in ((0, -HALO), (1, ez)):
            for g in range(HALO):
                for cc in range(c):
                    for f in range(ey):
                        at = self.lane3(first + g, cc, f)
                        row = self.w4 + side * self.halo4 + g * self.step4
                        widen[row + cc * ey + f, at] = 1
                        widen[row + c * ey + f, self.w3 + at] = 1
                        for k in range(p):
                            halo[(side * ey + f) * part + g * p + k, k, at] = 1
        self.halo = halo.reshape(128, -1).astype(jnp.bfloat16)
        self.widen = widen.astype(jnp.bfloat16)
        self.third = [self.block_terms(matrix) for matrix in (self.forward, self.forward.T, self.squared.T)]
        column = np.asarray([wj * wk for wj in self.weights for wk in self.weights], np.float32)
        self.table = np.ascontiguousarray(np.broadcast_to(column[:, None], (column.size, 128)))
        face = (ey * p, lanes)
        second = np.tile(np.arange(p), ey)[:, None]
        third = np.tile(np.arange(p), ez)[None, :]
        self.face_table = np.concatenate(
            [
                self.weights[second] * self.weights[third],
                np.broadcast_to(self.end[second], face),
                np.broadcast_to(self.end[third], face),
            ]
        ).astype(np.float32)

    def block_terms(self, matrix):
        size = self.rows // 4
        blocks = np.kron(np.eye(size // self.p), matrix).astype(np.float32)
        upper = blocks.astype(jnp.bfloat16)
        lower = (blocks - upper.astype(np.float32)).astype(jnp.bfloat16)
        return np.concatenate([upper, upper, lower], axis=1)


    def contract(self, x, matrix):
        p = self.p
        sign = 1.0 if matrix[0, 0] * matrix[p - 1, p - 1] > 0 else -1.0
        half = p // 2
        sums = [x[i] + x[p - 1 - i] for i in range(half)]
        differences = [x[i] - x[p - 1 - i] for i in range(half)]
        out = [None] * p
        for a in range(half):
            even, odd = None, None
            for i in range(half):
                first, second = float(matrix[a, i]), float(matrix[a, p - 1 - i])
                even = self.gather(even, 0.5 * (first + second), sums[i])
                odd = self.gather(odd, 0.5 * (first - second), differences[i])
            out[a] = odd + even
            out[p - 1 - a] = even - odd if sign > 0 else odd - even
        return out

    @staticmethod
    def gather(total, factor, x):
        if factor == 0.0:
            return total
        return factor * x if total is None else total + factor * x

    def along_j(self, x, matrix):
        x = x.reshape(self.p, self.p, x.shape[-1])
        return jnp.concatenate(self.contract([x[j] for j in range(self.p)], matrix), axis=0)

    def along_i(self, source, matrix, write):
        p, block = self.p, self.block
        for j in range(p):
            rows = [i * block + j * p for i in range(p)]
            for row, value in zip(rows, self.contract([source[r : r + p, :] for r in rows], matrix)):
                write(row, value)

    def along_k(self, source, table, out):
        size = table.shape[0]
        for start in range(0, self.rows, 2 * size):
            pieces = [split(source[at : at + size, :]) for at in (start, start + size)]
            upper, lower = (jnp.concatenate([piece[n] for piece in pieces], axis=1) for n in range(2))
            both = jnp.dot(
                table[...], jnp.concatenate([upper, lower, upper], axis=0), preferred_element_type=F32
            )
            width = source.shape[-1]
            out[start : start + size, :] = both[:, :width]
            out[start + size : start + 2 * size, :] = both[:, width:]

    def operator(self, v, g, out, slope, flux, third, work, ahead, back):
        block = self.block

        def store(row, value):
            slope[row : row + self.p, :] = value

        self.along_i(v, self.forward, store)
        self.along_k(v, ahead, third)
        for i in range(self.p):
            at = slice(i * block, (i + 1) * block)
            x, s1, s3 = v[at, :], slope[at, :], third[at, :]
            s2 = self.along_j(x, self.forward)
            xy, xz, yz = g[3, at, :], g[4, at, :], g[5, at, :]
            flux[at, :] = g[0, at, :] * s1 + xy * s2 + xz * s3
            f2 = xy * s1 + g[1, at, :] * s2 + yz * s3
            work[at, :] = xz * s1 + yz * s2 + g[2, at, :] * s3
            out[at, :] = self.along_j(f2, self.forward.T) + g[6, at, :] * x
        self.along_k(work, back, third)

        def add(row, value):
            out[row : row + self.p, :] += value + third[row : row + self.p, :]

        self.along_i(flux, self.forward.T, add)

    def fold_second(self, u):
        if self.ey == 1:
            return
        p, width = self.p, u.shape[-1]
        lane = lax.broadcasted_iota(jnp.int32, (p, width), 1)
        f = lax.rem(lane, self.ey)
        for start in range(0, u.shape[0], self.block):
            first, last = u[start : start + p, :], u[start + self.block - p : start + self.block, :]
            u[start + self.block - p : start + self.block, :] = last + jnp.where(
                f < self.ey - 1, pltpu.roll(first, width - 1, 1), 0.0
            )
            u[start : start + p, :] = first + jnp.where(f > 0, pltpu.roll(last, 1, 1), 0.0)

    def fold_third(self, u, step, take_upper, take_lower):
        p, (rows, width) = self.p, u.shape
        count = rows // p
        lane = lax.broadcasted_iota(jnp.int32, (count, width), 1)
        first, last = u[pl.ds(0, count, stride=p), :], u[pl.ds(p - 1, count, stride=p), :]
        u[pl.ds(p - 1, count, stride=p), :] = last + jnp.where(
            take_upper(lane), pltpu.roll(first, width - step, 1), 0.0
        )
        u[pl.ds(0, count, stride=p), :] = first + jnp.where(
            take_lower(lane), pltpu.roll(last, step, 1), 0.0
        )

    def emit(self, u, x_out, y_out):
        p, block = self.p, self.block
        for out, (high, _, _) in zip(x_out, roles("gx", self.sizes["gx"])):
            out[...] = jnp.where(high, u[self.rows - block :, :], u[:block, :])
        for out, (high, _, _) in zip(y_out, roles("gy", self.sizes["gy"])):
            for i in range(p):
                start = i * block
                out[i * p : (i + 1) * p, :] = jnp.where(
                    high, u[start + block - p : start + block, :], u[start : start + p, :]
                )

    def iteration_fold(self, u):
        self.fold_second(u)
        last = self.n3 - self.step3
        self.fold_third(u, self.step3, lambda l: l < last, lambda l: (l >= self.step3) & (l < self.n3))


    def pack_geometry(self, field, out):
        for target, (high, _, _) in zip(out, roles("gz", self.sizes["gz"])):
            rows, width = target.shape
            lane = lax.broadcasted_iota(jnp.int32, (rows, width), 1)
            total = jnp.zeros((rows, width), F32)
            for q in range(FIELDS):
                start = q * self.part
                upper = pltpu.roll(field(q), start + self.part, 1)
                lower = pltpu.roll(field(q), start, 1) if start else field(q)
                here = (lane >= start) & (lane < start + self.part)
                total = jnp.where(here, jnp.where(high, upper, lower), total)
            target[...] = total

    def by_nodes(self, upper, lower, table, width, store):
        for k in range(0, self.p, 2):
            columns = table[:, k * width : (k + 2) * width]
            both = jnp.dot(upper, columns, preferred_element_type=F32) + jnp.dot(
                lower, columns, preferred_element_type=F32
            )
            store(k, both[:, :width])
            store(k + 1, both[:, width:])

    def one_hot(self, slots, ids):
        count = slots.shape[-1]
        column = jnp.broadcast_to(slots[...], (count, count))
        column = jnp.concatenate([column, jnp.zeros((count, 128 - count), jnp.int32)], axis=1)
        column = jnp.concatenate([column, jnp.zeros((128 - count, 128), jnp.int32)], axis=0)
        column = column.astype(F32).T[:count, :1]
        return jnp.concatenate(
            [jnp.where(column == ids[n : n + 1, :].astype(F32), 1.0, 0.0) for n in range(self.c)], axis=0
        ).astype(BF16)

    def spread_tables(self, out3, out4):
        p, ey, ez = self.p, self.ey, self.ez
        for out, width, step, offset, first in (
            (out3, self.w3, self.step3, HALO, 0),
            (out4, self.w4, self.step4, 0, self.c * ey),
        ):
            row = lax.broadcasted_iota(jnp.int32, (ey * ez * p, width), 0)
            lane = lax.broadcasted_iota(jnp.int32, (1, width), 1)
            g = lane // step - offset
            inside = (g >= 0) & (g < ez) & (lax.rem(lane, step) >= first)
            same = row // p == jnp.where(inside, lax.rem(lane, ey) * ez + g, -1)
            node = lax.rem(row, p)
            for k in range(p):
                out[:, k * width : (k + 1) * width] = jnp.where(same & (node == k), 1.0, 0.0).astype(BF16)

    def prepare(self, n_x, n_y, *refs):
        geometry, viscosity, spread, table, right, slots, ids, square = refs[:8]
        s4, hot3 = refs[8:10]
        refs = refs[10:]
        x_out, y_out, work = refs[:n_x], refs[n_x : n_x + n_y], refs[n_x + n_y]
        p, c, block, rows, ey = self.p, self.c, self.block, self.rows, self.ey
        face = ey * p
        wjk, end_j, end_k = (table[n * face : (n + 1) * face, :] for n in range(3))
        stiff, second, third, rest = [], [], [], []
        for i in range(p):
            xx, yy, zz, xy, xz, yz = (geometry[q, i] for q in range(6))
            quadrature = float(self.weights[i]) * wjk
            weighted = quadrature * viscosity[i]
            mass = (helm_coefficient * quadrature) * (
                xx * (yy * zz - yz * yz) - xy * (xy * zz - yz * xz) + xz * (xy * yz - yy * xz)
            )
            cross = end_j * end_k * yz
            end = float(self.end[i])
            if end != 0.0:
                cross = cross + end * (end_j * xy + end_k * xz)
            stiff.append(weighted * xx)
            second.append(weighted * yy)
            third.append(weighted * zz)
            rest.append((2.0 * weighted) * cross + mass)
        upper, lower = split(jnp.concatenate(second, axis=0))
        diagonal = jnp.dot(
            square[...], jnp.concatenate([upper, lower, upper], axis=0), preferred_element_type=F32
        )
        upper, lower = split(jnp.concatenate(third, axis=0))
        diagonal = diagonal + lax.dot_general(
            jnp.concatenate([upper, lower, upper], axis=1),
            square[...],
            (((1,), (1,)), ((), ())),
            preferred_element_type=F32,
        )
        first = self.contract(stiff, self.squared.T)
        diagonal = diagonal + jnp.concatenate([x + y for x, y in zip(first, rest)], axis=0)
        width = diagonal.shape[-1]
        value = diagonal.reshape(p, ey, p, width)
        value = jnp.concatenate([value[:, f].reshape(block, width) for f in range(ey)], axis=1)

        def store(k, part):
            work[pl.ds(k, block, stride=p), :] = part

        self.by_nodes(*split(value), spread, self.w4, store)
        hot = self.one_hot(slots, ids)
        hot3[...] = self.one_hot(slots, ids[c:, :])
        total = work[...]
        for part in split(right[...].reshape(hot.shape[0], rows)):
            total = total + lax.dot_general(
                part, hot, (((0,), (0,)), ((), ())), preferred_element_type=F32
            )
        s4[...] = total
        self.fold_second(s4)
        last = self.n4 - self.step4
        self.fold_third(s4, self.step4, lambda l: l < last, lambda l: (l >= self.step4) & (l < self.n4))
        self.emit(s4, x_out, y_out)

    def convert(self, n_y, n_z, *refs):
        geometry, viscosity, spread, dirichlet = refs[:4]
        raw, ind = refs[4:6]
        refs = refs[6:]
        y_out, z_out, (upper, lower) = refs[:n_y], refs[n_y : n_y + n_z], refs[n_y + n_z :]
        p, c, block, ey = self.p, self.c, self.block, self.ey
        width = geometry.shape[-1]

        def field(q):
            return (geometry[q] if q < FIELDS - 1 else viscosity[...]).reshape(p * ey * p, width)

        for q in range(FIELDS):
            value = field(q).reshape(p, ey, p, width)
            for f in range(ey):
                at = (slice(q * block, (q + 1) * block), slice(f * width, (f + 1) * width))
                upper[at], lower[at] = split(value[:, f].reshape(block, width))
        first_flag, flags = FIELDS * block, 2 * p
        for cc in range(c):
            for f in range(ey):
                at = slice(f * p, (f + 1) * p)
                face = jnp.concatenate([dirichlet[0, cc, at, :], dirichlet[1, cc, at, :]], axis=0)
                to = slice(first_flag + cc * flags, first_flag + (cc + 1) * flags)
                upper[to, f * width : (f + 1) * width] = face.astype(F32).astype(BF16)
                lower[to, f * width : (f + 1) * width] = jnp.zeros((flags, width), BF16)
        row = lax.broadcasted_iota(jnp.int32, (flags, self.w3), 0)
        lane = lax.broadcasted_iota(jnp.int32, (flags, self.w3), 1)
        ends = (lax.axis_index("gx") == 0, lax.axis_index("gx") == self.sizes["gx"] - 1)
        here = ((row < p) & ends[0]) | ((row >= p) & ends[1])
        owner = lax.rem(lane, self.step3) // ey

        def store(k, value):
            raw[pl.ds(k, first_flag, stride=p), :] = value[:first_flag]
            total = jnp.zeros((flags, self.w3), F32)
            for cc in range(c):
                at = first_flag + cc * flags
                total = jnp.where(owner == cc, value[at : at + flags], total)
            ind[pl.ds(k, flags, stride=p), :] = jnp.where(here, total, 0.0)

        self.by_nodes(upper[...], lower[...], spread, self.w3, store)
        self.pack_geometry(field, z_out)
        self.fold_second(ind)
        first_own, end_own = HALO * self.step3, self.n3 - HALO * self.step3
        self.fold_third(
            ind,
            self.step3,
            lambda l: (l >= first_own) & (l < end_own - self.step3),
            lambda l: (l >= first_own + self.step3) & (l < end_own),
        )
        for out, (up, _, _) in zip(y_out, roles("gy", self.sizes["gy"])):
            for n in range(2):
                start = n * block
                out[n * p : (n + 1) * p, :] = jnp.where(
                    up, ind[start + block - p : start + block, :], ind[start : start + p, :]
                )

    def halo_geometry(self, n_z, *refs):
        raw, halo, table = refs[:3]
        z_in, g = refs[3 : 3 + n_z], refs[3 + n_z]
        upper, lower, total = refs[4 + n_z :]
        p, block, rows, ey = self.p, self.block, self.rows, self.ey
        source = raw
        if n_z:
            sides = both_sides([z[...] for z in z_in], roles("gz", self.sizes["gz"]))
            width, part = sides[0].shape[-1], self.part
            sides = [side.reshape(p, ey, p, width) for side in sides]
            lane = lax.broadcasted_iota(jnp.int32, (block, width), 1)
            for q in range(FIELDS):
                value = jnp.zeros((block, width), F32)
                for side in range(2):
                    for f in range(ey):
                        to = (side * ey + f) * part
                        shift = (to - q * part) % width
                        x = sides[side][:, f].reshape(block, width)
                        x = pltpu.roll(x, shift, 1) if shift else x
                        value = jnp.where((lane >= to) & (lane < to + part), x, value)
                at = slice(q * block, (q + 1) * block)
                upper[at, :], lower[at, :] = split(value)

            def store(k, value):
                at = pl.ds(k, FIELDS * block, stride=p)
                total[at, :] = raw[at, :] + value

            self.by_nodes(upper[...], lower[...], halo, self.w3, store)
            source = total
        wjk = table[...]
        for i in range(p):
            at = slice(i * block, (i + 1) * block)
            entries = [source[q * rows + i * block : q * rows + (i + 1) * block, :] for q in range(FIELDS)]
            xx, yy, zz, xy, xz, yz = entries[:6]
            quadrature = float(self.weights[i]) * wjk
            weighted = quadrature * entries[6]
            g[6, at, :] = (helm_coefficient * quadrature) * (
                xx * (yy * zz - yz * yz) - xy * (xy * zz - yz * xz) + xz * (xy * yz - yy * xz)
            )
            for q in range(6):
                g[q, at, :] = weighted * entries[q]

    def coefficients(self, low, high, coef):
        top, bottom = jnp.full((8, 128), high[0], F32), jnp.full((8, 128), low[0], F32)
        midpoint, halfwidth = (top + bottom) * 0.5, (top - bottom) * 0.5
        ratio = midpoint / halfwidth
        damping = 1.0 / ratio
        coef[0:8, :] = 1.0 / midpoint
        for n in range(ITERS - 1):
            following = 1.0 / (2.0 * ratio - damping)
            coef[8 * (2 * n + 1) : 8 * (2 * n + 2), :] = following * damping
            coef[8 * (2 * n + 2) : 8 * (2 * n + 3), :] = 2.0 * following / halfwidth
            damping = following

    def join(self, n_x, n_y, *refs):
        x_in, refs = refs[:n_x], refs[n_x:]
        y_raw, y_more, y_out = refs[:n_y], refs[n_y:-n_y], refs[-n_y:]
        p, block, ey = self.p, self.block, self.ey
        low, high = both_sides([x[...] for x in x_in], roles("gx", self.sizes["gx"]))
        for n, (up, _, _) in enumerate(roles("gy", self.sizes["gy"])):
            face = y_raw[n][...]
            width = face.shape[-1]
            if n_x:
                first, last = (jnp.where(up, x[block - p :], x[:p]) for x in (low, high))
                face = jnp.concatenate([face[:p] + first, face[p : block - p], face[block - p :] + last], axis=0)
            if y_more:
                face = jnp.concatenate([face, y_more[n][...]], axis=0)
            if ey == 1:
                y_out[n][...] = face
                continue
            half = face.shape[0] // 2
            first, second = face[:half], face[half:]
            f = lax.rem(lax.broadcasted_iota(jnp.int32, first.shape, 1), ey)
            below = jnp.where(f == 0, pltpu.roll(first, width - (ey - 1), 1), 0.0) + jnp.where(
                f == 1, pltpu.roll(second, (width - (ey - 2)) % width, 1) if ey != 2 else second, 0.0
            )
            above = jnp.where(f == ey - 1, pltpu.roll(first, ey - 1, 1), 0.0) + jnp.where(
                f == ey - 2, pltpu.roll(second, ey - 2, 1) if ey != 2 else second, 0.0
            )
            y_out[n][...] = jnp.where(up, below, above)

    def second_sides(self, received):
        role, ey = roles("gy", self.sizes["gy"]), self.ey
        faces = []
        for message, (_, from_high, _) in zip(received, role):
            data = message[...]
            if ey > 1:
                width = data.shape[-1]
                f = lax.rem(lax.broadcasted_iota(jnp.int32, data.shape, 1), ey)
                beside = jnp.where(from_high, pltpu.roll(data, 1, 1), pltpu.roll(data, width - 1, 1))
                here = f == jnp.where(from_high, ey - 1, 0)
                data = jnp.concatenate([jnp.where(here, x, 0.0) for x in (data, beside)], axis=0)
            faces.append(data)
        return both_sides(faces, role)

    def pack_first(self, n_x, *refs):
        s4, ind = refs[:2]
        x_in, s_out, z_out = refs[2 : 2 + n_x], refs[2 + n_x], refs[3 + n_x :]
        p, block, rows = self.p, self.block, self.rows
        s_out[...] = s4[...]
        if n_x:
            low, high = both_sides([x[...] for x in x_in], roles("gx", self.sizes["gx"]))
            s_out[:block, :] += low
            s_out[rows - block :, :] += high
        halo3 = HALO * self.step3
        for out, (up, _, _) in zip(z_out, roles("gz", self.sizes["gz"])):
            self.pack(out, s_out, block, 0, self.n4 - self.halo4, up, 0)
            self.pack(out, ind, p, halo3, self.n3 - 2 * halo3, up, block)

    def pack(self, out, u, count, first, last, up, start):
        p, width, size = self.p, self.w4, self.halo4
        lane = lax.broadcasted_iota(jnp.int32, (count, width), 1)
        for section in range(0, u.shape[0] // count, p):
            total = jnp.zeros((count, width), F32)
            for n in range(p):
                at, shift = (section + n) * count, n * size
                x = u[at : at + count, :]
                below = pltpu.roll(x, (shift - first) % width, 1) if (shift - first) % width else x
                above = pltpu.roll(x, (shift - last) % width, 1)
                here = (lane >= shift) & (lane < shift + size)
                total = jnp.where(here, jnp.where(up, above, below), total)
            row = start + section // p * count
            out[row : row + count, :] = total

    def pack_second(self, n_y, n_z, *refs):
        y_in, z_in, z_out = refs[:n_y], refs[n_y : n_y + n_z], refs[n_y + n_z :]
        p, block, width, size = self.p, self.block, self.w4, self.halo4
        low, high = self.second_sides(y_in)
        halo3 = HALO * self.step3
        lane = lax.broadcasted_iota(jnp.int32, (p, width), 1)
        for packed, out, (up, _, _) in zip(z_in, z_out, roles("gz", self.sizes["gz"])):
            out[...] = packed[...]
            for face, row in ((low, 0), (high, block - p)):
                total = jnp.zeros((p, width), F32)
                for n in range(p):
                    shift = n * size
                    x = face[n * p : (n + 1) * p]
                    below = pltpu.roll(x, shift, 1) if shift else x
                    above = pltpu.roll(x, (shift - self.n4 + size) % width, 1)
                    here = (lane >= shift) & (lane < shift + size)
                    total = jnp.where(here, jnp.where(up, above, below), total)
                out[row : row + p, :] += total
            for n in range(2):
                row = block + n * p
                for face, group in ((low, 0), (high, p - 1)):
                    shift = group * size
                    x = face[row : row + p]
                    below = pltpu.roll(x, (shift - halo3) % width, 1)
                    above = pltpu.roll(x, (shift - self.n3 + 2 * halo3) % width, 1)
                    here = (lane >= shift) & (lane < shift + size)
                    out[row : row + p, :] += jnp.where(here, jnp.where(up, above, below), 0.0)

    def own(self, n_y, *refs):
        s4, ind, widen = refs[:3]
        y_in, (r, scale, flag, work) = refs[3 : 3 + n_y], refs[3 + n_y :]
        p, block, w3 = self.p, self.block, self.w3
        work[...] = s4[...]
        flag[...] = ind[...]
        if n_y:
            low, high = self.second_sides(y_in)
            for u, first, count in ((work, 0, p), (flag, p, 2)):
                for i in range(count):
                    at, end, row = i * block, (i + 1) * block, (first + i) * p
                    u[at : at + p, :] += low[row : row + p]
                    u[end - p : end, :] += high[row : row + p]
        both = dot2(work[...], widen[: self.w4, :])
        r[...] = both[:, :w3]
        scale[...] = both[:, w3:]

    def start(self, n_x, n_y, n_z, *refs):
        r_own, diagonal_own, flag_own, g, widen, ahead, back = refs[:7]
        z_in = refs[7 : 7 + n_z]
        t, scale, v = refs[7 + n_z : 10 + n_z]
        refs = refs[10 + n_z :]
        x_out, y_out = refs[:n_x], refs[n_x : n_x + n_y]
        beside, r, flag = refs[n_x + n_y : n_x + n_y + 3]
        work = refs[n_x + n_y + 3 :]
        p, block, rows, w3, w4 = self.p, self.block, self.rows, self.w3, self.w4
        step, first_own, end_own = self.step3, HALO * self.step3, self.n3 - HALO * self.step3
        size, part = self.sizes["gz"], self.halo4
        if n_z:
            low, high = both_sides([z[...] for z in z_in], roles("gz", size))
        else:
            low = high = jnp.zeros((block + 2 * p, w4), F32)
        lane = lax.broadcasted_iota(jnp.int32, (block, w4), 1)
        for n in range(p):
            first = pltpu.roll(low[:block], w4 - n * part, 1) if n else low[:block]
            second = pltpu.roll(high[:block], (part - n * part) % w4, 1) if n != 1 else high[:block]
            beside[n * block : (n + 1) * block, :] = jnp.where(
                lane < part, first, jnp.where(lane < 2 * part, second, 0.0)
            )
        both = dot2(beside[...], widen[w4:, :])
        r[...] = r_own[...] + both[:, :w3]
        scale[...] = diagonal_own[...] + both[:, w3:]
        lane = lax.broadcasted_iota(jnp.int32, (p, w3), 1)
        for n in range(2 * p):
            row, shift = block + n // p * p, n % p * part
            first = pltpu.roll(low[row : row + p], w3 - shift, 1) if shift else low[row : row + p]
            second = pltpu.roll(high[row : row + p], (end_own - shift) % w3, 1)
            flag[n * p : (n + 1) * p, :] = jnp.where(
                lane < first_own,
                first,
                jnp.where(lane < end_own, flag_own[n * p : (n + 1) * p, :], jnp.where(lane < self.n3, second, 0.0)),
            )
        for u in (r, scale, flag):
            self.fold_third(
                u,
                step,
                lambda l: ((l >= first_own - step) & (l < first_own)) | ((l >= end_own - step) & (l < end_own)),
                lambda l: ((l >= first_own) & (l < first_own + step)) | ((l >= end_own) & (l < end_own + step)),
            )
        index = lax.axis_index("gz")
        begin = jnp.where(index > 0, 0, first_own)
        end = jnp.where(index < size - 1, self.n3, end_own)
        lane = lax.broadcasted_iota(jnp.int32, (block, w3), 1)
        valid = (lane >= begin) & (lane < end)
        for i in range(p):
            at = slice(i * block, (i + 1) * block)
            factor = jnp.where(valid, 1.0 / jnp.where(valid, scale[at, :], 1.0), 0.0)
            if i in (0, p - 1):
                row = 0 if i == 0 else block
                factor = jnp.where(flag[row : row + block, :] > 0.5, 0.0, factor)
            scale[at, :] = factor
            t[at, :] = factor * r[at, :]
        self.operator(t, g, v, *work, ahead, back)
        self.iteration_fold(v)
        self.emit(v, x_out, y_out)

    def factors(self, coef, n):
        rows = [coef[8 * m : 8 * m + 1, :] for m in (0, 2 * n + 1, 2 * n + 2)]
        return (rows[0] if n == 0 else None), rows[1], rows[2]

    def shares(self, faces, scale, image, at):
        low, high = faces
        p, block = self.p, self.block
        i = at // block
        out = []
        for start, face in ((at, low), (at + block - p, high)):
            value = scale[start : start + p, :] * face[i * p : (i + 1) * p]
            out.append((start, -value if image is None else -image * value))
        return out

    def preview(self, n_x, n_y, n, last, *refs):
        t, t_old, d, scale, v, coef, hot = refs[:7]
        refs = refs[7:]
        x_in, y_old, refs = refs[:n_x], refs[n_x : -2 if not last else -3], refs[-2 if not last else -3 :]
        p, block, rows = self.p, self.block, self.rows
        image, keep, gain = self.factors(coef, n)
        start = coef[0:1, :]
        if last:
            out, t_new, field = refs
        else:
            t_new, d_new = refs
        low, high = both_sides([x[...] for x in x_in], roles("gx", self.sizes["gx"]))
        if n:
            faces = self.second_sides(y_old) if n_y else None
            image_old = self.factors(coef, n - 1)[0]
        for i in range(p):
            at = slice(i * block, (i + 1) * block)
            value = v[at, :]
            if n_x and i in (0, p - 1):
                value = value + (low if i == 0 else high)
            value = scale[at, :] * value
            t_new[at, :] = t_old[at, :] - (value if image is None else image * value)
            if n and n_y:
                for row, share in self.shares(faces, scale, image_old, i * block):
                    t_new[row : row + p, :] += share
            direction = d[at, :] if n else start * t[at, :]
            following = keep * direction + gain * t_new[at, :]
            if last:
                field[at, :] = start * t[at, :] + following + (direction if n else 0.0)
            else:
                d_new[at, :] = following
        if last:
            out[...] = self.by_slots(hot, field[...])

    def by_slots(self, hot, field):
        value = None
        for part in split(field):
            term = lax.dot_general(
                hot[...], part, (((1,), (1,)), ((), ())), preferred_element_type=F32
            )
            value = term if value is None else value + term
        return value

    def middle(self, n_x, n_y, n, *refs):
        d, scale, g, coef, ahead, back = refs[:6]
        y_in, refs = refs[6 : 6 + n_y], refs[6 + n_y :]
        d_new, v = refs[:2]
        x_out, y_out, work = refs[2 : 2 + n_x], refs[2 + n_x : 2 + n_x + n_y], refs[2 + n_x + n_y :]
        d_new[...] = d[...]
        image, _, gain = self.factors(coef, n)
        if n_y:
            faces = self.second_sides(y_in)
            for i in range(self.p):
                for row, share in self.shares(faces, scale, image, i * self.block):
                    d_new[row : row + self.p, :] += gain * share
        self.operator(d_new, g, v, *work, ahead, back)
        self.iteration_fold(v)
        self.emit(v, x_out, y_out)

    def finish(self, n_y, n, *refs):
        part, scale, coef, hot = refs[:4]
        y_in, (out, field) = refs[4 : 4 + n_y], refs[4 + n_y :]
        value = part[...]
        image, _, gain = self.factors(coef, n)
        if n_y:
            faces = self.second_sides(y_in)
            field[...] = jnp.zeros(field.shape, F32)
            for i in range(self.p):
                for row, share in self.shares(faces, scale, image, i * self.block):
                    field[row : row + self.p, :] = gain * share
            value = value + self.by_slots(hot, field[...])
        out[...] = value.reshape(out.shape)


def shards(sizes, right_side, geometry, viscosity, eig_low, eig_high, element_slot, dirichlet):
    plan = Plan(right_side.shape[0], viscosity.shape, sizes)
    p, block, rows, w3, w4 = plan.p, plan.block, plan.rows, plan.w3, plan.w4
    x_pairs = pairings(("gx",), (sizes["gx"],), 0)
    y_pairs = pairings(("gy",), (sizes["gy"],), 0)
    z_pairs = pairings(("gx", "gz"), (sizes["gx"], sizes["gz"]), 1)
    n_x, n_y, n_z = len(x_pairs), len(y_pairs), len(z_pairs)

    def send(arrays, axis, pairs):
        return [lax.ppermute(x, axis, pair) for x, pair in zip(arrays, pairs)]

    def shape(*size, dtype=F32):
        return jax.ShapeDtypeStruct(size, dtype)

    def call(kernel, outputs, operands, scratch=(), spaces={}, flops=0, name=None):
        specs = [pl.BlockSpec(memory_space=spaces.get(n, pltpu.VMEM)) for n in range(len(operands))]
        return list(
            pl.pallas_call(
                kernel,
                out_shape=list(outputs),
                in_specs=specs,
                out_specs=[pl.BlockSpec(memory_space=pltpu.VMEM)] * len(outputs),
                scratch_shapes=list(scratch),
                compiler_params=pltpu.CompilerParams(vmem_limit_bytes=VMEM_BYTES),
                cost_estimate=pl.CostEstimate(flops=flops, bytes_accessed=0, transcendentals=0),
                name=name,
            )(*operands)
        )

    def vmem(*size, dtype=F32):
        return pltpu.VMEM(size, dtype)

    lanes = plan.ez * p
    table = jnp.asarray(plan.table)
    ahead, back = jnp.asarray(plan.third[0]), jnp.asarray(plan.third[1])
    field3, field4 = shape(rows, w3), shape(rows, w4)
    elements = element_slot.shape[-1]
    spread3, spread4 = call(
        plan.spread_tables,
        [shape(plan.ey * lanes, p * w, dtype=BF16) for w in (w3, w4)],
        (),
        flops=FLOPS,
        name="spread_tables",
    )
    results = call(
        functools.partial(plan.prepare, n_x, n_y),
        [field4, shape(plan.c * elements, w3, dtype=BF16)] + [shape(block, w4)] * (n_x + n_y),
        (
            geometry,
            viscosity,
            spread4,
            jnp.asarray(plan.face_table),
            jnp.swapaxes(right_side, 1, 2),
            element_slot,
            jnp.asarray(plan.ids),
            jnp.asarray(plan.third[2]),
        ),
        scratch=[vmem(rows, w4)],
        name="prepare",
    )
    s4, hot3 = results[:2]
    x_out, y_raw = results[2 : 2 + n_x], results[2 + n_x :]
    x_in = send(x_out, "gx", x_pairs)

    lhs = FIELDS * block + 2 * plan.c * p
    results = call(
        functools.partial(plan.convert, n_y, n_z),
        [shape(FIELDS * rows, w3), shape(2 * block, w3)]
        + [shape(2 * p, w3)] * n_y
        + [shape(p * plan.ey * p, lanes)] * n_z,
        (geometry, viscosity, spread3, dirichlet),
        scratch=[vmem(lhs, plan.ey * lanes, dtype=BF16)] * 2,
        name="convert",
    )
    raw, ind = results[:2]
    y_more, z_geometry = results[2 : 2 + n_y], results[2 + n_y :]

    def joined(x_in, y_raw, y_more=()):
        if not y_raw:
            return []
        count = y_raw[0].shape[0] + (y_more[0].shape[0] if y_more else 0)
        faces = [shape(count // 2 if plan.ey > 1 else count, y.shape[1]) for y in y_raw]
        return call(functools.partial(plan.join, n_x, n_y), faces, x_in + y_raw + list(y_more), name="join")

    y_in = send(joined(x_in, y_raw, y_more), "gy", y_pairs)
    z_geometry = send(z_geometry, ("gx", "gz"), z_pairs)
    g = call(
        functools.partial(plan.halo_geometry, n_z),
        [shape(FIELDS, rows, w3)],
        [raw, jnp.asarray(plan.halo), table] + z_geometry,
        scratch=[vmem(FIELDS * block, 128, dtype=BF16)] * 2 + [vmem(FIELDS * rows, w3)],
        name="halo_geometry",
    )[0]
    results = call(
        functools.partial(plan.pack_first, n_x),
        [field4] + [shape(block + 2 * p, w4)] * n_z,
        [s4, ind] + x_in,
        name="pack_first",
    )
    s4, z_out = results[0], results[1:]
    if n_y and n_z:
        z_out = call(
            functools.partial(plan.pack_second, n_y, n_z),
            [shape(*z.shape) for z in z_out],
            y_in + z_out,
            flops=FLOPS,
            name="pack_second",
        )
    z_in = send(z_out, ("gx", "gz"), z_pairs)
    widen = jnp.asarray(plan.widen)
    own = call(
        functools.partial(plan.own, n_y),
        [field3, field3, shape(2 * block, w3)],
        [s4, ind, widen] + y_in,
        scratch=[vmem(rows, w4)],
        name="own",
    )

    messages = [shape(block, w3)] * (n_x + n_y)
    results = call(
        functools.partial(plan.start, n_x, n_y, n_z),
        [field3] * 3 + messages,
        own + [g, widen, ahead, back] + z_in,
        scratch=[vmem(rows, w4), vmem(rows, w3), vmem(2 * block, w3)] + [vmem(rows, w3)] * 4,
        name="first_direction",
    )
    t, scale, v = results[:3]
    x_out, y_raw = results[3 : 3 + n_x], results[3 + n_x :]
    x_out, low, high = lax.optimization_barrier((x_out, eig_low, eig_high))
    coef = call(
        plan.coefficients,
        [shape(8 * (2 * ITERS - 1), 128)],
        (low, high),
        spaces={0: pltpu.SMEM, 1: pltpu.SMEM},
        name="coefficients",
    )[0]
    t_old, d, y_in = t, t, []
    for n in range(ITERS - 1):
        last = n == ITERS - 2
        x_in = send(x_out, "gx", x_pairs)
        y_old, y_in = y_in, send(joined(x_in, y_raw), "gy", y_pairs)
        results = call(
            functools.partial(plan.preview, n_x, n_y, n, last),
            [shape(plan.c * elements, rows)] if last else [field3, field3],
            [t, t_old, d, scale, v, coef, hot3] + x_in + y_old,
            scratch=[vmem(rows, w3)] * 2 if last else [],
            name="preview",
        )
        if last:
            break
        t_old, d = results
        results = call(
            functools.partial(plan.middle, n_x, n_y, n),
            [field3] * 2 + messages,
            [d, scale, g, coef, ahead, back] + y_in,
            scratch=[vmem(rows, w3)] * 4,
            name="direction",
        )
        d, v = results[:2]
        x_out, y_raw = results[2 : 2 + n_x], results[2 + n_x :]
    out = call(
        functools.partial(plan.finish, n_y, n),
        [shape(plan.c, elements, rows)],
        [results[0], scale, coef, hot3] + y_in,
        scratch=[vmem(rows, w3)],
        name="field",
    )[0]
    return jnp.swapaxes(out, 1, 2)


def solution(mesh):
    sizes = {name: mesh.shape[name] for name in ("gx", "gy", "gz")}
    return jax.shard_map(
        functools.partial(shards, sizes),
        mesh=mesh,
        in_specs=(
            P(None, None, ("gx", "gy", "gz")),
            P(None, "gx", "gy", "gz"),
            P("gx", "gy", "gz"),
            P(),
            P(),
            P(("gx", "gy", "gz"), None),
            P(None, None, "gy", "gz"),
        ),
        out_specs=P(None, None, ("gx", "gy", "gz")),
        check_vma=False,
    )
```

```python
import functools
import math

import jax
import jax.numpy as jnp
import numpy as np
from jax import lax
from jax.experimental import pallas as pl
from jax.experimental.pallas import tpu as pltpu
from jax.sharding import PartitionSpec as P

DEGREE = 7
ITERS = 3


helm_coefficient = 10.0


def legendre_pair(values, degree):
    previous = 0.0 * values + 1.0
    current = values.copy()
    for order in range(2, degree + 1):
        previous, current = (
            current,
            ((2 * order - 1) * values * current - (order - 1) * previous) / order,
        )
    return (current, previous)


def gll_tables(degree):
    start = np.cos(np.pi * np.arange(degree + 1) / degree)
    nodes_now = start.copy()
    for sweep in range(80):
        top_value, lower_value = legendre_pair(nodes_now, degree)
        nodes_now = nodes_now - (nodes_now * top_value - lower_value) / ((degree + 1) * top_value)
    gll_nodes = nodes_now[::-1].copy()
    gll_nodes[0] = -1.0
    gll_nodes[degree] = 1.0
    legendre_values = legendre_pair(gll_nodes, degree)[0]
    weights = 2.0 / (degree * (degree + 1) * legendre_values**2)
    differences = gll_nodes[:, None] - gll_nodes[None, :] + np.eye(degree + 1)
    derivative = legendre_values[:, None] / legendre_values[None, :] / differences
    derivative = derivative * (1.0 - np.eye(degree + 1))
    derivative[0, 0] = -degree * (degree + 1) / 4.0
    derivative[degree, degree] = degree * (degree + 1) / 4.0
    return (weights, derivative)


HALO = 2
FIELDS = 7
VMEM_BYTES = 40 * 1024 * 1024
FLOPS = 3 * 10**9
F32 = jnp.float32
BF16 = jnp.bfloat16


def pairings(names, sizes, dim):
    size = sizes[dim]
    if size == 1:
        return []
    if size % 2:
        shifts = (1, size - 1)
        partners = [[(i + shift) % size for i in range(size)] for shift in shifts]
    else:
        partners = [[i ^ 1 for i in range(size)]]
        if size > 2:
            partners.append([((i + 1) ^ 1) - 1 for i in range(size)])
    result = []
    for partner in partners:
        pairs = []
        for flat in range(math.prod(sizes)):
            place = list(np.unravel_index(flat, sizes))
            to = partner[place[dim]]
            if 0 <= to < size:
                place[dim] = to
            elif len(sizes) > 1 and sizes[1 - dim] % 2 == 0:
                place[1 - dim] ^= 1
            else:
                place[dim] = size - 1 - place[dim]
            pairs.append((flat, int(np.ravel_multi_index(place, sizes))))
        result.append(pairs)
    return result


def roles(name, size):
    if size == 1:
        return []
    index = lax.axis_index(name)
    low, high = index > 0, index < size - 1
    if size % 2:
        yes = index >= 0
        no = index < 0
        return [(yes, no, low), (no, yes, high)]
    even = lax.rem(index, 2) == 0
    odd = jnp.logical_not(even)
    result = [(even, even, index >= 0)]
    if size > 2:
        result.append((odd, odd, jnp.logical_or(jnp.logical_and(odd, high), jnp.logical_and(even, low))))
    return result


def both_sides(received, role):
    low, high = 0.0, 0.0
    for data, (_, from_high, used) in zip(received, role):
        high = high + jnp.where(jnp.logical_and(used, from_high), data, 0.0)
        low = low + jnp.where(jnp.logical_and(used, jnp.logical_not(from_high)), data, 0.0)
    return low, high


def split(x):
    upper = x.astype(BF16)
    return upper, (x - upper.astype(F32)).astype(BF16)


def dot2(x, table):
    return jnp.dot(
        jnp.concatenate(split(x), axis=1),
        jnp.concatenate([table, table], axis=0),
        preferred_element_type=F32,
    )


class Plan:
    def __init__(self, components, viscosity_shape, mesh_sizes):
        points = DEGREE + 1
        self.p, self.c = points, components
        self.sizes = mesh_sizes
        ex, ey, ez = (n // points for n in viscosity_shape)
        assert ex == 1 and ez >= HALO
        self.ey, self.ez = ey, ez
        self.rows = points**3
        self.block = points * points
        self.step3, self.step4 = components * ey, (components + 1) * ey
        self.n3, self.n4 = (ez + 2 * HALO) * self.step3, ez * self.step4
        self.w3, self.w4 = -(-self.n3 // 128) * 128, -(-self.n4 // 128) * 128
        self.halo4 = HALO * self.step4
        assert points * self.halo4 <= self.w4 and 2 * self.halo4 <= self.w4
        weights, derivative = gll_tables(DEGREE)
        self.forward = derivative.astype(np.float32)
        self.squared = self.forward * self.forward
        self.weights = weights.astype(np.float32)
        self.end = np.diagonal(self.forward)
        self.tables()

    def lane3(self, g, c, f):
        return (g + HALO) * self.step3 + c * self.ey + f

    def lane4(self, g, c, f):
        return g * self.step4 + c * self.ey + f

    def tables(self):
        p, c, ey, ez = self.p, self.c, self.ey, self.ez
        lanes = ez * p
        every = [(g, cc, f) for g in range(ez) for cc in range(c) for f in range(ey)]
        widen = np.zeros((2 * self.w4, 2 * self.w3), np.float32)
        ids = np.full((2 * c, 128, 128), -1, np.int32)
        for g, cc, f in every:
            widen[self.lane4(g, cc, f), self.lane3(g, cc, f)] = 1
            widen[self.lane4(g, c, f), self.w3 + self.lane3(g, cc, f)] = 1
            ids[cc, :, self.lane4(g, cc, f)] = f * ez + g
            ids[c + cc, :, self.lane3(g, cc, f)] = f * ez + g
        self.ids = np.ascontiguousarray(ids[:, :1, :]).reshape(2 * c, 128)
        part = HALO * p
        self.part = part
        assert FIELDS * part <= lanes and 2 * ey * part <= lanes // 2
        halo = np.zeros((lanes, p, self.w3), np.float32)
        for side, first in ((0, -HALO), (1, ez)):
            for g in range(HALO):
                for cc in range(c):
                    for f in range(ey):
                        at = self.lane3(first + g, cc, f)
                        row = self.w4 + side * self.halo4 + g * self.step4
                        widen[row + cc * ey + f, at] = 1
                        widen[row + c * ey + f, self.w3 + at] = 1
                        for k in range(p):
                            for half in range(2):
                                halo[half * lanes // 2 + (side * ey + f) * part + g * p + k, k, at] = 1
        self.halo = halo.reshape(lanes, -1).astype(jnp.bfloat16)
        self.widen = widen.astype(jnp.bfloat16)
        self.third = [self.block_terms(matrix) for matrix in (self.forward, self.forward.T, self.squared.T)]
        face = (ey * p, lanes)
        second = np.tile(np.arange(p), ey)[:, None]
        third = np.tile(np.arange(p), ez)[None, :]
        self.face_table = np.concatenate(
            [
                self.weights[second] * self.weights[third],
                np.broadcast_to(self.end[second], face),
                np.broadcast_to(self.end[third], face),
            ]
        ).astype(np.float32)

    def block_terms(self, matrix):
        size = self.rows // 4
        blocks = np.kron(np.eye(size // self.p), matrix).astype(np.float32)
        upper = blocks.astype(jnp.bfloat16)
        lower = (blocks - upper.astype(np.float32)).astype(jnp.bfloat16)
        return np.concatenate([upper, upper, lower], axis=1)


    def contract(self, x, matrix, wanted=None):
        p = self.p
        sign = 1.0 if matrix[0, 0] * matrix[p - 1, p - 1] > 0 else -1.0
        half = p // 2
        sums = [x[i] + x[p - 1 - i] for i in range(half)]
        differences = [x[i] - x[p - 1 - i] for i in range(half)]
        out = [None] * p
        for a in range(half) if wanted is None else wanted:
            even, odd = None, None
            for i in range(half):
                first, second = float(matrix[a, i]), float(matrix[a, p - 1 - i])
                even = self.gather(even, 0.5 * (first + second), sums[i])
                odd = self.gather(odd, 0.5 * (first - second), differences[i])
            out[a] = odd + even
            out[p - 1 - a] = even - odd if sign > 0 else odd - even
        return [x for x in out if x is not None]

    @staticmethod
    def gather(total, factor, x):
        if factor == 0.0:
            return total
        return factor * x if total is None else total + factor * x

    def along_j(self, x, matrix):
        x = x.reshape(self.p, self.p, x.shape[-1])
        return jnp.concatenate(self.contract([x[j] for j in range(self.p)], matrix), axis=0)

    def along_i(self, source, matrix, write):
        p, block = self.p, self.block
        for j in range(p):
            rows = [i * block + j * p for i in range(p)]
            for row, value in zip(rows, self.contract([source[r : r + p, :] for r in rows], matrix)):
                write(row, value)

    def along_k(self, source, table, out, start, end):
        size = table.shape[0]
        width = source.shape[-1]
        while start < end:
            count = min(2, (end - start) // size)
            pieces = [split(source[start + n * size : start + (n + 1) * size, :]) for n in range(count)]
            upper, lower = (jnp.concatenate([piece[n] for piece in pieces], axis=1) for n in range(2))
            both = jnp.dot(
                table[...], jnp.concatenate([upper, lower, upper], axis=0), preferred_element_type=F32
            )
            for n in range(count):
                out[start + n * size : start + (n + 1) * size, :] = both[:, n * width : (n + 1) * width]
            start += count * size

    def rows_of(self, g, q, at):
        return g[q * self.rows + at.start : q * self.rows + at.stop, :]

    def operator_first(self, v, g, ends, f1, f2, f3, slope, third, ahead, back):
        p, block, rows = self.p, self.block, self.rows

        def store(row, value):
            slope[row : row + p, :] = value

        self.along_i(v, self.forward, store)
        self.along_k(v, ahead, third, 0, rows)
        for i in range(p):
            at = slice(i * block, (i + 1) * block)
            x, s1, s3 = v[at, :], slope[at, :], third[at, :]
            s2 = self.along_j(x, self.forward)
            xy, xz, yz = self.rows_of(g, 3, at), self.rows_of(g, 4, at), self.rows_of(g, 5, at)
            f1[at, :] = self.rows_of(g, 0, at) * s1 + xy * s2 + xz * s3
            f2[at, :] = xy * s1 + self.rows_of(g, 1, at) * s2 + yz * s3
            f3[at, :] = xz * s1 + yz * s2 + self.rows_of(g, 2, at) * s3
        for n, start in enumerate((0, rows - block)):
            at = slice(start, start + block)
            ends[n * block : (n + 1) * block, :] = self.along_j(f2[at, :], self.forward.T) + self.rows_of(g, 6, at) * v[at, :]
            slope[n * block : (n + 1) * block, :] = f3[at, :]
        self.along_k(slope, back, third, 0, 2 * block)
        for j in range(p):
            x = [f1[i * block + j * p : i * block + (j + 1) * p, :] for i in range(p)]
            first, last = self.contract(x, self.forward.T, (0,))
            for row, value in ((j * p, first), (block + j * p, last)):
                ends[row : row + p, :] += value + third[row : row + p, :]

    def operator_second(self, n_x, n_y, *refs):
        v, g, ends, f1, f2, f3, back = refs[:7]
        out, y_out, third = refs[7], refs[8 : 8 + n_y], refs[8 + n_y]
        p, block, rows = self.p, self.block, self.rows
        out[:block, :], out[rows - block :, :] = ends[:block, :], ends[block:, :]
        self.along_k(f3, back, third, block, rows - block)
        for i in range(1, p - 1):
            at = slice(i * block, (i + 1) * block)
            out[at, :] = self.along_j(f2[at, :], self.forward.T) + self.rows_of(g, 6, at) * v[at, :] + third[at, :]
        for j in range(p):
            at = [slice(i * block + j * p, i * block + (j + 1) * p) for i in range(p)]
            values = self.contract([f1[r, :] for r in at], self.forward.T, range(1, p // 2))
            for r, value in zip(at[1 : p - 1], values):
                out[r, :] += value
        self.iteration_fold(out.at[block : rows - block, :])
        self.emit_second(out, y_out)

    def fold_second(self, u):
        if self.ey == 1:
            return
        p, width = self.p, u.shape[-1]
        lane = lax.broadcasted_iota(jnp.int32, (p, width), 1)
        f = lax.rem(lane, self.ey)
        for start in range(0, u.shape[0], self.block):
            first, last = u[start : start + p, :], u[start + self.block - p : start + self.block, :]
            u[start + self.block - p : start + self.block, :] = last + jnp.where(
                f < self.ey - 1, pltpu.roll(first, width - 1, 1), 0.0
            )
            u[start : start + p, :] = first + jnp.where(f > 0, pltpu.roll(last, 1, 1), 0.0)

    def fold_third(self, u, step, take_upper, take_lower):
        p, (rows, width) = self.p, u.shape
        count = rows // p
        lane = lax.broadcasted_iota(jnp.int32, (count, width), 1)
        first, last = u[pl.ds(0, count, stride=p), :], u[pl.ds(p - 1, count, stride=p), :]
        u[pl.ds(p - 1, count, stride=p), :] = last + jnp.where(
            take_upper(lane), pltpu.roll(first, width - step, 1), 0.0
        )
        u[pl.ds(0, count, stride=p), :] = first + jnp.where(
            take_lower(lane), pltpu.roll(last, step, 1), 0.0
        )

    def emit_first(self, ends, x_out):
        for out, (high, _, _) in zip(x_out, roles("gx", self.sizes["gx"])):
            out[...] = jnp.where(high, ends[1], ends[0])

    def emit_second(self, u, y_out):
        p, block = self.p, self.block
        for out, (high, _, _) in zip(y_out, roles("gy", self.sizes["gy"])):
            for i in range(p):
                start = i * block
                out[i * p : (i + 1) * p, :] = jnp.where(
                    high, u[start + block - p : start + block, :], u[start : start + p, :]
                )

    def iteration_fold(self, u):
        self.fold_second(u)
        last = self.n3 - self.step3
        self.fold_third(u, self.step3, lambda l: l < last, lambda l: (l >= self.step3) & (l < self.n3))


    def pack_fields(self, fields, out):
        for target, (high, _, _) in zip(out, roles("gz", self.sizes["gz"])):
            rows, width = target.shape
            lane = lax.broadcasted_iota(jnp.int32, (rows, width), 1)
            total = jnp.zeros((rows, width), F32)
            for q in range(FIELDS):
                start = q * self.part
                upper = pltpu.roll(fields[q], start + self.part, 1)
                lower = pltpu.roll(fields[q], start, 1) if start else fields[q]
                here = (lane >= start) & (lane < start + self.part)
                total = jnp.where(here, jnp.where(high, upper, lower), total)
            target[...] = total

    def by_nodes(self, upper, lower, table, width, store):
        for k in range(0, self.p, 2):
            columns = table[:, k * width : (k + 2) * width]
            both = jnp.dot(upper, columns, preferred_element_type=F32) + jnp.dot(
                lower, columns, preferred_element_type=F32
            )
            store(k, both[:, :width])
            store(k + 1, both[:, width:])

    def one_hot(self, slots, ids):
        count = slots.shape[-1]
        column = jnp.broadcast_to(slots[...], (count, count))
        column = jnp.concatenate([column, jnp.zeros((count, 128 - count), jnp.int32)], axis=1)
        column = jnp.concatenate([column, jnp.zeros((128 - count, 128), jnp.int32)], axis=0)
        column = column.astype(F32).T[:count, :1]
        return jnp.concatenate(
            [jnp.where(column == ids[n : n + 1, :].astype(F32), 1.0, 0.0) for n in range(self.c)], axis=0
        ).astype(BF16)

    def spread_tables(self, out3, out4):
        p, ey, ez = self.p, self.ey, self.ez
        for out, width, step, offset, first in (
            (out3, self.w3, self.step3, HALO, 0),
            (out4, self.w4, self.step4, 0, self.c * ey),
        ):
            row = lax.broadcasted_iota(jnp.int32, (ey * ez * p, width), 0)
            lane = lax.broadcasted_iota(jnp.int32, (1, width), 1)
            g = lane // step - offset
            inside = (g >= 0) & (g < ez) & (lax.rem(lane, step) >= first)
            same = row // p == jnp.where(inside, lax.rem(lane, ey) * ez + g, -1)
            node = lax.rem(row, p)
            for k in range(p):
                out[:, k * width : (k + 1) * width] = jnp.where(same & (node == k), 1.0, 0.0).astype(BF16)

    def prepare(self, n_x, n_y, *refs):
        geometry, viscosity, spread, table, right, slots, ids, square = refs[:8]
        s4, hot3, fields = refs[8:11]
        refs = refs[11:]
        x_out, y_out, work = refs[:n_x], refs[n_x : n_x + n_y], refs[n_x + n_y]
        p, c, block, rows, ey = self.p, self.c, self.block, self.rows, self.ey
        face = ey * p
        wjk, end_j, end_k = (table[n * face : (n + 1) * face, :] for n in range(3))
        stiff, second, third, rest = [], [], [], []
        for i in range(p):
            xx, yy, zz, xy, xz, yz = (geometry[q, i] for q in range(6))
            quadrature = float(self.weights[i]) * wjk
            weighted = quadrature * viscosity[i]
            mass = (helm_coefficient * quadrature) * (
                xx * (yy * zz - yz * yz) - xy * (xy * zz - yz * xz) + xz * (xy * yz - yy * xz)
            )
            cross = end_j * end_k * yz
            end = float(self.end[i])
            if end != 0.0:
                cross = cross + end * (end_j * xy + end_k * xz)
            entries = [weighted * entry for entry in (xx, yy, zz, xy, xz, yz)] + [mass]
            for q, entry in enumerate(entries):
                fields[q, i * face : (i + 1) * face, :] = entry
            stiff.append(entries[0])
            second.append(entries[1])
            third.append(entries[2])
            rest.append((2.0 * weighted) * cross + mass)
        upper, lower = split(jnp.concatenate(second, axis=0))
        diagonal = jnp.dot(
            square[...], jnp.concatenate([upper, lower, upper], axis=0), preferred_element_type=F32
        )
        upper, lower = split(jnp.concatenate(third, axis=0))
        diagonal = diagonal + lax.dot_general(
            jnp.concatenate([upper, lower, upper], axis=1),
            square[...],
            (((1,), (1,)), ((), ())),
            preferred_element_type=F32,
        )
        first = self.contract(stiff, self.squared.T)
        diagonal = diagonal + jnp.concatenate([x + y for x, y in zip(first, rest)], axis=0)
        width = diagonal.shape[-1]
        value = diagonal.reshape(p, ey, p, width)
        value = jnp.concatenate([value[:, f].reshape(block, width) for f in range(ey)], axis=1)

        def store(k, part):
            work[pl.ds(k, block, stride=p), :] = part

        self.by_nodes(*split(value), spread, self.w4, store)
        hot = self.one_hot(slots, ids)
        hot3[...] = self.one_hot(slots, ids[c:, :])
        total = work[...]
        for part in split(right[...].reshape(hot.shape[0], rows)):
            total = total + lax.dot_general(
                part, hot, (((0,), (0,)), ((), ())), preferred_element_type=F32
            )
        s4[...] = total
        self.fold_second(s4)
        last = self.n4 - self.step4
        self.fold_third(s4, self.step4, lambda l: l < last, lambda l: (l >= self.step4) & (l < self.n4))
        self.emit_first((s4[:block, :], s4[rows - block :, :]), x_out)
        self.emit_second(s4, y_out)

    def convert(self, n_y, n_z, *refs):
        fields, spread, dirichlet, s4 = refs[:4]
        g, ind = refs[4:6]
        refs = refs[6:]
        y_out, z_out, packed = refs[:n_y], refs[n_y : n_y + n_z], refs[n_y + n_z : n_y + 2 * n_z]
        upper, lower = refs[n_y + 2 * n_z :]
        p, c, block, ey = self.p, self.c, self.block, self.ey
        width = fields.shape[-1]
        for q in range(FIELDS):
            value = fields[q].reshape(p, ey, p, width)
            for f in range(ey):
                at = (slice(q * block, (q + 1) * block), slice(f * width, (f + 1) * width))
                upper[at], lower[at] = split(value[:, f].reshape(block, width))
        first_flag, flags = FIELDS * block, 2 * p
        for cc in range(c):
            for f in range(ey):
                at = slice(f * p, (f + 1) * p)
                face = jnp.concatenate([dirichlet[0, cc, at, :], dirichlet[1, cc, at, :]], axis=0)
                to = slice(first_flag + cc * flags, first_flag + (cc + 1) * flags)
                upper[to, f * width : (f + 1) * width] = face.astype(F32).astype(BF16)
                lower[to, f * width : (f + 1) * width] = jnp.zeros((flags, width), BF16)
        row = lax.broadcasted_iota(jnp.int32, (flags, self.w3), 0)
        lane = lax.broadcasted_iota(jnp.int32, (flags, self.w3), 1)
        ends = (lax.axis_index("gx") == 0, lax.axis_index("gx") == self.sizes["gx"] - 1)
        here = ((row < p) & ends[0]) | ((row >= p) & ends[1])
        owner = lax.rem(lane, self.step3) // ey

        def store(k, value):
            g[pl.ds(k, first_flag, stride=p), :] = value[:first_flag]
            total = jnp.zeros((flags, self.w3), F32)
            for cc in range(c):
                at = first_flag + cc * flags
                total = jnp.where(owner == cc, value[at : at + flags], total)
            ind[pl.ds(k, flags, stride=p), :] = jnp.where(here, total, 0.0)

        self.by_nodes(upper[...], lower[...], spread, self.w3, store)
        self.pack_fields(fields, z_out)
        self.fold_second(ind)
        first_own, end_own = HALO * self.step3, self.n3 - HALO * self.step3
        self.fold_third(
            ind,
            self.step3,
            lambda l: (l >= first_own) & (l < end_own - self.step3),
            lambda l: (l >= first_own + self.step3) & (l < end_own),
        )
        for out, (up, _, _) in zip(y_out, roles("gy", self.sizes["gy"])):
            for n in range(2):
                start = n * block
                out[n * p : (n + 1) * p, :] = jnp.where(
                    up, ind[start + block - p : start + block, :], ind[start : start + p, :]
                )
        for out, (up, _, _) in zip(packed, roles("gz", self.sizes["gz"])):
            self.pack(out, s4, block, 0, self.n4 - self.halo4, up, 0)
            self.pack(out, ind, p, first_own, end_own - first_own, up, block)

    def halo_fields(self, n_z, *refs):
        own, halo = refs[:2]
        z_in, g, terms = refs[2 : 2 + n_z], refs[2 + n_z], refs[3 + n_z]
        p, block, ey, part = self.p, self.block, self.ey, self.part
        sides = both_sides([z[...] for z in z_in], roles("gz", self.sizes["gz"]))
        width = sides[0].shape[-1]
        sides = [side.reshape(p, ey, p, width) for side in sides]
        lane = lax.broadcasted_iota(jnp.int32, (block, width), 1)
        for q in range(FIELDS):
            value = jnp.zeros((block, width), F32)
            for side in range(2):
                for f in range(ey):
                    to = (side * ey + f) * part
                    shift = (to - q * part) % width
                    x = sides[side][:, f].reshape(block, width)
                    x = pltpu.roll(x, shift, 1) if shift else x
                    value = jnp.where((lane >= to) & (lane < to + part), x, value)
            upper, lower = split(value)
            lower = pltpu.roll(lower.astype(F32), width // 2, 1).astype(BF16)
            terms[q * block : (q + 1) * block, :] = upper + lower

        for k in range(0, p, 2):
            columns = halo[:, k * self.w3 : (k + 2) * self.w3]
            both = jnp.dot(terms[...], columns, preferred_element_type=F32)
            for n in range(2):
                at = pl.ds(k + n, FIELDS * block, stride=p)
                g[at, :] = own[at, :] + both[:, n * self.w3 : (n + 1) * self.w3]

    def coefficients(self, low, high, coef):
        top, bottom = jnp.full((8, 128), high[0], F32), jnp.full((8, 128), low[0], F32)
        midpoint, halfwidth = (top + bottom) * 0.5, (top - bottom) * 0.5
        ratio = midpoint / halfwidth
        damping = 1.0 / ratio
        coef[0:8, :] = 1.0 / midpoint
        for n in range(ITERS - 1):
            following = 1.0 / (2.0 * ratio - damping)
            coef[8 * (2 * n + 1) : 8 * (2 * n + 2), :] = following * damping
            coef[8 * (2 * n + 2) : 8 * (2 * n + 3), :] = 2.0 * following / halfwidth
            damping = following

    def join(self, n_x, n_y, *refs):
        x_in, refs = refs[:n_x], refs[n_x:]
        y_raw, y_more, y_out = refs[:n_y], refs[n_y:-n_y], refs[-n_y:]
        p, block, ey = self.p, self.block, self.ey
        low, high = both_sides([x[...] for x in x_in], roles("gx", self.sizes["gx"]))
        for n, (up, _, _) in enumerate(roles("gy", self.sizes["gy"])):
            face = y_raw[n][...]
            width = face.shape[-1]
            if n_x:
                first, last = (jnp.where(up, x[block - p :], x[:p]) for x in (low, high))
                face = jnp.concatenate([face[:p] + first, face[p : block - p], face[block - p :] + last], axis=0)
            if y_more:
                face = jnp.concatenate([face, y_more[n][...]], axis=0)
            if ey == 1:
                y_out[n][...] = face
                continue
            half = face.shape[0] // 2
            first, second = face[:half], face[half:]
            f = lax.rem(lax.broadcasted_iota(jnp.int32, first.shape, 1), ey)
            below = jnp.where(f == 0, pltpu.roll(first, width - (ey - 1), 1), 0.0) + jnp.where(
                f == 1, pltpu.roll(second, (width - (ey - 2)) % width, 1) if ey != 2 else second, 0.0
            )
            above = jnp.where(f == ey - 1, pltpu.roll(first, ey - 1, 1), 0.0) + jnp.where(
                f == ey - 2, pltpu.roll(second, ey - 2, 1) if ey != 2 else second, 0.0
            )
            y_out[n][...] = jnp.where(up, below, above)

    def second_sides(self, received):
        role, ey = roles("gy", self.sizes["gy"]), self.ey
        faces = []
        for message, (_, from_high, _) in zip(received, role):
            data = message[...]
            if ey > 1:
                width = data.shape[-1]
                f = lax.rem(lax.broadcasted_iota(jnp.int32, data.shape, 1), ey)
                beside = jnp.where(from_high, pltpu.roll(data, 1, 1), pltpu.roll(data, width - 1, 1))
                here = f == jnp.where(from_high, ey - 1, 0)
                data = jnp.concatenate([jnp.where(here, x, 0.0) for x in (data, beside)], axis=0)
            faces.append(data)
        return both_sides(faces, role)

    def pack(self, out, u, count, first, last, up, start):
        p, width, size = self.p, self.w4, self.halo4
        lane = lax.broadcasted_iota(jnp.int32, (count, width), 1)
        for section in range(0, u.shape[0] // count, p):
            total = jnp.zeros((count, width), F32)
            for n in range(p):
                at, shift = (section + n) * count, n * size
                x = u[at : at + count, :]
                below = pltpu.roll(x, (shift - first) % width, 1) if (shift - first) % width else x
                above = pltpu.roll(x, (shift - last) % width, 1)
                here = (lane >= shift) & (lane < shift + size)
                total = jnp.where(here, jnp.where(up, above, below), total)
            row = start + section // p * count
            out[row : row + count, :] = total

    def pack_second(self, n_x, n_y, n_z, *refs):
        x_in, y_in, refs = refs[:n_x], refs[n_x : n_x + n_y], refs[n_x + n_y :]
        z_in, z_out = refs[:n_z], refs[n_z:]
        p, block, width, size = self.p, self.block, self.w4, self.halo4
        ends = both_sides([x[...] for x in x_in], roles("gx", self.sizes["gx"]))
        low, high = self.second_sides(y_in)
        halo3 = HALO * self.step3
        lane = lax.broadcasted_iota(jnp.int32, (p, width), 1)
        for packed, out, (up, _, _) in zip(z_in, z_out, roles("gz", self.sizes["gz"])):
            out[...] = packed[...]
            if n_x:
                total = 0.0
                for x, group in zip(ends, (0, p - 1)):
                    shift = group * size
                    below = pltpu.roll(x, shift, 1) if shift else x
                    back = (shift - self.n4 + size) % width
                    above = pltpu.roll(x, back, 1) if back else x
                    wide = lax.broadcasted_iota(jnp.int32, x.shape, 1)
                    here = (wide >= shift) & (wide < shift + size)
                    total = total + jnp.where(here, jnp.where(up, above, below), 0.0)
                out[:block, :] += total
            if not n_y:
                continue
            for face, row in ((low, 0), (high, block - p)):
                total = jnp.zeros((p, width), F32)
                for n in range(p):
                    shift = n * size
                    x = face[n * p : (n + 1) * p]
                    below = pltpu.roll(x, shift, 1) if shift else x
                    above = pltpu.roll(x, (shift - self.n4 + size) % width, 1)
                    here = (lane >= shift) & (lane < shift + size)
                    total = jnp.where(here, jnp.where(up, above, below), total)
                out[row : row + p, :] += total
            for n in range(2):
                row = block + n * p
                for face, group in ((low, 0), (high, p - 1)):
                    shift = group * size
                    x = face[row : row + p]
                    below = pltpu.roll(x, (shift - halo3) % width, 1)
                    above = pltpu.roll(x, (shift - self.n3 + 2 * halo3) % width, 1)
                    here = (lane >= shift) & (lane < shift + size)
                    out[row : row + p, :] += jnp.where(here, jnp.where(up, above, below), 0.0)

    def own(self, n_x, n_y, *refs):
        s4, ind, widen = refs[:3]
        x_in, y_in, (r, scale, flag, work) = refs[3 : 3 + n_x], refs[3 + n_x : 3 + n_x + n_y], refs[3 + n_x + n_y :]
        p, block, rows, w3 = self.p, self.block, self.rows, self.w3
        work[...] = s4[...]
        if n_x:
            low, high = both_sides([x[...] for x in x_in], roles("gx", self.sizes["gx"]))
            work[:block, :] += low
            work[rows - block :, :] += high
        flag[...] = ind[...]
        if n_y:
            low, high = self.second_sides(y_in)
            for u, first, count in ((work, 0, p), (flag, p, 2)):
                for i in range(count):
                    at, end, row = i * block, (i + 1) * block, (first + i) * p
                    u[at : at + p, :] += low[row : row + p]
                    u[end - p : end, :] += high[row : row + p]
        both = dot2(work[...], widen[: self.w4, :])
        r[...] = both[:, :w3]
        scale[...] = both[:, w3:]

    def start(self, n_x, n_z, *refs):
        r_own, diagonal_own, flag_own, g, widen, ahead, back = refs[:7]
        z_in = refs[7 : 7 + n_z]
        t, scale, ends, f1, f2, f3 = refs[7 + n_z : 13 + n_z]
        x_out, refs = refs[13 + n_z : 13 + n_z + n_x], refs[13 + n_z + n_x :]
        beside, r, flag, slope, third = refs
        p, block, rows, w3, w4 = self.p, self.block, self.rows, self.w3, self.w4
        step, first_own, end_own = self.step3, HALO * self.step3, self.n3 - HALO * self.step3
        size, part = self.sizes["gz"], self.halo4
        if n_z:
            low, high = both_sides([z[...] for z in z_in], roles("gz", size))
        else:
            low = high = jnp.zeros((block + 2 * p, w4), F32)
        lane = lax.broadcasted_iota(jnp.int32, (block, w4), 1)
        for n in range(p):
            first = pltpu.roll(low[:block], w4 - n * part, 1) if n else low[:block]
            second = pltpu.roll(high[:block], (part - n * part) % w4, 1) if n != 1 else high[:block]
            beside[n * block : (n + 1) * block, :] = jnp.where(
                lane < part, first, jnp.where(lane < 2 * part, second, 0.0)
            )
        both = dot2(beside[...], widen[w4:, :])
        r[...] = r_own[...] + both[:, :w3]
        scale[...] = diagonal_own[...] + both[:, w3:]
        lane = lax.broadcasted_iota(jnp.int32, (p, w3), 1)
        for n in range(2 * p):
            row, shift = block + n // p * p, n % p * part
            first = pltpu.roll(low[row : row + p], w3 - shift, 1) if shift else low[row : row + p]
            second = pltpu.roll(high[row : row + p], (end_own - shift) % w3, 1)
            flag[n * p : (n + 1) * p, :] = jnp.where(
                lane < first_own,
                first,
                jnp.where(lane < end_own, flag_own[n * p : (n + 1) * p, :], jnp.where(lane < self.n3, second, 0.0)),
            )
        for u in (r, scale, flag):
            self.fold_third(
                u,
                step,
                lambda l: ((l >= first_own - step) & (l < first_own)) | ((l >= end_own - step) & (l < end_own)),
                lambda l: ((l >= first_own) & (l < first_own + step)) | ((l >= end_own) & (l < end_own + step)),
            )
        index = lax.axis_index("gz")
        begin = jnp.where(index > 0, 0, first_own)
        end = jnp.where(index < size - 1, self.n3, end_own)
        lane = lax.broadcasted_iota(jnp.int32, (block, w3), 1)
        valid = (lane >= begin) & (lane < end)
        for i in range(p):
            at = slice(i * block, (i + 1) * block)
            factor = jnp.where(valid, 1.0 / jnp.where(valid, scale[at, :], 1.0), 0.0)
            if i in (0, p - 1):
                row = 0 if i == 0 else block
                factor = jnp.where(flag[row : row + block, :] > 0.5, 0.0, factor)
            scale[at, :] = factor
            t[at, :] = factor * r[at, :]
        self.operator_first(t, g, ends, f1, f2, f3, slope, third, ahead, back)
        self.iteration_fold(ends)
        self.emit_first((ends[:block, :], ends[block:, :]), x_out)

    def factors(self, coef, n):
        rows = [coef[8 * m : 8 * m + 1, :] for m in (0, 2 * n + 1, 2 * n + 2)]
        return (rows[0] if n == 0 else None), rows[1], rows[2]

    def shares(self, faces, scale, image, at):
        low, high = faces
        p, block = self.p, self.block
        i = at // block
        out = []
        for start, face in ((at, low), (at + block - p, high)):
            value = scale[start : start + p, :] * face[i * p : (i + 1) * p]
            out.append((start, -value if image is None else -image * value))
        return out

    def preview(self, n_x, n_y, n, last, *refs):
        t, t_old, d, scale, v, coef, hot = refs[:7]
        refs = refs[7:]
        x_in, y_old, refs = refs[:n_x], refs[n_x : -2 if not last else -3], refs[-2 if not last else -3 :]
        p, block, rows = self.p, self.block, self.rows
        image, keep, gain = self.factors(coef, n)
        start = coef[0:1, :]
        if last:
            out, t_new, field = refs
        else:
            t_new, d_new = refs
        low, high = both_sides([x[...] for x in x_in], roles("gx", self.sizes["gx"]))
        if n:
            faces = self.second_sides(y_old) if n_y else None
            image_old = self.factors(coef, n - 1)[0]
        for i in range(p):
            at = slice(i * block, (i + 1) * block)
            value = v[at, :]
            if n_x and i in (0, p - 1):
                value = value + (low if i == 0 else high)
            value = scale[at, :] * value
            t_new[at, :] = t_old[at, :] - (value if image is None else image * value)
            if n and n_y:
                for row, share in self.shares(faces, scale, image_old, i * block):
                    t_new[row : row + p, :] += share
            direction = d[at, :] if n else start * t[at, :]
            following = keep * direction + gain * t_new[at, :]
            if last:
                field[at, :] = start * t[at, :] + following + (direction if n else 0.0)
            else:
                d_new[at, :] = following
        if last:
            out[...] = self.by_slots(hot, field[...])

    def by_slots(self, hot, field):
        return lax.dot_general(
            jnp.concatenate([hot[...], hot[...]], axis=1),
            jnp.concatenate(split(field), axis=1),
            (((1,), (1,)), ((), ())),
            preferred_element_type=F32,
        )

    def middle(self, n_x, n_y, n, *refs):
        d, scale, g, coef, ahead, back = refs[:6]
        y_in, refs = refs[6 : 6 + n_y], refs[6 + n_y :]
        d_new, ends, f1, f2, f3 = refs[:5]
        x_out, (slope, third) = refs[5 : 5 + n_x], refs[5 + n_x :]
        d_new[...] = d[...]
        image, _, gain = self.factors(coef, n)
        if n_y:
            faces = self.second_sides(y_in)
            for i in range(self.p):
                for row, share in self.shares(faces, scale, image, i * self.block):
                    d_new[row : row + self.p, :] += gain * share
        self.operator_first(d_new, g, ends, f1, f2, f3, slope, third, ahead, back)
        self.iteration_fold(ends)
        self.emit_first((ends[: self.block, :], ends[self.block :, :]), x_out)

    def finish(self, n_y, n, *refs):
        part, scale, coef, hot = refs[:4]
        y_in, (out, field) = refs[4 : 4 + n_y], refs[4 + n_y :]
        value = part[...]
        image, _, gain = self.factors(coef, n)
        if n_y:
            faces = self.second_sides(y_in)
            field[...] = jnp.zeros(field.shape, F32)
            for i in range(self.p):
                for row, share in self.shares(faces, scale, image, i * self.block):
                    field[row : row + self.p, :] = gain * share
            value = value + self.by_slots(hot, field[...])
        out[...] = value.reshape(out.shape)


def shards(sizes, right_side, geometry, viscosity, eig_low, eig_high, element_slot, dirichlet):
    plan = Plan(right_side.shape[0], viscosity.shape, sizes)
    p, block, rows, w3, w4 = plan.p, plan.block, plan.rows, plan.w3, plan.w4
    x_pairs = pairings(("gx",), (sizes["gx"],), 0)
    y_pairs = pairings(("gy",), (sizes["gy"],), 0)
    z_pairs = pairings(("gx", "gz"), (sizes["gx"], sizes["gz"]), 1)
    n_x, n_y, n_z = len(x_pairs), len(y_pairs), len(z_pairs)

    def send(arrays, axis, pairs):
        return [lax.ppermute(x, axis, pair) for x, pair in zip(arrays, pairs)]

    def shape(*size, dtype=F32):
        return jax.ShapeDtypeStruct(size, dtype)

    def call(kernel, outputs, operands, scratch=(), spaces={}, flops=0, name=None):
        specs = [pl.BlockSpec(memory_space=spaces.get(n, pltpu.VMEM)) for n in range(len(operands))]
        return list(
            pl.pallas_call(
                kernel,
                out_shape=list(outputs),
                in_specs=specs,
                out_specs=[pl.BlockSpec(memory_space=pltpu.VMEM)] * len(outputs),
                scratch_shapes=list(scratch),
                compiler_params=pltpu.CompilerParams(vmem_limit_bytes=VMEM_BYTES),
                cost_estimate=pl.CostEstimate(flops=flops, bytes_accessed=0, transcendentals=0),
                name=name,
            )(*operands)
        )

    def vmem(*size, dtype=F32):
        return pltpu.VMEM(size, dtype)

    lanes = plan.ez * p
    ahead, back = jnp.asarray(plan.third[0]), jnp.asarray(plan.third[1])
    field3, field4 = shape(rows, w3), shape(rows, w4)
    elements = element_slot.shape[-1]
    spread3, spread4 = call(
        plan.spread_tables,
        [shape(plan.ey * lanes, p * w, dtype=BF16) for w in (w3, w4)],
        (),
        flops=FLOPS,
        name="spread_tables",
    )
    results = call(
        functools.partial(plan.prepare, n_x, n_y),
        [field4, shape(plan.c * elements, w3, dtype=BF16), shape(FIELDS, p * plan.ey * p, lanes)]
        + [shape(block, w4)] * (n_x + n_y),
        (
            geometry,
            viscosity,
            spread4,
            jnp.asarray(plan.face_table),
            jnp.swapaxes(right_side, 1, 2),
            element_slot,
            jnp.asarray(plan.ids),
            jnp.asarray(plan.third[2]),
        ),
        scratch=[vmem(rows, w4)],
        name="prepare",
    )
    s4, hot3, fields = results[:3]
    x_out, y_raw = results[3 : 3 + n_x], results[3 + n_x :]
    x_in = send(x_out, "gx", x_pairs)

    lhs = FIELDS * block + 2 * plan.c * p
    results = call(
        functools.partial(plan.convert, n_y, n_z),
        [shape(FIELDS * rows, w3), shape(2 * block, w3)]
        + [shape(2 * p, w3)] * n_y
        + [shape(p * plan.ey * p, lanes)] * n_z
        + [shape(block + 2 * p, w4)] * n_z,
        (fields, spread3, dirichlet, s4),
        scratch=[vmem(lhs, plan.ey * lanes, dtype=BF16)] * 2,
        name="convert",
    )
    g, ind = results[:2]
    y_more, results = results[2 : 2 + n_y], results[2 + n_y :]
    z_fields, z_out = results[:n_z], results[n_z:]

    def joined(x_in, y_raw, y_more=()):
        if not y_raw:
            return []
        count = y_raw[0].shape[0] + (y_more[0].shape[0] if y_more else 0)
        faces = [shape(count // 2 if plan.ey > 1 else count, y.shape[1]) for y in y_raw]
        return call(functools.partial(plan.join, n_x, n_y), faces, x_in + y_raw + list(y_more), name="join")

    y_in = send(joined(x_in, y_raw, y_more), "gy", y_pairs)
    z_fields = send(z_fields, ("gx", "gz"), z_pairs)
    if n_z:
        g = call(
            functools.partial(plan.halo_fields, n_z),
            [shape(FIELDS * rows, w3)],
            [g, jnp.asarray(plan.halo)] + z_fields,
            scratch=[vmem(FIELDS * block, lanes, dtype=BF16)],
            name="halo_fields",
        )[0]
    if n_z:
        z_out = call(
            functools.partial(plan.pack_second, n_x, n_y, n_z),
            [shape(*z.shape) for z in z_out],
            x_in + y_in + z_out,
            flops=FLOPS,
            name="pack_second",
        )
    z_in = send(z_out, ("gx", "gz"), z_pairs)
    widen = jnp.asarray(plan.widen)
    own = call(
        functools.partial(plan.own, n_x, n_y),
        [field3, field3, shape(2 * block, w3)],
        [s4, ind, widen] + x_in + y_in,
        scratch=[vmem(rows, w4)],
        name="own",
    )

    fluxes = [shape(2 * block, w3)] + [field3] * 3 + [shape(block, w3)] * n_x
    results = call(
        functools.partial(plan.start, n_x, n_z),
        [field3] * 2 + fluxes,
        own + [g, widen, ahead, back] + z_in,
        scratch=[vmem(rows, w4), vmem(rows, w3), vmem(2 * block, w3)] + [vmem(rows, w3)] * 2,
        name="first_direction",
    )
    t, scale = results[:2]
    ends, f1, f2, f3 = results[2:6]
    x_out = results[6:]
    x_out, low, high = lax.optimization_barrier((x_out, eig_low, eig_high))
    coef = call(
        plan.coefficients,
        [shape(8 * (2 * ITERS - 1), 128)],
        (low, high),
        spaces={0: pltpu.SMEM, 1: pltpu.SMEM},
        name="coefficients",
    )[0]
    t_old, d, y_in = t, t, []
    for n in range(ITERS - 1):
        last = n == ITERS - 2
        x_in = send(x_out, "gx", x_pairs)
        results = call(
            functools.partial(plan.operator_second, n_x, n_y),
            [field3] + [shape(block, w3)] * n_y,
            [d, g, ends, f1, f2, f3, back],
            scratch=[vmem(rows, w3)],
            name="operator_second",
        )
        v, y_raw = results[0], results[1:]
        y_old, y_in = y_in, send(joined(x_in, y_raw), "gy", y_pairs)
        results = call(
            functools.partial(plan.preview, n_x, n_y, n, last),
            [shape(plan.c * elements, rows)] if last else [field3, field3],
            [t, t_old, d, scale, v, coef, hot3] + x_in + y_old,
            scratch=[vmem(rows, w3)] * 2 if last else [],
            name="preview",
        )
        if last:
            break
        t_old, d = results
        results = call(
            functools.partial(plan.middle, n_x, n_y, n),
            [field3] + fluxes,
            [d, scale, g, coef, ahead, back] + y_in,
            scratch=[vmem(rows, w3)] * 2,
            name="direction",
        )
        d, ends, f1, f2, f3 = results[:5]
        x_out = results[5:]
    out = call(
        functools.partial(plan.finish, n_y, n),
        [shape(plan.c, elements, rows)],
        [results[0], scale, coef, hot3] + y_in,
        scratch=[vmem(rows, w3)],
        name="field",
    )[0]
    return jnp.swapaxes(out, 1, 2)


def solution(mesh):
    sizes = {name: mesh.shape[name] for name in ("gx", "gy", "gz")}
    return jax.shard_map(
        functools.partial(shards, sizes),
        mesh=mesh,
        in_specs=(
            P(None, None, ("gx", "gy", "gz")),
            P(None, "gx", "gy", "gz"),
            P("gx", "gy", "gz"),
            P(),
            P(),
            P(("gx", "gy", "gz"), None),
            P(None, None, "gy", "gz"),
        ),
        out_specs=P(None, None, ("gx", "gy", "gz")),
        check_vma=False,
    )
```

```python
import functools
import math

import jax
import jax.numpy as jnp
import numpy as np
from jax import lax
from jax.experimental import pallas as pl
from jax.experimental.pallas import tpu as pltpu
from jax.sharding import PartitionSpec as P

DEGREE = 7
ITERS = 3


helm_coefficient = 10.0


def legendre_pair(values, degree):
    previous = 0.0 * values + 1.0
    current = values.copy()
    for order in range(2, degree + 1):
        previous, current = (
            current,
            ((2 * order - 1) * values * current - (order - 1) * previous) / order,
        )
    return (current, previous)


def gll_tables(degree):
    start = np.cos(np.pi * np.arange(degree + 1) / degree)
    nodes_now = start.copy()
    for sweep in range(80):
        top_value, lower_value = legendre_pair(nodes_now, degree)
        nodes_now = nodes_now - (nodes_now * top_value - lower_value) / ((degree + 1) * top_value)
    gll_nodes = nodes_now[::-1].copy()
    gll_nodes[0] = -1.0
    gll_nodes[degree] = 1.0
    legendre_values = legendre_pair(gll_nodes, degree)[0]
    weights = 2.0 / (degree * (degree + 1) * legendre_values**2)
    differences = gll_nodes[:, None] - gll_nodes[None, :] + np.eye(degree + 1)
    derivative = legendre_values[:, None] / legendre_values[None, :] / differences
    derivative = derivative * (1.0 - np.eye(degree + 1))
    derivative[0, 0] = -degree * (degree + 1) / 4.0
    derivative[degree, degree] = degree * (degree + 1) / 4.0
    return (weights, derivative)


HALO = 2
FIELDS = 7
VMEM_BYTES = 40 * 1024 * 1024
FLOPS = 3 * 10**9
F32 = jnp.float32
BF16 = jnp.bfloat16


def pairings(names, sizes, dim):
    size = sizes[dim]
    if size == 1:
        return []
    if size % 2:
        shifts = (1, size - 1)
        partners = [[(i + shift) % size for i in range(size)] for shift in shifts]
    else:
        partners = [[i ^ 1 for i in range(size)]]
        if size > 2:
            partners.append([((i + 1) ^ 1) - 1 for i in range(size)])
    result = []
    for partner in partners:
        pairs = []
        for flat in range(math.prod(sizes)):
            place = list(np.unravel_index(flat, sizes))
            to = partner[place[dim]]
            if 0 <= to < size:
                place[dim] = to
            elif len(sizes) > 1 and sizes[1 - dim] % 2 == 0:
                place[1 - dim] ^= 1
            else:
                place[dim] = size - 1 - place[dim]
            pairs.append((flat, int(np.ravel_multi_index(place, sizes))))
        result.append(pairs)
    return result


def roles(name, size):
    if size == 1:
        return []
    index = lax.axis_index(name)
    low, high = index > 0, index < size - 1
    if size % 2:
        yes = index >= 0
        no = index < 0
        return [(yes, no, low), (no, yes, high)]
    even = lax.rem(index, 2) == 0
    odd = jnp.logical_not(even)
    result = [(even, even, index >= 0)]
    if size > 2:
        result.append((odd, odd, jnp.logical_or(jnp.logical_and(odd, high), jnp.logical_and(even, low))))
    return result


def both_sides(received, role):
    low, high = 0.0, 0.0
    for data, (_, from_high, used) in zip(received, role):
        high = high + jnp.where(jnp.logical_and(used, from_high), data, 0.0)
        low = low + jnp.where(jnp.logical_and(used, jnp.logical_not(from_high)), data, 0.0)
    return low, high


def split(x):
    upper = x.astype(BF16)
    return upper, (x - upper.astype(F32)).astype(BF16)


def dot2(x, table):
    return jnp.dot(
        jnp.concatenate(split(x), axis=1),
        jnp.concatenate([table, table], axis=0),
        preferred_element_type=F32,
    )


class Plan:
    def __init__(self, components, viscosity_shape, mesh_sizes):
        points = DEGREE + 1
        self.p, self.c = points, components
        self.sizes = mesh_sizes
        ex, ey, ez = (n // points for n in viscosity_shape)
        assert ex == 1 and ez >= HALO
        self.ey, self.ez = ey, ez
        self.rows = points**3
        self.block = points * points
        self.step3, self.step4 = components * ey, (components + 1) * ey
        self.n3, self.n4 = (ez + 2 * HALO) * self.step3, ez * self.step4
        self.w3, self.w4 = -(-self.n3 // 128) * 128, -(-self.n4 // 128) * 128
        self.halo4 = HALO * self.step4
        assert points * self.halo4 <= self.w4 and 2 * self.halo4 <= self.w4
        weights, derivative = gll_tables(DEGREE)
        self.forward = derivative.astype(np.float32)
        self.squared = self.forward * self.forward
        self.weights = weights.astype(np.float32)
        self.end = np.diagonal(self.forward)
        self.tables()

    def lane3(self, g, c, f):
        return (g + HALO) * self.step3 + c * self.ey + f

    def lane4(self, g, c, f):
        return g * self.step4 + c * self.ey + f

    def tables(self):
        p, c, ey, ez = self.p, self.c, self.ey, self.ez
        lanes = ez * p
        every = [(g, cc, f) for g in range(ez) for cc in range(c) for f in range(ey)]
        widen = np.zeros((2 * self.w4, 2 * self.w3), np.float32)
        ids = np.full((2 * c, 128, 128), -1, np.int32)
        for g, cc, f in every:
            widen[self.lane4(g, cc, f), self.lane3(g, cc, f)] = 1
            widen[self.lane4(g, c, f), self.w3 + self.lane3(g, cc, f)] = 1
            ids[cc, :, self.lane4(g, cc, f)] = f * ez + g
            ids[c + cc, :, self.lane3(g, cc, f)] = f * ez + g
        self.ids = np.ascontiguousarray(ids[:, :1, :]).reshape(2 * c, 128)
        part = HALO * p
        self.part = part
        assert FIELDS * part <= lanes and 2 * ey * part <= lanes // 2
        halo = np.zeros((lanes, p, self.w3), np.float32)
        for side, first in ((0, -HALO), (1, ez)):
            for g in range(HALO):
                for cc in range(c):
                    for f in range(ey):
                        at = self.lane3(first + g, cc, f)
                        row = self.w4 + side * self.halo4 + g * self.step4
                        widen[row + cc * ey + f, at] = 1
                        widen[row + c * ey + f, self.w3 + at] = 1
                        for k in range(p):
                            for half in range(2):
                                halo[half * lanes // 2 + (side * ey + f) * part + g * p + k, k, at] = 1
        self.halo = halo.reshape(lanes, -1).astype(jnp.bfloat16)
        self.widen = widen.astype(jnp.bfloat16)
        self.third = [self.block_terms(matrix) for matrix in (self.forward, self.forward.T, self.squared.T)]
        face = (ey * p, lanes)
        second = np.tile(np.arange(p), ey)[:, None]
        third = np.tile(np.arange(p), ez)[None, :]
        self.face_table = np.concatenate(
            [
                self.weights[second] * self.weights[third],
                np.broadcast_to(self.end[second], face),
                np.broadcast_to(self.end[third], face),
            ]
        ).astype(np.float32)

    def block_terms(self, matrix):
        size = self.rows // 4
        blocks = np.kron(np.eye(size // self.p), matrix).astype(np.float32)
        upper = blocks.astype(jnp.bfloat16)
        lower = (blocks - upper.astype(np.float32)).astype(jnp.bfloat16)
        return np.concatenate([upper, upper, lower], axis=1)


    def contract(self, x, matrix, wanted=None):
        p = self.p
        sign = 1.0 if matrix[0, 0] * matrix[p - 1, p - 1] > 0 else -1.0
        half = p // 2
        sums = [x[i] + x[p - 1 - i] for i in range(half)]
        differences = [x[i] - x[p - 1 - i] for i in range(half)]
        out = [None] * p
        for a in range(half) if wanted is None else wanted:
            even, odd = None, None
            for i in range(half):
                first, second = float(matrix[a, i]), float(matrix[a, p - 1 - i])
                even = self.gather(even, 0.5 * (first + second), sums[i])
                odd = self.gather(odd, 0.5 * (first - second), differences[i])
            out[a] = odd + even
            out[p - 1 - a] = even - odd if sign > 0 else odd - even
        return [x for x in out if x is not None]

    @staticmethod
    def gather(total, factor, x):
        if factor == 0.0:
            return total
        return factor * x if total is None else total + factor * x

    def along_j(self, x, matrix):
        x = x.reshape(self.p, self.p, x.shape[-1])
        return jnp.concatenate(self.contract([x[j] for j in range(self.p)], matrix), axis=0)

    def along_i(self, source, matrix, write):
        p, block = self.p, self.block
        for j in range(p):
            rows = [i * block + j * p for i in range(p)]
            for row, value in zip(rows, self.contract([source[r : r + p, :] for r in rows], matrix)):
                write(row, value)

    def along_k(self, source, table, out, start, end):
        size = table.shape[0]
        width = source.shape[-1]
        while start < end:
            count = min(2, (end - start) // size)
            pieces = [split(source[start + n * size : start + (n + 1) * size, :]) for n in range(count)]
            upper, lower = (jnp.concatenate([piece[n] for piece in pieces], axis=1) for n in range(2))
            both = jnp.dot(
                table[...], jnp.concatenate([upper, lower, upper], axis=0), preferred_element_type=F32
            )
            for n in range(count):
                out[start + n * size : start + (n + 1) * size, :] = both[:, n * width : (n + 1) * width]
            start += count * size

    def rows_of(self, g, q, at):
        return g[q * self.rows + at.start : q * self.rows + at.stop, :]

    def fluxes(self, v, g, f1, f2, f3, slope, third, ahead):
        p, block, rows = self.p, self.block, self.rows

        def store(row, value):
            slope[row : row + p, :] = value

        self.along_i(v, self.forward, store)
        self.along_k(v, ahead, third, 0, rows)
        for i in range(p):
            at = slice(i * block, (i + 1) * block)
            x, s1, s3 = v[at, :], slope[at, :], third[at, :]
            s2 = self.along_j(x, self.forward)
            xy, xz, yz = (self.rows_of(g, q, at) for q in (3, 4, 5))
            f1[at, :] = self.rows_of(g, 0, at) * s1 + xy * s2 + xz * s3
            f2[at, :] = xy * s1 + self.rows_of(g, 1, at) * s2 + yz * s3
            f3[at, :] = xz * s1 + yz * s2 + self.rows_of(g, 2, at) * s3

    def share_fluxes(self, shares, g, third, ahead, whole, write):
        p, block = self.p, self.block
        x = shares[...]
        ends = [[x[(2 * i + n) * p : (2 * i + n + 1) * p] for i in range(p)] for n in range(2)]
        s1 = [self.contract(column, self.forward) for column in ends]
        self.along_k(shares, ahead, third, 0, 2 * block)
        for i in range(p):
            first, last = ends[0][i], ends[1][i]
            count = 3 if whole or i in (0, p - 1) else 1
            for j in range(p):
                at = slice(i * block + j * p, i * block + (j + 1) * p)
                s2 = float(self.forward[j, 0]) * first + float(self.forward[j, p - 1]) * last
                rows = ((0, 3, 4), (3, 1, 5), (4, 5, 2))[:count]
                values = [self.rows_of(g, row[1], at) * s2 for row in rows]
                if j in (0, p - 1):
                    n = int(j > 0)
                    line = (2 * i + n) * p
                    e1, e3 = s1[n][i], third[line : line + p, :]
                    values = [
                        value + self.rows_of(g, row[0], at) * e1 + self.rows_of(g, row[2], at) * e3
                        for value, row in zip(values, rows)
                    ]
                write(i, j, values)

    def end_planes(self, v, g, ends, f1, f2, f3, slope, third, back):
        p, block, rows = self.p, self.block, self.rows
        for n, start in enumerate((0, rows - block)):
            at = slice(start, start + block)
            ends[n * block : (n + 1) * block, :] = (
                self.along_j(f2[at, :], self.forward.T) + self.rows_of(g, 6, at) * v[at, :]
            )
            slope[n * block : (n + 1) * block, :] = f3[at, :]
        self.along_k(slope, back, third, 0, 2 * block)
        for j in range(p):
            x = [f1[i * block + j * p : i * block + (j + 1) * p, :] for i in range(p)]
            first, last = self.contract(x, self.forward.T, (0,))
            for row, value in ((j * p, first), (block + j * p, last)):
                ends[row : row + p, :] += value + third[row : row + p, :]

    def operator_second(self, n_x, n_y, shared, *refs):
        v, g, ends, f1, f2, f3, back = refs[:7]
        refs = refs[7:]
        p, block, rows = self.p, self.block, self.rows
        if shared:
            shares, ahead, out = refs[:3]
            y_out, (v_new, third, *new) = refs[3 : 3 + n_y], refs[3 + n_y :]

            def write(i, j, values):
                at = slice(i * block + j * p, i * block + (j + 1) * p)
                for f_old, f_new, value in zip((f1, f2, f3), new, values):
                    f_new[at, :] = f_old[at, :] + value

            self.share_fluxes(shares, g, third, ahead, True, write)
            v_new[...] = v[...]
            for i in range(p):
                for m, row in enumerate((i * block, (i + 1) * block - p)):
                    v_new[row : row + p, :] += shares[(2 * i + m) * p : (2 * i + m + 1) * p, :]
            v, (f1, f2, f3) = v_new, new
        else:
            out, y_out, third = refs[0], refs[1 : 1 + n_y], refs[1 + n_y]
        out[:block, :], out[rows - block :, :] = ends[:block, :], ends[block:, :]
        self.along_k(f3, back, third, block, rows - block)
        for i in range(1, p - 1):
            at = slice(i * block, (i + 1) * block)
            out[at, :] = (
                self.along_j(f2[at, :], self.forward.T) + self.rows_of(g, 6, at) * v[at, :] + third[at, :]
            )
        for j in range(p):
            at = [slice(i * block + j * p, i * block + (j + 1) * p) for i in range(p)]
            values = self.contract([f1[r, :] for r in at], self.forward.T, range(1, p // 2))
            for r, value in zip(at[1 : p - 1], values):
                out[r, :] += value
        self.iteration_fold(out.at[block : rows - block, :])
        self.emit_second(out, y_out)

    def fold_second(self, u):
        if self.ey == 1:
            return
        p, width = self.p, u.shape[-1]
        lane = lax.broadcasted_iota(jnp.int32, (p, width), 1)
        f = lax.rem(lane, self.ey)
        for start in range(0, u.shape[0], self.block):
            first, last = u[start : start + p, :], u[start + self.block - p : start + self.block, :]
            u[start + self.block - p : start + self.block, :] = last + jnp.where(
                f < self.ey - 1, pltpu.roll(first, width - 1, 1), 0.0
            )
            u[start : start + p, :] = first + jnp.where(f > 0, pltpu.roll(last, 1, 1), 0.0)

    def fold_third(self, u, step, take_upper, take_lower):
        p, (rows, width) = self.p, u.shape
        count = rows // p
        lane = lax.broadcasted_iota(jnp.int32, (count, width), 1)
        first, last = u[pl.ds(0, count, stride=p), :], u[pl.ds(p - 1, count, stride=p), :]
        u[pl.ds(p - 1, count, stride=p), :] = last + jnp.where(
            take_upper(lane), pltpu.roll(first, width - step, 1), 0.0
        )
        u[pl.ds(0, count, stride=p), :] = first + jnp.where(
            take_lower(lane), pltpu.roll(last, step, 1), 0.0
        )

    def emit_first(self, ends, x_out):
        for out, (high, _, _) in zip(x_out, roles("gx", self.sizes["gx"])):
            out[...] = jnp.where(high, ends[1], ends[0])

    def emit_second(self, u, y_out):
        p, block = self.p, self.block
        for out, (high, _, _) in zip(y_out, roles("gy", self.sizes["gy"])):
            for i in range(p):
                start = i * block
                out[i * p : (i + 1) * p, :] = jnp.where(
                    high, u[start + block - p : start + block, :], u[start : start + p, :]
                )

    def iteration_fold(self, u):
        self.fold_second(u)
        last = self.n3 - self.step3
        self.fold_third(u, self.step3, lambda l: l < last, lambda l: (l >= self.step3) & (l < self.n3))


    def pack_fields(self, fields, out):
        for target, (high, _, _) in zip(out, roles("gz", self.sizes["gz"])):
            rows, width = target.shape
            lane = lax.broadcasted_iota(jnp.int32, (rows, width), 1)
            total = jnp.zeros((rows, width), F32)
            for q in range(FIELDS):
                start = q * self.part
                upper = pltpu.roll(fields[q], start + self.part, 1)
                lower = pltpu.roll(fields[q], start, 1) if start else fields[q]
                here = (lane >= start) & (lane < start + self.part)
                total = jnp.where(here, jnp.where(high, upper, lower), total)
            target[...] = total

    def by_nodes(self, upper, lower, table, width, store):
        for k in range(0, self.p, 2):
            columns = table[:, k * width : (k + 2) * width]
            both = jnp.dot(upper, columns, preferred_element_type=F32) + jnp.dot(
                lower, columns, preferred_element_type=F32
            )
            store(k, both[:, :width])
            store(k + 1, both[:, width:])

    def one_hot(self, slots, ids):
        count = slots.shape[-1]
        column = jnp.broadcast_to(slots[...], (count, count))
        column = jnp.concatenate([column, jnp.zeros((count, 128 - count), jnp.int32)], axis=1)
        column = jnp.concatenate([column, jnp.zeros((128 - count, 128), jnp.int32)], axis=0)
        column = column.astype(F32).T[:count, :1]
        return jnp.concatenate(
            [jnp.where(column == ids[n : n + 1, :].astype(F32), 1.0, 0.0) for n in range(self.c)], axis=0
        ).astype(BF16)

    def spread_tables(self, out3, out4):
        p, ey, ez = self.p, self.ey, self.ez
        for out, width, step, offset, first in (
            (out3, self.w3, self.step3, HALO, 0),
            (out4, self.w4, self.step4, 0, self.c * ey),
        ):
            row = lax.broadcasted_iota(jnp.int32, (ey * ez * p, width), 0)
            lane = lax.broadcasted_iota(jnp.int32, (1, width), 1)
            g = lane // step - offset
            inside = (g >= 0) & (g < ez) & (lax.rem(lane, step) >= first)
            same = row // p == jnp.where(inside, lax.rem(lane, ey) * ez + g, -1)
            node = lax.rem(row, p)
            for k in range(p):
                out[:, k * width : (k + 1) * width] = jnp.where(same & (node == k), 1.0, 0.0).astype(BF16)

    def prepare(self, n_x, n_y, *refs):
        geometry, viscosity, spread, table, right, slots, ids, square = refs[:8]
        s4, hot3, fields = refs[8:11]
        refs = refs[11:]
        x_out, y_out, work = refs[:n_x], refs[n_x : n_x + n_y], refs[n_x + n_y]
        p, c, block, rows, ey = self.p, self.c, self.block, self.rows, self.ey
        face = ey * p
        wjk, end_j, end_k = (table[n * face : (n + 1) * face, :] for n in range(3))
        stiff, second, third, rest = [], [], [], []
        for i in range(p):
            xx, yy, zz, xy, xz, yz = (geometry[q, i] for q in range(6))
            quadrature = float(self.weights[i]) * wjk
            weighted = quadrature * viscosity[i]
            mass = (helm_coefficient * quadrature) * (
                xx * (yy * zz - yz * yz) - xy * (xy * zz - yz * xz) + xz * (xy * yz - yy * xz)
            )
            cross = end_j * end_k * yz
            end = float(self.end[i])
            if end != 0.0:
                cross = cross + end * (end_j * xy + end_k * xz)
            entries = [weighted * entry for entry in (xx, yy, zz, xy, xz, yz)] + [mass]
            for q, entry in enumerate(entries):
                fields[q, i * face : (i + 1) * face, :] = entry
            stiff.append(entries[0])
            second.append(entries[1])
            third.append(entries[2])
            rest.append((2.0 * weighted) * cross + mass)
        upper, lower = split(jnp.concatenate(second, axis=0))
        diagonal = jnp.dot(
            square[...], jnp.concatenate([upper, lower, upper], axis=0), preferred_element_type=F32
        )
        upper, lower = split(jnp.concatenate(third, axis=0))
        diagonal = diagonal + lax.dot_general(
            jnp.concatenate([upper, lower, upper], axis=1),
            square[...],
            (((1,), (1,)), ((), ())),
            preferred_element_type=F32,
        )
        first = self.contract(stiff, self.squared.T)
        diagonal = diagonal + jnp.concatenate([x + y for x, y in zip(first, rest)], axis=0)
        width = diagonal.shape[-1]
        value = diagonal.reshape(p, ey, p, width)
        value = jnp.concatenate([value[:, f].reshape(block, width) for f in range(ey)], axis=1)

        def store(k, part):
            work[pl.ds(k, block, stride=p), :] = part

        self.by_nodes(*split(value), spread, self.w4, store)
        hot = self.one_hot(slots, ids)
        hot3[...] = self.one_hot(slots, ids[c:, :])
        total = work[...]
        for part in split(right[...].reshape(hot.shape[0], rows)):
            total = total + lax.dot_general(
                part, hot, (((0,), (0,)), ((), ())), preferred_element_type=F32
            )
        s4[...] = total
        self.fold_second(s4)
        last = self.n4 - self.step4
        self.fold_third(s4, self.step4, lambda l: l < last, lambda l: (l >= self.step4) & (l < self.n4))
        self.emit_first((s4[:block, :], s4[rows - block :, :]), x_out)
        self.emit_second(s4, y_out)

    def convert(self, n_y, n_z, *refs):
        fields, spread, dirichlet, s4 = refs[:4]
        g, ind = refs[4:6]
        refs = refs[6:]
        y_out, z_out, packed = refs[:n_y], refs[n_y : n_y + n_z], refs[n_y + n_z : n_y + 2 * n_z]
        upper, lower = refs[n_y + 2 * n_z :]
        p, c, block, ey = self.p, self.c, self.block, self.ey
        width = fields.shape[-1]
        for q in range(FIELDS):
            value = fields[q].reshape(p, ey, p, width)
            for f in range(ey):
                at = (slice(q * block, (q + 1) * block), slice(f * width, (f + 1) * width))
                upper[at], lower[at] = split(value[:, f].reshape(block, width))
        first_flag, flags = FIELDS * block, 2 * p
        for cc in range(c):
            for f in range(ey):
                at = slice(f * p, (f + 1) * p)
                face = jnp.concatenate([dirichlet[0, cc, at, :], dirichlet[1, cc, at, :]], axis=0)
                to = slice(first_flag + cc * flags, first_flag + (cc + 1) * flags)
                upper[to, f * width : (f + 1) * width] = face.astype(F32).astype(BF16)
                lower[to, f * width : (f + 1) * width] = jnp.zeros((flags, width), BF16)
        row = lax.broadcasted_iota(jnp.int32, (flags, self.w3), 0)
        lane = lax.broadcasted_iota(jnp.int32, (flags, self.w3), 1)
        ends = (lax.axis_index("gx") == 0, lax.axis_index("gx") == self.sizes["gx"] - 1)
        here = ((row < p) & ends[0]) | ((row >= p) & ends[1])
        owner = lax.rem(lane, self.step3) // ey

        def store(k, value):
            g[pl.ds(k, first_flag, stride=p), :] = value[:first_flag]
            total = jnp.zeros((flags, self.w3), F32)
            for cc in range(c):
                at = first_flag + cc * flags
                total = jnp.where(owner == cc, value[at : at + flags], total)
            ind[pl.ds(k, flags, stride=p), :] = jnp.where(here, total, 0.0)

        self.by_nodes(upper[...], lower[...], spread, self.w3, store)
        self.pack_fields(fields, z_out)
        self.fold_second(ind)
        first_own, end_own = HALO * self.step3, self.n3 - HALO * self.step3
        self.fold_third(
            ind,
            self.step3,
            lambda l: (l >= first_own) & (l < end_own - self.step3),
            lambda l: (l >= first_own + self.step3) & (l < end_own),
        )
        for out, (up, _, _) in zip(y_out, roles("gy", self.sizes["gy"])):
            for n in range(2):
                start = n * block
                out[n * p : (n + 1) * p, :] = jnp.where(
                    up, ind[start + block - p : start + block, :], ind[start : start + p, :]
                )
        for out, (up, _, _) in zip(packed, roles("gz", self.sizes["gz"])):
            self.pack(out, s4, block, 0, self.n4 - self.halo4, up, 0)
            self.pack(out, ind, p, first_own, end_own - first_own, up, block)

    def halo_fields(self, n_z, *refs):
        own, halo = refs[:2]
        z_in, g, terms = refs[2 : 2 + n_z], refs[2 + n_z], refs[3 + n_z]
        p, block, ey, part = self.p, self.block, self.ey, self.part
        sides = both_sides([z[...] for z in z_in], roles("gz", self.sizes["gz"]))
        width = sides[0].shape[-1]
        sides = [side.reshape(p, ey, p, width) for side in sides]
        lane = lax.broadcasted_iota(jnp.int32, (block, width), 1)
        for q in range(FIELDS):
            value = jnp.zeros((block, width), F32)
            for side in range(2):
                for f in range(ey):
                    to = (side * ey + f) * part
                    shift = (to - q * part) % width
                    x = sides[side][:, f].reshape(block, width)
                    x = pltpu.roll(x, shift, 1) if shift else x
                    value = jnp.where((lane >= to) & (lane < to + part), x, value)
            upper, lower = split(value)
            lower = pltpu.roll(lower.astype(F32), width // 2, 1).astype(BF16)
            terms[q * block : (q + 1) * block, :] = upper + lower

        for k in range(0, p, 2):
            columns = halo[:, k * self.w3 : (k + 2) * self.w3]
            both = jnp.dot(terms[...], columns, preferred_element_type=F32)
            for n in range(2):
                at = pl.ds(k + n, FIELDS * block, stride=p)
                g[at, :] = own[at, :] + both[:, n * self.w3 : (n + 1) * self.w3]

    def coefficients(self, low, high, coef):
        top, bottom = jnp.full((8, 128), high[0], F32), jnp.full((8, 128), low[0], F32)
        midpoint, halfwidth = (top + bottom) * 0.5, (top - bottom) * 0.5
        ratio = midpoint / halfwidth
        damping = 1.0 / ratio
        coef[0:8, :] = 1.0 / midpoint
        for n in range(ITERS - 1):
            following = 1.0 / (2.0 * ratio - damping)
            coef[8 * (2 * n + 1) : 8 * (2 * n + 2), :] = following * damping
            coef[8 * (2 * n + 2) : 8 * (2 * n + 3), :] = 2.0 * following / halfwidth
            damping = following

    def join(self, n_x, n_y, *refs):
        x_in, refs = refs[:n_x], refs[n_x:]
        y_raw, y_more, y_out = refs[:n_y], refs[n_y:-n_y], refs[-n_y:]
        p, block, ey = self.p, self.block, self.ey
        low, high = both_sides([x[...] for x in x_in], roles("gx", self.sizes["gx"]))
        for n, (up, _, _) in enumerate(roles("gy", self.sizes["gy"])):
            face = y_raw[n][...]
            width = face.shape[-1]
            if n_x:
                first, last = (jnp.where(up, x[block - p :], x[:p]) for x in (low, high))
                face = jnp.concatenate([face[:p] + first, face[p : block - p], face[block - p :] + last], axis=0)
            if y_more:
                face = jnp.concatenate([face, y_more[n][...]], axis=0)
            if ey == 1:
                y_out[n][...] = face
                continue
            half = face.shape[0] // 2
            first, second = face[:half], face[half:]
            f = lax.rem(lax.broadcasted_iota(jnp.int32, first.shape, 1), ey)
            below = jnp.where(f == 0, pltpu.roll(first, width - (ey - 1), 1), 0.0) + jnp.where(
                f == 1, pltpu.roll(second, (width - (ey - 2)) % width, 1) if ey != 2 else second, 0.0
            )
            above = jnp.where(f == ey - 1, pltpu.roll(first, ey - 1, 1), 0.0) + jnp.where(
                f == ey - 2, pltpu.roll(second, ey - 2, 1) if ey != 2 else second, 0.0
            )
            y_out[n][...] = jnp.where(up, below, above)

    def second_sides(self, received):
        role, ey = roles("gy", self.sizes["gy"]), self.ey
        faces = []
        for message, (_, from_high, _) in zip(received, role):
            data = message[...]
            if ey > 1:
                width = data.shape[-1]
                f = lax.rem(lax.broadcasted_iota(jnp.int32, data.shape, 1), ey)
                beside = jnp.where(from_high, pltpu.roll(data, 1, 1), pltpu.roll(data, width - 1, 1))
                here = f == jnp.where(from_high, ey - 1, 0)
                data = jnp.concatenate([jnp.where(here, x, 0.0) for x in (data, beside)], axis=0)
            faces.append(data)
        return both_sides(faces, role)

    def pack(self, out, u, count, first, last, up, start):
        p, width, size = self.p, self.w4, self.halo4
        lane = lax.broadcasted_iota(jnp.int32, (count, width), 1)
        for section in range(0, u.shape[0] // count, p):
            total = jnp.zeros((count, width), F32)
            for n in range(p):
                at, shift = (section + n) * count, n * size
                x = u[at : at + count, :]
                below = pltpu.roll(x, (shift - first) % width, 1) if (shift - first) % width else x
                above = pltpu.roll(x, (shift - last) % width, 1)
                here = (lane >= shift) & (lane < shift + size)
                total = jnp.where(here, jnp.where(up, above, below), total)
            row = start + section // p * count
            out[row : row + count, :] = total

    def pack_second(self, n_x, n_y, n_z, *refs):
        x_in, y_in, refs = refs[:n_x], refs[n_x : n_x + n_y], refs[n_x + n_y :]
        z_in, z_out = refs[:n_z], refs[n_z:]
        p, block, width, size = self.p, self.block, self.w4, self.halo4
        ends = both_sides([x[...] for x in x_in], roles("gx", self.sizes["gx"]))
        low, high = self.second_sides(y_in)
        halo3 = HALO * self.step3
        lane = lax.broadcasted_iota(jnp.int32, (p, width), 1)
        for packed, out, (up, _, _) in zip(z_in, z_out, roles("gz", self.sizes["gz"])):
            out[...] = packed[...]
            if n_x:
                total = 0.0
                for x, group in zip(ends, (0, p - 1)):
                    shift = group * size
                    below = pltpu.roll(x, shift, 1) if shift else x
                    back = (shift - self.n4 + size) % width
                    above = pltpu.roll(x, back, 1) if back else x
                    wide = lax.broadcasted_iota(jnp.int32, x.shape, 1)
                    here = (wide >= shift) & (wide < shift + size)
                    total = total + jnp.where(here, jnp.where(up, above, below), 0.0)
                out[:block, :] += total
            if not n_y:
                continue
            for face, row in ((low, 0), (high, block - p)):
                total = jnp.zeros((p, width), F32)
                for n in range(p):
                    shift = n * size
                    x = face[n * p : (n + 1) * p]
                    below = pltpu.roll(x, shift, 1) if shift else x
                    above = pltpu.roll(x, (shift - self.n4 + size) % width, 1)
                    here = (lane >= shift) & (lane < shift + size)
                    total = jnp.where(here, jnp.where(up, above, below), total)
                out[row : row + p, :] += total
            for n in range(2):
                row = block + n * p
                for face, group in ((low, 0), (high, p - 1)):
                    shift = group * size
                    x = face[row : row + p]
                    below = pltpu.roll(x, (shift - halo3) % width, 1)
                    above = pltpu.roll(x, (shift - self.n3 + 2 * halo3) % width, 1)
                    here = (lane >= shift) & (lane < shift + size)
                    out[row : row + p, :] += jnp.where(here, jnp.where(up, above, below), 0.0)

    def own(self, n_x, n_y, *refs):
        s4, ind, widen = refs[:3]
        x_in, y_in, (r, scale, flag, work) = refs[3 : 3 + n_x], refs[3 + n_x : 3 + n_x + n_y], refs[3 + n_x + n_y :]
        p, block, rows, w3 = self.p, self.block, self.rows, self.w3
        work[...] = s4[...]
        if n_x:
            low, high = both_sides([x[...] for x in x_in], roles("gx", self.sizes["gx"]))
            work[:block, :] += low
            work[rows - block :, :] += high
        flag[...] = ind[...]
        if n_y:
            low, high = self.second_sides(y_in)
            for u, first, count in ((work, 0, p), (flag, p, 2)):
                for i in range(count):
                    at, end, row = i * block, (i + 1) * block, (first + i) * p
                    u[at : at + p, :] += low[row : row + p]
                    u[end - p : end, :] += high[row : row + p]
        both = dot2(work[...], widen[: self.w4, :])
        r[...] = both[:, :w3]
        scale[...] = both[:, w3:]

    def start(self, n_x, n_z, *refs):
        r_own, diagonal_own, flag_own, g, widen, ahead, back = refs[:7]
        z_in = refs[7 : 7 + n_z]
        t, scale, ends, f1, f2, f3 = refs[7 + n_z : 13 + n_z]
        x_out, refs = refs[13 + n_z : 13 + n_z + n_x], refs[13 + n_z + n_x :]
        beside, r, flag, slope, third = refs
        p, block, rows, w3, w4 = self.p, self.block, self.rows, self.w3, self.w4
        step, first_own, end_own = self.step3, HALO * self.step3, self.n3 - HALO * self.step3
        size, part = self.sizes["gz"], self.halo4
        if n_z:
            low, high = both_sides([z[...] for z in z_in], roles("gz", size))
        else:
            low = high = jnp.zeros((block + 2 * p, w4), F32)
        lane = lax.broadcasted_iota(jnp.int32, (block, w4), 1)
        for n in range(p):
            first = pltpu.roll(low[:block], w4 - n * part, 1) if n else low[:block]
            second = pltpu.roll(high[:block], (part - n * part) % w4, 1) if n != 1 else high[:block]
            beside[n * block : (n + 1) * block, :] = jnp.where(
                lane < part, first, jnp.where(lane < 2 * part, second, 0.0)
            )
        both = dot2(beside[...], widen[w4:, :])
        r[...] = r_own[...] + both[:, :w3]
        scale[...] = diagonal_own[...] + both[:, w3:]
        lane = lax.broadcasted_iota(jnp.int32, (p, w3), 1)
        for n in range(2 * p):
            row, shift = block + n // p * p, n % p * part
            first = pltpu.roll(low[row : row + p], w3 - shift, 1) if shift else low[row : row + p]
            second = pltpu.roll(high[row : row + p], (end_own - shift) % w3, 1)
            flag[n * p : (n + 1) * p, :] = jnp.where(
                lane < first_own,
                first,
                jnp.where(lane < end_own, flag_own[n * p : (n + 1) * p, :], jnp.where(lane < self.n3, second, 0.0)),
            )
        for u in (r, scale, flag):
            self.fold_third(
                u,
                step,
                lambda l: ((l >= first_own - step) & (l < first_own)) | ((l >= end_own - step) & (l < end_own)),
                lambda l: ((l >= first_own) & (l < first_own + step)) | ((l >= end_own) & (l < end_own + step)),
            )
        index = lax.axis_index("gz")
        begin = jnp.where(index > 0, 0, first_own)
        end = jnp.where(index < size - 1, self.n3, end_own)
        lane = lax.broadcasted_iota(jnp.int32, (block, w3), 1)
        valid = (lane >= begin) & (lane < end)
        for i in range(p):
            at = slice(i * block, (i + 1) * block)
            factor = jnp.where(valid, 1.0 / jnp.where(valid, scale[at, :], 1.0), 0.0)
            if i in (0, p - 1):
                row = 0 if i == 0 else block
                factor = jnp.where(flag[row : row + block, :] > 0.5, 0.0, factor)
            scale[at, :] = factor
            t[at, :] = factor * r[at, :]
        self.fluxes(t, g, f1, f2, f3, slope, third, ahead)
        self.end_planes(t, g, ends, f1, f2, f3, slope, third, back)
        self.iteration_fold(ends)
        self.emit_first((ends[:block, :], ends[block:, :]), x_out)

    def factors(self, coef, n):
        rows = [coef[8 * m : 8 * m + 1, :] for m in (0, 2 * n + 1, 2 * n + 2)]
        return (rows[0] if n == 0 else None), rows[1], rows[2]

    def shares(self, faces, scale, image, at):
        low, high = faces
        p, block = self.p, self.block
        i = at // block
        out = []
        for start, face in ((at, low), (at + block - p, high)):
            value = scale[start : start + p, :] * face[i * p : (i + 1) * p]
            out.append((start, -value if image is None else -image * value))
        return out

    def preview(self, n_x, n_y, n, last, *refs):
        t, t_old, d, scale, v, coef = refs[:6]
        refs = refs[6:]
        x_in, y_old, refs = refs[:n_x], refs[n_x : n_x + (n_y if n else 0)], refs[n_x + (n_y if n else 0) :]
        p, block, rows = self.p, self.block, self.rows
        image, keep, gain = self.factors(coef, n)
        start = coef[0:1, :]
        if last:
            hot, out, t_new, field = refs
        else:
            g, ahead, back, t_new, d_new, f1, f2, f3, ends, slope, third = refs
        low, high = both_sides([x[...] for x in x_in], roles("gx", self.sizes["gx"]))
        if n:
            faces = self.second_sides(y_old) if n_y else None
            image_old = self.factors(coef, n - 1)[0]
        for i in range(p):
            at = slice(i * block, (i + 1) * block)
            value = v[at, :]
            if n_x and i in (0, p - 1):
                value = value + (low if i == 0 else high)
            value = scale[at, :] * value
            t_new[at, :] = t_old[at, :] - (value if image is None else image * value)
            if n and n_y:
                for row, share in self.shares(faces, scale, image_old, i * block):
                    t_new[row : row + p, :] += share
            direction = d[at, :] if n else start * t[at, :]
            following = keep * direction + gain * t_new[at, :]
            if last:
                field[at, :] = start * t[at, :] + following + (direction if n else 0.0)
            else:
                d_new[at, :] = following
        if last:
            out[...] = self.by_slots(hot, field[...])
        else:
            self.fluxes(d_new, g, f1, f2, f3, slope, third, ahead)
            self.end_planes(d_new, g, ends, f1, f2, f3, slope, third, back)

    def by_slots(self, hot, field):
        return lax.dot_general(
            jnp.concatenate([hot[...], hot[...]], axis=1),
            jnp.concatenate(split(field), axis=1),
            (((1,), (1,)), ((), ())),
            preferred_element_type=F32,
        )

    def middle(self, n_x, n_y, n, *refs):
        part, scale, g, coef, ahead, back = refs[:6]
        y_in, refs = refs[6 : 6 + n_y], refs[6 + n_y :]
        ends, shares, refs = refs[0], refs[1], refs[2:]
        x_out, (f1, f2, f3, third) = refs[:n_x], refs[n_x:]
        p, block, rows = self.p, self.block, self.rows
        image, _, gain = self.factors(coef, n)
        ends[...] = part[...]
        if n_y:
            faces = self.second_sides(y_in)
            for i in range(p):
                for m, (_, share) in enumerate(self.shares(faces, scale, image, i * block)):
                    shares[(2 * i + m) * p : (2 * i + m + 1) * p, :] = gain * share

            def write(i, j, values):
                f1[i * block + j * p : i * block + (j + 1) * p, :] = values[0]
                if len(values) > 1:
                    row = (block if i else 0) + j * p
                    f2[row : row + p, :], f3[row : row + p, :] = values[1], values[2]

            self.share_fluxes(shares, g, third, ahead, False, write)
            self.along_k(f3, back, third, 0, 2 * block)
            for m, i in enumerate((0, p - 1)):
                at = slice(m * block, (m + 1) * block)
                ends[at, :] += self.along_j(f2[at, :], self.forward.T) + third[at, :]
                for n_face, j in enumerate((0, p - 1)):
                    row, at = m * block + j * p, slice(i * block + j * p, i * block + (j + 1) * p)
                    line = (2 * i + n_face) * p
                    ends[row : row + p, :] += self.rows_of(g, 6, at) * shares[line : line + p, :]
            for j in range(p):
                x = [f1[i * block + j * p : i * block + (j + 1) * p, :] for i in range(p)]
                for row, value in zip((j * p, block + j * p), self.contract(x, self.forward.T, (0,))):
                    ends[row : row + p, :] += value
        else:
            shares[...] = jnp.zeros(shares.shape, F32)
        self.iteration_fold(ends)
        self.emit_first((ends[:block, :], ends[block:, :]), x_out)

    def finish(self, n_y, n, *refs):
        part, scale, coef, hot = refs[:4]
        y_in, (out, field) = refs[4 : 4 + n_y], refs[4 + n_y :]
        value = part[...]
        image, _, gain = self.factors(coef, n)
        if n_y:
            faces = self.second_sides(y_in)
            field[...] = jnp.zeros(field.shape, F32)
            for i in range(self.p):
                for row, share in self.shares(faces, scale, image, i * self.block):
                    field[row : row + self.p, :] = gain * share
            value = value + self.by_slots(hot, field[...])
        out[...] = value.reshape(out.shape)


def shards(sizes, right_side, geometry, viscosity, eig_low, eig_high, element_slot, dirichlet):
    plan = Plan(right_side.shape[0], viscosity.shape, sizes)
    p, block, rows, w3, w4 = plan.p, plan.block, plan.rows, plan.w3, plan.w4
    x_pairs = pairings(("gx",), (sizes["gx"],), 0)
    y_pairs = pairings(("gy",), (sizes["gy"],), 0)
    z_pairs = pairings(("gx", "gz"), (sizes["gx"], sizes["gz"]), 1)
    n_x, n_y, n_z = len(x_pairs), len(y_pairs), len(z_pairs)

    def send(arrays, axis, pairs):
        return [lax.ppermute(x, axis, pair) for x, pair in zip(arrays, pairs)]

    def shape(*size, dtype=F32):
        return jax.ShapeDtypeStruct(size, dtype)

    def call(kernel, outputs, operands, scratch=(), spaces={}, flops=0, name=None):
        specs = [pl.BlockSpec(memory_space=spaces.get(n, pltpu.VMEM)) for n in range(len(operands))]
        return list(
            pl.pallas_call(
                kernel,
                out_shape=list(outputs),
                in_specs=specs,
                out_specs=[pl.BlockSpec(memory_space=pltpu.VMEM)] * len(outputs),
                scratch_shapes=list(scratch),
                compiler_params=pltpu.CompilerParams(vmem_limit_bytes=VMEM_BYTES),
                cost_estimate=pl.CostEstimate(flops=flops, bytes_accessed=0, transcendentals=0),
                name=name,
            )(*operands)
        )

    def vmem(*size, dtype=F32):
        return pltpu.VMEM(size, dtype)

    lanes = plan.ez * p
    ahead, back = jnp.asarray(plan.third[0]), jnp.asarray(plan.third[1])
    field3, field4 = shape(rows, w3), shape(rows, w4)
    elements = element_slot.shape[-1]
    spread3, spread4 = call(
        plan.spread_tables,
        [shape(plan.ey * lanes, p * w, dtype=BF16) for w in (w3, w4)],
        (),
        flops=FLOPS,
        name="spread_tables",
    )
    results = call(
        functools.partial(plan.prepare, n_x, n_y),
        [field4, shape(plan.c * elements, w3, dtype=BF16), shape(FIELDS, p * plan.ey * p, lanes)]
        + [shape(block, w4)] * (n_x + n_y),
        (
            geometry,
            viscosity,
            spread4,
            jnp.asarray(plan.face_table),
            jnp.swapaxes(right_side, 1, 2),
            element_slot,
            jnp.asarray(plan.ids),
            jnp.asarray(plan.third[2]),
        ),
        scratch=[vmem(rows, w4)],
        name="prepare",
    )
    s4, hot3, fields = results[:3]
    x_out, y_raw = results[3 : 3 + n_x], results[3 + n_x :]
    x_in = send(x_out, "gx", x_pairs)

    lhs = FIELDS * block + 2 * plan.c * p
    results = call(
        functools.partial(plan.convert, n_y, n_z),
        [shape(FIELDS * rows, w3), shape(2 * block, w3)]
        + [shape(2 * p, w3)] * n_y
        + [shape(p * plan.ey * p, lanes)] * n_z
        + [shape(block + 2 * p, w4)] * n_z,
        (fields, spread3, dirichlet, s4),
        scratch=[vmem(lhs, plan.ey * lanes, dtype=BF16)] * 2,
        name="convert",
    )
    g, ind = results[:2]
    y_more, results = results[2 : 2 + n_y], results[2 + n_y :]
    z_fields, z_out = results[:n_z], results[n_z:]

    def joined(x_in, y_raw, y_more=()):
        if not y_raw:
            return []
        count = y_raw[0].shape[0] + (y_more[0].shape[0] if y_more else 0)
        faces = [shape(count // 2 if plan.ey > 1 else count, y.shape[1]) for y in y_raw]
        return call(functools.partial(plan.join, n_x, n_y), faces, x_in + y_raw + list(y_more), name="join")

    y_in = send(joined(x_in, y_raw, y_more), "gy", y_pairs)
    z_fields = send(z_fields, ("gx", "gz"), z_pairs)
    if n_z:
        g = call(
            functools.partial(plan.halo_fields, n_z),
            [shape(FIELDS * rows, w3)],
            [g, jnp.asarray(plan.halo)] + z_fields,
            scratch=[vmem(FIELDS * block, lanes, dtype=BF16)],
            name="halo_fields",
        )[0]
    if n_z:
        z_out = call(
            functools.partial(plan.pack_second, n_x, n_y, n_z),
            [shape(*z.shape) for z in z_out],
            x_in + y_in + z_out,
            flops=FLOPS,
            name="pack_second",
        )
    z_in = send(z_out, ("gx", "gz"), z_pairs)
    widen = jnp.asarray(plan.widen)
    own = call(
        functools.partial(plan.own, n_x, n_y),
        [field3, field3, shape(2 * block, w3)],
        [s4, ind, widen] + x_in + y_in,
        scratch=[vmem(rows, w4)],
        name="own",
    )

    fluxes = [shape(2 * block, w3)] + [field3] * 3 + [shape(block, w3)] * n_x
    results = call(
        functools.partial(plan.start, n_x, n_z),
        [field3] * 2 + fluxes,
        own + [g, widen, ahead, back] + z_in,
        scratch=[vmem(rows, w4), vmem(rows, w3), vmem(2 * block, w3)] + [vmem(rows, w3)] * 2,
        name="first_direction",
    )
    t, scale = results[:2]
    ends, f1, f2, f3 = results[2:6]
    x_out = results[6:]
    x_out, low, high = lax.optimization_barrier((x_out, eig_low, eig_high))
    coef = call(
        plan.coefficients,
        [shape(8 * (2 * ITERS - 1), 128)],
        (low, high),
        spaces={0: pltpu.SMEM, 1: pltpu.SMEM},
        name="coefficients",
    )[0]
    t_old, d, y_in = t, t, []
    for n in range(ITERS - 1):
        last = n == ITERS - 2
        x_in = send(x_out, "gx", x_pairs)
        outputs = [field3] + [shape(block, w3)] * n_y
        if n:
            results = call(
                functools.partial(plan.operator_second, n_x, n_y, True),
                outputs + [field3],
                [d, g, ends, f1, f2, f3, back, shares, ahead],
                scratch=[vmem(rows, w3)] * 4,
                name="operator_second",
            )
            v, y_raw, d = results[0], results[1 : 1 + n_y], results[1 + n_y]
        else:
            results = call(
                functools.partial(plan.operator_second, n_x, n_y, False),
                outputs,
                [d, g, ends, f1, f2, f3, back],
                scratch=[vmem(rows, w3)],
                name="operator_second",
            )
            v, y_raw = results[0], results[1:]
        y_old, y_in = y_in, send(joined(x_in, y_raw), "gy", y_pairs)
        results = call(
            functools.partial(plan.preview, n_x, n_y, n, last),
            [shape(plan.c * elements, rows)] if last else [field3] * 5 + [shape(2 * block, w3)],
            [t, t_old, d, scale, v, coef] + x_in + y_old + ([hot3] if last else [g, ahead, back]),
            scratch=[vmem(rows, w3)] * 2,
            name="preview",
        )
        if last:
            break
        t_old, d, f1, f2, f3, ends = results
        results = call(
            functools.partial(plan.middle, n_x, n_y, n),
            [shape(2 * block, w3)] * 2 + [shape(block, w3)] * n_x,
            [ends, scale, g, coef, ahead, back] + y_in,
            scratch=[vmem(rows, w3)] + [vmem(2 * block, w3)] * 3,
            name="direction",
        )
        ends, shares, x_out = results[0], results[1], results[2:]
    out = call(
        functools.partial(plan.finish, n_y, n),
        [shape(plan.c, elements, rows)],
        [results[0], scale, coef, hot3] + y_in,
        scratch=[vmem(rows, w3)],
        name="field",
    )[0]
    return jnp.swapaxes(out, 1, 2)


def solution(mesh):
    sizes = {name: mesh.shape[name] for name in ("gx", "gy", "gz")}
    return jax.shard_map(
        functools.partial(shards, sizes),
        mesh=mesh,
        in_specs=(
            P(None, None, ("gx", "gy", "gz")),
            P(None, "gx", "gy", "gz"),
            P("gx", "gy", "gz"),
            P(),
            P(),
            P(("gx", "gy", "gz"), None),
            P(None, None, "gy", "gz"),
        ),
        out_specs=P(None, None, ("gx", "gy", "gz")),
        check_vma=False,
    )
```

```python
import functools
import math

import jax
import jax.numpy as jnp
import numpy as np
from jax import lax
from jax.experimental import pallas as pl
from jax.experimental.pallas import tpu as pltpu
from jax.sharding import PartitionSpec as P

DEGREE = 7
ITERS = 3


helm_coefficient = 10.0


def legendre_pair(values, degree):
    previous = 0.0 * values + 1.0
    current = values.copy()
    for order in range(2, degree + 1):
        previous, current = (
            current,
            ((2 * order - 1) * values * current - (order - 1) * previous) / order,
        )
    return (current, previous)


def gll_tables(degree):
    start = np.cos(np.pi * np.arange(degree + 1) / degree)
    nodes_now = start.copy()
    for sweep in range(80):
        top_value, lower_value = legendre_pair(nodes_now, degree)
        nodes_now = nodes_now - (nodes_now * top_value - lower_value) / ((degree + 1) * top_value)
    gll_nodes = nodes_now[::-1].copy()
    gll_nodes[0] = -1.0
    gll_nodes[degree] = 1.0
    legendre_values = legendre_pair(gll_nodes, degree)[0]
    weights = 2.0 / (degree * (degree + 1) * legendre_values**2)
    differences = gll_nodes[:, None] - gll_nodes[None, :] + np.eye(degree + 1)
    derivative = legendre_values[:, None] / legendre_values[None, :] / differences
    derivative = derivative * (1.0 - np.eye(degree + 1))
    derivative[0, 0] = -degree * (degree + 1) / 4.0
    derivative[degree, degree] = degree * (degree + 1) / 4.0
    return (weights, derivative)


HALO = 2
FIELDS = 7
VMEM_BYTES = 40 * 1024 * 1024
FLOPS = 3 * 10**9
F32 = jnp.float32
BF16 = jnp.bfloat16


def pairings(names, sizes, dim):
    size = sizes[dim]
    if size == 1:
        return []
    if size % 2:
        shifts = (1, size - 1)
        partners = [[(i + shift) % size for i in range(size)] for shift in shifts]
    else:
        partners = [[i ^ 1 for i in range(size)]]
        if size > 2:
            partners.append([((i + 1) ^ 1) - 1 for i in range(size)])
    result = []
    for partner in partners:
        pairs = []
        for flat in range(math.prod(sizes)):
            place = list(np.unravel_index(flat, sizes))
            to = partner[place[dim]]
            if 0 <= to < size:
                place[dim] = to
            elif len(sizes) > 1 and sizes[1 - dim] % 2 == 0:
                place[1 - dim] ^= 1
            else:
                place[dim] = size - 1 - place[dim]
            pairs.append((flat, int(np.ravel_multi_index(place, sizes))))
        result.append(pairs)
    return result


def roles(name, size):
    if size == 1:
        return []
    index = lax.axis_index(name)
    low, high = index > 0, index < size - 1
    if size % 2:
        yes = index >= 0
        no = index < 0
        return [(yes, no, low), (no, yes, high)]
    even = lax.rem(index, 2) == 0
    odd = jnp.logical_not(even)
    result = [(even, even, index >= 0)]
    if size > 2:
        result.append((odd, odd, jnp.logical_or(jnp.logical_and(odd, high), jnp.logical_and(even, low))))
    return result


def both_sides(received, role):
    low, high = 0.0, 0.0
    for data, (_, from_high, used) in zip(received, role):
        high = high + jnp.where(jnp.logical_and(used, from_high), data, 0.0)
        low = low + jnp.where(jnp.logical_and(used, jnp.logical_not(from_high)), data, 0.0)
    return low, high


def split(x):
    upper = x.astype(BF16)
    return upper, (x - upper.astype(F32)).astype(BF16)


def dot2(x, table):
    return jnp.dot(
        jnp.concatenate(split(x), axis=1),
        jnp.concatenate([table, table], axis=0),
        preferred_element_type=F32,
    )


class Plan:
    def __init__(self, components, viscosity_shape, mesh_sizes):
        points = DEGREE + 1
        self.p, self.c = points, components
        self.sizes = mesh_sizes
        ex, ey, ez = (n // points for n in viscosity_shape)
        assert ex == 1 and ez >= HALO
        self.ey, self.ez = ey, ez
        self.rows = points**3
        self.block = points * points
        self.step3, self.step4 = components * ey, (components + 1) * ey
        self.n3, self.n4 = (ez + 2 * HALO) * self.step3, ez * self.step4
        self.w3, self.w4 = -(-self.n3 // 128) * 128, -(-self.n4 // 128) * 128
        self.halo4 = HALO * self.step4
        assert points * self.halo4 <= self.w4 and 2 * self.halo4 <= self.w4
        weights, derivative = gll_tables(DEGREE)
        self.forward = derivative.astype(np.float32)
        self.squared = self.forward * self.forward
        self.weights = weights.astype(np.float32)
        self.end = np.diagonal(self.forward)
        self.tables()

    def lane3(self, g, c, f):
        return (g + HALO) * self.step3 + c * self.ey + f

    def lane4(self, g, c, f):
        return g * self.step4 + c * self.ey + f

    def tables(self):
        p, c, ey, ez = self.p, self.c, self.ey, self.ez
        lanes = ez * p
        every = [(g, cc, f) for g in range(ez) for cc in range(c) for f in range(ey)]
        widen = np.zeros((2 * self.w4, 2 * self.w3), np.float32)
        ids = np.full((2 * c, 128, 128), -1, np.int32)
        for g, cc, f in every:
            widen[self.lane4(g, cc, f), self.lane3(g, cc, f)] = 1
            widen[self.lane4(g, c, f), self.w3 + self.lane3(g, cc, f)] = 1
            ids[cc, :, self.lane4(g, cc, f)] = f * ez + g
            ids[c + cc, :, self.lane3(g, cc, f)] = f * ez + g
        self.ids = np.ascontiguousarray(ids[:, :1, :]).reshape(2 * c, 128)
        part = HALO * p
        self.part = part
        assert FIELDS * part <= lanes and 2 * ey * part <= lanes // 2
        halo = np.zeros((lanes, p, self.w3), np.float32)
        for side, first in ((0, -HALO), (1, ez)):
            for g in range(HALO):
                for cc in range(c):
                    for f in range(ey):
                        at = self.lane3(first + g, cc, f)
                        row = self.w4 + side * self.halo4 + g * self.step4
                        widen[row + cc * ey + f, at] = 1
                        widen[row + c * ey + f, self.w3 + at] = 1
                        for k in range(p):
                            for half in range(2):
                                halo[half * lanes // 2 + (side * ey + f) * part + g * p + k, k, at] = 1
        self.halo = halo.reshape(lanes, -1).astype(jnp.bfloat16)
        self.widen = widen.astype(jnp.bfloat16)
        self.third = [self.block_terms(matrix) for matrix in (self.forward, self.forward.T)]
        face = (ey * p, lanes)
        second = np.tile(np.arange(p), ey)[:, None]
        third = np.tile(np.arange(p), ez)[None, :]
        self.face_table = np.concatenate(
            [
                self.weights[second] * self.weights[third],
                np.broadcast_to(self.end[second], face),
                np.broadcast_to(self.end[third], face),
            ]
        ).astype(np.float32)

    def block_terms(self, matrix):
        size = self.rows // 4
        blocks = np.kron(np.eye(size // self.p), matrix).astype(np.float32)
        upper = blocks.astype(jnp.bfloat16)
        lower = (blocks - upper.astype(np.float32)).astype(jnp.bfloat16)
        return np.concatenate([upper, upper, lower], axis=1)


    def contract(self, x, matrix, wanted=None):
        p = self.p
        sign = 1.0 if matrix[0, 0] * matrix[p - 1, p - 1] > 0 else -1.0
        half = p // 2
        sums = [x[i] + x[p - 1 - i] for i in range(half)]
        differences = [x[i] - x[p - 1 - i] for i in range(half)]
        out = [None] * p
        for a in range(half) if wanted is None else wanted:
            even, odd = None, None
            for i in range(half):
                first, second = float(matrix[a, i]), float(matrix[a, p - 1 - i])
                even = self.gather(even, 0.5 * (first + second), sums[i])
                odd = self.gather(odd, 0.5 * (first - second), differences[i])
            out[a] = odd + even
            out[p - 1 - a] = even - odd if sign > 0 else odd - even
        return [x for x in out if x is not None]

    @staticmethod
    def gather(total, factor, x):
        if factor == 0.0:
            return total
        return factor * x if total is None else total + factor * x

    def along_j(self, x, matrix):
        x = x.reshape(self.p, self.p, x.shape[-1])
        return jnp.concatenate(self.contract([x[j] for j in range(self.p)], matrix), axis=0)

    def along_i(self, source, matrix, write):
        p, block = self.p, self.block
        for j in range(p):
            rows = [i * block + j * p for i in range(p)]
            for row, value in zip(rows, self.contract([source[r : r + p, :] for r in rows], matrix)):
                write(row, value)

    def along_k(self, source, table, out, start, end):
        size = table.shape[0]
        width = source.shape[-1]
        while start < end:
            count = min(2, (end - start) // size)
            pieces = [split(source[start + n * size : start + (n + 1) * size, :]) for n in range(count)]
            upper, lower = (jnp.concatenate([piece[n] for piece in pieces], axis=1) for n in range(2))
            both = jnp.dot(
                table[...], jnp.concatenate([upper, lower, upper], axis=0), preferred_element_type=F32
            )
            for n in range(count):
                out[start + n * size : start + (n + 1) * size, :] = both[:, n * width : (n + 1) * width]
            start += count * size

    def rows_of(self, g, q, at):
        return g[q * self.rows + at.start : q * self.rows + at.stop, :]

    def fluxes(self, v, g, f1, f2, f3, slope, third, ahead):
        p, block, rows = self.p, self.block, self.rows

        def store(row, value):
            slope[row : row + p, :] = value

        self.along_i(v, self.forward, store)
        self.along_k(v, ahead, third, 0, rows)
        for i in range(p):
            at = slice(i * block, (i + 1) * block)
            x, s1, s3 = v[at, :], slope[at, :], third[at, :]
            s2 = self.along_j(x, self.forward)
            xy, xz, yz = (self.rows_of(g, q, at) for q in (3, 4, 5))
            f1[at, :] = self.rows_of(g, 0, at) * s1 + xy * s2 + xz * s3
            f2[at, :] = xy * s1 + self.rows_of(g, 1, at) * s2 + yz * s3
            f3[at, :] = xz * s1 + yz * s2 + self.rows_of(g, 2, at) * s3

    def share_fluxes(self, shares, g, third, ahead, whole, write):
        p, block = self.p, self.block
        x = shares[...]
        ends = [[x[(2 * i + n) * p : (2 * i + n + 1) * p] for i in range(p)] for n in range(2)]
        s1 = [self.contract(column, self.forward) for column in ends]
        self.along_k(shares, ahead, third, 0, 2 * block)
        for i in range(p):
            first, last = ends[0][i], ends[1][i]
            count = 3 if whole or i in (0, p - 1) else 1
            for j in range(p):
                at = slice(i * block + j * p, i * block + (j + 1) * p)
                s2 = float(self.forward[j, 0]) * first + float(self.forward[j, p - 1]) * last
                rows = ((0, 3, 4), (3, 1, 5), (4, 5, 2))[:count]
                values = [self.rows_of(g, row[1], at) * s2 for row in rows]
                if j in (0, p - 1):
                    n = int(j > 0)
                    line = (2 * i + n) * p
                    e1, e3 = s1[n][i], third[line : line + p, :]
                    values = [
                        value + self.rows_of(g, row[0], at) * e1 + self.rows_of(g, row[2], at) * e3
                        for value, row in zip(values, rows)
                    ]
                write(i, j, values)

    def end_planes(self, v, g, ends, f1, f2, f3, slope, third, back):
        p, block, rows = self.p, self.block, self.rows
        for n, start in enumerate((0, rows - block)):
            at = slice(start, start + block)
            ends[n * block : (n + 1) * block, :] = (
                self.along_j(f2[at, :], self.forward.T) + self.rows_of(g, 6, at) * v[at, :]
            )
            slope[n * block : (n + 1) * block, :] = f3[at, :]
        self.along_k(slope, back, third, 0, 2 * block)
        for j in range(p):
            x = [f1[i * block + j * p : i * block + (j + 1) * p, :] for i in range(p)]
            first, last = self.contract(x, self.forward.T, (0,))
            for row, value in ((j * p, first), (block + j * p, last)):
                ends[row : row + p, :] += value + third[row : row + p, :]

    def operator_second(self, n_x, n_y, shared, *refs):
        v, g, ends, f1, f2, f3, back = refs[:7]
        refs = refs[7:]
        p, block, rows = self.p, self.block, self.rows
        if shared:
            shares, ahead, out = refs[:3]
            y_out, (v_new, third, *new) = refs[3 : 3 + n_y], refs[3 + n_y :]

            def write(i, j, values):
                at = slice(i * block + j * p, i * block + (j + 1) * p)
                for f_old, f_new, value in zip((f1, f2, f3), new, values):
                    f_new[at, :] = f_old[at, :] + value

            self.share_fluxes(shares, g, third, ahead, True, write)
            v_new[...] = v[...]
            for i in range(p):
                for m, row in enumerate((i * block, (i + 1) * block - p)):
                    v_new[row : row + p, :] += shares[(2 * i + m) * p : (2 * i + m + 1) * p, :]
            v, (f1, f2, f3) = v_new, new
        else:
            out, y_out, third = refs[0], refs[1 : 1 + n_y], refs[1 + n_y]
        out[:block, :], out[rows - block :, :] = ends[:block, :], ends[block:, :]
        self.along_k(f3, back, third, block, rows - block)
        for i in range(1, p - 1):
            at = slice(i * block, (i + 1) * block)
            out[at, :] = (
                self.along_j(f2[at, :], self.forward.T) + self.rows_of(g, 6, at) * v[at, :] + third[at, :]
            )
        for j in range(p):
            at = [slice(i * block + j * p, i * block + (j + 1) * p) for i in range(p)]
            values = self.contract([f1[r, :] for r in at], self.forward.T, range(1, p // 2))
            for r, value in zip(at[1 : p - 1], values):
                out[r, :] += value
        self.iteration_fold(out.at[block : rows - block, :])
        self.emit_second(out, y_out)

    def fold_second(self, u):
        if self.ey == 1:
            return
        p, width = self.p, u.shape[-1]
        lane = lax.broadcasted_iota(jnp.int32, (p, width), 1)
        f = lax.rem(lane, self.ey)
        for start in range(0, u.shape[0], self.block):
            first, last = u[start : start + p, :], u[start + self.block - p : start + self.block, :]
            u[start + self.block - p : start + self.block, :] = last + jnp.where(
                f < self.ey - 1, pltpu.roll(first, width - 1, 1), 0.0
            )
            u[start : start + p, :] = first + jnp.where(f > 0, pltpu.roll(last, 1, 1), 0.0)

    def fold_third(self, u, step, take_upper, take_lower):
        p, (rows, width) = self.p, u.shape
        count = rows // p
        lane = lax.broadcasted_iota(jnp.int32, (count, width), 1)
        first, last = u[pl.ds(0, count, stride=p), :], u[pl.ds(p - 1, count, stride=p), :]
        u[pl.ds(p - 1, count, stride=p), :] = last + jnp.where(
            take_upper(lane), pltpu.roll(first, width - step, 1), 0.0
        )
        u[pl.ds(0, count, stride=p), :] = first + jnp.where(
            take_lower(lane), pltpu.roll(last, step, 1), 0.0
        )

    def emit_first(self, ends, x_out):
        for out, (high, _, _) in zip(x_out, roles("gx", self.sizes["gx"])):
            out[...] = jnp.where(high, ends[1], ends[0])

    def emit_second(self, u, y_out):
        p, block = self.p, self.block
        for out, (high, _, _) in zip(y_out, roles("gy", self.sizes["gy"])):
            for i in range(p):
                start = i * block
                out[i * p : (i + 1) * p, :] = jnp.where(
                    high, u[start + block - p : start + block, :], u[start : start + p, :]
                )

    def iteration_fold(self, u):
        self.fold_second(u)
        last = self.n3 - self.step3
        self.fold_third(u, self.step3, lambda l: l < last, lambda l: (l >= self.step3) & (l < self.n3))


    def pack_fields(self, fields, out):
        for target, (high, _, _) in zip(out, roles("gz", self.sizes["gz"])):
            rows, width = target.shape
            lane = lax.broadcasted_iota(jnp.int32, (rows, width), 1)
            total = jnp.zeros((rows, width), F32)
            for q in range(FIELDS):
                start = q * self.part
                upper = pltpu.roll(fields[q], start + self.part, 1)
                lower = pltpu.roll(fields[q], start, 1) if start else fields[q]
                here = (lane >= start) & (lane < start + self.part)
                total = jnp.where(here, jnp.where(high, upper, lower), total)
            target[...] = total

    def by_nodes(self, upper, lower, table, width, store):
        for k in range(0, self.p, 2):
            columns = table[:, k * width : (k + 2) * width]
            both = jnp.dot(upper, columns, preferred_element_type=F32) + jnp.dot(
                lower, columns, preferred_element_type=F32
            )
            store(k, both[:, :width])
            store(k + 1, both[:, width:])

    def one_hot(self, slots, ids):
        count = slots.shape[-1]
        column = jnp.broadcast_to(slots[...], (count, count))
        column = jnp.concatenate([column, jnp.zeros((count, 128 - count), jnp.int32)], axis=1)
        column = jnp.concatenate([column, jnp.zeros((128 - count, 128), jnp.int32)], axis=0)
        column = column.astype(F32).T[:count, :1]
        return jnp.concatenate(
            [jnp.where(column == ids[n : n + 1, :].astype(F32), 1.0, 0.0) for n in range(self.c)], axis=0
        ).astype(BF16)

    def block_table(self, matrix, out):
        p, size = self.p, out.shape[0]
        row = lax.broadcasted_iota(jnp.int32, (p, size), 0)
        node = lax.rem(lax.broadcasted_iota(jnp.int32, (p, size), 1), p)
        tile = jnp.zeros((p, size), F32)
        for a in range(p):
            line = jnp.zeros((p, size), F32)
            for i in range(p):
                line = jnp.where(node == i, float(matrix[a, i]), line)
            tile = jnp.where(row == a, line, tile)
        whole = jnp.concatenate([tile] * (size // p), axis=0)
        same = lax.broadcasted_iota(jnp.int32, (size, size), 0) // p == (
            lax.broadcasted_iota(jnp.int32, (size, size), 1) // p
        )
        upper, lower = split(jnp.where(same, whole, 0.0))
        out[...] = jnp.concatenate([upper, upper, lower], axis=1)

    def spread_tables(self, out3, out4, square):
        self.block_table(self.squared.T, square)
        p, ey, ez = self.p, self.ey, self.ez
        for out, width, step, offset, first in (
            (out3, self.w3, self.step3, HALO, 0),
            (out4, self.w4, self.step4, 0, self.c * ey),
        ):
            row = lax.broadcasted_iota(jnp.int32, (ey * ez * p, width), 0)
            lane = lax.broadcasted_iota(jnp.int32, (1, width), 1)
            g = lane // step - offset
            inside = (g >= 0) & (g < ez) & (lax.rem(lane, step) >= first)
            same = row // p == jnp.where(inside, lax.rem(lane, ey) * ez + g, -1)
            node = lax.rem(row, p)
            for k in range(p):
                out[:, k * width : (k + 1) * width] = jnp.where(same & (node == k), 1.0, 0.0).astype(BF16)

    def prepare(self, n_x, n_y, *refs):
        geometry, viscosity, spread, table, right, slots, ids, square = refs[:8]
        s4, hot3, fields = refs[8:11]
        refs = refs[11:]
        x_out, y_out, work = refs[:n_x], refs[n_x : n_x + n_y], refs[n_x + n_y]
        p, c, block, rows, ey = self.p, self.c, self.block, self.rows, self.ey
        face = ey * p
        wjk, end_j, end_k = (table[n * face : (n + 1) * face, :] for n in range(3))
        stiff, second, third, rest = [], [], [], []
        for i in range(p):
            xx, yy, zz, xy, xz, yz = (geometry[q, i] for q in range(6))
            quadrature = float(self.weights[i]) * wjk
            weighted = quadrature * viscosity[i]
            mass = (helm_coefficient * quadrature) * (
                xx * (yy * zz - yz * yz) - xy * (xy * zz - yz * xz) + xz * (xy * yz - yy * xz)
            )
            cross = end_j * end_k * yz
            end = float(self.end[i])
            if end != 0.0:
                cross = cross + end * (end_j * xy + end_k * xz)
            entries = [weighted * entry for entry in (xx, yy, zz, xy, xz, yz)] + [mass]
            for q, entry in enumerate(entries):
                fields[q, i * face : (i + 1) * face, :] = entry
            stiff.append(entries[0])
            second.append(entries[1])
            third.append(entries[2])
            rest.append((2.0 * weighted) * cross + mass)
        upper, lower = split(jnp.concatenate(second, axis=0))
        diagonal = jnp.dot(
            square[...], jnp.concatenate([upper, lower, upper], axis=0), preferred_element_type=F32
        )
        upper, lower = split(jnp.concatenate(third, axis=0))
        diagonal = diagonal + lax.dot_general(
            jnp.concatenate([upper, lower, upper], axis=1),
            square[...],
            (((1,), (1,)), ((), ())),
            preferred_element_type=F32,
        )
        first = self.contract(stiff, self.squared.T)
        diagonal = diagonal + jnp.concatenate([x + y for x, y in zip(first, rest)], axis=0)
        width = diagonal.shape[-1]
        value = diagonal.reshape(p, ey, p, width)
        value = jnp.concatenate([value[:, f].reshape(block, width) for f in range(ey)], axis=1)

        def store(k, part):
            work[pl.ds(k, block, stride=p), :] = part

        self.by_nodes(*split(value), spread, self.w4, store)
        hot = self.one_hot(slots, ids)
        hot3[...] = self.one_hot(slots, ids[c:, :])
        total = work[...]
        for part in split(right[...].reshape(hot.shape[0], rows)):
            total = total + lax.dot_general(
                part, hot, (((0,), (0,)), ((), ())), preferred_element_type=F32
            )
        s4[...] = total
        self.fold_second(s4)
        last = self.n4 - self.step4
        self.fold_third(s4, self.step4, lambda l: l < last, lambda l: (l >= self.step4) & (l < self.n4))
        self.emit_first((s4[:block, :], s4[rows - block :, :]), x_out)
        self.emit_second(s4, y_out)

    def convert(self, n_y, n_z, *refs):
        fields, spread, dirichlet, s4 = refs[:4]
        g, ind = refs[4:6]
        refs = refs[6:]
        y_out, z_out, packed = refs[:n_y], refs[n_y : n_y + n_z], refs[n_y + n_z : n_y + 2 * n_z]
        upper, lower = refs[n_y + 2 * n_z :]
        p, c, block, ey = self.p, self.c, self.block, self.ey
        width = fields.shape[-1]
        for q in range(FIELDS):
            value = fields[q].reshape(p, ey, p, width)
            for f in range(ey):
                at = (slice(q * block, (q + 1) * block), slice(f * width, (f + 1) * width))
                upper[at], lower[at] = split(value[:, f].reshape(block, width))
        first_flag, flags = FIELDS * block, 2 * p
        for cc in range(c):
            for f in range(ey):
                at = slice(f * p, (f + 1) * p)
                face = jnp.concatenate([dirichlet[0, cc, at, :], dirichlet[1, cc, at, :]], axis=0)
                to = slice(first_flag + cc * flags, first_flag + (cc + 1) * flags)
                upper[to, f * width : (f + 1) * width] = face.astype(F32).astype(BF16)
                lower[to, f * width : (f + 1) * width] = jnp.zeros((flags, width), BF16)
        row = lax.broadcasted_iota(jnp.int32, (flags, self.w3), 0)
        lane = lax.broadcasted_iota(jnp.int32, (flags, self.w3), 1)
        ends = (lax.axis_index("gx") == 0, lax.axis_index("gx") == self.sizes["gx"] - 1)
        here = ((row < p) & ends[0]) | ((row >= p) & ends[1])
        owner = lax.rem(lane, self.step3) // ey

        def store(k, value):
            g[pl.ds(k, first_flag, stride=p), :] = value[:first_flag]
            total = jnp.zeros((flags, self.w3), F32)
            for cc in range(c):
                at = first_flag + cc * flags
                total = jnp.where(owner == cc, value[at : at + flags], total)
            ind[pl.ds(k, flags, stride=p), :] = jnp.where(here, total, 0.0)

        self.by_nodes(upper[...], lower[...], spread, self.w3, store)
        self.pack_fields(fields, z_out)
        self.fold_second(ind)
        first_own, end_own = HALO * self.step3, self.n3 - HALO * self.step3
        self.fold_third(
            ind,
            self.step3,
            lambda l: (l >= first_own) & (l < end_own - self.step3),
            lambda l: (l >= first_own + self.step3) & (l < end_own),
        )
        for out, (up, _, _) in zip(y_out, roles("gy", self.sizes["gy"])):
            for n in range(2):
                start = n * block
                out[n * p : (n + 1) * p, :] = jnp.where(
                    up, ind[start + block - p : start + block, :], ind[start : start + p, :]
                )
        for out, (up, _, _) in zip(packed, roles("gz", self.sizes["gz"])):
            self.pack(out, s4, block, 0, self.n4 - self.halo4, up, 0)
            self.pack(out, ind, p, first_own, end_own - first_own, up, block)

    def halo_fields(self, n_z, *refs):
        own, halo = refs[:2]
        z_in, g, terms = refs[2 : 2 + n_z], refs[2 + n_z], refs[3 + n_z]
        p, block, ey, part = self.p, self.block, self.ey, self.part
        sides = both_sides([z[...] for z in z_in], roles("gz", self.sizes["gz"]))
        width = sides[0].shape[-1]
        sides = [side.reshape(p, ey, p, width) for side in sides]
        lane = lax.broadcasted_iota(jnp.int32, (block, width), 1)
        for q in range(FIELDS):
            value = jnp.zeros((block, width), F32)
            for side in range(2):
                for f in range(ey):
                    to = (side * ey + f) * part
                    shift = (to - q * part) % width
                    x = sides[side][:, f].reshape(block, width)
                    x = pltpu.roll(x, shift, 1) if shift else x
                    value = jnp.where((lane >= to) & (lane < to + part), x, value)
            upper, lower = split(value)
            lower = pltpu.roll(lower.astype(F32), width // 2, 1).astype(BF16)
            terms[q * block : (q + 1) * block, :] = upper + lower

        for k in range(0, p, 2):
            columns = halo[:, k * self.w3 : (k + 2) * self.w3]
            both = jnp.dot(terms[...], columns, preferred_element_type=F32)
            for n in range(2):
                at = pl.ds(k + n, FIELDS * block, stride=p)
                g[at, :] = own[at, :] + both[:, n * self.w3 : (n + 1) * self.w3]

    def coefficients(self, low, high, coef):
        top, bottom = jnp.full((8, 128), high[0], F32), jnp.full((8, 128), low[0], F32)
        midpoint, halfwidth = (top + bottom) * 0.5, (top - bottom) * 0.5
        ratio = midpoint / halfwidth
        damping = 1.0 / ratio
        coef[0:8, :] = 1.0 / midpoint
        for n in range(ITERS - 1):
            following = 1.0 / (2.0 * ratio - damping)
            coef[8 * (2 * n + 1) : 8 * (2 * n + 2), :] = following * damping
            coef[8 * (2 * n + 2) : 8 * (2 * n + 3), :] = 2.0 * following / halfwidth
            damping = following

    def join(self, n_x, n_y, *refs):
        x_in, refs = refs[:n_x], refs[n_x:]
        y_raw, y_more, y_out = refs[:n_y], refs[n_y:-n_y], refs[-n_y:]
        p, block, ey = self.p, self.block, self.ey
        low, high = both_sides([x[...] for x in x_in], roles("gx", self.sizes["gx"]))
        for n, (up, _, _) in enumerate(roles("gy", self.sizes["gy"])):
            face = y_raw[n][...]
            width = face.shape[-1]
            if n_x:
                first, last = (jnp.where(up, x[block - p :], x[:p]) for x in (low, high))
                face = jnp.concatenate([face[:p] + first, face[p : block - p], face[block - p :] + last], axis=0)
            if y_more:
                face = jnp.concatenate([face, y_more[n][...]], axis=0)
            if ey == 1:
                y_out[n][...] = face
                continue
            half = face.shape[0] // 2
            first, second = face[:half], face[half:]
            f = lax.rem(lax.broadcasted_iota(jnp.int32, first.shape, 1), ey)
            below = jnp.where(f == 0, pltpu.roll(first, width - (ey - 1), 1), 0.0) + jnp.where(
                f == 1, pltpu.roll(second, (width - (ey - 2)) % width, 1) if ey != 2 else second, 0.0
            )
            above = jnp.where(f == ey - 1, pltpu.roll(first, ey - 1, 1), 0.0) + jnp.where(
                f == ey - 2, pltpu.roll(second, ey - 2, 1) if ey != 2 else second, 0.0
            )
            y_out[n][...] = jnp.where(up, below, above)

    def second_sides(self, received):
        role, ey = roles("gy", self.sizes["gy"]), self.ey
        faces = []
        for message, (_, from_high, _) in zip(received, role):
            data = message[...]
            if ey > 1:
                width = data.shape[-1]
                f = lax.rem(lax.broadcasted_iota(jnp.int32, data.shape, 1), ey)
                beside = jnp.where(from_high, pltpu.roll(data, 1, 1), pltpu.roll(data, width - 1, 1))
                here = f == jnp.where(from_high, ey - 1, 0)
                data = jnp.concatenate([jnp.where(here, x, 0.0) for x in (data, beside)], axis=0)
            faces.append(data)
        return both_sides(faces, role)

    def pack(self, out, u, count, first, last, up, start):
        p, width, size = self.p, self.w4, self.halo4
        lane = lax.broadcasted_iota(jnp.int32, (count, width), 1)
        for section in range(0, u.shape[0] // count, p):
            total = jnp.zeros((count, width), F32)
            for n in range(p):
                at, shift = (section + n) * count, n * size
                x = u[at : at + count, :]
                below = pltpu.roll(x, (shift - first) % width, 1) if (shift - first) % width else x
                above = pltpu.roll(x, (shift - last) % width, 1)
                here = (lane >= shift) & (lane < shift + size)
                total = jnp.where(here, jnp.where(up, above, below), total)
            row = start + section // p * count
            out[row : row + count, :] = total

    def pack_second(self, n_x, n_y, n_z, *refs):
        x_in, y_in, refs = refs[:n_x], refs[n_x : n_x + n_y], refs[n_x + n_y :]
        z_in, z_out = refs[:n_z], refs[n_z:]
        p, block, width, size = self.p, self.block, self.w4, self.halo4
        ends = both_sides([x[...] for x in x_in], roles("gx", self.sizes["gx"]))
        low, high = self.second_sides(y_in)
        halo3 = HALO * self.step3
        lane = lax.broadcasted_iota(jnp.int32, (p, width), 1)
        for packed, out, (up, _, _) in zip(z_in, z_out, roles("gz", self.sizes["gz"])):
            out[...] = packed[...]
            if n_x:
                total = 0.0
                for x, group in zip(ends, (0, p - 1)):
                    shift = group * size
                    below = pltpu.roll(x, shift, 1) if shift else x
                    back = (shift - self.n4 + size) % width
                    above = pltpu.roll(x, back, 1) if back else x
                    wide = lax.broadcasted_iota(jnp.int32, x.shape, 1)
                    here = (wide >= shift) & (wide < shift + size)
                    total = total + jnp.where(here, jnp.where(up, above, below), 0.0)
                out[:block, :] += total
            if not n_y:
                continue
            for face, row in ((low, 0), (high, block - p)):
                total = jnp.zeros((p, width), F32)
                for n in range(p):
                    shift = n * size
                    x = face[n * p : (n + 1) * p]
                    below = pltpu.roll(x, shift, 1) if shift else x
                    above = pltpu.roll(x, (shift - self.n4 + size) % width, 1)
                    here = (lane >= shift) & (lane < shift + size)
                    total = jnp.where(here, jnp.where(up, above, below), total)
                out[row : row + p, :] += total
            for n in range(2):
                row = block + n * p
                for face, group in ((low, 0), (high, p - 1)):
                    shift = group * size
                    x = face[row : row + p]
                    below = pltpu.roll(x, (shift - halo3) % width, 1)
                    above = pltpu.roll(x, (shift - self.n3 + 2 * halo3) % width, 1)
                    here = (lane >= shift) & (lane < shift + size)
                    out[row : row + p, :] += jnp.where(here, jnp.where(up, above, below), 0.0)

    def own(self, n_x, n_y, *refs):
        s4, ind, widen = refs[:3]
        x_in, y_in, (r, scale, flag, work) = refs[3 : 3 + n_x], refs[3 + n_x : 3 + n_x + n_y], refs[3 + n_x + n_y :]
        p, block, rows, w3 = self.p, self.block, self.rows, self.w3
        work[...] = s4[...]
        if n_x:
            low, high = both_sides([x[...] for x in x_in], roles("gx", self.sizes["gx"]))
            work[:block, :] += low
            work[rows - block :, :] += high
        flag[...] = ind[...]
        if n_y:
            low, high = self.second_sides(y_in)
            for u, first, count in ((work, 0, p), (flag, p, 2)):
                for i in range(count):
                    at, end, row = i * block, (i + 1) * block, (first + i) * p
                    u[at : at + p, :] += low[row : row + p]
                    u[end - p : end, :] += high[row : row + p]
        both = dot2(work[...], widen[: self.w4, :])
        r[...] = both[:, :w3]
        scale[...] = both[:, w3:]

    def start(self, n_x, n_z, *refs):
        r_own, diagonal_own, flag_own, g, widen, ahead, back = refs[:7]
        z_in = refs[7 : 7 + n_z]
        t, scale, ends, f1, f2, f3 = refs[7 + n_z : 13 + n_z]
        x_out, refs = refs[13 + n_z : 13 + n_z + n_x], refs[13 + n_z + n_x :]
        beside, r, flag, slope, third = refs
        p, block, rows, w3, w4 = self.p, self.block, self.rows, self.w3, self.w4
        step, first_own, end_own = self.step3, HALO * self.step3, self.n3 - HALO * self.step3
        size, part = self.sizes["gz"], self.halo4
        if n_z:
            low, high = both_sides([z[...] for z in z_in], roles("gz", size))
        else:
            low = high = jnp.zeros((block + 2 * p, w4), F32)
        lane = lax.broadcasted_iota(jnp.int32, (block, w4), 1)
        for n in range(p):
            first = pltpu.roll(low[:block], w4 - n * part, 1) if n else low[:block]
            second = pltpu.roll(high[:block], (part - n * part) % w4, 1) if n != 1 else high[:block]
            beside[n * block : (n + 1) * block, :] = jnp.where(
                lane < part, first, jnp.where(lane < 2 * part, second, 0.0)
            )
        both = dot2(beside[...], widen[w4:, :])
        r[...] = r_own[...] + both[:, :w3]
        scale[...] = diagonal_own[...] + both[:, w3:]
        lane = lax.broadcasted_iota(jnp.int32, (p, w3), 1)
        for n in range(2 * p):
            row, shift = block + n // p * p, n % p * part
            first = pltpu.roll(low[row : row + p], w3 - shift, 1) if shift else low[row : row + p]
            second = pltpu.roll(high[row : row + p], (end_own - shift) % w3, 1)
            flag[n * p : (n + 1) * p, :] = jnp.where(
                lane < first_own,
                first,
                jnp.where(lane < end_own, flag_own[n * p : (n + 1) * p, :], jnp.where(lane < self.n3, second, 0.0)),
            )
        for u in (r, scale, flag):
            self.fold_third(
                u,
                step,
                lambda l: ((l >= first_own - step) & (l < first_own)) | ((l >= end_own - step) & (l < end_own)),
                lambda l: ((l >= first_own) & (l < first_own + step)) | ((l >= end_own) & (l < end_own + step)),
            )
        index = lax.axis_index("gz")
        begin = jnp.where(index > 0, 0, first_own)
        end = jnp.where(index < size - 1, self.n3, end_own)
        lane = lax.broadcasted_iota(jnp.int32, (block, w3), 1)
        valid = (lane >= begin) & (lane < end)
        for i in range(p):
            at = slice(i * block, (i + 1) * block)
            factor = jnp.where(valid, 1.0 / jnp.where(valid, scale[at, :], 1.0), 0.0)
            if i in (0, p - 1):
                row = 0 if i == 0 else block
                factor = jnp.where(flag[row : row + block, :] > 0.5, 0.0, factor)
            scale[at, :] = factor
            t[at, :] = factor * r[at, :]
        self.fluxes(t, g, f1, f2, f3, slope, third, ahead)
        self.end_planes(t, g, ends, f1, f2, f3, slope, third, back)
        self.iteration_fold(ends)
        self.emit_first((ends[:block, :], ends[block:, :]), x_out)

    def factors(self, coef, n):
        rows = [coef[8 * m : 8 * m + 1, :] for m in (0, 2 * n + 1, 2 * n + 2)]
        return (rows[0] if n == 0 else None), rows[1], rows[2]

    def shares(self, faces, scale, image, at):
        low, high = faces
        p, block = self.p, self.block
        i = at // block
        out = []
        for start, face in ((at, low), (at + block - p, high)):
            value = scale[start : start + p, :] * face[i * p : (i + 1) * p]
            out.append((start, -value if image is None else -image * value))
        return out

    def preview(self, n_x, n_y, n, last, *refs):
        t, t_old, d, scale, v, coef = refs[:6]
        refs = refs[6:]
        x_in, y_old, refs = refs[:n_x], refs[n_x : n_x + (n_y if n else 0)], refs[n_x + (n_y if n else 0) :]
        p, block, rows = self.p, self.block, self.rows
        image, keep, gain = self.factors(coef, n)
        start = coef[0:1, :]
        if last:
            hot, out, t_new, field = refs
        else:
            g, ahead, back, t_new, d_new, f1, f2, f3, ends, slope, third = refs
        low, high = both_sides([x[...] for x in x_in], roles("gx", self.sizes["gx"]))
        if n:
            faces = self.second_sides(y_old) if n_y else None
            image_old = self.factors(coef, n - 1)[0]
        for i in range(p):
            at = slice(i * block, (i + 1) * block)
            value = v[at, :]
            if n_x and i in (0, p - 1):
                value = value + (low if i == 0 else high)
            value = scale[at, :] * value
            t_new[at, :] = t_old[at, :] - (value if image is None else image * value)
            if n and n_y:
                for row, share in self.shares(faces, scale, image_old, i * block):
                    t_new[row : row + p, :] += share
            direction = d[at, :] if n else start * t[at, :]
            following = keep * direction + gain * t_new[at, :]
            if last:
                field[at, :] = start * t[at, :] + following + (direction if n else 0.0)
            else:
                d_new[at, :] = following
        if last:
            out[...] = self.by_slots(hot, field[...])
        else:
            self.fluxes(d_new, g, f1, f2, f3, slope, third, ahead)
            self.end_planes(d_new, g, ends, f1, f2, f3, slope, third, back)

    def by_slots(self, hot, field):
        return lax.dot_general(
            jnp.concatenate([hot[...], hot[...]], axis=1),
            jnp.concatenate(split(field), axis=1),
            (((1,), (1,)), ((), ())),
            preferred_element_type=F32,
        )

    def middle(self, n_x, n_y, n, *refs):
        part, scale, g, coef, ahead, back = refs[:6]
        y_in, refs = refs[6 : 6 + n_y], refs[6 + n_y :]
        ends, shares, refs = refs[0], refs[1], refs[2:]
        x_out, (f1, f2, f3, third) = refs[:n_x], refs[n_x:]
        p, block, rows = self.p, self.block, self.rows
        image, _, gain = self.factors(coef, n)
        ends[...] = part[...]
        if n_y:
            faces = self.second_sides(y_in)
            for i in range(p):
                for m, (_, share) in enumerate(self.shares(faces, scale, image, i * block)):
                    shares[(2 * i + m) * p : (2 * i + m + 1) * p, :] = gain * share

            def write(i, j, values):
                f1[i * block + j * p : i * block + (j + 1) * p, :] = values[0]
                if len(values) > 1:
                    row = (block if i else 0) + j * p
                    f2[row : row + p, :], f3[row : row + p, :] = values[1], values[2]

            self.share_fluxes(shares, g, third, ahead, False, write)
            self.along_k(f3, back, third, 0, 2 * block)
            for m, i in enumerate((0, p - 1)):
                at = slice(m * block, (m + 1) * block)
                ends[at, :] += self.along_j(f2[at, :], self.forward.T) + third[at, :]
                for n_face, j in enumerate((0, p - 1)):
                    row, at = m * block + j * p, slice(i * block + j * p, i * block + (j + 1) * p)
                    line = (2 * i + n_face) * p
                    ends[row : row + p, :] += self.rows_of(g, 6, at) * shares[line : line + p, :]
            for j in range(p):
                x = [f1[i * block + j * p : i * block + (j + 1) * p, :] for i in range(p)]
                for row, value in zip((j * p, block + j * p), self.contract(x, self.forward.T, (0,))):
                    ends[row : row + p, :] += value
        else:
            shares[...] = jnp.zeros(shares.shape, F32)
        self.iteration_fold(ends)
        self.emit_first((ends[:block, :], ends[block:, :]), x_out)

    def finish(self, n_y, n, *refs):
        part, scale, coef, hot = refs[:4]
        y_in, (out, field) = refs[4 : 4 + n_y], refs[4 + n_y :]
        value = part[...]
        image, _, gain = self.factors(coef, n)
        if n_y:
            faces = self.second_sides(y_in)
            field[...] = jnp.zeros(field.shape, F32)
            for i in range(self.p):
                for row, share in self.shares(faces, scale, image, i * self.block):
                    field[row : row + self.p, :] = gain * share
            value = value + self.by_slots(hot, field[...])
        out[...] = value.reshape(out.shape)


def shards(sizes, right_side, geometry, viscosity, eig_low, eig_high, element_slot, dirichlet):
    plan = Plan(right_side.shape[0], viscosity.shape, sizes)
    p, block, rows, w3, w4 = plan.p, plan.block, plan.rows, plan.w3, plan.w4
    x_pairs = pairings(("gx",), (sizes["gx"],), 0)
    y_pairs = pairings(("gy",), (sizes["gy"],), 0)
    z_pairs = pairings(("gx", "gz"), (sizes["gx"], sizes["gz"]), 1)
    n_x, n_y, n_z = len(x_pairs), len(y_pairs), len(z_pairs)

    def send(arrays, axis, pairs):
        return [lax.ppermute(x, axis, pair) for x, pair in zip(arrays, pairs)]

    def shape(*size, dtype=F32):
        return jax.ShapeDtypeStruct(size, dtype)

    def call(kernel, outputs, operands, scratch=(), spaces={}, flops=0, name=None):
        specs = [pl.BlockSpec(memory_space=spaces.get(n, pltpu.VMEM)) for n in range(len(operands))]
        return list(
            pl.pallas_call(
                kernel,
                out_shape=list(outputs),
                in_specs=specs,
                out_specs=[pl.BlockSpec(memory_space=pltpu.VMEM)] * len(outputs),
                scratch_shapes=list(scratch),
                compiler_params=pltpu.CompilerParams(vmem_limit_bytes=VMEM_BYTES),
                cost_estimate=pl.CostEstimate(flops=flops, bytes_accessed=0, transcendentals=0),
                name=name,
            )(*operands)
        )

    def vmem(*size, dtype=F32):
        return pltpu.VMEM(size, dtype)

    lanes = plan.ez * p
    ahead, back = jnp.asarray(plan.third[0]), jnp.asarray(plan.third[1])
    field3, field4 = shape(rows, w3), shape(rows, w4)
    elements = element_slot.shape[-1]
    spread3, spread4, square = call(
        plan.spread_tables,
        [shape(plan.ey * lanes, p * w, dtype=BF16) for w in (w3, w4)]
        + [shape(*plan.third[0].shape, dtype=BF16)],
        (),
        flops=FLOPS,
        name="spread_tables",
    )
    results = call(
        functools.partial(plan.prepare, n_x, n_y),
        [field4, shape(plan.c * elements, w3, dtype=BF16), shape(FIELDS, p * plan.ey * p, lanes)]
        + [shape(block, w4)] * (n_x + n_y),
        (
            geometry,
            viscosity,
            spread4,
            jnp.asarray(plan.face_table),
            jnp.swapaxes(right_side, 1, 2),
            element_slot,
            jnp.asarray(plan.ids),
            square,
        ),
        scratch=[vmem(rows, w4)],
        name="prepare",
    )
    s4, hot3, fields = results[:3]
    x_out, y_raw = results[3 : 3 + n_x], results[3 + n_x :]
    x_in = send(x_out, "gx", x_pairs)

    lhs = FIELDS * block + 2 * plan.c * p
    results = call(
        functools.partial(plan.convert, n_y, n_z),
        [shape(FIELDS * rows, w3), shape(2 * block, w3)]
        + [shape(2 * p, w3)] * n_y
        + [shape(p * plan.ey * p, lanes)] * n_z
        + [shape(block + 2 * p, w4)] * n_z,
        (fields, spread3, dirichlet, s4),
        scratch=[vmem(lhs, plan.ey * lanes, dtype=BF16)] * 2,
        name="convert",
    )
    g, ind = results[:2]
    y_more, results = results[2 : 2 + n_y], results[2 + n_y :]
    z_fields, z_out = results[:n_z], results[n_z:]

    def joined(x_in, y_raw, y_more=()):
        if not y_raw:
            return []
        count = y_raw[0].shape[0] + (y_more[0].shape[0] if y_more else 0)
        faces = [shape(count // 2 if plan.ey > 1 else count, y.shape[1]) for y in y_raw]
        return call(functools.partial(plan.join, n_x, n_y), faces, x_in + y_raw + list(y_more), name="join")

    y_in = send(joined(x_in, y_raw, y_more), "gy", y_pairs)
    z_fields = send(z_fields, ("gx", "gz"), z_pairs)
    if n_z:
        g = call(
            functools.partial(plan.halo_fields, n_z),
            [shape(FIELDS * rows, w3)],
            [g, jnp.asarray(plan.halo)] + z_fields,
            scratch=[vmem(FIELDS * block, lanes, dtype=BF16)],
            name="halo_fields",
        )[0]
    if n_z:
        z_out = call(
            functools.partial(plan.pack_second, n_x, n_y, n_z),
            [shape(*z.shape) for z in z_out],
            x_in + y_in + z_out,
            flops=FLOPS,
            name="pack_second",
        )
    z_in = send(z_out, ("gx", "gz"), z_pairs)
    widen = jnp.asarray(plan.widen)
    own = call(
        functools.partial(plan.own, n_x, n_y),
        [field3, field3, shape(2 * block, w3)],
        [s4, ind, widen] + x_in + y_in,
        scratch=[vmem(rows, w4)],
        name="own",
    )

    fluxes = [shape(2 * block, w3)] + [field3] * 3 + [shape(block, w3)] * n_x
    results = call(
        functools.partial(plan.start, n_x, n_z),
        [field3] * 2 + fluxes,
        own + [g, widen, ahead, back] + z_in,
        scratch=[vmem(rows, w4), vmem(rows, w3), vmem(2 * block, w3)] + [vmem(rows, w3)] * 2,
        name="first_direction",
    )
    t, scale = results[:2]
    ends, f1, f2, f3 = results[2:6]
    x_out = results[6:]
    x_out, low, high = lax.optimization_barrier((x_out, eig_low, eig_high))
    coef = call(
        plan.coefficients,
        [shape(8 * (2 * ITERS - 1), 128)],
        (low, high),
        spaces={0: pltpu.SMEM, 1: pltpu.SMEM},
        name="coefficients",
    )[0]
    t_old, d, y_in = t, t, []
    for n in range(ITERS - 1):
        last = n == ITERS - 2
        x_in = send(x_out, "gx", x_pairs)
        outputs = [field3] + [shape(block, w3)] * n_y
        if n:
            results = call(
                functools.partial(plan.operator_second, n_x, n_y, True),
                outputs + [field3],
                [d, g, ends, f1, f2, f3, back, shares, ahead],
                scratch=[vmem(rows, w3)] * 4,
                name="operator_second",
            )
            v, y_raw, d = results[0], results[1 : 1 + n_y], results[1 + n_y]
        else:
            results = call(
                functools.partial(plan.operator_second, n_x, n_y, False),
                outputs,
                [d, g, ends, f1, f2, f3, back],
                scratch=[vmem(rows, w3)],
                name="operator_second",
            )
            v, y_raw = results[0], results[1:]
        y_old, y_in = y_in, send(joined(x_in, y_raw), "gy", y_pairs)
        results = call(
            functools.partial(plan.preview, n_x, n_y, n, last),
            [shape(plan.c * elements, rows)] if last else [field3] * 5 + [shape(2 * block, w3)],
            [t, t_old, d, scale, v, coef] + x_in + y_old + ([hot3] if last else [g, ahead, back]),
            scratch=[vmem(rows, w3)] * 2,
            name="preview",
        )
        if last:
            break
        t_old, d, f1, f2, f3, ends = results
        results = call(
            functools.partial(plan.middle, n_x, n_y, n),
            [shape(2 * block, w3)] * 2 + [shape(block, w3)] * n_x,
            [ends, scale, g, coef, ahead, back] + y_in,
            scratch=[vmem(rows, w3)] + [vmem(2 * block, w3)] * 3,
            name="direction",
        )
        ends, shares, x_out = results[0], results[1], results[2:]
    out = call(
        functools.partial(plan.finish, n_y, n),
        [shape(plan.c, elements, rows)],
        [results[0], scale, coef, hot3] + y_in,
        scratch=[vmem(rows, w3)],
        name="field",
    )[0]
    return jnp.swapaxes(out, 1, 2)


def solution(mesh):
    sizes = {name: mesh.shape[name] for name in ("gx", "gy", "gz")}
    return jax.shard_map(
        functools.partial(shards, sizes),
        mesh=mesh,
        in_specs=(
            P(None, None, ("gx", "gy", "gz")),
            P(None, "gx", "gy", "gz"),
            P("gx", "gy", "gz"),
            P(),
            P(),
            P(("gx", "gy", "gz"), None),
            P(None, None, "gy", "gz"),
        ),
        out_specs=P(None, None, ("gx", "gy", "gz")),
        check_vma=False,
    )
```

```python
import functools
import math

import jax
import jax.numpy as jnp
import numpy as np
from jax import lax
from jax.experimental import pallas as pl
from jax.experimental.pallas import tpu as pltpu
from jax.sharding import PartitionSpec as P

DEGREE = 7
ITERS = 3


helm_coefficient = 10.0


def legendre_pair(values, degree):
    previous = 0.0 * values + 1.0
    current = values.copy()
    for order in range(2, degree + 1):
        previous, current = (
            current,
            ((2 * order - 1) * values * current - (order - 1) * previous) / order,
        )
    return (current, previous)


def gll_tables(degree):
    start = np.cos(np.pi * np.arange(degree + 1) / degree)
    nodes_now = start.copy()
    for sweep in range(80):
        top_value, lower_value = legendre_pair(nodes_now, degree)
        nodes_now = nodes_now - (nodes_now * top_value - lower_value) / ((degree + 1) * top_value)
    gll_nodes = nodes_now[::-1].copy()
    gll_nodes[0] = -1.0
    gll_nodes[degree] = 1.0
    legendre_values = legendre_pair(gll_nodes, degree)[0]
    weights = 2.0 / (degree * (degree + 1) * legendre_values**2)
    differences = gll_nodes[:, None] - gll_nodes[None, :] + np.eye(degree + 1)
    derivative = legendre_values[:, None] / legendre_values[None, :] / differences
    derivative = derivative * (1.0 - np.eye(degree + 1))
    derivative[0, 0] = -degree * (degree + 1) / 4.0
    derivative[degree, degree] = degree * (degree + 1) / 4.0
    return (weights, derivative)


HALO = 2
FIELDS = 7
VMEM_BYTES = 40 * 1024 * 1024
FLOPS = 3 * 10**9
F32 = jnp.float32
BF16 = jnp.bfloat16


def pairings(names, sizes, dim):
    size = sizes[dim]
    if size == 1:
        return []
    if size % 2:
        shifts = (1, size - 1)
        partners = [[(i + shift) % size for i in range(size)] for shift in shifts]
    else:
        partners = [[i ^ 1 for i in range(size)]]
        if size > 2:
            partners.append([((i + 1) ^ 1) - 1 for i in range(size)])
    result = []
    for partner in partners:
        pairs = []
        for flat in range(math.prod(sizes)):
            place = list(np.unravel_index(flat, sizes))
            to = partner[place[dim]]
            if 0 <= to < size:
                place[dim] = to
            elif len(sizes) > 1 and sizes[1 - dim] % 2 == 0:
                place[1 - dim] ^= 1
            else:
                place[dim] = size - 1 - place[dim]
            pairs.append((flat, int(np.ravel_multi_index(place, sizes))))
        result.append(pairs)
    return result


def roles(name, size):
    if size == 1:
        return []
    index = lax.axis_index(name)
    low, high = index > 0, index < size - 1
    if size % 2:
        yes = index >= 0
        no = index < 0
        return [(yes, no, low), (no, yes, high)]
    even = lax.rem(index, 2) == 0
    odd = jnp.logical_not(even)
    result = [(even, even, index >= 0)]
    if size > 2:
        result.append((odd, odd, jnp.logical_or(jnp.logical_and(odd, high), jnp.logical_and(even, low))))
    return result


def both_sides(received, role):
    low, high = 0.0, 0.0
    for data, (_, from_high, used) in zip(received, role):
        high = high + jnp.where(jnp.logical_and(used, from_high), data, 0.0)
        low = low + jnp.where(jnp.logical_and(used, jnp.logical_not(from_high)), data, 0.0)
    return low, high


def split(x):
    upper = x.astype(BF16)
    return upper, (x - upper.astype(F32)).astype(BF16)


def dot2(x, table):
    return jnp.dot(
        jnp.concatenate(split(x), axis=1),
        jnp.concatenate([table, table], axis=0),
        preferred_element_type=F32,
    )


class Plan:
    def __init__(self, components, viscosity_shape, mesh_sizes):
        points = DEGREE + 1
        self.p, self.c = points, components
        self.sizes = mesh_sizes
        ex, ey, ez = (n // points for n in viscosity_shape)
        assert ex == 1 and ez >= HALO
        self.ey, self.ez = ey, ez
        self.rows = points**3
        self.block = points * points
        self.step3, self.step4 = components * ey, (components + 1) * ey
        self.n3, self.n4 = (ez + 2 * HALO) * self.step3, ez * self.step4
        self.w3, self.w4 = -(-self.n3 // 128) * 128, -(-self.n4 // 128) * 128
        self.halo4 = HALO * self.step4
        assert points * self.halo4 <= self.w4 and 2 * self.halo4 <= self.w4
        weights, derivative = gll_tables(DEGREE)
        self.forward = derivative.astype(np.float32)
        self.squared = self.forward * self.forward
        self.weights = weights.astype(np.float32)
        self.end = np.diagonal(self.forward)
        self.tables()

    def lane3(self, g, c, f):
        return (g + HALO) * self.step3 + c * self.ey + f

    def lane4(self, g, c, f):
        return g * self.step4 + c * self.ey + f

    def tables(self):
        p, c, ey, ez = self.p, self.c, self.ey, self.ez
        lanes = ez * p
        every = [(g, cc, f) for g in range(ez) for cc in range(c) for f in range(ey)]
        widen = np.zeros((2 * self.w4, 2 * self.w3), np.float32)
        ids = np.full((2 * c, 128, 128), -1, np.int32)
        for g, cc, f in every:
            widen[self.lane4(g, cc, f), self.lane3(g, cc, f)] = 1
            widen[self.lane4(g, c, f), self.w3 + self.lane3(g, cc, f)] = 1
            ids[cc, :, self.lane4(g, cc, f)] = f * ez + g
            ids[c + cc, :, self.lane3(g, cc, f)] = f * ez + g
        self.ids = np.ascontiguousarray(ids[:, :1, :]).reshape(2 * c, 128)
        part = HALO * p
        self.part = part
        assert FIELDS * part + part == lanes == p * ey * p and 2 * ey * part <= lanes // 2
        halo = np.zeros((lanes, p, self.w3), np.float32)
        for side, first in ((0, -HALO), (1, ez)):
            for g in range(HALO):
                for cc in range(c):
                    for f in range(ey):
                        at = self.lane3(first + g, cc, f)
                        row = self.w4 + side * self.halo4 + g * self.step4
                        widen[row + cc * ey + f, at] = 1
                        widen[row + c * ey + f, self.w3 + at] = 1
                        for k in range(p):
                            for half in range(2):
                                halo[half * lanes // 2 + (side * ey + f) * part + g * p + k, k, at] = 1
        self.halo = halo.reshape(lanes, -1).astype(jnp.bfloat16)
        self.widen = widen.astype(jnp.bfloat16)
        self.third = [self.block_terms(matrix) for matrix in (self.forward, self.forward.T)]
        face = (ey * p, lanes)
        second = np.tile(np.arange(p), ey)[:, None]
        third = np.tile(np.arange(p), ez)[None, :]
        self.face_table = np.concatenate(
            [
                self.weights[second] * self.weights[third],
                np.broadcast_to(self.end[second], face),
                np.broadcast_to(self.end[third], face),
            ]
        ).astype(np.float32)

    def block_terms(self, matrix):
        size = self.rows // 4
        blocks = np.kron(np.eye(size // self.p), matrix).astype(np.float32)
        upper = blocks.astype(jnp.bfloat16)
        lower = (blocks - upper.astype(np.float32)).astype(jnp.bfloat16)
        return np.concatenate([upper, upper, lower], axis=1)


    def contract(self, x, matrix, wanted=None):
        p = self.p
        sign = 1.0 if matrix[0, 0] * matrix[p - 1, p - 1] > 0 else -1.0
        half = p // 2
        sums = [x[i] + x[p - 1 - i] for i in range(half)]
        differences = [x[i] - x[p - 1 - i] for i in range(half)]
        out = [None] * p
        for a in range(half) if wanted is None else wanted:
            even, odd = None, None
            for i in range(half):
                first, second = float(matrix[a, i]), float(matrix[a, p - 1 - i])
                even = self.gather(even, 0.5 * (first + second), sums[i])
                odd = self.gather(odd, 0.5 * (first - second), differences[i])
            out[a] = odd + even
            out[p - 1 - a] = even - odd if sign > 0 else odd - even
        return [x for x in out if x is not None]

    @staticmethod
    def gather(total, factor, x):
        if factor == 0.0:
            return total
        return factor * x if total is None else total + factor * x

    def along_j(self, x, matrix):
        x = x.reshape(self.p, self.p, x.shape[-1])
        return jnp.concatenate(self.contract([x[j] for j in range(self.p)], matrix), axis=0)

    def along_i(self, source, matrix, write):
        p, block = self.p, self.block
        for j in range(p):
            rows = [i * block + j * p for i in range(p)]
            for row, value in zip(rows, self.contract([source[r : r + p, :] for r in rows], matrix)):
                write(row, value)

    def along_k(self, source, table, out, start, end):
        size = table.shape[0]
        width = source.shape[-1]
        while start < end:
            count = min(2, (end - start) // size)
            pieces = [split(source[start + n * size : start + (n + 1) * size, :]) for n in range(count)]
            upper, lower = (jnp.concatenate([piece[n] for piece in pieces], axis=1) for n in range(2))
            both = jnp.dot(
                table[...], jnp.concatenate([upper, lower, upper], axis=0), preferred_element_type=F32
            )
            for n in range(count):
                out[start + n * size : start + (n + 1) * size, :] = both[:, n * width : (n + 1) * width]
            start += count * size

    def rows_of(self, g, q, at):
        return g[q * self.rows + at.start : q * self.rows + at.stop, :]

    def fluxes(self, v, g, f1, f2, f3, slope, third, ahead):
        p, block, rows = self.p, self.block, self.rows

        def store(row, value):
            slope[row : row + p, :] = value

        self.along_i(v, self.forward, store)
        self.along_k(v, ahead, third, 0, rows)
        for i in range(p):
            at = slice(i * block, (i + 1) * block)
            x, s1, s3 = v[at, :], slope[at, :], third[at, :]
            s2 = self.along_j(x, self.forward)
            xy, xz, yz = (self.rows_of(g, q, at) for q in (3, 4, 5))
            f1[at, :] = self.rows_of(g, 0, at) * s1 + xy * s2 + xz * s3
            f2[at, :] = xy * s1 + self.rows_of(g, 1, at) * s2 + yz * s3
            f3[at, :] = xz * s1 + yz * s2 + self.rows_of(g, 2, at) * s3

    def share_fluxes(self, shares, g, third, ahead, whole, write):
        p, block = self.p, self.block
        x = shares[...]
        ends = [[x[(2 * i + n) * p : (2 * i + n + 1) * p] for i in range(p)] for n in range(2)]
        s1 = [self.contract(column, self.forward) for column in ends]
        self.along_k(shares, ahead, third, 0, 2 * block)
        for i in range(p):
            first, last = ends[0][i], ends[1][i]
            count = 3 if whole or i in (0, p - 1) else 1
            for j in range(p):
                at = slice(i * block + j * p, i * block + (j + 1) * p)
                s2 = float(self.forward[j, 0]) * first + float(self.forward[j, p - 1]) * last
                rows = ((0, 3, 4), (3, 1, 5), (4, 5, 2))[:count]
                values = [self.rows_of(g, row[1], at) * s2 for row in rows]
                if j in (0, p - 1):
                    n = int(j > 0)
                    line = (2 * i + n) * p
                    e1, e3 = s1[n][i], third[line : line + p, :]
                    values = [
                        value + self.rows_of(g, row[0], at) * e1 + self.rows_of(g, row[2], at) * e3
                        for value, row in zip(values, rows)
                    ]
                write(i, j, values)

    def end_planes(self, v, g, ends, f1, f2, f3, slope, third, back):
        p, block, rows = self.p, self.block, self.rows
        for n, start in enumerate((0, rows - block)):
            at = slice(start, start + block)
            ends[n * block : (n + 1) * block, :] = (
                self.along_j(f2[at, :], self.forward.T) + self.rows_of(g, 6, at) * v[at, :]
            )
            slope[n * block : (n + 1) * block, :] = f3[at, :]
        self.along_k(slope, back, third, 0, 2 * block)
        for j in range(p):
            x = [f1[i * block + j * p : i * block + (j + 1) * p, :] for i in range(p)]
            first, last = self.contract(x, self.forward.T, (0,))
            for row, value in ((j * p, first), (block + j * p, last)):
                ends[row : row + p, :] += value + third[row : row + p, :]

    def operator_second(self, n_x, n_y, shared, *refs):
        v, g, ends, f1, f2, f3, back = refs[:7]
        refs = refs[7:]
        p, block, rows = self.p, self.block, self.rows
        if shared:
            shares, ahead, out = refs[:3]
            y_out, (v_new, third, *new) = refs[3 : 3 + n_y], refs[3 + n_y :]

            def write(i, j, values):
                at = slice(i * block + j * p, i * block + (j + 1) * p)
                for f_old, f_new, value in zip((f1, f2, f3), new, values):
                    f_new[at, :] = f_old[at, :] + value

            self.share_fluxes(shares, g, third, ahead, True, write)
            v_new[...] = v[...]
            for i in range(p):
                for m, row in enumerate((i * block, (i + 1) * block - p)):
                    v_new[row : row + p, :] += shares[(2 * i + m) * p : (2 * i + m + 1) * p, :]
            v, (f1, f2, f3) = v_new, new
        else:
            out, y_out, third = refs[0], refs[1 : 1 + n_y], refs[1 + n_y]
        out[:block, :], out[rows - block :, :] = ends[:block, :], ends[block:, :]
        self.along_k(f3, back, third, block, rows - block)
        for i in range(1, p - 1):
            at = slice(i * block, (i + 1) * block)
            out[at, :] = (
                self.along_j(f2[at, :], self.forward.T) + self.rows_of(g, 6, at) * v[at, :] + third[at, :]
            )
        for j in range(p):
            at = [slice(i * block + j * p, i * block + (j + 1) * p) for i in range(p)]
            values = self.contract([f1[r, :] for r in at], self.forward.T, range(1, p // 2))
            for r, value in zip(at[1 : p - 1], values):
                out[r, :] += value
        self.iteration_fold(out.at[block : rows - block, :])
        self.emit_second(out, y_out)

    def fold_second(self, u):
        if self.ey == 1:
            return
        p, width = self.p, u.shape[-1]
        lane = lax.broadcasted_iota(jnp.int32, (p, width), 1)
        f = lax.rem(lane, self.ey)
        for start in range(0, u.shape[0], self.block):
            first, last = u[start : start + p, :], u[start + self.block - p : start + self.block, :]
            u[start + self.block - p : start + self.block, :] = last + jnp.where(
                f < self.ey - 1, pltpu.roll(first, width - 1, 1), 0.0
            )
            u[start : start + p, :] = first + jnp.where(f > 0, pltpu.roll(last, 1, 1), 0.0)

    def fold_third(self, u, step, take_upper, take_lower):
        p, (rows, width) = self.p, u.shape
        count = rows // p
        lane = lax.broadcasted_iota(jnp.int32, (count, width), 1)
        first, last = u[pl.ds(0, count, stride=p), :], u[pl.ds(p - 1, count, stride=p), :]
        u[pl.ds(p - 1, count, stride=p), :] = last + jnp.where(
            take_upper(lane), pltpu.roll(first, width - step, 1), 0.0
        )
        u[pl.ds(0, count, stride=p), :] = first + jnp.where(
            take_lower(lane), pltpu.roll(last, step, 1), 0.0
        )

    def emit_first(self, ends, x_out):
        for out, (high, _, _) in zip(x_out, roles("gx", self.sizes["gx"])):
            out[...] = jnp.where(high, ends[1], ends[0])

    def emit_second(self, u, y_out):
        p, block = self.p, self.block
        for out, (high, _, _) in zip(y_out, roles("gy", self.sizes["gy"])):
            for i in range(p):
                start = i * block
                out[i * p : (i + 1) * p, :] = jnp.where(
                    high, u[start + block - p : start + block, :], u[start : start + p, :]
                )

    def iteration_fold(self, u):
        self.fold_second(u)
        last = self.n3 - self.step3
        self.fold_third(u, self.step3, lambda l: l < last, lambda l: (l >= self.step3) & (l < self.n3))


    def pack_fields(self, fields, out):
        part = self.part
        for target, (high, _, _) in zip(out, roles("gz", self.sizes["gz"])):
            _, rows, width = fields.shape
            lane = lax.broadcasted_iota(jnp.int32, (rows, width), 1)
            total = jnp.zeros((rows, width), F32)
            for q in range(FIELDS):
                start = q * part
                upper = pltpu.roll(fields[q], start + part, 1)
                lower = pltpu.roll(fields[q], start, 1) if start else fields[q]
                here = (lane >= start) & (lane < start + part)
                total = jnp.where(here, jnp.where(high, upper, lower), total)
            kept = FIELDS * part
            free = lane[:part] >= kept
            target[...] = jnp.concatenate(
                [
                    jnp.where(free, pltpu.roll(total[kept:], kept - q * part, 1), total[q * part : (q + 1) * part])
                    for q in range(FIELDS)
                ],
                axis=0,
            )

    def unpack_fields(self, message):
        part = self.part
        kept, width = message.shape
        lane = lax.broadcasted_iota(jnp.int32, (part, width), 1)
        last = jnp.zeros((part, width), F32)
        for q in range(FIELDS):
            x = pltpu.roll(message[q * part : (q + 1) * part], width - (kept - q * part), 1)
            last = jnp.where((lane >= q * part) & (lane < (q + 1) * part), x, last)
        return jnp.concatenate([message, last], axis=0)

    def by_nodes(self, upper, lower, table, width, store):
        for k in range(0, self.p, 2):
            columns = table[:, k * width : (k + 2) * width]
            both = jnp.dot(upper, columns, preferred_element_type=F32) + jnp.dot(
                lower, columns, preferred_element_type=F32
            )
            store(k, both[:, :width])
            store(k + 1, both[:, width:])

    def one_hot(self, slots, ids):
        count = slots.shape[-1]
        column = jnp.broadcast_to(slots[...], (count, count))
        column = jnp.concatenate([column, jnp.zeros((count, 128 - count), jnp.int32)], axis=1)
        column = jnp.concatenate([column, jnp.zeros((128 - count, 128), jnp.int32)], axis=0)
        column = column.astype(F32).T[:count, :1]
        return jnp.concatenate(
            [jnp.where(column == ids[n : n + 1, :].astype(F32), 1.0, 0.0) for n in range(self.c)], axis=0
        ).astype(BF16)

    def block_table(self, matrix, out):
        p, size = self.p, out.shape[0]
        row = lax.broadcasted_iota(jnp.int32, (p, size), 0)
        node = lax.rem(lax.broadcasted_iota(jnp.int32, (p, size), 1), p)
        tile = jnp.zeros((p, size), F32)
        for a in range(p):
            line = jnp.zeros((p, size), F32)
            for i in range(p):
                line = jnp.where(node == i, float(matrix[a, i]), line)
            tile = jnp.where(row == a, line, tile)
        whole = jnp.concatenate([tile] * (size // p), axis=0)
        same = lax.broadcasted_iota(jnp.int32, (size, size), 0) // p == (
            lax.broadcasted_iota(jnp.int32, (size, size), 1) // p
        )
        upper, lower = split(jnp.where(same, whole, 0.0))
        out[...] = jnp.concatenate([upper, upper, lower], axis=1)

    def spread_tables(self, out3, out4, square):
        self.block_table(self.squared.T, square)
        p, ey, ez = self.p, self.ey, self.ez
        for out, width, step, offset, first in (
            (out3, self.w3, self.step3, HALO, 0),
            (out4, self.w4, self.step4, 0, self.c * ey),
        ):
            row = lax.broadcasted_iota(jnp.int32, (ey * ez * p, width), 0)
            lane = lax.broadcasted_iota(jnp.int32, (1, width), 1)
            g = lane // step - offset
            inside = (g >= 0) & (g < ez) & (lax.rem(lane, step) >= first)
            same = row // p == jnp.where(inside, lax.rem(lane, ey) * ez + g, -1)
            node = lax.rem(row, p)
            for k in range(p):
                out[:, k * width : (k + 1) * width] = jnp.where(same & (node == k), 1.0, 0.0).astype(BF16)

    def prepare(self, n_x, n_y, *refs):
        geometry, viscosity, spread, table, right, slots, ids, square = refs[:8]
        s4, hot3, fields = refs[8:11]
        refs = refs[11:]
        x_out, y_out, work = refs[:n_x], refs[n_x : n_x + n_y], refs[n_x + n_y]
        p, c, block, rows, ey = self.p, self.c, self.block, self.rows, self.ey
        face = ey * p
        wjk, end_j, end_k = (table[n * face : (n + 1) * face, :] for n in range(3))
        stiff, second, third, rest = [], [], [], []
        for i in range(p):
            xx, yy, zz, xy, xz, yz = (geometry[q, i] for q in range(6))
            quadrature = float(self.weights[i]) * wjk
            weighted = quadrature * viscosity[i]
            mass = (helm_coefficient * quadrature) * (
                xx * (yy * zz - yz * yz) - xy * (xy * zz - yz * xz) + xz * (xy * yz - yy * xz)
            )
            cross = end_j * end_k * yz
            end = float(self.end[i])
            if end != 0.0:
                cross = cross + end * (end_j * xy + end_k * xz)
            entries = [weighted * entry for entry in (xx, yy, zz, xy, xz, yz)] + [mass]
            for q, entry in enumerate(entries):
                fields[q, i * face : (i + 1) * face, :] = entry
            stiff.append(entries[0])
            second.append(entries[1])
            third.append(entries[2])
            rest.append((2.0 * weighted) * cross + mass)
        upper, lower = split(jnp.concatenate(second, axis=0))
        diagonal = jnp.dot(
            square[...], jnp.concatenate([upper, lower, upper], axis=0), preferred_element_type=F32
        )
        upper, lower = split(jnp.concatenate(third, axis=0))
        diagonal = diagonal + lax.dot_general(
            jnp.concatenate([upper, lower, upper], axis=1),
            square[...],
            (((1,), (1,)), ((), ())),
            preferred_element_type=F32,
        )
        first = self.contract(stiff, self.squared.T)
        diagonal = diagonal + jnp.concatenate([x + y for x, y in zip(first, rest)], axis=0)
        width = diagonal.shape[-1]
        value = diagonal.reshape(p, ey, p, width)
        value = jnp.concatenate([value[:, f].reshape(block, width) for f in range(ey)], axis=1)

        def store(k, part):
            work[pl.ds(k, block, stride=p), :] = part

        self.by_nodes(*split(value), spread, self.w4, store)
        hot = self.one_hot(slots, ids)
        hot3[...] = self.one_hot(slots, ids[c:, :])
        total = work[...]
        for part in split(right[...].reshape(hot.shape[0], rows)):
            total = total + lax.dot_general(
                part, hot, (((0,), (0,)), ((), ())), preferred_element_type=F32
            )
        s4[...] = total
        self.fold_second(s4)
        last = self.n4 - self.step4
        self.fold_third(s4, self.step4, lambda l: l < last, lambda l: (l >= self.step4) & (l < self.n4))
        self.emit_first((s4[:block, :], s4[rows - block :, :]), x_out)
        self.emit_second(s4, y_out)

    def convert(self, n_y, n_z, *refs):
        fields, spread, dirichlet, s4 = refs[:4]
        g, ind = refs[4:6]
        refs = refs[6:]
        y_out, z_out, packed = refs[:n_y], refs[n_y : n_y + n_z], refs[n_y + n_z : n_y + 2 * n_z]
        upper, lower = refs[n_y + 2 * n_z :]
        p, c, block, ey = self.p, self.c, self.block, self.ey
        width = fields.shape[-1]
        for q in range(FIELDS):
            value = fields[q].reshape(p, ey, p, width)
            for f in range(ey):
                at = (slice(q * block, (q + 1) * block), slice(f * width, (f + 1) * width))
                upper[at], lower[at] = split(value[:, f].reshape(block, width))
        first_flag, flags = FIELDS * block, 2 * p
        for cc in range(c):
            for f in range(ey):
                at = slice(f * p, (f + 1) * p)
                face = jnp.concatenate([dirichlet[0, cc, at, :], dirichlet[1, cc, at, :]], axis=0)
                to = slice(first_flag + cc * flags, first_flag + (cc + 1) * flags)
                upper[to, f * width : (f + 1) * width] = face.astype(F32).astype(BF16)
                lower[to, f * width : (f + 1) * width] = jnp.zeros((flags, width), BF16)
        row = lax.broadcasted_iota(jnp.int32, (flags, self.w3), 0)
        lane = lax.broadcasted_iota(jnp.int32, (flags, self.w3), 1)
        ends = (lax.axis_index("gx") == 0, lax.axis_index("gx") == self.sizes["gx"] - 1)
        here = ((row < p) & ends[0]) | ((row >= p) & ends[1])
        owner = lax.rem(lane, self.step3) // ey

        def store(k, value):
            g[pl.ds(k, first_flag, stride=p), :] = value[:first_flag]
            total = jnp.zeros((flags, self.w3), F32)
            for cc in range(c):
                at = first_flag + cc * flags
                total = jnp.where(owner == cc, value[at : at + flags], total)
            ind[pl.ds(k, flags, stride=p), :] = jnp.where(here, total, 0.0)

        self.by_nodes(upper[...], lower[...], spread, self.w3, store)
        self.pack_fields(fields, z_out)
        self.fold_second(ind)
        first_own, end_own = HALO * self.step3, self.n3 - HALO * self.step3
        self.fold_third(
            ind,
            self.step3,
            lambda l: (l >= first_own) & (l < end_own - self.step3),
            lambda l: (l >= first_own + self.step3) & (l < end_own),
        )
        for out, (up, _, _) in zip(y_out, roles("gy", self.sizes["gy"])):
            for n in range(2):
                start = n * block
                out[n * p : (n + 1) * p, :] = jnp.where(
                    up, ind[start + block - p : start + block, :], ind[start : start + p, :]
                )
        for out, (up, _, _) in zip(packed, roles("gz", self.sizes["gz"])):
            self.pack(out, s4, block, 0, self.n4 - self.halo4, up, 0)
            self.pack(out, ind, p, first_own, end_own - first_own, up, block)

    def halo_fields(self, n_z, *refs):
        own, halo = refs[:2]
        z_in, g, terms = refs[2 : 2 + n_z], refs[2 + n_z], refs[3 + n_z]
        p, block, ey, part = self.p, self.block, self.ey, self.part
        sides = both_sides([z[...] for z in z_in], roles("gz", self.sizes["gz"]))
        sides = [self.unpack_fields(side) for side in sides]
        width = sides[0].shape[-1]
        sides = [side.reshape(p, ey, p, width) for side in sides]
        lane = lax.broadcasted_iota(jnp.int32, (block, width), 1)
        for q in range(FIELDS):
            value = jnp.zeros((block, width), F32)
            for side in range(2):
                for f in range(ey):
                    to = (side * ey + f) * part
                    shift = (to - q * part) % width
                    x = sides[side][:, f].reshape(block, width)
                    x = pltpu.roll(x, shift, 1) if shift else x
                    value = jnp.where((lane >= to) & (lane < to + part), x, value)
            upper, lower = split(value)
            lower = pltpu.roll(lower.astype(F32), width // 2, 1).astype(BF16)
            terms[q * block : (q + 1) * block, :] = upper + lower

        for k in range(0, p, 2):
            columns = halo[:, k * self.w3 : (k + 2) * self.w3]
            both = jnp.dot(terms[...], columns, preferred_element_type=F32)
            for n in range(2):
                at = pl.ds(k + n, FIELDS * block, stride=p)
                g[at, :] = own[at, :] + both[:, n * self.w3 : (n + 1) * self.w3]

    def coefficients(self, low, high, coef):
        top, bottom = jnp.full((8, 128), high[0], F32), jnp.full((8, 128), low[0], F32)
        midpoint, halfwidth = (top + bottom) * 0.5, (top - bottom) * 0.5
        ratio = midpoint / halfwidth
        damping = 1.0 / ratio
        coef[0:8, :] = 1.0 / midpoint
        for n in range(ITERS - 1):
            following = 1.0 / (2.0 * ratio - damping)
            coef[8 * (2 * n + 1) : 8 * (2 * n + 2), :] = following * damping
            coef[8 * (2 * n + 2) : 8 * (2 * n + 3), :] = 2.0 * following / halfwidth
            damping = following

    def join(self, n_x, n_y, *refs):
        x_in, refs = refs[:n_x], refs[n_x:]
        y_raw, y_more, y_out = refs[:n_y], refs[n_y:-n_y], refs[-n_y:]
        p, block, ey = self.p, self.block, self.ey
        low, high = both_sides([x[...] for x in x_in], roles("gx", self.sizes["gx"]))
        for n, (up, _, _) in enumerate(roles("gy", self.sizes["gy"])):
            face = y_raw[n][...]
            width = face.shape[-1]
            if n_x:
                first, last = (jnp.where(up, x[block - p :], x[:p]) for x in (low, high))
                face = jnp.concatenate([face[:p] + first, face[p : block - p], face[block - p :] + last], axis=0)
            if y_more:
                face = jnp.concatenate([face, y_more[n][...]], axis=0)
            if ey == 1:
                y_out[n][...] = face
                continue
            half = face.shape[0] // 2
            first, second = face[:half], face[half:]
            f = lax.rem(lax.broadcasted_iota(jnp.int32, first.shape, 1), ey)
            below = jnp.where(f == 0, pltpu.roll(first, width - (ey - 1), 1), 0.0) + jnp.where(
                f == 1, pltpu.roll(second, (width - (ey - 2)) % width, 1) if ey != 2 else second, 0.0
            )
            above = jnp.where(f == ey - 1, pltpu.roll(first, ey - 1, 1), 0.0) + jnp.where(
                f == ey - 2, pltpu.roll(second, ey - 2, 1) if ey != 2 else second, 0.0
            )
            y_out[n][...] = jnp.where(up, below, above)

    def second_sides(self, received):
        role, ey = roles("gy", self.sizes["gy"]), self.ey
        faces = []
        for message, (_, from_high, _) in zip(received, role):
            data = message[...]
            if ey > 1:
                width = data.shape[-1]
                f = lax.rem(lax.broadcasted_iota(jnp.int32, data.shape, 1), ey)
                beside = jnp.where(from_high, pltpu.roll(data, 1, 1), pltpu.roll(data, width - 1, 1))
                here = f == jnp.where(from_high, ey - 1, 0)
                data = jnp.concatenate([jnp.where(here, x, 0.0) for x in (data, beside)], axis=0)
            faces.append(data)
        return both_sides(faces, role)

    def pack(self, out, u, count, first, last, up, start):
        p, width, size = self.p, self.w4, self.halo4
        lane = lax.broadcasted_iota(jnp.int32, (count, width), 1)
        for section in range(0, u.shape[0] // count, p):
            total = jnp.zeros((count, width), F32)
            for n in range(p):
                at, shift = (section + n) * count, n * size
                x = u[at : at + count, :]
                below = pltpu.roll(x, (shift - first) % width, 1) if (shift - first) % width else x
                above = pltpu.roll(x, (shift - last) % width, 1)
                here = (lane >= shift) & (lane < shift + size)
                total = jnp.where(here, jnp.where(up, above, below), total)
            row = start + section // p * count
            out[row : row + count, :] = total

    def pack_second(self, n_x, n_y, n_z, *refs):
        x_in, y_in, refs = refs[:n_x], refs[n_x : n_x + n_y], refs[n_x + n_y :]
        z_in, z_out = refs[:n_z], refs[n_z:]
        p, block, width, size = self.p, self.block, self.w4, self.halo4
        ends = both_sides([x[...] for x in x_in], roles("gx", self.sizes["gx"]))
        low, high = self.second_sides(y_in)
        halo3 = HALO * self.step3
        lane = lax.broadcasted_iota(jnp.int32, (p, width), 1)
        for packed, out, (up, _, _) in zip(z_in, z_out, roles("gz", self.sizes["gz"])):
            out[...] = packed[...]
            if n_x:
                total = 0.0
                for x, group in zip(ends, (0, p - 1)):
                    shift = group * size
                    below = pltpu.roll(x, shift, 1) if shift else x
                    back = (shift - self.n4 + size) % width
                    above = pltpu.roll(x, back, 1) if back else x
                    wide = lax.broadcasted_iota(jnp.int32, x.shape, 1)
                    here = (wide >= shift) & (wide < shift + size)
                    total = total + jnp.where(here, jnp.where(up, above, below), 0.0)
                out[:block, :] += total
            if not n_y:
                continue
            for face, row in ((low, 0), (high, block - p)):
                total = jnp.zeros((p, width), F32)
                for n in range(p):
                    shift = n * size
                    x = face[n * p : (n + 1) * p]
                    below = pltpu.roll(x, shift, 1) if shift else x
                    above = pltpu.roll(x, (shift - self.n4 + size) % width, 1)
                    here = (lane >= shift) & (lane < shift + size)
                    total = jnp.where(here, jnp.where(up, above, below), total)
                out[row : row + p, :] += total
            for n in range(2):
                row = block + n * p
                for face, group in ((low, 0), (high, p - 1)):
                    shift = group * size
                    x = face[row : row + p]
                    below = pltpu.roll(x, (shift - halo3) % width, 1)
                    above = pltpu.roll(x, (shift - self.n3 + 2 * halo3) % width, 1)
                    here = (lane >= shift) & (lane < shift + size)
                    out[row : row + p, :] += jnp.where(here, jnp.where(up, above, below), 0.0)

    def own(self, n_x, n_y, *refs):
        s4, ind, widen = refs[:3]
        x_in, y_in, (r, scale, flag, work) = refs[3 : 3 + n_x], refs[3 + n_x : 3 + n_x + n_y], refs[3 + n_x + n_y :]
        p, block, rows, w3 = self.p, self.block, self.rows, self.w3
        work[...] = s4[...]
        if n_x:
            low, high = both_sides([x[...] for x in x_in], roles("gx", self.sizes["gx"]))
            work[:block, :] += low
            work[rows - block :, :] += high
        flag[...] = ind[...]
        if n_y:
            low, high = self.second_sides(y_in)
            for u, first, count in ((work, 0, p), (flag, p, 2)):
                for i in range(count):
                    at, end, row = i * block, (i + 1) * block, (first + i) * p
                    u[at : at + p, :] += low[row : row + p]
                    u[end - p : end, :] += high[row : row + p]
        both = dot2(work[...], widen[: self.w4, :])
        r[...] = both[:, :w3]
        scale[...] = both[:, w3:]

    def start(self, n_x, n_z, *refs):
        r_own, diagonal_own, flag_own, g, widen, ahead, back = refs[:7]
        z_in = refs[7 : 7 + n_z]
        t, scale, ends, f1, f2, f3 = refs[7 + n_z : 13 + n_z]
        x_out, refs = refs[13 + n_z : 13 + n_z + n_x], refs[13 + n_z + n_x :]
        beside, r, flag, slope, third = refs
        p, block, rows, w3, w4 = self.p, self.block, self.rows, self.w3, self.w4
        step, first_own, end_own = self.step3, HALO * self.step3, self.n3 - HALO * self.step3
        size, part = self.sizes["gz"], self.halo4
        if n_z:
            low, high = both_sides([z[...] for z in z_in], roles("gz", size))
        else:
            low = high = jnp.zeros((block + 2 * p, w4), F32)
        lane = lax.broadcasted_iota(jnp.int32, (block, w4), 1)
        for n in range(p):
            first = pltpu.roll(low[:block], w4 - n * part, 1) if n else low[:block]
            second = pltpu.roll(high[:block], (part - n * part) % w4, 1) if n != 1 else high[:block]
            beside[n * block : (n + 1) * block, :] = jnp.where(
                lane < part, first, jnp.where(lane < 2 * part, second, 0.0)
            )
        both = dot2(beside[...], widen[w4:, :])
        r[...] = r_own[...] + both[:, :w3]
        scale[...] = diagonal_own[...] + both[:, w3:]
        lane = lax.broadcasted_iota(jnp.int32, (p, w3), 1)
        for n in range(2 * p):
            row, shift = block + n // p * p, n % p * part
            first = pltpu.roll(low[row : row + p], w3 - shift, 1) if shift else low[row : row + p]
            second = pltpu.roll(high[row : row + p], (end_own - shift) % w3, 1)
            flag[n * p : (n + 1) * p, :] = jnp.where(
                lane < first_own,
                first,
                jnp.where(lane < end_own, flag_own[n * p : (n + 1) * p, :], jnp.where(lane < self.n3, second, 0.0)),
            )
        for u in (r, scale, flag):
            self.fold_third(
                u,
                step,
                lambda l: ((l >= first_own - step) & (l < first_own)) | ((l >= end_own - step) & (l < end_own)),
                lambda l: ((l >= first_own) & (l < first_own + step)) | ((l >= end_own) & (l < end_own + step)),
            )
        index = lax.axis_index("gz")
        begin = jnp.where(index > 0, 0, first_own)
        end = jnp.where(index < size - 1, self.n3, end_own)
        lane = lax.broadcasted_iota(jnp.int32, (block, w3), 1)
        valid = (lane >= begin) & (lane < end)
        for i in range(p):
            at = slice(i * block, (i + 1) * block)
            factor = jnp.where(valid, 1.0 / jnp.where(valid, scale[at, :], 1.0), 0.0)
            if i in (0, p - 1):
                row = 0 if i == 0 else block
                factor = jnp.where(flag[row : row + block, :] > 0.5, 0.0, factor)
            scale[at, :] = factor
            t[at, :] = factor * r[at, :]
        self.fluxes(t, g, f1, f2, f3, slope, third, ahead)
        self.end_planes(t, g, ends, f1, f2, f3, slope, third, back)
        self.iteration_fold(ends)
        self.emit_first((ends[:block, :], ends[block:, :]), x_out)

    def factors(self, coef, n):
        rows = [coef[8 * m : 8 * m + 1, :] for m in (0, 2 * n + 1, 2 * n + 2)]
        return (rows[0] if n == 0 else None), rows[1], rows[2]

    def shares(self, faces, scale, image, at):
        low, high = faces
        p, block = self.p, self.block
        i = at // block
        out = []
        for start, face in ((at, low), (at + block - p, high)):
            value = scale[start : start + p, :] * face[i * p : (i + 1) * p]
            out.append((start, -value if image is None else -image * value))
        return out

    def preview(self, n_x, n_y, n, last, *refs):
        t, t_old, d, scale, v, coef = refs[:6]
        refs = refs[6:]
        x_in, y_old, refs = refs[:n_x], refs[n_x : n_x + (n_y if n else 0)], refs[n_x + (n_y if n else 0) :]
        p, block, rows = self.p, self.block, self.rows
        image, keep, gain = self.factors(coef, n)
        start = coef[0:1, :]
        if last:
            hot, out, t_new, field = refs
        else:
            g, ahead, back, t_new, d_new, f1, f2, f3, ends, slope, third = refs
        low, high = both_sides([x[...] for x in x_in], roles("gx", self.sizes["gx"]))
        if n:
            faces = self.second_sides(y_old) if n_y else None
            image_old = self.factors(coef, n - 1)[0]
        for i in range(p):
            at = slice(i * block, (i + 1) * block)
            value = v[at, :]
            if n_x and i in (0, p - 1):
                value = value + (low if i == 0 else high)
            value = scale[at, :] * value
            t_new[at, :] = t_old[at, :] - (value if image is None else image * value)
            if n and n_y:
                for row, share in self.shares(faces, scale, image_old, i * block):
                    t_new[row : row + p, :] += share
            direction = d[at, :] if n else start * t[at, :]
            following = keep * direction + gain * t_new[at, :]
            if last:
                field[at, :] = start * t[at, :] + following + (direction if n else 0.0)
            else:
                d_new[at, :] = following
        if last:
            out[...] = self.by_slots(hot, field[...])
        else:
            self.fluxes(d_new, g, f1, f2, f3, slope, third, ahead)
            self.end_planes(d_new, g, ends, f1, f2, f3, slope, third, back)

    def by_slots(self, hot, field):
        return lax.dot_general(
            jnp.concatenate([hot[...], hot[...]], axis=1),
            jnp.concatenate(split(field), axis=1),
            (((1,), (1,)), ((), ())),
            preferred_element_type=F32,
        )

    def middle(self, n_x, n_y, n, *refs):
        part, scale, g, coef, ahead, back = refs[:6]
        y_in, refs = refs[6 : 6 + n_y], refs[6 + n_y :]
        ends, shares, refs = refs[0], refs[1], refs[2:]
        x_out, (f1, f2, f3, third) = refs[:n_x], refs[n_x:]
        p, block, rows = self.p, self.block, self.rows
        image, _, gain = self.factors(coef, n)
        ends[...] = part[...]
        if n_y:
            faces = self.second_sides(y_in)
            for i in range(p):
                for m, (_, share) in enumerate(self.shares(faces, scale, image, i * block)):
                    shares[(2 * i + m) * p : (2 * i + m + 1) * p, :] = gain * share

            def write(i, j, values):
                f1[i * block + j * p : i * block + (j + 1) * p, :] = values[0]
                if len(values) > 1:
                    row = (block if i else 0) + j * p
                    f2[row : row + p, :], f3[row : row + p, :] = values[1], values[2]

            self.share_fluxes(shares, g, third, ahead, False, write)
            self.along_k(f3, back, third, 0, 2 * block)
            for m, i in enumerate((0, p - 1)):
                at = slice(m * block, (m + 1) * block)
                ends[at, :] += self.along_j(f2[at, :], self.forward.T) + third[at, :]
                for n_face, j in enumerate((0, p - 1)):
                    row, at = m * block + j * p, slice(i * block + j * p, i * block + (j + 1) * p)
                    line = (2 * i + n_face) * p
                    ends[row : row + p, :] += self.rows_of(g, 6, at) * shares[line : line + p, :]
            for j in range(p):
                x = [f1[i * block + j * p : i * block + (j + 1) * p, :] for i in range(p)]
                for row, value in zip((j * p, block + j * p), self.contract(x, self.forward.T, (0,))):
                    ends[row : row + p, :] += value
        else:
            shares[...] = jnp.zeros(shares.shape, F32)
        self.iteration_fold(ends)
        self.emit_first((ends[:block, :], ends[block:, :]), x_out)

    def finish(self, n_y, n, *refs):
        part, scale, coef, hot = refs[:4]
        y_in, (out, field) = refs[4 : 4 + n_y], refs[4 + n_y :]
        value = part[...]
        image, _, gain = self.factors(coef, n)
        if n_y:
            faces = self.second_sides(y_in)
            field[...] = jnp.zeros(field.shape, F32)
            for i in range(self.p):
                for row, share in self.shares(faces, scale, image, i * self.block):
                    field[row : row + self.p, :] = gain * share
            value = value + self.by_slots(hot, field[...])
        out[...] = value.reshape(out.shape)


def shards(sizes, right_side, geometry, viscosity, eig_low, eig_high, element_slot, dirichlet):
    plan = Plan(right_side.shape[0], viscosity.shape, sizes)
    p, block, rows, w3, w4 = plan.p, plan.block, plan.rows, plan.w3, plan.w4
    x_pairs = pairings(("gx",), (sizes["gx"],), 0)
    y_pairs = pairings(("gy",), (sizes["gy"],), 0)
    z_pairs = pairings(("gx", "gz"), (sizes["gx"], sizes["gz"]), 1)
    n_x, n_y, n_z = len(x_pairs), len(y_pairs), len(z_pairs)

    def send(arrays, axis, pairs):
        return [lax.ppermute(x, axis, pair) for x, pair in zip(arrays, pairs)]

    def shape(*size, dtype=F32):
        return jax.ShapeDtypeStruct(size, dtype)

    def call(kernel, outputs, operands, scratch=(), spaces={}, flops=0, name=None):
        specs = [pl.BlockSpec(memory_space=spaces.get(n, pltpu.VMEM)) for n in range(len(operands))]
        return list(
            pl.pallas_call(
                kernel,
                out_shape=list(outputs),
                in_specs=specs,
                out_specs=[pl.BlockSpec(memory_space=pltpu.VMEM)] * len(outputs),
                scratch_shapes=list(scratch),
                compiler_params=pltpu.CompilerParams(vmem_limit_bytes=VMEM_BYTES),
                cost_estimate=pl.CostEstimate(flops=flops, bytes_accessed=0, transcendentals=0),
                name=name,
            )(*operands)
        )

    def vmem(*size, dtype=F32):
        return pltpu.VMEM(size, dtype)

    lanes = plan.ez * p
    ahead, back = jnp.asarray(plan.third[0]), jnp.asarray(plan.third[1])
    field3, field4 = shape(rows, w3), shape(rows, w4)
    elements = element_slot.shape[-1]
    spread3, spread4, square = call(
        plan.spread_tables,
        [shape(plan.ey * lanes, p * w, dtype=BF16) for w in (w3, w4)]
        + [shape(*plan.third[0].shape, dtype=BF16)],
        (),
        flops=FLOPS,
        name="spread_tables",
    )
    results = call(
        functools.partial(plan.prepare, n_x, n_y),
        [field4, shape(plan.c * elements, w3, dtype=BF16), shape(FIELDS, p * plan.ey * p, lanes)]
        + [shape(block, w4)] * (n_x + n_y),
        (
            geometry,
            viscosity,
            spread4,
            jnp.asarray(plan.face_table),
            jnp.swapaxes(right_side, 1, 2),
            element_slot,
            jnp.asarray(plan.ids),
            square,
        ),
        scratch=[vmem(rows, w4)],
        name="prepare",
    )
    s4, hot3, fields = results[:3]
    x_out, y_raw = results[3 : 3 + n_x], results[3 + n_x :]
    x_in = send(x_out, "gx", x_pairs)

    lhs = FIELDS * block + 2 * plan.c * p
    results = call(
        functools.partial(plan.convert, n_y, n_z),
        [shape(FIELDS * rows, w3), shape(2 * block, w3)]
        + [shape(2 * p, w3)] * n_y
        + [shape(FIELDS * plan.part, lanes)] * n_z
        + [shape(block + 2 * p, w4)] * n_z,
        (fields, spread3, dirichlet, s4),
        scratch=[vmem(lhs, plan.ey * lanes, dtype=BF16)] * 2,
        name="convert",
    )
    g, ind = results[:2]
    y_more, results = results[2 : 2 + n_y], results[2 + n_y :]
    z_fields, z_out = results[:n_z], results[n_z:]

    def joined(x_in, y_raw, y_more=()):
        if not y_raw:
            return []
        count = y_raw[0].shape[0] + (y_more[0].shape[0] if y_more else 0)
        faces = [shape(count // 2 if plan.ey > 1 else count, y.shape[1]) for y in y_raw]
        return call(functools.partial(plan.join, n_x, n_y), faces, x_in + y_raw + list(y_more), name="join")

    y_in = send(joined(x_in, y_raw, y_more), "gy", y_pairs)
    z_fields = send(z_fields, ("gx", "gz"), z_pairs)
    if n_z:
        g = call(
            functools.partial(plan.halo_fields, n_z),
            [shape(FIELDS * rows, w3)],
            [g, jnp.asarray(plan.halo)] + z_fields,
            scratch=[vmem(FIELDS * block, lanes, dtype=BF16)],
            name="halo_fields",
        )[0]
    if n_z:
        z_out = call(
            functools.partial(plan.pack_second, n_x, n_y, n_z),
            [shape(*z.shape) for z in z_out],
            x_in + y_in + z_out,
            flops=FLOPS,
            name="pack_second",
        )
    z_in = send(z_out, ("gx", "gz"), z_pairs)
    widen = jnp.asarray(plan.widen)
    own = call(
        functools.partial(plan.own, n_x, n_y),
        [field3, field3, shape(2 * block, w3)],
        [s4, ind, widen] + x_in + y_in,
        scratch=[vmem(rows, w4)],
        name="own",
    )

    fluxes = [shape(2 * block, w3)] + [field3] * 3 + [shape(block, w3)] * n_x
    results = call(
        functools.partial(plan.start, n_x, n_z),
        [field3] * 2 + fluxes,
        own + [g, widen, ahead, back] + z_in,
        scratch=[vmem(rows, w4), vmem(rows, w3), vmem(2 * block, w3)] + [vmem(rows, w3)] * 2,
        name="first_direction",
    )
    t, scale = results[:2]
    ends, f1, f2, f3 = results[2:6]
    x_out = results[6:]
    x_out, low, high = lax.optimization_barrier((x_out, eig_low, eig_high))
    coef = call(
        plan.coefficients,
        [shape(8 * (2 * ITERS - 1), 128)],
        (low, high),
        spaces={0: pltpu.SMEM, 1: pltpu.SMEM},
        name="coefficients",
    )[0]
    t_old, d, y_in = t, t, []
    for n in range(ITERS - 1):
        last = n == ITERS - 2
        x_in = send(x_out, "gx", x_pairs)
        outputs = [field3] + [shape(block, w3)] * n_y
        if n:
            results = call(
                functools.partial(plan.operator_second, n_x, n_y, True),
                outputs + [field3],
                [d, g, ends, f1, f2, f3, back, shares, ahead],
                scratch=[vmem(rows, w3)] * 4,
                name="operator_second",
            )
            v, y_raw, d = results[0], results[1 : 1 + n_y], results[1 + n_y]
        else:
            results = call(
                functools.partial(plan.operator_second, n_x, n_y, False),
                outputs,
                [d, g, ends, f1, f2, f3, back],
                scratch=[vmem(rows, w3)],
                name="operator_second",
            )
            v, y_raw = results[0], results[1:]
        y_old, y_in = y_in, send(joined(x_in, y_raw), "gy", y_pairs)
        results = call(
            functools.partial(plan.preview, n_x, n_y, n, last),
            [shape(plan.c * elements, rows)] if last else [field3] * 5 + [shape(2 * block, w3)],
            [t, t_old, d, scale, v, coef] + x_in + y_old + ([hot3] if last else [g, ahead, back]),
            scratch=[vmem(rows, w3)] * 2,
            name="preview",
        )
        if last:
            break
        t_old, d, f1, f2, f3, ends = results
        results = call(
            functools.partial(plan.middle, n_x, n_y, n),
            [shape(2 * block, w3)] * 2 + [shape(block, w3)] * n_x,
            [ends, scale, g, coef, ahead, back] + y_in,
            scratch=[vmem(rows, w3)] + [vmem(2 * block, w3)] * 3,
            name="direction",
        )
        ends, shares, x_out = results[0], results[1], results[2:]
    out = call(
        functools.partial(plan.finish, n_y, n),
        [shape(plan.c, elements, rows)],
        [results[0], scale, coef, hot3] + y_in,
        scratch=[vmem(rows, w3)],
        name="field",
    )[0]
    return jnp.swapaxes(out, 1, 2)


def solution(mesh):
    sizes = {name: mesh.shape[name] for name in ("gx", "gy", "gz")}
    return jax.shard_map(
        functools.partial(shards, sizes),
        mesh=mesh,
        in_specs=(
            P(None, None, ("gx", "gy", "gz")),
            P(None, "gx", "gy", "gz"),
            P("gx", "gy", "gz"),
            P(),
            P(),
            P(("gx", "gy", "gz"), None),
            P(None, None, "gy", "gz"),
        ),
        out_specs=P(None, None, ("gx", "gy", "gz")),
        check_vma=False,
    )
```

```python
import functools
import math

import jax
import jax.numpy as jnp
import numpy as np
from jax import lax
from jax.experimental import pallas as pl
from jax.experimental.pallas import tpu as pltpu
from jax.sharding import PartitionSpec as P

DEGREE = 7
ITERS = 3


helm_coefficient = 10.0


def legendre_pair(values, degree):
    previous = 0.0 * values + 1.0
    current = values.copy()
    for order in range(2, degree + 1):
        previous, current = (
            current,
            ((2 * order - 1) * values * current - (order - 1) * previous) / order,
        )
    return (current, previous)


def gll_tables(degree):
    start = np.cos(np.pi * np.arange(degree + 1) / degree)
    nodes_now = start.copy()
    for sweep in range(80):
        top_value, lower_value = legendre_pair(nodes_now, degree)
        nodes_now = nodes_now - (nodes_now * top_value - lower_value) / ((degree + 1) * top_value)
    gll_nodes = nodes_now[::-1].copy()
    gll_nodes[0] = -1.0
    gll_nodes[degree] = 1.0
    legendre_values = legendre_pair(gll_nodes, degree)[0]
    weights = 2.0 / (degree * (degree + 1) * legendre_values**2)
    differences = gll_nodes[:, None] - gll_nodes[None, :] + np.eye(degree + 1)
    derivative = legendre_values[:, None] / legendre_values[None, :] / differences
    derivative = derivative * (1.0 - np.eye(degree + 1))
    derivative[0, 0] = -degree * (degree + 1) / 4.0
    derivative[degree, degree] = degree * (degree + 1) / 4.0
    return (weights, derivative)


HALO = 2
FIELDS = 7
VMEM_BYTES = 40 * 1024 * 1024
FLOPS = 3 * 10**9
F32 = jnp.float32
BF16 = jnp.bfloat16


def pairings(names, sizes, dim):
    size = sizes[dim]
    if size == 1:
        return []
    if size % 2:
        shifts = (1, size - 1)
        partners = [[(i + shift) % size for i in range(size)] for shift in shifts]
    else:
        partners = [[i ^ 1 for i in range(size)]]
        if size > 2:
            partners.append([((i + 1) ^ 1) - 1 for i in range(size)])
    result = []
    for partner in partners:
        pairs = []
        for flat in range(math.prod(sizes)):
            place = list(np.unravel_index(flat, sizes))
            to = partner[place[dim]]
            if 0 <= to < size:
                place[dim] = to
            elif len(sizes) > 1 and sizes[1 - dim] % 2 == 0:
                place[1 - dim] ^= 1
            else:
                place[dim] = size - 1 - place[dim]
            pairs.append((flat, int(np.ravel_multi_index(place, sizes))))
        result.append(pairs)
    return result


def roles(name, size):
    if size == 1:
        return []
    index = lax.axis_index(name)
    low, high = index > 0, index < size - 1
    if size % 2:
        yes = index >= 0
        no = index < 0
        return [(yes, no, low), (no, yes, high)]
    even = lax.rem(index, 2) == 0
    odd = jnp.logical_not(even)
    result = [(even, even, index >= 0)]
    if size > 2:
        result.append((odd, odd, jnp.logical_or(jnp.logical_and(odd, high), jnp.logical_and(even, low))))
    return result


def both_sides(received, role):
    low, high = 0.0, 0.0
    for data, (_, from_high, used) in zip(received, role):
        high = high + jnp.where(jnp.logical_and(used, from_high), data, 0.0)
        low = low + jnp.where(jnp.logical_and(used, jnp.logical_not(from_high)), data, 0.0)
    return low, high


def split(x):
    upper = x.astype(BF16)
    return upper, (x - upper.astype(F32)).astype(BF16)


def dot2(x, table):
    return jnp.dot(
        jnp.concatenate(split(x), axis=1),
        jnp.concatenate([table, table], axis=0),
        preferred_element_type=F32,
    )


class Plan:
    def __init__(self, components, viscosity_shape, mesh_sizes):
        points = DEGREE + 1
        self.p, self.c = points, components
        self.sizes = mesh_sizes
        ex, ey, ez = (n // points for n in viscosity_shape)
        assert ex == 1 and ez >= HALO
        self.ey, self.ez = ey, ez
        self.rows = points**3
        self.block = points * points
        self.step3, self.step4 = components * ey, (components + 1) * ey
        self.n3, self.n4 = (ez + 2 * HALO) * self.step3, ez * self.step4
        self.w3, self.w4 = -(-self.n3 // 128) * 128, -(-self.n4 // 128) * 128
        self.halo4 = HALO * self.step4
        assert points * self.halo4 <= self.w4 and 2 * self.halo4 <= self.w4
        weights, derivative = gll_tables(DEGREE)
        self.forward = derivative.astype(np.float32)
        self.squared = self.forward * self.forward
        self.weights = weights.astype(np.float32)
        self.end = np.diagonal(self.forward)
        self.tables()

    def lane3(self, g, c, f):
        return (g + HALO) * self.step3 + c * self.ey + f

    def lane4(self, g, c, f):
        return g * self.step4 + c * self.ey + f

    def tables(self):
        p, c, ey, ez = self.p, self.c, self.ey, self.ez
        lanes = ez * p
        every = [(g, cc, f) for g in range(ez) for cc in range(c) for f in range(ey)]
        widen = np.zeros((2 * self.w4, 2 * self.w3), np.float32)
        ids = np.full((2 * c, 128, 128), -1, np.int32)
        for g, cc, f in every:
            widen[self.lane4(g, cc, f), self.lane3(g, cc, f)] = 1
            widen[self.lane4(g, c, f), self.w3 + self.lane3(g, cc, f)] = 1
            ids[cc, :, self.lane4(g, cc, f)] = f * ez + g
            ids[c + cc, :, self.lane3(g, cc, f)] = f * ez + g
        self.ids = np.ascontiguousarray(ids[:, :1, :]).reshape(2 * c, 128)
        part = HALO * p
        self.part = part
        assert FIELDS * part + part == lanes == p * ey * p and 2 * ey * part <= lanes // 2
        halo = np.zeros((lanes, p, self.w3), np.float32)
        for side, first in ((0, -HALO), (1, ez)):
            for g in range(HALO):
                for cc in range(c):
                    for f in range(ey):
                        at = self.lane3(first + g, cc, f)
                        row = self.w4 + side * self.halo4 + g * self.step4
                        widen[row + cc * ey + f, at] = 1
                        widen[row + c * ey + f, self.w3 + at] = 1
                        for k in range(p):
                            for half in range(2):
                                halo[half * lanes // 2 + (side * ey + f) * part + g * p + k, k, at] = 1
        self.halo = halo.reshape(lanes, -1).astype(jnp.bfloat16)
        self.widen = widen.astype(jnp.bfloat16)
        self.third = [self.block_terms(matrix) for matrix in (self.forward, self.forward.T)]
        face = (ey * p, lanes)
        second = np.tile(np.arange(p), ey)[:, None]
        third = np.tile(np.arange(p), ez)[None, :]
        self.face_table = np.concatenate(
            [
                self.weights[second] * self.weights[third],
                np.broadcast_to(self.end[second], face),
                np.broadcast_to(self.end[third], face),
            ]
        ).astype(np.float32)

    def block_terms(self, matrix):
        size = self.rows // 4
        blocks = np.kron(np.eye(size // self.p), matrix).astype(np.float32)
        upper = blocks.astype(jnp.bfloat16)
        lower = (blocks - upper.astype(np.float32)).astype(jnp.bfloat16)
        return np.concatenate([upper, upper, lower], axis=1)


    def contract(self, x, matrix, wanted=None):
        p = self.p
        sign = 1.0 if matrix[0, 0] * matrix[p - 1, p - 1] > 0 else -1.0
        half = p // 2
        sums = [x[i] + x[p - 1 - i] for i in range(half)]
        differences = [x[i] - x[p - 1 - i] for i in range(half)]
        out = [None] * p
        for a in range(half) if wanted is None else wanted:
            even, odd = None, None
            for i in range(half):
                first, second = float(matrix[a, i]), float(matrix[a, p - 1 - i])
                even = self.gather(even, 0.5 * (first + second), sums[i])
                odd = self.gather(odd, 0.5 * (first - second), differences[i])
            out[a] = odd + even
            out[p - 1 - a] = even - odd if sign > 0 else odd - even
        return [x for x in out if x is not None]

    @staticmethod
    def gather(total, factor, x):
        if factor == 0.0:
            return total
        return factor * x if total is None else total + factor * x

    def along_j(self, x, matrix):
        x = x.reshape(self.p, self.p, x.shape[-1])
        return jnp.concatenate(self.contract([x[j] for j in range(self.p)], matrix), axis=0)

    def along_i(self, source, matrix, write):
        p, block = self.p, self.block
        for j in range(p):
            rows = [i * block + j * p for i in range(p)]
            for row, value in zip(rows, self.contract([source[r : r + p, :] for r in rows], matrix)):
                write(row, value)

    def along_k(self, source, table, out, start, end):
        size = table.shape[0]
        width = source.shape[-1]
        while start < end:
            count = min(2, (end - start) // size)
            pieces = [split(source[start + n * size : start + (n + 1) * size, :]) for n in range(count)]
            upper, lower = (jnp.concatenate([piece[n] for piece in pieces], axis=1) for n in range(2))
            both = jnp.dot(
                table[...], jnp.concatenate([upper, lower, upper], axis=0), preferred_element_type=F32
            )
            for n in range(count):
                out[start + n * size : start + (n + 1) * size, :] = both[:, n * width : (n + 1) * width]
            start += count * size

    def rows_of(self, g, q, at):
        return g[q * self.rows + at.start : q * self.rows + at.stop, :]

    def fluxes(self, v, g, f1, f2, f3, slope, third, ahead):
        p, block, rows = self.p, self.block, self.rows

        def store(row, value):
            slope[row : row + p, :] = value

        self.along_i(v, self.forward, store)
        self.along_k(v, ahead, third, 0, rows)
        for i in range(p):
            at = slice(i * block, (i + 1) * block)
            x, s1, s3 = v[at, :], slope[at, :], third[at, :]
            s2 = self.along_j(x, self.forward)
            xy, xz, yz = (self.rows_of(g, q, at) for q in (3, 4, 5))
            f1[at, :] = self.rows_of(g, 0, at) * s1 + xy * s2 + xz * s3
            f2[at, :] = xy * s1 + self.rows_of(g, 1, at) * s2 + yz * s3
            f3[at, :] = xz * s1 + yz * s2 + self.rows_of(g, 2, at) * s3

    def share_fluxes(self, shares, g, third, ahead, whole, write):
        p, block = self.p, self.block
        x = shares[...]
        ends = [[x[(2 * i + n) * p : (2 * i + n + 1) * p] for i in range(p)] for n in range(2)]
        s1 = [self.contract(column, self.forward) for column in ends]
        self.along_k(shares, ahead, third, 0, 2 * block)
        for i in range(p):
            first, last = ends[0][i], ends[1][i]
            count = 3 if whole or i in (0, p - 1) else 1
            for j in range(p):
                at = slice(i * block + j * p, i * block + (j + 1) * p)
                s2 = float(self.forward[j, 0]) * first + float(self.forward[j, p - 1]) * last
                rows = ((0, 3, 4), (3, 1, 5), (4, 5, 2))[:count]
                values = [self.rows_of(g, row[1], at) * s2 for row in rows]
                if j in (0, p - 1):
                    n = int(j > 0)
                    line = (2 * i + n) * p
                    e1, e3 = s1[n][i], third[line : line + p, :]
                    values = [
                        value + self.rows_of(g, row[0], at) * e1 + self.rows_of(g, row[2], at) * e3
                        for value, row in zip(values, rows)
                    ]
                write(i, j, values)

    def end_planes(self, v, g, ends, f1, f2, f3, slope, third, back):
        p, block, rows = self.p, self.block, self.rows
        for n, start in enumerate((0, rows - block)):
            at = slice(start, start + block)
            ends[n * block : (n + 1) * block, :] = (
                self.along_j(f2[at, :], self.forward.T) + self.rows_of(g, 6, at) * v[at, :]
            )
            slope[n * block : (n + 1) * block, :] = f3[at, :]
        self.along_k(slope, back, third, 0, 2 * block)
        for j in range(p):
            x = [f1[i * block + j * p : i * block + (j + 1) * p, :] for i in range(p)]
            first, last = self.contract(x, self.forward.T, (0,))
            for row, value in ((j * p, first), (block + j * p, last)):
                ends[row : row + p, :] += value + third[row : row + p, :]

    def operator_second(self, n_x, n_y, shared, *refs):
        v, g, ends, f1, f2, f3, back = refs[:7]
        refs = refs[7:]
        p, block, rows = self.p, self.block, self.rows
        if shared:
            shares, ahead, out = refs[:3]
            y_out, (v_new, third, *new) = refs[3 : 3 + n_y], refs[3 + n_y :]

            def write(i, j, values):
                at = slice(i * block + j * p, i * block + (j + 1) * p)
                for f_old, f_new, value in zip((f1, f2, f3), new, values):
                    f_new[at, :] = f_old[at, :] + value

            self.share_fluxes(shares, g, third, ahead, True, write)
            v_new[...] = v[...]
            for i in range(p):
                for m, row in enumerate((i * block, (i + 1) * block - p)):
                    v_new[row : row + p, :] += shares[(2 * i + m) * p : (2 * i + m + 1) * p, :]
            v, (f1, f2, f3) = v_new, new
        else:
            out, y_out, third = refs[0], refs[1 : 1 + n_y], refs[1 + n_y]
        out[:block, :], out[rows - block :, :] = ends[:block, :], ends[block:, :]
        self.along_k(f3, back, third, block, rows - block)
        for i in range(1, p - 1):
            at = slice(i * block, (i + 1) * block)
            out[at, :] = (
                self.along_j(f2[at, :], self.forward.T) + self.rows_of(g, 6, at) * v[at, :] + third[at, :]
            )
        for j in range(p):
            at = [slice(i * block + j * p, i * block + (j + 1) * p) for i in range(p)]
            values = self.contract([f1[r, :] for r in at], self.forward.T, range(1, p // 2))
            for r, value in zip(at[1 : p - 1], values):
                out[r, :] += value
        self.iteration_fold(out.at[block : rows - block, :])
        self.emit_second(out, y_out)

    def fold_second(self, u):
        if self.ey == 1:
            return
        p, width = self.p, u.shape[-1]
        lane = lax.broadcasted_iota(jnp.int32, (p, width), 1)
        f = lax.rem(lane, self.ey)
        for start in range(0, u.shape[0], self.block):
            first, last = u[start : start + p, :], u[start + self.block - p : start + self.block, :]
            u[start + self.block - p : start + self.block, :] = last + jnp.where(
                f < self.ey - 1, pltpu.roll(first, width - 1, 1), 0.0
            )
            u[start : start + p, :] = first + jnp.where(f > 0, pltpu.roll(last, 1, 1), 0.0)

    def fold_third(self, u, step, take_upper, take_lower):
        p, (rows, width) = self.p, u.shape
        count = rows // p
        lane = lax.broadcasted_iota(jnp.int32, (count, width), 1)
        first, last = u[pl.ds(0, count, stride=p), :], u[pl.ds(p - 1, count, stride=p), :]
        u[pl.ds(p - 1, count, stride=p), :] = last + jnp.where(
            take_upper(lane), pltpu.roll(first, width - step, 1), 0.0
        )
        u[pl.ds(0, count, stride=p), :] = first + jnp.where(
            take_lower(lane), pltpu.roll(last, step, 1), 0.0
        )

    def emit_first(self, ends, x_out):
        for out, (high, _, _) in zip(x_out, roles("gx", self.sizes["gx"])):
            out[...] = jnp.where(high, ends[1], ends[0])

    def emit_second(self, u, y_out):
        p, block = self.p, self.block
        for out, (high, _, _) in zip(y_out, roles("gy", self.sizes["gy"])):
            for i in range(p):
                start = i * block
                out[i * p : (i + 1) * p, :] = jnp.where(
                    high, u[start + block - p : start + block, :], u[start : start + p, :]
                )

    def iteration_fold(self, u):
        self.fold_second(u)
        last = self.n3 - self.step3
        self.fold_third(u, self.step3, lambda l: l < last, lambda l: (l >= self.step3) & (l < self.n3))


    def pack_fields(self, fields, out):
        part = self.part
        for target, (high, _, _) in zip(out, roles("gz", self.sizes["gz"])):
            _, rows, width = fields.shape
            lane = lax.broadcasted_iota(jnp.int32, (rows, width), 1)
            total = jnp.zeros((rows, width), F32)
            for q in range(FIELDS):
                start = q * part
                upper = pltpu.roll(fields[q], start + part, 1)
                lower = pltpu.roll(fields[q], start, 1) if start else fields[q]
                here = (lane >= start) & (lane < start + part)
                total = jnp.where(here, jnp.where(high, upper, lower), total)
            kept = FIELDS * part
            free = lane[:part] >= kept
            target[...] = jnp.concatenate(
                [
                    jnp.where(free, pltpu.roll(total[kept:], kept - q * part, 1), total[q * part : (q + 1) * part])
                    for q in range(FIELDS)
                ],
                axis=0,
            )

    def unpack_fields(self, message):
        part = self.part
        kept, width = message.shape
        lane = lax.broadcasted_iota(jnp.int32, (part, width), 1)
        last = jnp.zeros((part, width), F32)
        for q in range(FIELDS):
            x = pltpu.roll(message[q * part : (q + 1) * part], width - (kept - q * part), 1)
            last = jnp.where((lane >= q * part) & (lane < (q + 1) * part), x, last)
        return jnp.concatenate([message, last], axis=0)

    def by_nodes(self, upper, lower, table, width, store):
        for k in range(0, self.p, 2):
            columns = table[:, k * width : (k + 2) * width]
            both = jnp.dot(upper, columns, preferred_element_type=F32) + jnp.dot(
                lower, columns, preferred_element_type=F32
            )
            store(k, both[:, :width])
            store(k + 1, both[:, width:])

    def one_hot(self, slots, ids):
        count = slots.shape[-1]
        column = jnp.broadcast_to(slots[...], (count, count))
        column = jnp.concatenate([column, jnp.zeros((count, 128 - count), jnp.int32)], axis=1)
        column = jnp.concatenate([column, jnp.zeros((128 - count, 128), jnp.int32)], axis=0)
        column = column.astype(F32).T[:count, :1]
        return jnp.concatenate(
            [jnp.where(column == ids[n : n + 1, :].astype(F32), 1.0, 0.0) for n in range(self.c)], axis=0
        ).astype(BF16)

    def block_table(self, matrix, out):
        p, size = self.p, out.shape[0]
        row = lax.broadcasted_iota(jnp.int32, (p, size), 0)
        node = lax.rem(lax.broadcasted_iota(jnp.int32, (p, size), 1), p)
        tile = jnp.zeros((p, size), F32)
        for a in range(p):
            line = jnp.zeros((p, size), F32)
            for i in range(p):
                line = jnp.where(node == i, float(matrix[a, i]), line)
            tile = jnp.where(row == a, line, tile)
        whole = jnp.concatenate([tile] * (size // p), axis=0)
        same = lax.broadcasted_iota(jnp.int32, (size, size), 0) // p == (
            lax.broadcasted_iota(jnp.int32, (size, size), 1) // p
        )
        upper, lower = split(jnp.where(same, whole, 0.0))
        out[...] = jnp.concatenate([upper, upper, lower], axis=1)

    def spread_tables(self, out3, out4, square, ahead, back):
        self.block_table(self.squared.T, square)
        self.block_table(self.forward, ahead)
        self.block_table(self.forward.T, back)
        p, ey, ez = self.p, self.ey, self.ez
        for out, width, step, offset, first in (
            (out3, self.w3, self.step3, HALO, 0),
            (out4, self.w4, self.step4, 0, self.c * ey),
        ):
            row = lax.broadcasted_iota(jnp.int32, (ey * ez * p, width), 0)
            lane = lax.broadcasted_iota(jnp.int32, (1, width), 1)
            g = lane // step - offset
            inside = (g >= 0) & (g < ez) & (lax.rem(lane, step) >= first)
            same = row // p == jnp.where(inside, lax.rem(lane, ey) * ez + g, -1)
            node = lax.rem(row, p)
            for k in range(p):
                out[:, k * width : (k + 1) * width] = jnp.where(same & (node == k), 1.0, 0.0).astype(BF16)

    def prepare(self, n_x, n_y, *refs):
        geometry, viscosity, spread, table, right, slots, ids, square = refs[:8]
        s4, hot3, fields = refs[8:11]
        refs = refs[11:]
        x_out, y_out, work = refs[:n_x], refs[n_x : n_x + n_y], refs[n_x + n_y]
        p, c, block, rows, ey = self.p, self.c, self.block, self.rows, self.ey
        face = ey * p
        wjk, end_j, end_k = (table[n * face : (n + 1) * face, :] for n in range(3))
        stiff, second, third, rest = [], [], [], []
        for i in range(p):
            xx, yy, zz, xy, xz, yz = (geometry[q, i] for q in range(6))
            quadrature = float(self.weights[i]) * wjk
            weighted = quadrature * viscosity[i]
            mass = (helm_coefficient * quadrature) * (
                xx * (yy * zz - yz * yz) - xy * (xy * zz - yz * xz) + xz * (xy * yz - yy * xz)
            )
            cross = end_j * end_k * yz
            end = float(self.end[i])
            if end != 0.0:
                cross = cross + end * (end_j * xy + end_k * xz)
            entries = [weighted * entry for entry in (xx, yy, zz, xy, xz, yz)] + [mass]
            for q, entry in enumerate(entries):
                fields[q, i * face : (i + 1) * face, :] = entry
            stiff.append(entries[0])
            second.append(entries[1])
            third.append(entries[2])
            rest.append((2.0 * weighted) * cross + mass)
        upper, lower = split(jnp.concatenate(second, axis=0))
        diagonal = jnp.dot(
            square[...], jnp.concatenate([upper, lower, upper], axis=0), preferred_element_type=F32
        )
        upper, lower = split(jnp.concatenate(third, axis=0))
        diagonal = diagonal + lax.dot_general(
            jnp.concatenate([upper, lower, upper], axis=1),
            square[...],
            (((1,), (1,)), ((), ())),
            preferred_element_type=F32,
        )
        first = self.contract(stiff, self.squared.T)
        diagonal = diagonal + jnp.concatenate([x + y for x, y in zip(first, rest)], axis=0)
        width = diagonal.shape[-1]
        value = diagonal.reshape(p, ey, p, width)
        value = jnp.concatenate([value[:, f].reshape(block, width) for f in range(ey)], axis=1)

        def store(k, part):
            work[pl.ds(k, block, stride=p), :] = part

        self.by_nodes(*split(value), spread, self.w4, store)
        hot = self.one_hot(slots, ids)
        hot3[...] = self.one_hot(slots, ids[c:, :])
        total = work[...]
        for part in split(right[...].reshape(hot.shape[0], rows)):
            total = total + lax.dot_general(
                part, hot, (((0,), (0,)), ((), ())), preferred_element_type=F32
            )
        s4[...] = total
        self.fold_second(s4)
        last = self.n4 - self.step4
        self.fold_third(s4, self.step4, lambda l: l < last, lambda l: (l >= self.step4) & (l < self.n4))
        self.emit_first((s4[:block, :], s4[rows - block :, :]), x_out)
        self.emit_second(s4, y_out)

    def convert(self, n_y, n_z, *refs):
        fields, spread, dirichlet, s4 = refs[:4]
        g, ind = refs[4:6]
        refs = refs[6:]
        y_out, z_out, packed = refs[:n_y], refs[n_y : n_y + n_z], refs[n_y + n_z : n_y + 2 * n_z]
        upper, lower = refs[n_y + 2 * n_z :]
        p, c, block, ey = self.p, self.c, self.block, self.ey
        width = fields.shape[-1]
        for q in range(FIELDS):
            value = fields[q].reshape(p, ey, p, width)
            for f in range(ey):
                at = (slice(q * block, (q + 1) * block), slice(f * width, (f + 1) * width))
                upper[at], lower[at] = split(value[:, f].reshape(block, width))
        first_flag, flags = FIELDS * block, 2 * p
        for cc in range(c):
            for f in range(ey):
                at = slice(f * p, (f + 1) * p)
                face = jnp.concatenate([dirichlet[0, cc, at, :], dirichlet[1, cc, at, :]], axis=0)
                to = slice(first_flag + cc * flags, first_flag + (cc + 1) * flags)
                upper[to, f * width : (f + 1) * width] = face.astype(F32).astype(BF16)
                lower[to, f * width : (f + 1) * width] = jnp.zeros((flags, width), BF16)
        row = lax.broadcasted_iota(jnp.int32, (flags, self.w3), 0)
        lane = lax.broadcasted_iota(jnp.int32, (flags, self.w3), 1)
        ends = (lax.axis_index("gx") == 0, lax.axis_index("gx") == self.sizes["gx"] - 1)
        here = ((row < p) & ends[0]) | ((row >= p) & ends[1])
        owner = lax.rem(lane, self.step3) // ey

        def store(k, value):
            g[pl.ds(k, first_flag, stride=p), :] = value[:first_flag]
            total = jnp.zeros((flags, self.w3), F32)
            for cc in range(c):
                at = first_flag + cc * flags
                total = jnp.where(owner == cc, value[at : at + flags], total)
            ind[pl.ds(k, flags, stride=p), :] = jnp.where(here, total, 0.0)

        self.by_nodes(upper[...], lower[...], spread, self.w3, store)
        self.pack_fields(fields, z_out)
        self.fold_second(ind)
        first_own, end_own = HALO * self.step3, self.n3 - HALO * self.step3
        self.fold_third(
            ind,
            self.step3,
            lambda l: (l >= first_own) & (l < end_own - self.step3),
            lambda l: (l >= first_own + self.step3) & (l < end_own),
        )
        for out, (up, _, _) in zip(y_out, roles("gy", self.sizes["gy"])):
            for n in range(2):
                start = n * block
                out[n * p : (n + 1) * p, :] = jnp.where(
                    up, ind[start + block - p : start + block, :], ind[start : start + p, :]
                )
        for out, (up, _, _) in zip(packed, roles("gz", self.sizes["gz"])):
            self.pack(out, s4, block, 0, self.n4 - self.halo4, up, 0)
            self.pack(out, ind, p, first_own, end_own - first_own, up, block)

    def halo_fields(self, n_z, *refs):
        own, halo = refs[:2]
        z_in, g, terms = refs[2 : 2 + n_z], refs[2 + n_z], refs[3 + n_z]
        p, block, ey, part = self.p, self.block, self.ey, self.part
        sides = both_sides([z[...] for z in z_in], roles("gz", self.sizes["gz"]))
        sides = [self.unpack_fields(side) for side in sides]
        width = sides[0].shape[-1]
        sides = [side.reshape(p, ey, p, width) for side in sides]
        lane = lax.broadcasted_iota(jnp.int32, (block, width), 1)
        for q in range(FIELDS):
            value = jnp.zeros((block, width), F32)
            for side in range(2):
                for f in range(ey):
                    to = (side * ey + f) * part
                    shift = (to - q * part) % width
                    x = sides[side][:, f].reshape(block, width)
                    x = pltpu.roll(x, shift, 1) if shift else x
                    value = jnp.where((lane >= to) & (lane < to + part), x, value)
            upper, lower = split(value)
            lower = pltpu.roll(lower.astype(F32), width // 2, 1).astype(BF16)
            terms[q * block : (q + 1) * block, :] = upper + lower

        for k in range(0, p, 2):
            columns = halo[:, k * self.w3 : (k + 2) * self.w3]
            both = jnp.dot(terms[...], columns, preferred_element_type=F32)
            for n in range(2):
                at = pl.ds(k + n, FIELDS * block, stride=p)
                g[at, :] = own[at, :] + both[:, n * self.w3 : (n + 1) * self.w3]

    def coefficients(self, low, high, coef):
        top, bottom = jnp.full((8, 128), high[0], F32), jnp.full((8, 128), low[0], F32)
        midpoint, halfwidth = (top + bottom) * 0.5, (top - bottom) * 0.5
        ratio = midpoint / halfwidth
        damping = 1.0 / ratio
        coef[0:8, :] = 1.0 / midpoint
        for n in range(ITERS - 1):
            following = 1.0 / (2.0 * ratio - damping)
            coef[8 * (2 * n + 1) : 8 * (2 * n + 2), :] = following * damping
            coef[8 * (2 * n + 2) : 8 * (2 * n + 3), :] = 2.0 * following / halfwidth
            damping = following

    def join(self, n_x, n_y, *refs):
        x_in, refs = refs[:n_x], refs[n_x:]
        y_raw, y_more, y_out = refs[:n_y], refs[n_y:-n_y], refs[-n_y:]
        p, block, ey = self.p, self.block, self.ey
        low, high = both_sides([x[...] for x in x_in], roles("gx", self.sizes["gx"]))
        for n, (up, _, _) in enumerate(roles("gy", self.sizes["gy"])):
            face = y_raw[n][...]
            width = face.shape[-1]
            if n_x:
                first, last = (jnp.where(up, x[block - p :], x[:p]) for x in (low, high))
                face = jnp.concatenate([face[:p] + first, face[p : block - p], face[block - p :] + last], axis=0)
            if y_more:
                face = jnp.concatenate([face, y_more[n][...]], axis=0)
            if ey == 1:
                y_out[n][...] = face
                continue
            half = face.shape[0] // 2
            first, second = face[:half], face[half:]
            f = lax.rem(lax.broadcasted_iota(jnp.int32, first.shape, 1), ey)
            below = jnp.where(f == 0, pltpu.roll(first, width - (ey - 1), 1), 0.0) + jnp.where(
                f == 1, pltpu.roll(second, (width - (ey - 2)) % width, 1) if ey != 2 else second, 0.0
            )
            above = jnp.where(f == ey - 1, pltpu.roll(first, ey - 1, 1), 0.0) + jnp.where(
                f == ey - 2, pltpu.roll(second, ey - 2, 1) if ey != 2 else second, 0.0
            )
            y_out[n][...] = jnp.where(up, below, above)

    def second_sides(self, received):
        role, ey = roles("gy", self.sizes["gy"]), self.ey
        faces = []
        for message, (_, from_high, _) in zip(received, role):
            data = message[...]
            if ey > 1:
                width = data.shape[-1]
                f = lax.rem(lax.broadcasted_iota(jnp.int32, data.shape, 1), ey)
                beside = jnp.where(from_high, pltpu.roll(data, 1, 1), pltpu.roll(data, width - 1, 1))
                here = f == jnp.where(from_high, ey - 1, 0)
                data = jnp.concatenate([jnp.where(here, x, 0.0) for x in (data, beside)], axis=0)
            faces.append(data)
        return both_sides(faces, role)

    def pack(self, out, u, count, first, last, up, start):
        p, width, size = self.p, self.w4, self.halo4
        lane = lax.broadcasted_iota(jnp.int32, (count, width), 1)
        for section in range(0, u.shape[0] // count, p):
            total = jnp.zeros((count, width), F32)
            for n in range(p):
                at, shift = (section + n) * count, n * size
                x = u[at : at + count, :]
                below = pltpu.roll(x, (shift - first) % width, 1) if (shift - first) % width else x
                above = pltpu.roll(x, (shift - last) % width, 1)
                here = (lane >= shift) & (lane < shift + size)
                total = jnp.where(here, jnp.where(up, above, below), total)
            row = start + section // p * count
            out[row : row + count, :] = total

    def pack_second(self, n_x, n_y, n_z, *refs):
        x_in, y_in, refs = refs[:n_x], refs[n_x : n_x + n_y], refs[n_x + n_y :]
        z_in, z_out = refs[:n_z], refs[n_z:]
        p, block, width, size = self.p, self.block, self.w4, self.halo4
        ends = both_sides([x[...] for x in x_in], roles("gx", self.sizes["gx"]))
        low, high = self.second_sides(y_in)
        halo3 = HALO * self.step3
        lane = lax.broadcasted_iota(jnp.int32, (p, width), 1)
        for packed, out, (up, _, _) in zip(z_in, z_out, roles("gz", self.sizes["gz"])):
            out[...] = packed[...]
            if n_x:
                total = 0.0
                for x, group in zip(ends, (0, p - 1)):
                    shift = group * size
                    below = pltpu.roll(x, shift, 1) if shift else x
                    back = (shift - self.n4 + size) % width
                    above = pltpu.roll(x, back, 1) if back else x
                    wide = lax.broadcasted_iota(jnp.int32, x.shape, 1)
                    here = (wide >= shift) & (wide < shift + size)
                    total = total + jnp.where(here, jnp.where(up, above, below), 0.0)
                out[:block, :] += total
            if not n_y:
                continue
            for face, row in ((low, 0), (high, block - p)):
                total = jnp.zeros((p, width), F32)
                for n in range(p):
                    shift = n * size
                    x = face[n * p : (n + 1) * p]
                    below = pltpu.roll(x, shift, 1) if shift else x
                    above = pltpu.roll(x, (shift - self.n4 + size) % width, 1)
                    here = (lane >= shift) & (lane < shift + size)
                    total = jnp.where(here, jnp.where(up, above, below), total)
                out[row : row + p, :] += total
            for n in range(2):
                row = block + n * p
                for face, group in ((low, 0), (high, p - 1)):
                    shift = group * size
                    x = face[row : row + p]
                    below = pltpu.roll(x, (shift - halo3) % width, 1)
                    above = pltpu.roll(x, (shift - self.n3 + 2 * halo3) % width, 1)
                    here = (lane >= shift) & (lane < shift + size)
                    out[row : row + p, :] += jnp.where(here, jnp.where(up, above, below), 0.0)

    def own(self, n_x, n_y, *refs):
        s4, ind, widen = refs[:3]
        x_in, y_in, (r, scale, flag, work) = refs[3 : 3 + n_x], refs[3 + n_x : 3 + n_x + n_y], refs[3 + n_x + n_y :]
        p, block, rows, w3 = self.p, self.block, self.rows, self.w3
        work[...] = s4[...]
        if n_x:
            low, high = both_sides([x[...] for x in x_in], roles("gx", self.sizes["gx"]))
            work[:block, :] += low
            work[rows - block :, :] += high
        flag[...] = ind[...]
        if n_y:
            low, high = self.second_sides(y_in)
            for u, first, count in ((work, 0, p), (flag, p, 2)):
                for i in range(count):
                    at, end, row = i * block, (i + 1) * block, (first + i) * p
                    u[at : at + p, :] += low[row : row + p]
                    u[end - p : end, :] += high[row : row + p]
        both = dot2(work[...], widen[: self.w4, :])
        r[...] = both[:, :w3]
        scale[...] = both[:, w3:]

    def start(self, n_x, n_z, *refs):
        r_own, diagonal_own, flag_own, g, widen, ahead, back = refs[:7]
        z_in = refs[7 : 7 + n_z]
        t, scale, ends, f1, f2, f3 = refs[7 + n_z : 13 + n_z]
        x_out, refs = refs[13 + n_z : 13 + n_z + n_x], refs[13 + n_z + n_x :]
        beside, r, flag, slope, third = refs
        p, block, rows, w3, w4 = self.p, self.block, self.rows, self.w3, self.w4
        step, first_own, end_own = self.step3, HALO * self.step3, self.n3 - HALO * self.step3
        size, part = self.sizes["gz"], self.halo4
        if n_z:
            low, high = both_sides([z[...] for z in z_in], roles("gz", size))
        else:
            low = high = jnp.zeros((block + 2 * p, w4), F32)
        lane = lax.broadcasted_iota(jnp.int32, (block, w4), 1)
        for n in range(p):
            first = pltpu.roll(low[:block], w4 - n * part, 1) if n else low[:block]
            second = pltpu.roll(high[:block], (part - n * part) % w4, 1) if n != 1 else high[:block]
            beside[n * block : (n + 1) * block, :] = jnp.where(
                lane < part, first, jnp.where(lane < 2 * part, second, 0.0)
            )
        both = dot2(beside[...], widen[w4:, :])
        r[...] = r_own[...] + both[:, :w3]
        scale[...] = diagonal_own[...] + both[:, w3:]
        lane = lax.broadcasted_iota(jnp.int32, (p, w3), 1)
        for n in range(2 * p):
            row, shift = block + n // p * p, n % p * part
            first = pltpu.roll(low[row : row + p], w3 - shift, 1) if shift else low[row : row + p]
            second = pltpu.roll(high[row : row + p], (end_own - shift) % w3, 1)
            flag[n * p : (n + 1) * p, :] = jnp.where(
                lane < first_own,
                first,
                jnp.where(lane < end_own, flag_own[n * p : (n + 1) * p, :], jnp.where(lane < self.n3, second, 0.0)),
            )
        for u in (r, scale, flag):
            self.fold_third(
                u,
                step,
                lambda l: ((l >= first_own - step) & (l < first_own)) | ((l >= end_own - step) & (l < end_own)),
                lambda l: ((l >= first_own) & (l < first_own + step)) | ((l >= end_own) & (l < end_own + step)),
            )
        index = lax.axis_index("gz")
        begin = jnp.where(index > 0, 0, first_own)
        end = jnp.where(index < size - 1, self.n3, end_own)
        lane = lax.broadcasted_iota(jnp.int32, (block, w3), 1)
        valid = (lane >= begin) & (lane < end)
        for i in range(p):
            at = slice(i * block, (i + 1) * block)
            factor = jnp.where(valid, 1.0 / jnp.where(valid, scale[at, :], 1.0), 0.0)
            if i in (0, p - 1):
                row = 0 if i == 0 else block
                factor = jnp.where(flag[row : row + block, :] > 0.5, 0.0, factor)
            scale[at, :] = factor
            t[at, :] = factor * r[at, :]
        self.fluxes(t, g, f1, f2, f3, slope, third, ahead)
        self.end_planes(t, g, ends, f1, f2, f3, slope, third, back)
        self.iteration_fold(ends)
        self.emit_first((ends[:block, :], ends[block:, :]), x_out)

    def factors(self, coef, n):
        rows = [coef[8 * m : 8 * m + 1, :] for m in (0, 2 * n + 1, 2 * n + 2)]
        return (rows[0] if n == 0 else None), rows[1], rows[2]

    def shares(self, faces, scale, image, at):
        low, high = faces
        p, block = self.p, self.block
        i = at // block
        out = []
        for start, face in ((at, low), (at + block - p, high)):
            value = scale[start : start + p, :] * face[i * p : (i + 1) * p]
            out.append((start, -value if image is None else -image * value))
        return out

    def preview(self, n_x, n_y, n, last, *refs):
        t, t_old, d, scale, v, coef = refs[:6]
        refs = refs[6:]
        x_in, y_old, refs = refs[:n_x], refs[n_x : n_x + (n_y if n else 0)], refs[n_x + (n_y if n else 0) :]
        p, block, rows = self.p, self.block, self.rows
        image, keep, gain = self.factors(coef, n)
        start = coef[0:1, :]
        if last:
            hot, out, t_new, field = refs
        else:
            g, ahead, back, t_new, d_new, f1, f2, f3, ends, slope, third = refs
        low, high = both_sides([x[...] for x in x_in], roles("gx", self.sizes["gx"]))
        if n:
            faces = self.second_sides(y_old) if n_y else None
            image_old = self.factors(coef, n - 1)[0]
        for i in range(p):
            at = slice(i * block, (i + 1) * block)
            value = v[at, :]
            if n_x and i in (0, p - 1):
                value = value + (low if i == 0 else high)
            value = scale[at, :] * value
            t_new[at, :] = t_old[at, :] - (value if image is None else image * value)
            if n and n_y:
                for row, share in self.shares(faces, scale, image_old, i * block):
                    t_new[row : row + p, :] += share
            direction = d[at, :] if n else start * t[at, :]
            following = keep * direction + gain * t_new[at, :]
            if last:
                field[at, :] = start * t[at, :] + following + (direction if n else 0.0)
            else:
                d_new[at, :] = following
        if last:
            out[...] = self.by_slots(hot, field[...])
        else:
            self.fluxes(d_new, g, f1, f2, f3, slope, third, ahead)
            self.end_planes(d_new, g, ends, f1, f2, f3, slope, third, back)

    def by_slots(self, hot, field):
        return lax.dot_general(
            jnp.concatenate([hot[...], hot[...]], axis=1),
            jnp.concatenate(split(field), axis=1),
            (((1,), (1,)), ((), ())),
            preferred_element_type=F32,
        )

    def middle(self, n_x, n_y, n, *refs):
        part, scale, g, coef, ahead, back = refs[:6]
        y_in, refs = refs[6 : 6 + n_y], refs[6 + n_y :]
        ends, shares, refs = refs[0], refs[1], refs[2:]
        x_out, (f1, f2, f3, third) = refs[:n_x], refs[n_x:]
        p, block, rows = self.p, self.block, self.rows
        image, _, gain = self.factors(coef, n)
        ends[...] = part[...]
        if n_y:
            faces = self.second_sides(y_in)
            for i in range(p):
                for m, (_, share) in enumerate(self.shares(faces, scale, image, i * block)):
                    shares[(2 * i + m) * p : (2 * i + m + 1) * p, :] = gain * share

            def write(i, j, values):
                f1[i * block + j * p : i * block + (j + 1) * p, :] = values[0]
                if len(values) > 1:
                    row = (block if i else 0) + j * p
                    f2[row : row + p, :], f3[row : row + p, :] = values[1], values[2]

            self.share_fluxes(shares, g, third, ahead, False, write)
            self.along_k(f3, back, third, 0, 2 * block)
            for m, i in enumerate((0, p - 1)):
                at = slice(m * block, (m + 1) * block)
                ends[at, :] += self.along_j(f2[at, :], self.forward.T) + third[at, :]
                for n_face, j in enumerate((0, p - 1)):
                    row, at = m * block + j * p, slice(i * block + j * p, i * block + (j + 1) * p)
                    line = (2 * i + n_face) * p
                    ends[row : row + p, :] += self.rows_of(g, 6, at) * shares[line : line + p, :]
            for j in range(p):
                x = [f1[i * block + j * p : i * block + (j + 1) * p, :] for i in range(p)]
                for row, value in zip((j * p, block + j * p), self.contract(x, self.forward.T, (0,))):
                    ends[row : row + p, :] += value
        else:
            shares[...] = jnp.zeros(shares.shape, F32)
        self.iteration_fold(ends)
        self.emit_first((ends[:block, :], ends[block:, :]), x_out)

    def finish(self, n_y, n, *refs):
        part, scale, coef, hot = refs[:4]
        y_in, (out, field) = refs[4 : 4 + n_y], refs[4 + n_y :]
        value = part[...]
        image, _, gain = self.factors(coef, n)
        if n_y:
            faces = self.second_sides(y_in)
            field[...] = jnp.zeros(field.shape, F32)
            for i in range(self.p):
                for row, share in self.shares(faces, scale, image, i * self.block):
                    field[row : row + self.p, :] = gain * share
            value = value + self.by_slots(hot, field[...])
        out[...] = value.reshape(out.shape)


def shards(sizes, right_side, geometry, viscosity, eig_low, eig_high, element_slot, dirichlet):
    plan = Plan(right_side.shape[0], viscosity.shape, sizes)
    p, block, rows, w3, w4 = plan.p, plan.block, plan.rows, plan.w3, plan.w4
    x_pairs = pairings(("gx",), (sizes["gx"],), 0)
    y_pairs = pairings(("gy",), (sizes["gy"],), 0)
    z_pairs = pairings(("gx", "gz"), (sizes["gx"], sizes["gz"]), 1)
    n_x, n_y, n_z = len(x_pairs), len(y_pairs), len(z_pairs)

    def send(arrays, axis, pairs):
        return [lax.ppermute(x, axis, pair) for x, pair in zip(arrays, pairs)]

    def shape(*size, dtype=F32):
        return jax.ShapeDtypeStruct(size, dtype)

    def call(kernel, outputs, operands, scratch=(), spaces={}, flops=0, name=None):
        specs = [pl.BlockSpec(memory_space=spaces.get(n, pltpu.VMEM)) for n in range(len(operands))]
        return list(
            pl.pallas_call(
                kernel,
                out_shape=list(outputs),
                in_specs=specs,
                out_specs=[pl.BlockSpec(memory_space=pltpu.VMEM)] * len(outputs),
                scratch_shapes=list(scratch),
                compiler_params=pltpu.CompilerParams(vmem_limit_bytes=VMEM_BYTES),
                cost_estimate=pl.CostEstimate(flops=flops, bytes_accessed=0, transcendentals=0),
                name=name,
            )(*operands)
        )

    def vmem(*size, dtype=F32):
        return pltpu.VMEM(size, dtype)

    lanes = plan.ez * p
    field3, field4 = shape(rows, w3), shape(rows, w4)
    elements = element_slot.shape[-1]
    spread3, spread4, square, ahead, back = call(
        plan.spread_tables,
        [shape(plan.ey * lanes, p * w, dtype=BF16) for w in (w3, w4)]
        + [shape(*plan.third[0].shape, dtype=BF16)] * 3,
        (),
        flops=FLOPS,
        name="spread_tables",
    )
    results = call(
        functools.partial(plan.prepare, n_x, n_y),
        [field4, shape(plan.c * elements, w3, dtype=BF16), shape(FIELDS, p * plan.ey * p, lanes)]
        + [shape(block, w4)] * (n_x + n_y),
        (
            geometry,
            viscosity,
            spread4,
            jnp.asarray(plan.face_table),
            jnp.swapaxes(right_side, 1, 2),
            element_slot,
            jnp.asarray(plan.ids),
            square,
        ),
        scratch=[vmem(rows, w4)],
        name="prepare",
    )
    s4, hot3, fields = results[:3]
    x_out, y_raw = results[3 : 3 + n_x], results[3 + n_x :]
    x_in = send(x_out, "gx", x_pairs)

    lhs = FIELDS * block + 2 * plan.c * p
    results = call(
        functools.partial(plan.convert, n_y, n_z),
        [shape(FIELDS * rows, w3), shape(2 * block, w3)]
        + [shape(2 * p, w3)] * n_y
        + [shape(FIELDS * plan.part, lanes)] * n_z
        + [shape(block + 2 * p, w4)] * n_z,
        (fields, spread3, dirichlet, s4),
        scratch=[vmem(lhs, plan.ey * lanes, dtype=BF16)] * 2,
        name="convert",
    )
    g, ind = results[:2]
    y_more, results = results[2 : 2 + n_y], results[2 + n_y :]
    z_fields, z_out = results[:n_z], results[n_z:]

    def joined(x_in, y_raw, y_more=()):
        if not y_raw:
            return []
        count = y_raw[0].shape[0] + (y_more[0].shape[0] if y_more else 0)
        faces = [shape(count // 2 if plan.ey > 1 else count, y.shape[1]) for y in y_raw]
        return call(functools.partial(plan.join, n_x, n_y), faces, x_in + y_raw + list(y_more), name="join")

    y_in = send(joined(x_in, y_raw, y_more), "gy", y_pairs)
    z_fields = send(z_fields, ("gx", "gz"), z_pairs)
    if n_z:
        g = call(
            functools.partial(plan.halo_fields, n_z),
            [shape(FIELDS * rows, w3)],
            [g, jnp.asarray(plan.halo)] + z_fields,
            scratch=[vmem(FIELDS * block, lanes, dtype=BF16)],
            name="halo_fields",
        )[0]
    if n_z:
        z_out = call(
            functools.partial(plan.pack_second, n_x, n_y, n_z),
            [shape(*z.shape) for z in z_out],
            x_in + y_in + z_out,
            flops=FLOPS,
            name="pack_second",
        )
    z_in = send(z_out, ("gx", "gz"), z_pairs)
    widen = jnp.asarray(plan.widen)
    own = call(
        functools.partial(plan.own, n_x, n_y),
        [field3, field3, shape(2 * block, w3)],
        [s4, ind, widen] + x_in + y_in,
        scratch=[vmem(rows, w4)],
        name="own",
    )

    fluxes = [shape(2 * block, w3)] + [field3] * 3 + [shape(block, w3)] * n_x
    results = call(
        functools.partial(plan.start, n_x, n_z),
        [field3] * 2 + fluxes,
        own + [g, widen, ahead, back] + z_in,
        scratch=[vmem(rows, w4), vmem(rows, w3), vmem(2 * block, w3)] + [vmem(rows, w3)] * 2,
        name="first_direction",
    )
    t, scale = results[:2]
    ends, f1, f2, f3 = results[2:6]
    x_out = results[6:]
    x_out, low, high = lax.optimization_barrier((x_out, eig_low, eig_high))
    coef = call(
        plan.coefficients,
        [shape(8 * (2 * ITERS - 1), 128)],
        (low, high),
        spaces={0: pltpu.SMEM, 1: pltpu.SMEM},
        name="coefficients",
    )[0]
    t_old, d, y_in = t, t, []
    for n in range(ITERS - 1):
        last = n == ITERS - 2
        x_in = send(x_out, "gx", x_pairs)
        outputs = [field3] + [shape(block, w3)] * n_y
        if n:
            results = call(
                functools.partial(plan.operator_second, n_x, n_y, True),
                outputs + [field3],
                [d, g, ends, f1, f2, f3, back, shares, ahead],
                scratch=[vmem(rows, w3)] * 4,
                name="operator_second",
            )
            v, y_raw, d = results[0], results[1 : 1 + n_y], results[1 + n_y]
        else:
            results = call(
                functools.partial(plan.operator_second, n_x, n_y, False),
                outputs,
                [d, g, ends, f1, f2, f3, back],
                scratch=[vmem(rows, w3)],
                name="operator_second",
            )
            v, y_raw = results[0], results[1:]
        y_old, y_in = y_in, send(joined(x_in, y_raw), "gy", y_pairs)
        results = call(
            functools.partial(plan.preview, n_x, n_y, n, last),
            [shape(plan.c * elements, rows)] if last else [field3] * 5 + [shape(2 * block, w3)],
            [t, t_old, d, scale, v, coef] + x_in + y_old + ([hot3] if last else [g, ahead, back]),
            scratch=[vmem(rows, w3)] * 2,
            name="preview",
        )
        if last:
            break
        t_old, d, f1, f2, f3, ends = results
        results = call(
            functools.partial(plan.middle, n_x, n_y, n),
            [shape(2 * block, w3)] * 2 + [shape(block, w3)] * n_x,
            [ends, scale, g, coef, ahead, back] + y_in,
            scratch=[vmem(rows, w3)] + [vmem(2 * block, w3)] * 3,
            name="direction",
        )
        ends, shares, x_out = results[0], results[1], results[2:]
    out = call(
        functools.partial(plan.finish, n_y, n),
        [shape(plan.c, elements, rows)],
        [results[0], scale, coef, hot3] + y_in,
        scratch=[vmem(rows, w3)],
        name="field",
    )[0]
    return jnp.swapaxes(out, 1, 2)


def solution(mesh):
    sizes = {name: mesh.shape[name] for name in ("gx", "gy", "gz")}
    return jax.shard_map(
        functools.partial(shards, sizes),
        mesh=mesh,
        in_specs=(
            P(None, None, ("gx", "gy", "gz")),
            P(None, "gx", "gy", "gz"),
            P("gx", "gy", "gz"),
            P(),
            P(),
            P(("gx", "gy", "gz"), None),
            P(None, None, "gy", "gz"),
        ),
        out_specs=P(None, None, ("gx", "gy", "gz")),
        check_vma=False,
    )
```
